32 devices in a mesh: section: 4 (over x, core), batch: 8 (over z, y).
Axes of the slice: x: 2, y: 2, z: 4, core: 2. Of those that a mesh axis runs over, the one named last changes fastest.
Arguments:
- char_ids: int32 [3072, 50], P(('section', 'batch')), may hold values from 0 to 261
- word_lengths: int32 [3072], P(('section', 'batch')), may hold values from 1 to 50, as said below
- params: bfloat16 [4, 18366464], P('section'), may hold values from -6 to 6
- cotangent: bfloat16 [3072, 768], P(('section', 'batch')), may hold values from -6 to 6
Outputs:
- layer_out: bfloat16 [3072, 768], P(('section', 'batch'))
- param_grads: float32 [4, 18366464], P('section', 'batch')
The draws below stay inside these ranges and needn't reach their ends.
Inputs may be any that keep to these rules, and one draw needn't show every extreme that they name: `word_lengths`: word lengths are heavy-tailed; in every draw some word has 50 characters and some word has 1.
All inputs are finite; a program needn't handle non-finite values.
Results may differ from the reference program's by a relative error of at most 0.011.
Values may be sent and summed in bfloat16 or wider, within the bound.
A program may use at most 704 MiB of HBM per device.

```python
import math
from functools import partial
import jax
import jax.numpy as jnp
from jax import lax

D = 768
HEADS = 12
HEAD_DIM = 64
FF = 3072
CHAR_DIM = 16
CHARS = 262
CHAR_LEN = 50
CH_UNIT = 32
SEQ_LEN = 192
GROUP_WORDS = 384
WORDS = 3072
PARAMS = 18366464
N_SECTION = 4
N_BATCH = 8


channel_steps = (1, 1, 2, 4, 8, 16, 32)


def layouts_drawn():
    conv_width = 64 * CH_UNIT
    char_part = [('table', (CHARS, CHAR_DIM))]
    for number in range(7):
        char_part.append(('filter' + str(number), (number + 1, CHAR_DIM, channel_steps[number] * CH_UNIT)))
    char_part.append(('conv_bias', (conv_width,)))
    highway_part = [('hw_weight0', (conv_width, 2 * conv_width)), ('hw_bias0', (2 * conv_width,)), ('hw_weight1', (conv_width, 2 * conv_width)), ('hw_bias1', (2 * conv_width,)), ('proj_weight', (conv_width, D)), ('proj_bias', (D,))]
    attention_part = [('qkv_weight', (D, 3 * D)), ('query_bias', (D,)), ('value_bias', (D,)), ('out_weight', (D, D)), ('out_bias', (D,)), ('norm_gain1', (D,)), ('norm_shift1', (D,))]
    ffn_part = [('up_weight', (D, FF)), ('up_bias', (FF,)), ('down_weight', (FF, D)), ('down_bias', (D,)), ('norm_gain2', (D,)), ('norm_shift2', (D,))]
    return [char_part, highway_part, attention_part, ffn_part]


def entry_law(entry_name, entry_shape):
    if entry_name == 'table':
        return (1.0, 0.0)
    if entry_name[:9] == 'norm_gain':
        return (0.1, 1.0)
    if len(entry_shape) == 1:
        return (0.1, 0.0)
    if entry_name == 'qkv_weight':
        return ((2.0 * D) ** (-0.5), 0.0)
    if entry_name == 'out_weight':
        return (float(max(D // 64, 1)) ** (-0.5), 0.0)
    return (float(math.prod(entry_shape[:-1])) ** (-0.5), 0.0)


def draw_params(key, part):
    bounds = []
    scales = []
    centers = []
    for row_number, layout in enumerate(layouts_drawn()):
        offset = row_number * PARAMS
        for entry_name, entry_shape in layout:
            entry_scale, entry_center = entry_law(entry_name, entry_shape)
            bounds.append(offset)
            scales.append(entry_scale)
            centers.append(entry_center)
            offset += math.prod(entry_shape)
        bounds.append(offset)
        scales.append(1.0)
        centers.append(0.0)
    total_size = N_SECTION * PARAMS
    seg_index = jnp.searchsorted(jnp.array(bounds, jnp.int32), jnp.arange(total_size, dtype=jnp.int32), side='right') - 1
    base_noise = jax.random.truncated_normal(key, -6.0, 6.0, (total_size,), jnp.float32)
    values = jnp.array(centers, jnp.float32)[seg_index] + jnp.array(scales, jnp.float32)[seg_index] * base_noise
    return values.reshape(N_SECTION, PARAMS).astype(jnp.bfloat16)


def draw_word_lengths(key, part):
    first_key, second_key = jax.random.split(key)
    base_len = jax.random.randint(first_key, (WORDS,), 1, 9)
    divisor = jax.random.randint(second_key, (WORDS,), 1, 257)
    tail_len = 64 // divisor
    lengths_out = jnp.minimum(base_len + tail_len, CHAR_LEN)
    lengths_out = lengths_out.at[0].set(CHAR_LEN).at[1].set(1)
    return lengths_out.astype(jnp.int32)


def with_ends(drawn, stream_key, smallest, largest):
    longest = drawn.shape.index(max(drawn.shape))
    spots = []
    for shift in (0, 1):
        where = [jax.random.randint(jax.random.fold_in(stream_key, axis), (), 0, length) for axis, length in enumerate(drawn.shape)]
        where[longest] = (where[longest] + shift) % drawn.shape[longest]
        spots.append(tuple(where))
    return drawn.at[spots[0]].set(smallest).at[spots[1]].set(largest)


def levels(rng, extent, cuts, smallest, high):
    loudness = 1.0
    for axis_at, shards_of in cuts:
        draws = jax.random.uniform(jax.random.fold_in(jax.random.fold_in(rng, 6), axis_at), (shards_of,), jnp.float32, smallest / len(cuts), high / len(cuts))
        loudness = loudness * jnp.repeat(jnp.exp(draws), extent[axis_at] // shards_of).reshape((-1,) + (1,) * (len(extent) - 1 - axis_at))
    return loudness


def noise(rng, dims, scale, limit, cuts=(), kind=jnp.bfloat16):
    entries = scale * jax.random.normal(rng, dims, jnp.float32)
    if cuts:
        entries = entries * levels(rng, dims, cuts, -0.22, 0.18)
    return jnp.clip(entries, -limit, limit).astype(kind)


def setup_inputs(seed: int = 0) -> dict:
    seeds = jax.random.split(jax.random.key(seed), 5)
    char_ids = with_ends(jax.random.randint(seeds[0], (WORDS, CHAR_LEN), 0, CHARS), jax.random.fold_in(seeds[0], 1), 0, CHARS - 1).astype(jnp.int32)
    word_lengths = draw_word_lengths(jax.random.fold_in(seeds[4], 71), 0)
    params = draw_params(jax.random.fold_in(seeds[4], 71), 0)
    cotangent = noise(seeds[3], (WORDS, D), 1.0, 6.0, ((0, 32),))
    return dict(char_ids=char_ids, word_lengths=word_lengths, params=params, cotangent=cotangent)


@jax.custom_vjp
def low(v):
    return lax.optimization_barrier(v.astype(jnp.bfloat16)).astype(jnp.float32)

@jax.custom_vjp
def low_back(v):
    return v

def low_keep(v):
    return (low(v), None)

def low_pass(kept, grad):
    return (grad,)

def back_keep(v):
    return (v, None)

def back_low(kept, grad):
    return (low(grad),)
low.defvjp(low_keep, low_pass)
low_back.defvjp(back_keep, back_low)
channel_steps = (1, 1, 2, 4, 8, 16, 32)
layer_eps = 1e-12

def layouts():
    conv_width = 64 * CH_UNIT
    char_part = [('table', (CHARS, CHAR_DIM))]
    for number in range(7):
        char_part.append(('filter' + str(number), (number + 1, CHAR_DIM, channel_steps[number] * CH_UNIT)))
    char_part.append(('conv_bias', (conv_width,)))
    highway_part = [('hw_weight0', (conv_width, 2 * conv_width)), ('hw_bias0', (2 * conv_width,)), ('hw_weight1', (conv_width, 2 * conv_width)), ('hw_bias1', (2 * conv_width,)), ('proj_weight', (conv_width, D)), ('proj_bias', (D,))]
    attention_part = [('qkv_weight', (D, 3 * D)), ('query_bias', (D,)), ('value_bias', (D,)), ('out_weight', (D, D)), ('out_bias', (D,)), ('norm_gain1', (D,)), ('norm_shift1', (D,))]
    ffn_part = [('up_weight', (D, FF)), ('up_bias', (FF,)), ('down_weight', (FF, D)), ('down_bias', (D,)), ('norm_gain2', (D,)), ('norm_shift2', (D,))]
    return [char_part, highway_part, attention_part, ffn_part]

def carve(flat_row, layout):
    pieces = {}
    offset = 0
    for entry_name, entry_shape in layout:
        entry_size = math.prod(entry_shape)
        pieces[entry_name] = flat_row[offset:offset + entry_size].reshape(entry_shape)
        offset += entry_size
    return pieces

def matmul(left_in, right_in):
    return jnp.dot(left_in, right_in, precision=lax.Precision.HIGHEST, preferred_element_type=jnp.float32)

def layer_norm(residual, norm_gain, norm_shift):
    centered = residual - lax.optimization_barrier(jnp.mean(residual, axis=-1, keepdims=True))
    inverse = lax.rsqrt(lax.optimization_barrier(jnp.mean(centered * centered, axis=-1, keepdims=True)) + layer_eps)
    return centered * inverse * norm_gain + norm_shift

def char_block(weights, pair_in):
    ids_block, length_block = pair_in
    embedded = low_back(jnp.take(weights['table'], ids_block, axis=0))
    positions = jnp.arange(CHAR_LEN, dtype=jnp.int32)
    pooled = []
    offset = 0
    for number in range(7):
        width_k = number + 1
        channels = channel_steps[number] * CH_UNIT
        kernel = weights['filter' + str(number)]
        spot_count = CHAR_LEN - number
        conv_sum = jnp.zeros((ids_block.shape[0], spot_count, channels), jnp.float32)
        for shift_by in range(width_k):
            conv_sum = conv_sum + jnp.einsum('wpd,dc->wpc', embedded[:, shift_by:shift_by + spot_count], kernel[shift_by], precision=lax.Precision.HIGHEST)
        pre_act = low_back(conv_sum + weights['conv_bias'][offset:offset + channels])
        is_valid = positions[:spot_count][None, :, None] + width_k <= length_block.astype(jnp.int32)[:, None, None]
        masked = jnp.where(is_valid, jnp.maximum(pre_act, 0.0), 0.0)
        pooled.append(lax.optimization_barrier(jnp.max(masked, axis=1)))
        offset += channels
    return low(jnp.concatenate(pooled, axis=1))

def highway_part(weights, pooled):
    layer_in = low_back(pooled)
    for number in range(2):
        projection = low_back(matmul(layer_in, weights['hw_weight' + str(number)]) + weights['hw_bias' + str(number)])
        half_width = projection.shape[1] // 2
        gate_open = jax.nn.sigmoid(projection[:, half_width:])
        layer_in = low(gate_open * layer_in + (1.0 - gate_open) * jnp.maximum(projection[:, :half_width], 0.0))
    return low(matmul(layer_in, weights['proj_weight']) + weights['proj_bias'])

def attention_part(weights, narrow_in):
    hidden = low_back(low(narrow_in))
    joined = matmul(hidden, weights['qkv_weight'])
    query_rows = low_back(low(joined[:, :D] + weights['query_bias']))
    key_rows = low_back(low(joined[:, D:2 * D]))
    value_rows = low_back(low(joined[:, 2 * D:] + weights['value_bias']))
    query_heads = query_rows.reshape(SEQ_LEN, HEADS, HEAD_DIM)
    key_heads = key_rows.reshape(SEQ_LEN, HEADS, HEAD_DIM)
    value_heads = value_rows.reshape(SEQ_LEN, HEADS, HEAD_DIM)
    scores = low_back(jnp.einsum('qhd,khd->hqk', query_heads, key_heads, precision=lax.Precision.HIGHEST) * HEAD_DIM ** (-0.5))
    row_max = lax.optimization_barrier(jnp.max(scores, axis=-1, keepdims=True))
    exponent = jnp.exp(scores - row_max)
    softmax_out = low(exponent / lax.optimization_barrier(jnp.sum(exponent, axis=-1, keepdims=True)))
    mixed_heads = low_back(low(jnp.einsum('hqk,khd->qhd', softmax_out, value_heads, precision=lax.Precision.HIGHEST).reshape(SEQ_LEN, D)))
    attended = low_back(matmul(mixed_heads, weights['out_weight']) + weights['out_bias'])
    return layer_norm(hidden + attended, weights['norm_gain1'], weights['norm_shift1'])

def ffn_part(weights, narrow_in):
    inputs_low = low_back(low(narrow_in))
    inner_act = low_back(matmul(inputs_low, weights['up_weight']) + weights['up_bias'])
    activated = low(jax.nn.gelu(inner_act, approximate=False))
    branch = low_back(matmul(activated, weights['down_weight']) + weights['down_bias'])
    return layer_norm(inputs_low + branch, weights['norm_gain2'], weights['norm_shift2'])

def encode(section_parts, ids_seq, length_seq):
    word_block = math.gcd(SEQ_LEN, 64)
    pooled = lax.map(jax.checkpoint(partial(char_block, section_parts[0])), (ids_seq.reshape(-1, word_block, CHAR_LEN), length_seq.reshape(-1, word_block)))
    pooled = pooled.reshape(SEQ_LEN, 64 * CH_UNIT)
    projected = highway_part(section_parts[1], pooled)
    normed = attention_part(section_parts[2], projected)
    return ffn_part(section_parts[3], normed)

def arrange(array_in):
    quarter = GROUP_WORDS // N_SECTION
    shaped = array_in.reshape((N_SECTION, N_BATCH, quarter) + array_in.shape[1:])
    shaped = jnp.swapaxes(shaped, 0, 1)
    return shaped.reshape((N_BATCH * GROUP_WORDS // SEQ_LEN, SEQ_LEN) + array_in.shape[1:])

def restore(array_in):
    quarter = GROUP_WORDS // N_SECTION
    shaped = array_in.reshape((N_BATCH, N_SECTION, quarter) + array_in.shape[2:])
    return jnp.swapaxes(shaped, 0, 1).reshape((WORDS,) + array_in.shape[2:])

def reference(char_ids, word_lengths, params, cotangent):
    ids_seq = arrange(char_ids)
    length_seq = arrange(word_lengths)

    def forward(flat_params):
        all_layouts = layouts()
        section_parts = [carve(flat_params[number], all_layouts[number]) for number in range(4)]

        def one_sequence(carry_in, pair_in):
            return (carry_in, encode(section_parts, pair_in[0], pair_in[1]))
        unused, outputs = lax.scan(jax.checkpoint(one_sequence), jnp.zeros((), jnp.float32), (ids_seq, length_seq))
        return outputs
    outputs, pullback = jax.vjp(forward, params.astype(jnp.float32))
    param_grads, = pullback(arrange(cotangent).astype(jnp.float32))
    return (restore(outputs).astype(jnp.bfloat16), param_grads)
```

```python
import functools
import math

import jax
import jax.numpy as jnp
from jax import lax
from jax.experimental import pallas as pl
from jax.experimental.pallas import tpu as pltpu
from jax.sharding import PartitionSpec as P

D = 768
HEADS = 12
HEAD_DIM = 64
FF = 3072
CHAR_DIM = 16
CHARS = 262
CHAR_LEN = 50
CH_UNIT = 32
SEQ_LEN = 192
CONV = 64 * CH_UNIT
LANES = 128
MESH = pl.DeviceIdType.MESH
BF = jnp.bfloat16
F32 = jnp.float32
HUGE = 1e30
CNN = (0, 2, 3)

channel_steps = (1, 1, 2, 4, 8, 16, 32)
layer_eps = 1e-12

HW_BIAS0 = CONV * 2 * CONV
HW_W1 = HW_BIAS0 + 2 * CONV
HW_BIAS1 = HW_W1 + CONV * 2 * CONV
PROJ_W = HW_BIAS1 + 2 * CONV
PROJ_B = PROJ_W + CONV * D
Q_BIAS = D * 3 * D
V_BIAS = Q_BIAS + D
OUT_W = V_BIAS + D
OUT_B = OUT_W + D * D
UP_B = D * FF
DOWN_W = UP_B + FF
DOWN_B = DOWN_W + FF * D
TABLE = CHARS * CHAR_DIM
CNN_FLAT = TABLE + sum((n + 1) * CHAR_DIM * c * CH_UNIT for n, c in enumerate(channel_steps)) + CONV


def hbm():
    return pl.BlockSpec(memory_space=pl.ANY)


def vmem():
    return pl.BlockSpec(memory_space=pltpu.VMEM)


def as_float(array_in):
    return array_in.astype(F32)


def to_low(array_in):
    return array_in.astype(BF)


def matmul(left_in, right_in):
    return jnp.dot(left_in, right_in, preferred_element_type=F32)


def matmul_tn(left_in, right_in):
    return lax.dot_general(left_in, right_in, (((0,), (0,)), ((), ())), preferred_element_type=F32)


def matmul_nt(left_in, right_in):
    return lax.dot_general(left_in, right_in, (((1,), (1,)), ((), ())), preferred_element_type=F32)


def cut_kernel(p_ref, w0, w1, wp, wqkv, wo, wu, wd, vec, raw, sems):
    section = lax.axis_index("section")

    def matrix(offset, target, rows):
        count, columns = target.shape

        def body(in_ref, out_ref):
            out_ref[...] = in_ref[...].reshape(rows, columns)

        pltpu.emit_pipeline(
            body,
            grid=(count // rows,),
            in_specs=[pl.BlockSpec((1, rows * columns), lambda i: (0, i))],
            out_specs=[pl.BlockSpec((rows, columns), lambda i: (i, 0))],
        )(p_ref.at[:, pl.ds(offset, count * columns)], target)

    def vectors(entries):
        copies = []
        for row, (offset, size) in enumerate(entries):
            copy = pltpu.make_async_copy(
                p_ref.at[:, pl.ds(offset, size)], raw.at[row, :, pl.ds(0, size)], sems.at[row]
            )
            copy.start()
            copies.append(copy)
        for copy in copies:
            copy.wait()
        for row, (offset, size) in enumerate(entries):
            vec[row : row + 1, 0:size] = as_float(raw[row, :, 0:size])

    @pl.when(section == 1)
    def _():
        vectors([(HW_BIAS0, 2 * CONV), (HW_BIAS1, 2 * CONV), (PROJ_B, D)])
        matrix(0, w0, 256)
        matrix(HW_W1, w1, 256)
        matrix(PROJ_W, wp, 512)

    @pl.when(section == 2)
    def _():
        vectors([(Q_BIAS, D), (V_BIAS, D), (OUT_B, D), (OUT_B + D, D), (OUT_B + 2 * D, D)])
        matrix(0, wqkv, 256)
        matrix(OUT_W, wo, 384)

    @pl.when(section == 3)
    def _():
        vectors([(UP_B, FF), (DOWN_B, D), (DOWN_B + D, D), (DOWN_B + 2 * D, D)])
        matrix(0, wu, 256)
        matrix(DOWN_W, wd, 512)


def cut_weights(params):
    shapes = [(CONV, 2 * CONV), (CONV, 2 * CONV), (CONV, D), (D, 3 * D), (D, D), (D, FF), (FF, D)]
    return pl.pallas_call(
        cut_kernel,
        out_shape=[jax.ShapeDtypeStruct(s, BF) for s in shapes]
        + [jax.ShapeDtypeStruct((8, 2 * CONV), F32)],
        in_specs=[hbm()],
        out_specs=[hbm()] * len(shapes) + [vmem()],
        scratch_shapes=[pltpu.VMEM((5, 1, 2 * CONV), BF), pltpu.SemaphoreType.DMA((5,))],
        compiler_params=pltpu.CompilerParams(vmem_limit_bytes=40 << 20),
    )(params)


CNN_ROWS = 1600
TABLE_ROWS = 384


def cnn_params_kernel(p_ref, ck_ref, tt_ref, raw, flat, kernel, table, sem, send, recv):
    section = lax.axis_index("section")
    others = [s for s in CNN if s]
    lane = lax.broadcasted_iota(jnp.int32, (1, LANES), 1)
    barrier = pltpu.get_barrier_semaphore()

    @pl.when(section == 0)
    def _():
        copy = pltpu.make_async_copy(p_ref.at[:, pl.ds(0, CNN_ROWS * LANES)], raw, sem)
        copy.start()
        for s in others:
            pl.semaphore_signal(barrier, inc=1, device_id={"section": s}, device_id_type=MESH)
        copy.wait()
        flat[...] = as_float(raw[...]).reshape(CNN_ROWS, LANES)
        table[...] = jnp.zeros_like(table)
        head = flat[0:40, :]
        for b in range(8):
            mixed = jnp.zeros_like(head)
            for g in range(7):
                rolled = head if g == b else pltpu.roll(head, (g - b) * CHAR_DIM % LANES, 1)
                mixed = jnp.where((lane >= g * CHAR_DIM) & (lane < (g + 1) * CHAR_DIM), rolled, mixed)
            table[pl.ds(b, 33, stride=8), :] = mixed[0:33]
        tt_ref[...] = to_low(table[...])
        rolled = pltpu.roll(flat[...], 32, 1)
        flat[...] = rolled
        count = CNN_ROWS - 40
        flat[0:count, :] = jnp.where(
            lane < 32, flat[32 : 32 + count, :], flat[33 : 33 + count, :]
        )
        kernel[...] = jnp.zeros_like(kernel)
        first, second, third = flat[0:8, :], flat[4:12, :], flat[12:36, :]
        narrow = lax.broadcasted_iota(jnp.int32, (8, LANES), 0) < 4
        for b in range(4):
            one = first if b == 0 else pltpu.roll(first, -b * 32 % LANES, 1)
            two = second if b == 1 else pltpu.roll(second, (32 - b * 32) % LANES, 1)
            kernel[0, pl.ds(b, 8, stride=4), :] = jnp.where(
                lane < 32, jnp.where(narrow, one, 0.0), jnp.where(lane < 64, two, 0.0)
            )
        for b in range(2):
            three = third if b == 1 else pltpu.roll(third, 64, 1)
            kernel[0, pl.ds(b, 24, stride=2), :] = jnp.where(
                lane >= 64, three, kernel[0, pl.ds(b, 24, stride=2), :]
            )
        row, tile = 36, 1
        for number in range(3, 7):
            parts = channel_steps[number] * CH_UNIT // LANES
            depth = (number + 1) * CHAR_DIM
            for c in range(parts):
                kernel[tile, 0:depth, :] = flat[pl.ds(row + c, depth, stride=parts), :]
                tile += 1
            row += depth * parts
        bound = 0
        for number in range(7):
            upper = bound + channel_steps[number] * CH_UNIT
            for c in range(bound // LANES, -(-upper // LANES)):
                kernel[c, 112 + number : 113 + number, :] = jnp.where(
                    (lane + c * LANES >= bound) & (lane + c * LANES < upper), -HUGE, 0.0
                )
            bound = upper
        for c in range(CONV // LANES):
            kernel[c, 119:120, :] = flat[row + c : row + c + 1, :]
            ck_ref[:, c * LANES : (c + 1) * LANES] = to_low(kernel[c])
        pl.semaphore_wait(barrier, len(others))
        copies = []
        for i, s in enumerate(others):
            for j, ref in enumerate((ck_ref, tt_ref)):
                copies.append(
                    pltpu.make_async_remote_copy(
                        ref, ref, send.at[i, j], recv.at[j], device_id={"section": s}, device_id_type=MESH
                    )
                )
        for copy in copies:
            copy.start()
        for copy in copies:
            copy.wait_send()

    for s in others:

        @pl.when(section == s)
        def _():
            pl.semaphore_signal(barrier, inc=1, device_id={"section": 0}, device_id_type=MESH)
            pl.semaphore_wait(barrier, 1)
            for j, ref in enumerate((ck_ref, tt_ref)):
                pltpu.make_async_remote_copy(
                    ref, ref, send.at[0, j], recv.at[j], device_id={"section": 0}, device_id_type=MESH
                ).wait_recv()


def cnn_params(params):
    return pl.pallas_call(
        cnn_params_kernel,
        out_shape=[
            jax.ShapeDtypeStruct((LANES, CONV), BF),
            jax.ShapeDtypeStruct((TABLE_ROWS, LANES), BF),
        ],
        in_specs=[hbm()],
        out_specs=[vmem(), vmem()],
        scratch_shapes=[
            pltpu.VMEM((1, CNN_ROWS * LANES), BF),
            pltpu.VMEM((CNN_ROWS, LANES), F32),
            pltpu.VMEM((CONV // LANES, LANES, LANES), F32),
            pltpu.VMEM((TABLE_ROWS, LANES), F32),
            pltpu.SemaphoreType.DMA,
            pltpu.SemaphoreType.DMA((len(CNN) - 1, 2)),
            pltpu.SemaphoreType.DMA((2,)),
        ],
        compiler_params=pltpu.CompilerParams(
            collective_id=0, has_side_effects=True, vmem_limit_bytes=24 << 20
        ),
    )(params)


def lane_masks():
    lane = lax.broadcasted_iota(jnp.int32, (1, LANES), 1)
    return [
        jnp.where((lane >= j * CHAR_DIM) & (lane < (j + 1) * CHAR_DIM), 1.0, 0.0).astype(BF)
        for j in range(7)
    ]


def embed(position, words, ids_ref, tt_ref, embedded):
    start = pl.multiple_of(position * words, words)
    ids = ids_ref[pl.ds(start, words), :]
    hot = ids == lax.broadcasted_iota(jnp.int32, (words, TABLE_ROWS), 1)
    embedded[pl.ds(start, words), :] = to_low(matmul(jnp.where(hot, 1.0, 0.0).astype(BF), tt_ref[...]))


def window(position, words, length, embedded, masks):
    total = None
    for j in range(7):
        start = pl.multiple_of((position + j) * words, words)
        term = embedded[pl.ds(start, words), :] * masks[j]
        total = term if total is None else total + term
    lane = lax.broadcasted_iota(jnp.int32, (words, LANES), 1)
    out = (lane >= 112) & (lane < 119) & (position + lane - 111 > length)
    return total + jnp.where(out | (lane == 119), 1.0, 0.0).astype(BF)


def chars_forward_kernel(words, top_ref, ids_ref, length_ref, ck_ref, tt_ref, out_ref, embedded, best):
    top = top_ref[0]
    embedded[...] = jnp.zeros_like(embedded)
    best[...] = jnp.full_like(best, -HUGE)
    masks = lane_masks()
    length = length_ref[...]

    def first(p, carry):
        embed(p, words, ids_ref, tt_ref, embedded)
        return carry

    def second(p, carry):
        rows = window(p, words, length, embedded, masks)
        for c in range(0, CONV, 512):
            best[:, c : c + 512] = jnp.maximum(
                best[:, c : c + 512], matmul(rows, ck_ref[:, c : c + 512])
            )
        return carry

    lax.fori_loop(0, top, first, 0)
    lax.fori_loop(0, top, second, 0)
    out_ref[...] = to_low(jnp.maximum(best[...], 0.0))


def chars_backward_kernel(
    words, top_ref, ids_ref, id_rows_ref, length_ref, ck_ref, tt_ref, grad_ref,
    out_ref, embedded, best, share, backs, sums,
):
    top = top_ref[0]
    table_rows = pl.ds(CONV, TABLE_ROWS)

    @pl.when(top > 0)
    def _():
        embedded[...] = jnp.zeros_like(embedded)
        backs[...] = jnp.zeros_like(backs)
        best[...] = jnp.full_like(best, -HUGE)
        share[...] = jnp.zeros_like(share)
        sums[...] = jnp.zeros_like(sums)
        out_ref[table_rows, :] = jnp.zeros((TABLE_ROWS, LANES), F32)
    masks = lane_masks()
    length = length_ref[...]

    def first(p, carry):
        embed(p, words, ids_ref, tt_ref, embedded)
        return carry

    def second(p, carry):
        rows = window(p, words, length, embedded, masks)
        for c in range(0, CONV, 512):
            part = slice(c, c + 512)
            pre = matmul(rows, ck_ref[:, part])
            top_now, hits = best[:, part], share[:, part]
            share[:, part] = jnp.where(
                pre > top_now, 1.0, hits + jnp.where(pre == top_now, 1.0, 0.0)
            )
            best[:, part] = jnp.maximum(top_now, pre)
        return carry

    lax.fori_loop(0, top, first, 0)
    lax.fori_loop(0, top, second, 0)

    @pl.when(top > 0)
    def _():
        share[...] = as_float(grad_ref[...]) / share[...]
        best[...] = jnp.where(best[...] > 0.0, best[...], 3e38)

    def third(p, carry):
        rows = window(p, words, length, embedded, masks)
        back = jnp.zeros((words, LANES), F32)
        for c in range(0, CONV, 512):
            part = slice(c, c + 512)
            pre = matmul(rows, ck_ref[:, part])
            grad = to_low(jnp.where(pre == best[:, part], share[:, part], 0.0))
            sums[:, part] += matmul_tn(rows, grad)
            back = back + matmul_nt(grad, ck_ref[:, part])
        backs[pl.ds(pl.multiple_of((p + 6) * words, words), words), :] = to_low(back)
        return carry

    def fourth(q, carry):
        total = jnp.zeros((words, LANES), F32)
        lane = lax.broadcasted_iota(jnp.int32, (words, LANES), 1)
        for j in range(7):
            start = pl.multiple_of((q + 6 - j) * words, words)
            value = as_float(backs[pl.ds(start, words), :])
            total = jnp.where((lane >= j * CHAR_DIM) & (lane < (j + 1) * CHAR_DIM), value, total)
        hot = id_rows_ref[pl.ds(q, 1), :] == lax.broadcasted_iota(jnp.int32, (TABLE_ROWS, words), 0)
        out_ref[table_rows, :] += matmul(jnp.where(hot, 1.0, 0.0).astype(BF), to_low(total))
        return carry

    lax.fori_loop(0, top, third, 0)
    lax.fori_loop(0, top, fourth, 0)

    @pl.when(top > 0)
    def _():
        for c in range(CONV // LANES):
            out_ref[c * LANES : (c + 1) * LANES, :] = sums[:, c * LANES : (c + 1) * LANES]


def chars_forward(ids_column, length_column, top, ck, tt):
    words = length_column.shape[0]
    return pl.pallas_call(
        functools.partial(chars_forward_kernel, words),
        out_shape=jax.ShapeDtypeStruct((words, CONV), BF),
        in_specs=[pl.BlockSpec(memory_space=pltpu.SMEM)] + [vmem()] * 4,
        out_specs=vmem(),
        scratch_shapes=[
            pltpu.VMEM(((CHAR_LEN + 6) * words, LANES), BF),
            pltpu.VMEM((words, CONV), F32),
        ],
        compiler_params=pltpu.CompilerParams(vmem_limit_bytes=32 << 20),
    )(top, ids_column, length_column, ck, tt)


def chars_backward(ids_column, id_rows, length_column, top, ck, tt, grad):
    words = length_column.shape[0]
    return pl.pallas_call(
        functools.partial(chars_backward_kernel, words),
        out_shape=jax.ShapeDtypeStruct((CNN_GRADS, LANES), F32),
        in_specs=[pl.BlockSpec(memory_space=pltpu.SMEM)] + [vmem()] * 6,
        out_specs=vmem(),
        scratch_shapes=[
            pltpu.VMEM(((CHAR_LEN + 6) * words, LANES), BF),
            pltpu.VMEM((words, CONV), F32),
            pltpu.VMEM((words, CONV), F32),
            pltpu.VMEM(((CHAR_LEN + 6) * words, LANES), BF),
            pltpu.VMEM((LANES, CONV), F32),
        ],
        compiler_params=pltpu.CompilerParams(vmem_limit_bytes=32 << 20),
    )(top, ids_column, id_rows, length_column, ck, tt, grad)


def cnn_gradient(grads):
    table_grad = grads[CONV:]
    kernel_grad = jnp.swapaxes(grads[:CONV].reshape(-1, LANES, LANES), 0, 1).reshape(LANES, CONV)
    pieces = [
        sum(table_grad[:CHARS, g * CHAR_DIM : (g + 1) * CHAR_DIM] for g in range(7)).reshape(-1)
    ]
    offset = 0
    for number in range(7):
        channels = channel_steps[number] * CH_UNIT
        pieces.append(
            kernel_grad[: (number + 1) * CHAR_DIM, offset : offset + channels].reshape(-1)
        )
        offset += channels
    pieces.append(kernel_grad[119])
    return jnp.concatenate(pieces)


def norm_forward(residual, norm_gain, norm_shift):
    centered = residual - jnp.mean(residual, axis=-1, keepdims=True)
    inverse = lax.rsqrt(jnp.mean(centered * centered, axis=-1, keepdims=True) + layer_eps)
    scaled = centered * inverse
    return (scaled * norm_gain + norm_shift, scaled, inverse)


def norm_backward(upstream, scaled, inverse, norm_gain):
    weighted = upstream * norm_gain
    first_mean = jnp.mean(weighted, axis=-1, keepdims=True)
    cross_mean = jnp.mean(weighted * scaled, axis=-1, keepdims=True)
    back_flow = inverse * (weighted - first_mean - scaled * cross_mean)
    return (back_flow, jnp.sum(upstream * scaled, axis=0), jnp.sum(upstream, axis=0))


def highway_mix(projection, carried):
    gate_open = jax.nn.sigmoid(projection[:, CONV:])
    return gate_open * carried + (1.0 - gate_open) * jnp.maximum(projection[:, :CONV], 0.0)


def highway_forward(w0, w1, wp, vec, wide_in):
    proj0 = matmul(wide_in, w0) + vec[0]
    x1 = to_low(highway_mix(proj0, as_float(wide_in)))
    proj1 = matmul(x1, w1) + vec[1]
    x2 = to_low(highway_mix(proj1, as_float(x1)))
    projected = to_low(matmul(x2, wp) + vec[2, :D])
    return (projected, x1, x2, proj0, proj1)


def highway_backward(w0, w1, wp, wide_in, x1, proj0, proj1, upstream):
    flowing = matmul_nt(upstream, wp)
    grads = []
    for weight, carried, projection in ((w1, x1, proj1), (w0, wide_in, proj0)):
        carried = as_float(carried)
        gate_open = jax.nn.sigmoid(projection[:, CONV:])
        nonlinear = jnp.maximum(projection[:, :CONV], 0.0)
        grad_left = flowing * (1.0 - gate_open) * (projection[:, :CONV] > 0.0)
        grad_right = flowing * (carried - nonlinear) * gate_open * (1.0 - gate_open)
        grad_proj = to_low(jnp.concatenate([grad_left, grad_right], axis=1))
        grads.append(grad_proj)
        flowing = flowing * gate_open + matmul_nt(grad_proj, weight)
    return (to_low(flowing), jnp.concatenate([grads[1], grads[0]], axis=1))


def attention_forward(wqkv, wo, vec, narrow_in):
    row_count = narrow_in.shape[0]
    seq_count = row_count // SEQ_LEN
    joined = matmul(narrow_in, wqkv)
    query_rows = to_low(joined[:, :D] + vec[0, :D])
    key_rows = to_low(joined[:, D : 2 * D])
    value_rows = to_low(joined[:, 2 * D :] + vec[1, :D])
    heads_shape = (seq_count, SEQ_LEN, HEADS, HEAD_DIM)
    scores = jnp.einsum(
        "sqhd,skhd->shqk",
        query_rows.reshape(heads_shape),
        key_rows.reshape(heads_shape),
        preferred_element_type=F32,
    ) * HEAD_DIM ** (-0.5)
    row_max = jnp.max(scores, axis=-1, keepdims=True)
    exponent = jnp.exp(scores - row_max)
    softmax_out = exponent / jnp.sum(exponent, axis=-1, keepdims=True)
    softmax_low = to_low(softmax_out)
    mixed_heads = to_low(
        jnp.einsum(
            "shqk,skhd->sqhd",
            softmax_low,
            value_rows.reshape(heads_shape),
            preferred_element_type=F32,
        ).reshape(row_count, D)
    )
    residual = as_float(narrow_in) + matmul(mixed_heads, wo) + vec[2, :D]
    normed, scaled, inverse = norm_forward(residual, vec[3, :D], vec[4, :D])
    return (
        to_low(normed),
        (query_rows, key_rows, value_rows, softmax_out, mixed_heads, scaled, inverse),
    )


def attention_backward(wqkv, wo, vec, narrow_in, kept, upstream):
    row_count = narrow_in.shape[0]
    seq_count = row_count // SEQ_LEN
    heads_shape = (seq_count, SEQ_LEN, HEADS, HEAD_DIM)
    query_rows, key_rows, value_rows, softmax_out, mixed_heads, scaled, inverse = kept
    softmax_low = to_low(softmax_out)
    grad_resid, gain_grad, shift_grad = norm_backward(as_float(upstream), scaled, inverse, vec[3, :D])
    grad_att = to_low(grad_resid)
    grad_mixed = to_low(matmul_nt(grad_att, wo)).reshape(heads_shape)
    query_heads = query_rows.reshape(heads_shape)
    key_heads = key_rows.reshape(heads_shape)
    grad_soft = jnp.einsum(
        "sqhd,skhd->shqk",
        grad_mixed,
        value_rows.reshape(heads_shape),
        preferred_element_type=F32,
    )
    grad_value = to_low(
        jnp.einsum("shqk,sqhd->skhd", softmax_low, grad_mixed, preferred_element_type=F32)
    )
    grad_scores = to_low(
        softmax_out * (grad_soft - jnp.sum(grad_soft * softmax_out, axis=-1, keepdims=True))
    )
    grad_query = to_low(
        jnp.einsum("shqk,skhd->sqhd", grad_scores, key_heads, preferred_element_type=F32)
        * HEAD_DIM ** (-0.5)
    )
    grad_key = to_low(
        jnp.einsum("shqk,sqhd->skhd", grad_scores, query_heads, preferred_element_type=F32)
        * HEAD_DIM ** (-0.5)
    )
    grad_joined = jnp.concatenate(
        [grad.reshape(row_count, D) for grad in (grad_query, grad_key, grad_value)], axis=1
    )
    flowing = grad_resid + matmul_nt(grad_joined, wqkv)
    return (to_low(flowing), grad_joined, grad_att, gain_grad, shift_grad)


def attention_gradient(narrow_in, mixed_heads, grad_joined, grad_att, gain_grad, shift_grad):
    group = narrow_in.shape[0]
    ones = jnp.ones((1, group), BF)
    bias = matmul(ones, grad_joined)[0]
    return side_row(
        [
            matmul_tn(narrow_in, grad_joined), bias[:D], bias[2 * D :], matmul_tn(mixed_heads, grad_att),
            matmul(ones, grad_att)[0], gain_grad, shift_grad,
        ]
    )


def ffn_gradient(narrow_in, activated, grad_inner, grad_branch, gain_grad, shift_grad):
    ones = jnp.ones((1, narrow_in.shape[0]), BF)
    return side_row(
        [
            matmul_tn(narrow_in, grad_inner), matmul(ones, grad_inner)[0], matmul_tn(activated, grad_branch),
            matmul(ones, grad_branch)[0], gain_grad, shift_grad,
        ]
    )


def side_row(pieces):
    return jnp.concatenate([to_low(piece).reshape(-1) for piece in pieces])


def ffn_both(wu, wd, vec, narrow_in, upstream):
    inner_act = matmul(narrow_in, wu) + vec[0, :FF]
    phi = 0.5 * (1.0 + lax.erf(inner_act * 0.7071067811865476))
    activated = to_low(inner_act * phi)
    residual = as_float(narrow_in) + matmul(activated, wd) + vec[1, :D]
    normed, scaled, inverse = norm_forward(residual, vec[2, :D], vec[3, :D])
    grad_resid, gain_grad, shift_grad = norm_backward(as_float(upstream), scaled, inverse, vec[2, :D])
    grad_branch = to_low(grad_resid)
    grad_act = matmul_nt(grad_branch, wd)
    slope = phi + inner_act * jnp.exp(-0.5 * inner_act * inner_act) * 0.3989422804014327
    grad_inner = to_low(grad_act * slope)
    flowing = grad_resid + matmul_nt(grad_inner, wu)
    return (to_low(normed), to_low(flowing), activated, grad_inner, grad_branch, gain_grad, shift_grad)


SLICE = 608
CHUNK = 512
N_CHUNK = 2 * CONV // CHUNK
STACK = CONV + 16
PROJ_STACK = 5 * 416
FRONT = 80
Z = 4


def reduce_kernel(
    share, xt_ref, x2t_ref, g_ref, gp_ref, side_ref, cnn_ref, out_ref, land_ref,
    tile, flat, y_out, y_in, z_out, z_in, y_send, y_recv, z_send, z_recv, sem,
):
    section = lax.axis_index("section")
    b = lax.axis_index("batch")
    y, z = lax.rem(b, 2), lax.div(b, 2)
    steps = Z * N_CHUNK

    def owner(step):
        o = lax.rem(step, Z)
        up = jnp.where(z == 0, 3 - o, jnp.where(o == 0, 3, jnp.where(o == 1, 0, jnp.where(o == 2, 2, 1))))
        down = jnp.where(z == 3, o, jnp.where(o == 0, 0, jnp.where(o == 1, 3, jnp.where(o == 2, 1, 2))))
        return jnp.where(z < 2, up, down)

    def product(part, j):
        column = pl.multiple_of(j * CHUNK, CHUNK)

        @pl.when((part != 3) & (part != 7))
        def _():
            row = pl.multiple_of((35 * part + jnp.where(part >= 4, 1, 0)) * 16, 16)
            col = pl.multiple_of(column + jnp.where(part >= 4, 2 * CONV, 0), CHUNK)
            tile[...] = matmul(xt_ref[pl.ds(row, SLICE), :], g_ref[:, pl.ds(col, CHUNK)])

        @pl.when(part == 3)
        def _():
            tile[0:384, :] = matmul(xt_ref[1680:STACK, :], g_ref[:, pl.ds(column, CHUNK)])
            tile[384:SLICE, :] = matmul(
                xt_ref[STACK : STACK + 224, :], g_ref[:, pl.ds(pl.multiple_of(column + 2 * CONV, CHUNK), CHUNK)]
            )

        @pl.when(part == 7)
        def _():
            tile[0:192, :] = matmul(
                xt_ref[2 * STACK - 192 : 2 * STACK, :], g_ref[:, pl.ds(pl.multiple_of(column + 2 * CONV, CHUNK), CHUNK)]
            )
            for t in range(2):
                h = 2 * j + t
                row = pl.multiple_of(lax.rem(h, 5) * 416, 16)
                col = pl.multiple_of(jnp.minimum(lax.div(h, 5), 2) * 256, 256)
                tile[192:SLICE, t * 256 : (t + 1) * 256] = matmul(
                    x2t_ref[pl.ds(row, 416), :], gp_ref[:, pl.ds(col, 256)]
                )

    def y_copy(step):
        slot = lax.rem(step, 3)
        return pltpu.make_async_remote_copy(
            y_out.at[slot], y_in.at[step], y_send.at[slot], y_recv.at[step],
            device_id={"batch": b + 1 - 2 * y}, device_id_type=MESH,
        )

    def z_copy(step, down):
        o, j = lax.rem(step, Z), lax.div(step, Z)
        slot = owner(step) * N_CHUNK + j
        side = 0 if down else 1
        return pltpu.make_async_remote_copy(
            z_out.at[o], land_ref.at[side, slot], z_send.at[o], z_recv.at[side, slot],
            device_id={"batch": b - 2 if down else b + 2}, device_id_type=MESH,
        )

    def send_y(step):
        product(2 * owner(step) + 1 - y, lax.div(step, Z))

        @pl.when(step >= 3)
        def _():
            y_copy(step - 3).wait_send()

        y_out[lax.rem(step, 3)] = to_low(tile[...])
        y_copy(step).start()

    def arrived(side, slot):
        pltpu.make_async_remote_copy(
            z_out.at[0], land_ref.at[side, slot], z_send.at[0], z_recv.at[side, slot],
            device_id={"batch": b}, device_id_type=MESH,
        ).wait_recv()
        copy = pltpu.make_async_copy(land_ref.at[side, slot], z_in, sem)
        copy.start()
        copy.wait()
        tile[...] += as_float(z_in[...])

    def keep(j):
        base = FRONT - 16 * b + jnp.where(b >= 4, 32, 0) + j * (CHUNK // LANES)

        def rows(first, count, start, column, stride):
            flat[pl.ds(start, count, stride=stride), :] = tile[first : first + count, column : column + LANES]

        @pl.when((b != 3) & (b != 7))
        def _():
            for c in range(CHUNK // LANES):
                rows(0, SLICE, base + c, c * LANES, 32)

        @pl.when(b == 3)
        def _():
            for c in range(CHUNK // LANES):
                rows(0, 369, base + c, c * LANES, 32)
                rows(384, 224, FRONT + 11760 + j * (CHUNK // LANES) + c, c * LANES, 32)

        @pl.when(b == 7)
        def _():
            for c in range(CHUNK // LANES):
                rows(0, 177, base + c, c * LANES, 32)
            for t in range(2):
                h = 2 * j + t

                @pl.when(h < 15)
                def _():
                    start = FRONT + 5584 + lax.rem(h, 5) * (416 * 6) + lax.div(h, 5) * 2
                    for c in range(2):
                        rows(192, 416, start + c, t * 256 + c * LANES, 6)

    def combine(step):
        part, o, j = owner(step), lax.rem(step, Z), lax.div(step, Z)
        slot = part * N_CHUNK + j
        product(2 * part + y, j)
        y_copy(step).wait_recv()
        tile[...] += as_float(y_in[step])

        @pl.when((part <= z) & (z < Z - 1))
        def _():
            arrived(0, slot)

        @pl.when((part >= z) & (z > 0))
        def _():
            arrived(1, slot)

        @pl.when(part == z)
        def _():
            keep(j)

        @pl.when(part != z)
        def _():
            @pl.when(j > 0)
            def _():
                z_copy(step - Z, True).wait_send()

            z_out[o] = to_low(tile[...])

            @pl.when(part < z)
            def _():
                z_copy(step, True).start()

            @pl.when(part > z)
            def _():
                z_copy(step, False).start()

    @pl.when(section == 1)
    def _():
        barrier = pltpu.get_barrier_semaphore()
        pl.semaphore_signal(barrier, inc=1, device_id={"batch": b + 1 - 2 * y}, device_id_type=MESH)

        @pl.when(z > 0)
        def _():
            pl.semaphore_signal(barrier, inc=1, device_id={"batch": b - 2}, device_id_type=MESH)

        @pl.when(z < Z - 1)
        def _():
            pl.semaphore_signal(barrier, inc=1, device_id={"batch": b + 2}, device_id_type=MESH)

        pl.semaphore_wait(barrier, 1 + jnp.where(z > 0, 1, 0) + jnp.where(z < Z - 1, 1, 0))
        lag = 2

        def step_body(step, carry):
            @pl.when(step < steps)
            def _():
                send_y(step)

            @pl.when(step >= lag)
            def _():
                combine(step - lag)

            return carry

        lax.fori_loop(0, steps + lag, step_body, 0)
        for step in range(steps - 3, steps):
            y_copy(step).wait_send()
        for step in range(steps - Z, steps - 1):
            z_copy(step, True).wait_send()
        copy = pltpu.make_async_copy(flat.at[pl.ds(FRONT, share)], out_ref, sem)
        copy.start()
        copy.wait()

    @pl.when((section == 0) & (b == 0))
    def _():
        copy = pltpu.make_async_copy(cnn_ref, out_ref.at[pl.ds(0, CNN_ROWS)], sem)
        copy.start()
        copy.wait()


def reduce_highways(xt, x2t, g, gp, side, cnn):
    share = side.shape[0]
    chunk = (SLICE, CHUNK)
    return pl.pallas_call(
        functools.partial(reduce_kernel, share),
        out_shape=[
            jax.ShapeDtypeStruct(side.shape, F32),
            jax.ShapeDtypeStruct((2, Z * N_CHUNK) + chunk, BF),
        ],
        in_specs=[vmem()] * 4 + [hbm(), hbm()],
        out_specs=[hbm(), hbm()],
        input_output_aliases={4: 0},
        scratch_shapes=[
            pltpu.VMEM(chunk, F32),
            pltpu.VMEM((FRONT + SLICE * 32, LANES), F32),
            pltpu.VMEM((3,) + chunk, BF),
            pltpu.VMEM((Z * N_CHUNK,) + chunk, BF),
            pltpu.VMEM((Z - 1,) + chunk, BF),
            pltpu.VMEM(chunk, BF),
            pltpu.SemaphoreType.DMA((3,)),
            pltpu.SemaphoreType.DMA((Z * N_CHUNK,)),
            pltpu.SemaphoreType.DMA((Z - 1,)),
            pltpu.SemaphoreType.DMA((2, Z * N_CHUNK)),
            pltpu.SemaphoreType.DMA,
        ],
        compiler_params=pltpu.CompilerParams(
            collective_id=1, has_side_effects=True, vmem_limit_bytes=58 << 20
        ),
    )(xt, x2t, g, gp, side, cnn)


SIDE_ROWS = 1200
SIDE_CHUNKS = 16
SIDE_REST = 1040
SIDE_SHARE = 17936


def side_kernel(
    share, row_ref, out_ref, own, y_in, z_in, z_out, total,
    y_send, y_recv, z_send, z_recv, l_send, l_recv, sem,
):
    section = lax.axis_index("section")
    b = lax.axis_index("batch")
    y, z = lax.rem(b, 2), lax.div(b, 2)

    def count(half):
        return jnp.where((section == 2) & (half == 1), 1, SIDE_CHUNKS)

    def rows(half, i):
        return pl.ds(pl.multiple_of(half * share + i * SIDE_ROWS, 16), SIDE_ROWS)

    def y_copy(i):
        return pltpu.make_async_remote_copy(
            row_ref.at[rows(1 - y, i)], y_in.at[i], y_send.at[i], y_recv.at[i],
            device_id={"batch": b + 1 - 2 * y}, device_id_type=MESH,
        )

    def z_copy(i):
        return pltpu.make_async_remote_copy(
            z_out.at[i], z_in.at[i], z_send.at[i], z_recv.at[i],
            device_id={"batch": b - 2}, device_id_type=MESH,
        )

    def rest_copy():
        return pltpu.make_async_remote_copy(
            total.at[pl.ds(share, SIDE_REST)], total.at[pl.ds(0, SIDE_REST)], l_send, l_recv,
            device_id={"batch": 2}, device_id_type=MESH,
        )

    def write():
        copy = pltpu.make_async_copy(total.at[pl.ds(0, share)], out_ref, sem)
        copy.start()
        copy.wait()

    @pl.when(section != 1)
    def _():
        total[...] = jnp.zeros_like(total)

    @pl.when(section == 0)
    def _():
        write()

    @pl.when(section >= 2)
    def _():
        barrier = pltpu.get_barrier_semaphore()

        pl.semaphore_signal(barrier, inc=1, device_id={"batch": b + 1 - 2 * y}, device_id_type=MESH)
        pairs = [(z > 0, b - 2), (z < Z - 1, b + 2), (b == 1, 2), (b == 2, 1)]
        for condition, other in pairs:

            @pl.when(condition)
            def _():
                pl.semaphore_signal(barrier, inc=1, device_id={"batch": other}, device_id_type=MESH)

        pl.semaphore_wait(barrier, 1 + sum(jnp.where(condition, 1, 0) for condition, _ in pairs))

        def send(i, carry):
            y_copy(i).start()
            return carry

        def combine(i, carry):
            copy = pltpu.make_async_copy(row_ref.at[rows(y, i)], own, sem)
            copy.start()
            copy.wait()
            y_copy(i).wait_recv()
            here = pl.ds(pl.multiple_of(i * SIDE_ROWS, 16), SIDE_ROWS)

            @pl.when(z == Z - 1)
            def _():
                z_out[i] = to_low(as_float(own[...]) + as_float(y_in[i]))

            @pl.when(z < Z - 1)
            def _():
                z_copy(i).wait_recv()

                @pl.when(z > 0)
                def _():
                    z_out[i] = to_low(as_float(own[...]) + as_float(y_in[i]) + as_float(z_in[i]))

                @pl.when(z == 0)
                def _():
                    total[here] = as_float(own[...]) + as_float(y_in[i]) + as_float(z_in[i])

            @pl.when(z > 0)
            def _():
                z_copy(i).start()

            return carry

        def drain(i, carry):
            y_copy(i).wait_send()
            return carry

        def drain_z(i, carry):
            z_copy(i).wait_send()
            return carry

        lax.fori_loop(0, count(1 - y), send, 0)
        lax.fori_loop(0, count(y), combine, 0)

        @pl.when((section == 3) & (b == 1))
        def _():
            rest_copy().start()
            rest_copy().wait_send()

        @pl.when((section == 3) & (b == 2))
        def _():
            rest_copy().wait_recv()

        write()
        lax.fori_loop(0, count(1 - y), drain, 0)

        @pl.when(z > 0)
        def _():
            lax.fori_loop(0, count(y), drain_z, 0)


def reduce_sides(row, share):
    chunk = (SIDE_ROWS, LANES)
    dma = pltpu.SemaphoreType.DMA
    return pl.pallas_call(
        functools.partial(side_kernel, share),
        out_shape=jax.ShapeDtypeStruct((share, LANES), F32),
        in_specs=[hbm()],
        out_specs=hbm(),
        scratch_shapes=[
            pltpu.VMEM(chunk, BF),
            pltpu.VMEM((SIDE_CHUNKS,) + chunk, BF),
            pltpu.VMEM((SIDE_CHUNKS,) + chunk, BF),
            pltpu.VMEM((SIDE_CHUNKS,) + chunk, BF),
            pltpu.VMEM((SIDE_CHUNKS * SIDE_ROWS, LANES), F32),
            dma((SIDE_CHUNKS,)),
            dma((SIDE_CHUNKS,)),
            dma((SIDE_CHUNKS,)),
            dma((SIDE_CHUNKS,)),
            dma,
            dma,
            dma,
        ],
        compiler_params=pltpu.CompilerParams(
            collective_id=2, has_side_effects=True, vmem_limit_bytes=40 << 20
        ),
    )(row)


CNN_GRADS = (CONV // LANES) * LANES + TABLE_ROWS


def cnn_sum_kernel(in_ref, out_ref, low, group_in, y_in, z_in, send, group_recv, recv):
    section = lax.axis_index("section")
    b = lax.axis_index("batch")
    y, z = lax.rem(b, 2), lax.div(b, 2)
    others = [s for s in CNN if s]
    barrier = pltpu.get_barrier_semaphore()

    def to_head(i):
        return pltpu.make_async_remote_copy(
            low, group_in.at[i], send, group_recv.at[i], device_id={"section": 0}, device_id_type=MESH
        )

    def along(target, other, i):
        return pltpu.make_async_remote_copy(
            low, target, send, recv.at[i], device_id={"batch": other}, device_id_type=MESH
        )

    for i, s in enumerate(others):

        @pl.when(section == s)
        def _():
            pl.semaphore_signal(barrier, inc=1, device_id={"section": 0}, device_id_type=MESH)
            low[...] = to_low(in_ref[...])
            pl.semaphore_wait(barrier, 1)
            to_head(i).start()
            to_head(i).wait_send()

    @pl.when(section == 0)
    def _():
        for s in others:
            pl.semaphore_signal(barrier, inc=1, device_id={"section": s}, device_id_type=MESH)
        pairs = [(y == 0, b + 1), (y == 1, b - 1), ((y == 0) & (z > 0), b - 2), ((y == 0) & (z < Z - 1), b + 2)]
        for condition, other in pairs:

            @pl.when(condition)
            def _():
                pl.semaphore_signal(barrier, inc=1, device_id={"batch": other}, device_id_type=MESH)

        pl.semaphore_wait(barrier, len(others) + sum(jnp.where(condition, 1, 0) for condition, _ in pairs))
        out_ref[...] = in_ref[...]
        for i in range(len(others)):
            to_head(i).wait_recv()
            out_ref[...] += as_float(group_in[i])

        @pl.when(y == 1)
        def _():
            low[...] = to_low(out_ref[...])
            along(y_in, b - 1, 0).start()
            along(y_in, b - 1, 0).wait_send()

        @pl.when(y == 0)
        def _():
            along(y_in, b + 1, 0).wait_recv()
            out_ref[...] += as_float(y_in[...])

            @pl.when(z < Z - 1)
            def _():
                along(z_in, b + 2, 1).wait_recv()
                out_ref[...] += as_float(z_in[...])

            @pl.when(z > 0)
            def _():
                low[...] = to_low(out_ref[...])
                along(z_in, b - 2, 1).start()
                along(z_in, b - 2, 1).wait_send()


def cnn_sum(grads):
    low = pltpu.VMEM((CNN_GRADS, LANES), BF)
    dma = pltpu.SemaphoreType.DMA
    return pl.pallas_call(
        cnn_sum_kernel,
        out_shape=jax.ShapeDtypeStruct((CNN_GRADS, LANES), F32),
        in_specs=[vmem()],
        out_specs=vmem(),
        scratch_shapes=[
            low,
            pltpu.VMEM((len(CNN) - 1, CNN_GRADS, LANES), BF),
            low,
            low,
            dma,
            dma((len(CNN) - 1,)),
            dma((2,)),
        ],
        compiler_params=pltpu.CompilerParams(
            collective_id=3, has_side_effects=True, vmem_limit_bytes=24 << 20
        ),
    )(grads)


def on_section(number, function, *operands):
    shapes = jax.eval_shape(function, *operands)

    def idle(*unused):
        return jax.tree.map(lambda s: jnp.zeros(s.shape, s.dtype), shapes)

    return lax.cond(lax.axis_index("section") == number, function, idle, *operands)


def moved(value, source, target):
    return lax.ppermute(value, "section", [(source, target)])


def shards(char_ids, word_lengths, params, cotangent):
    section = lax.axis_index("section")
    n_batch = lax.axis_size("batch")
    w0, w1, wp, wqkv, wo, wu, wd, vec = cut_weights(params)
    ck, tt = cnn_params(params)
    ids_all = lax.all_gather(char_ids, "section", axis=0, tiled=True)
    lengths_all = lax.all_gather(word_lengths, "section", axis=0, tiled=True)
    cot_all = lax.all_gather(cotangent, "section", axis=0, tiled=True)
    group = lengths_all.shape[0]
    words = group // len(CNN)
    place = jnp.maximum(section - 1, 0)
    ids = lax.dynamic_slice_in_dim(ids_all, place * words, words, 0)
    lengths = lax.dynamic_slice_in_dim(lengths_all, place * words, words, 0)
    top = jnp.where(section == 1, 0, jnp.max(lengths)).reshape(1)
    id_rows = ids.T
    ids_column = id_rows.reshape(-1, 1)
    length_column = lengths.reshape(-1, 1)

    pooled_part = chars_forward(ids_column, length_column, top, ck, tt)
    pooled = jnp.concatenate([moved(pooled_part, s, 1) for s in CNN], axis=0)
    projected, x1, x2, proj0, proj1 = on_section(1, highway_forward, w0, w1, wp, vec, pooled)
    attention_in = moved(projected, 1, 2)

    def stacks(pooled, x1, x2):
        fill = jnp.concatenate([jnp.ones((1, group), BF), jnp.zeros((31, group), BF)])
        xt = jnp.concatenate([pooled.T, fill[:16], x1.T, fill[:16]])
        return xt, jnp.concatenate([x2.T, fill])

    normed, kept = on_section(2, attention_forward, wqkv, wo, vec, attention_in)
    ffn_in = moved(normed, 2, 3)
    layer, grad_normed, *ffn_kept = on_section(3, ffn_both, wu, wd, vec, ffn_in, cot_all)
    grad_attention = moved(grad_normed, 3, 2)
    quarter = group // 4
    delivered = lax.all_to_all(layer.reshape(4, quarter, D), "section", split_axis=0, concat_axis=0, tiled=True)
    layer_out = delivered[3]
    grad_projected, *attention_kept = on_section(
        2, attention_backward, wqkv, wo, vec, attention_in, kept, grad_attention
    )
    grad_highway = moved(grad_projected, 2, 1)
    grad_pooled, grad_both = on_section(
        1, highway_backward, w0, w1, wp, pooled, x1, proj0, proj1, grad_highway
    )
    grad_part = sum(
        moved(grad_pooled[i * words : (i + 1) * words], 1, s) for i, s in enumerate(CNN)
    )
    xt, x2t = on_section(1, stacks, pooled, x1, x2)
    cnn_part = chars_backward(ids_column, id_rows, length_column, top, ck, tt, grad_part)
    share = params.shape[1] // n_batch // LANES
    if n_batch != 2 * Z or share != SIDE_SHARE:
        return (layer_out, summed_rows(params.shape[1], cnn_part, pooled, x1, x2, grad_both, grad_highway,
                                       (attention_in, kept[4], *attention_kept), (ffn_in, *ffn_kept)))
    cnn_total = cnn_sum(cnn_part)

    def first_row(grads):
        flat = cnn_gradient(grads)
        return jnp.pad(flat, (0, CNN_ROWS * LANES - flat.shape[0])).reshape(-1, LANES)

    cnn_row = on_section(0, first_row, cnn_total)

    def pad_side(flat):
        size = (SIDE_SHARE + SIDE_ROWS * SIDE_CHUNKS) * LANES
        return jnp.pad(flat, (0, size - flat.shape[0])).reshape(-1, LANES)

    row = lax.switch(
        jnp.maximum(section - 1, 0),
        [
            lambda: pad_side(jnp.zeros((LANES,), BF)),
            lambda: pad_side(attention_gradient(attention_in, kept[4], *attention_kept)),
            lambda: pad_side(ffn_gradient(ffn_in, *ffn_kept)),
        ],
    )
    sides = reduce_sides(row, SIDE_SHARE)
    sums, _ = reduce_highways(xt, x2t, grad_both, grad_highway, sides, cnn_row)
    return (layer_out, sums.reshape(1, -1))


def summed_rows(size, cnn_part, pooled, x1, x2, grad_both, grad_highway, attention_kept, ffn_kept):
    first = lax.axis_index("batch") == 0
    cnn_flat = cnn_gradient(lax.psum(jnp.where(lax.axis_index("section") == 1, 0.0, cnn_part), ("section", "batch")))

    def wide(flat):
        return jnp.pad(as_float(flat), (0, size - flat.shape[0]))

    def highways():
        ones = jnp.ones((1, pooled.shape[0]), BF)
        pieces = []
        for x, g in ((pooled, grad_both[:, : 2 * CONV]), (x1, grad_both[:, 2 * CONV :]), (x2, grad_highway)):
            pieces += [matmul_tn(x, g).reshape(-1), matmul(ones, g).reshape(-1)]
        return wide(jnp.concatenate(pieces))

    row = lax.switch(
        lax.axis_index("section"),
        [
            lambda: wide(jnp.where(first, cnn_flat, 0.0)),
            highways,
            lambda: wide(attention_gradient(*attention_kept)),
            lambda: wide(ffn_gradient(*ffn_kept)),
        ],
    )
    return lax.psum_scatter(row, "batch", scatter_dimension=0, tiled=True).reshape(1, -1)


def solution(mesh):
    return jax.shard_map(
        shards,
        mesh=mesh,
        in_specs=(
            P(("section", "batch"), None),
            P(("section", "batch")),
            P("section", None),
            P(("section", "batch"), None),
        ),
        out_specs=(P(("section", "batch"), None), P("section", "batch")),
        check_vma=False,
    )
```

```python
import functools
import math

import jax
import jax.numpy as jnp
from jax import lax
from jax.experimental import pallas as pl
from jax.experimental.pallas import tpu as pltpu
from jax.sharding import PartitionSpec as P

D = 768
HEADS = 12
HEAD_DIM = 64
FF = 3072
CHAR_DIM = 16
CHARS = 262
CHAR_LEN = 50
CH_UNIT = 32
SEQ_LEN = 192
CONV = 64 * CH_UNIT
LANES = 128
MESH = pl.DeviceIdType.MESH
BF = jnp.bfloat16
F32 = jnp.float32
HUGE = 1e30
CNN = (0, 2, 3)

HW_CHUNK = 256
HW_SHAPE = (CONV // HW_CHUNK, CONV, 2 * HW_CHUNK)
channel_steps = (1, 1, 2, 4, 8, 16, 32)
layer_eps = 1e-12

HW_BIAS0 = CONV * 2 * CONV
HW_W1 = HW_BIAS0 + 2 * CONV
HW_BIAS1 = HW_W1 + CONV * 2 * CONV
PROJ_W = HW_BIAS1 + 2 * CONV
PROJ_B = PROJ_W + CONV * D
Q_BIAS = D * 3 * D
V_BIAS = Q_BIAS + D
OUT_W = V_BIAS + D
OUT_B = OUT_W + D * D
UP_B = D * FF
DOWN_W = UP_B + FF
DOWN_B = DOWN_W + FF * D
TABLE = CHARS * CHAR_DIM
CNN_FLAT = TABLE + sum((n + 1) * CHAR_DIM * c * CH_UNIT for n, c in enumerate(channel_steps)) + CONV


def hbm():
    return pl.BlockSpec(memory_space=pltpu.HBM)


def vmem():
    return pl.BlockSpec(memory_space=pltpu.VMEM)


def as_float(array_in):
    return array_in.astype(F32)


def to_low(array_in):
    return array_in.astype(BF)


def matmul(left_in, right_in):
    return jnp.dot(left_in, right_in, preferred_element_type=F32)


def matmul_tn(left_in, right_in):
    return lax.dot_general(left_in, right_in, (((0,), (0,)), ((), ())), preferred_element_type=F32)


def matmul_nt(left_in, right_in):
    return lax.dot_general(left_in, right_in, (((1,), (1,)), ((), ())), preferred_element_type=F32)


class Transfers:
    def __init__(self, items):
        self.items = items

    def copy(self, i, operands, outputs, send, recv):
        source, target, operand, first, rows, output, there = self.items[i]
        from_ref = operands[operand].at[pl.ds(first, rows)]
        to_ref = outputs[output].at[pl.ds(there, rows)]
        if source == target:
            return pltpu.make_async_copy(from_ref, to_ref, send.at[i])
        return pltpu.make_async_remote_copy(
            from_ref, to_ref, send.at[i], recv.at[i], device_id={"section": target}, device_id_type=MESH
        )

    def partners(self, s):
        pairs = {(item[0], item[1]) for item in self.items if item[0] != item[1]}
        return sorted({b for a, b in pairs if a == s} | {a for a, b in pairs if b == s})

    def run(self, operands, outputs, send, recv, work=None):
        section = lax.axis_index("section")
        for s in range(4):
            mine = [i for i, item in enumerate(self.items) if s in item[:2]]
            work_here = (work or {}).get(s)
            if not mine and work_here is None:
                continue

            @pl.when(section == s)
            def _(s=s, mine=mine, work_here=work_here):
                partners = self.partners(s)
                barrier = pltpu.get_barrier_semaphore()
                for other in partners:
                    pl.semaphore_signal(barrier, inc=1, device_id={"section": other}, device_id_type=MESH)
                if work_here is not None:
                    work_here()
                if partners:
                    pl.semaphore_wait(barrier, len(partners))
                outgoing = [i for i in mine if self.items[i][0] == s]
                for i in outgoing:
                    self.copy(i, operands, outputs, send, recv).start()
                for i in mine:
                    copy = self.copy(i, operands, outputs, send, recv)
                    if self.items[i][0] == self.items[i][1]:
                        copy.wait()
                    elif i in outgoing:
                        copy.wait_send()
                    else:
                        copy.wait_recv()


def hand_over(collective_id, items, operands, out_shapes):
    transfers = Transfers(items)

    def kernel(*refs):
        n, m = len(operands), len(out_shapes)
        transfers.run(refs[:n], refs[n : n + m], *refs[n + m :])

    return pl.pallas_call(
        kernel,
        out_shape=[jax.ShapeDtypeStruct(*shape) for shape in out_shapes],
        in_specs=[hbm()] * len(operands),
        out_specs=[hbm()] * len(out_shapes),
        scratch_shapes=[pltpu.SemaphoreType.DMA((len(items),))] * 2,
        compiler_params=pltpu.CompilerParams(collective_id=collective_id, has_side_effects=True),
    )(*operands)


def cut_tools(p_ref, raw, sems):
    def matrix(offset, target, rows):
        count, columns = target.shape

        def body(in_ref, out_ref):
            out_ref[...] = in_ref[...].reshape(rows, columns)

        pltpu.emit_pipeline(
            body,
            grid=(count // rows,),
            in_specs=[pl.BlockSpec((1, rows * columns), lambda i: (0, i))],
            out_specs=[pl.BlockSpec((rows, columns), lambda i: (i, 0))],
        )(p_ref.at[:, pl.ds(offset, count * columns)], target)

    def vectors(entries, vec):
        copies = []
        for row, (offset, size) in enumerate(entries):
            copy = pltpu.make_async_copy(
                p_ref.at[:, pl.ds(offset, size)], raw.at[row, :, pl.ds(0, size)], sems.at[row]
            )
            copy.start()
            copies.append(copy)
        for copy in copies:
            copy.wait()
        for row, (offset, size) in enumerate(entries):
            vec[row : row + 1, 0:size] = as_float(raw[row, :, 0:size])

    def chunks(offset, target, rows):
        def body(in_ref, out_ref):
            value = in_ref[...].reshape(rows, 2 * CONV)
            for c in range(CONV // HW_CHUNK):
                for half in range(2):
                    start = half * CONV + c * HW_CHUNK
                    out_ref[c, :, half * HW_CHUNK : (half + 1) * HW_CHUNK] = value[:, start : start + HW_CHUNK]

        pltpu.emit_pipeline(
            body,
            grid=(CONV // rows,),
            in_specs=[pl.BlockSpec((1, rows * 2 * CONV), lambda i: (0, i))],
            out_specs=[pl.BlockSpec((CONV // HW_CHUNK, rows, 2 * HW_CHUNK), lambda i: (0, i, 0))],
        )(p_ref.at[:, pl.ds(offset, CONV * 2 * CONV)], target)

    return matrix, vectors, chunks


def vector_store(vec, target, sem):
    copy = pltpu.make_async_copy(vec, target, sem)
    copy.start()
    copy.wait()


def start_highways(params, pooled_part, cotangent):
    words, quarter = pooled_part.shape[0], cotangent.shape[0]
    items = [(s, 1, 0, 0, words, 0, i * words) for i, s in enumerate(CNN)]
    items += [(s, 2 + s // 2, 1, 0, quarter, 1, s % 2 * quarter) for s in range(4)]
    transfers = Transfers(items)

    def kernel(pooled_ref, cot_ref, p_ref, pooled, cot, w0, w1, wp, vec_ref, vec, raw, sems, send, recv):
        matrix, vectors, chunks = cut_tools(p_ref, raw, sems)

        def work():
            vectors([(HW_BIAS0, 2 * CONV), (HW_BIAS1, 2 * CONV), (PROJ_B, D)], vec)
            vector_store(vec, vec_ref, sems.at[0])
            chunks(0, w0, 256)
            chunks(HW_W1, w1, 256)
            matrix(PROJ_W, wp, 512)

        transfers.run((pooled_ref, cot_ref), (pooled, cot), send, recv, {1: work})

    shapes = [(words * len(CNN), CONV), (2 * quarter, D), HW_SHAPE, HW_SHAPE, (CONV, D)]
    return pl.pallas_call(
        kernel,
        out_shape=[jax.ShapeDtypeStruct(s, BF) for s in shapes] + [jax.ShapeDtypeStruct((8, 2 * CONV), F32)],
        in_specs=[hbm()] * 3,
        out_specs=[hbm()] * 6,
        scratch_shapes=[
            pltpu.VMEM((8, 2 * CONV), F32),
            pltpu.VMEM((5, 1, 2 * CONV), BF),
            pltpu.SemaphoreType.DMA((5,)),
            pltpu.SemaphoreType.DMA((len(items),)),
            pltpu.SemaphoreType.DMA((len(items),)),
        ],
        compiler_params=pltpu.CompilerParams(
            collective_id=4, has_side_effects=True, vmem_limit_bytes=40 << 20
        ),
    )(pooled_part, cotangent, params)


def start_encoder(params):
    shapes = [(D, 3 * D), (D, D), (D, FF), (FF, D)]
    owners = (2, 2, 3, 3)
    items = [(s, 5 - s, i, 0, shape[0], i, 0) for i, (s, shape) in enumerate(zip(owners, shapes, strict=True))]
    items += [(2, 3, 4, 0, 8, 4, 0), (3, 2, 5, 0, 8, 5, 0)]
    transfers = Transfers(items)

    def kernel(p_ref, wqkv, wo, wu, wd, vec2, vec3, vec, raw, sems, send, recv):
        matrix, vectors, _ = cut_tools(p_ref, raw, sems)

        def work2():
            vectors([(Q_BIAS, D), (V_BIAS, D), (OUT_B, D), (OUT_B + D, D), (OUT_B + 2 * D, D)], vec)
            vector_store(vec, vec2, sems.at[0])
            matrix(0, wqkv, 256)
            matrix(OUT_W, wo, 384)

        def work3():
            vectors([(UP_B, FF), (DOWN_B, D), (DOWN_B + D, D), (DOWN_B + 2 * D, D)], vec)
            vector_store(vec, vec3, sems.at[0])
            matrix(0, wu, 256)
            matrix(DOWN_W, wd, 512)

        outputs = (wqkv, wo, wu, wd, vec2, vec3)
        transfers.run(outputs, outputs, send, recv, {2: work2, 3: work3})

    return pl.pallas_call(
        kernel,
        out_shape=[jax.ShapeDtypeStruct(s, BF) for s in shapes] + [jax.ShapeDtypeStruct((8, 2 * CONV), F32)] * 2,
        in_specs=[hbm()],
        out_specs=[hbm()] * 6,
        scratch_shapes=[
            pltpu.VMEM((8, 2 * CONV), F32),
            pltpu.VMEM((5, 1, 2 * CONV), BF),
            pltpu.SemaphoreType.DMA((5,)),
            pltpu.SemaphoreType.DMA((len(items),)),
            pltpu.SemaphoreType.DMA((len(items),)),
        ],
        compiler_params=pltpu.CompilerParams(
            collective_id=5, has_side_effects=True, vmem_limit_bytes=40 << 20
        ),
    )(params)


CNN_ROWS = 1600
TABLE_ROWS = 384


def cnn_params_kernel(p_ref, ck_ref, tt_ref, raw, flat, kernel, table, sem, send, recv):
    section = lax.axis_index("section")
    others = [s for s in CNN if s]
    lane = lax.broadcasted_iota(jnp.int32, (1, LANES), 1)
    barrier = pltpu.get_barrier_semaphore()

    @pl.when(section == 0)
    def _():
        copy = pltpu.make_async_copy(p_ref.at[:, pl.ds(0, CNN_ROWS * LANES)], raw, sem)
        copy.start()
        for s in others:
            pl.semaphore_signal(barrier, inc=1, device_id={"section": s}, device_id_type=MESH)
        copy.wait()
        flat[...] = as_float(raw[...]).reshape(CNN_ROWS, LANES)
        table[...] = jnp.zeros_like(table)
        head = flat[0:40, :]
        for b in range(8):
            mixed = jnp.zeros_like(head)
            for g in range(7):
                rolled = head if g == b else pltpu.roll(head, (g - b) * CHAR_DIM % LANES, 1)
                mixed = jnp.where((lane >= g * CHAR_DIM) & (lane < (g + 1) * CHAR_DIM), rolled, mixed)
            table[pl.ds(b, 33, stride=8), :] = mixed[0:33]
        tt_ref[...] = to_low(table[...])
        rolled = pltpu.roll(flat[...], 32, 1)
        flat[...] = rolled
        count = CNN_ROWS - 40
        flat[0:count, :] = jnp.where(
            lane < 32, flat[32 : 32 + count, :], flat[33 : 33 + count, :]
        )
        kernel[...] = jnp.zeros_like(kernel)
        first, second, third = flat[0:8, :], flat[4:12, :], flat[12:36, :]
        narrow = lax.broadcasted_iota(jnp.int32, (8, LANES), 0) < 4
        for b in range(4):
            one = first if b == 0 else pltpu.roll(first, -b * 32 % LANES, 1)
            two = second if b == 1 else pltpu.roll(second, (32 - b * 32) % LANES, 1)
            kernel[0, pl.ds(b, 8, stride=4), :] = jnp.where(
                lane < 32, jnp.where(narrow, one, 0.0), jnp.where(lane < 64, two, 0.0)
            )
        for b in range(2):
            three = third if b == 1 else pltpu.roll(third, 64, 1)
            kernel[0, pl.ds(b, 24, stride=2), :] = jnp.where(
                lane >= 64, three, kernel[0, pl.ds(b, 24, stride=2), :]
            )
        row, tile = 36, 1
        for number in range(3, 7):
            parts = channel_steps[number] * CH_UNIT // LANES
            depth = (number + 1) * CHAR_DIM
            for c in range(parts):
                kernel[tile, 0:depth, :] = flat[pl.ds(row + c, depth, stride=parts), :]
                tile += 1
            row += depth * parts
        bound = 0
        for number in range(7):
            upper = bound + channel_steps[number] * CH_UNIT
            for c in range(bound // LANES, -(-upper // LANES)):
                kernel[c, 112 + number : 113 + number, :] = jnp.where(
                    (lane + c * LANES >= bound) & (lane + c * LANES < upper), -HUGE, 0.0
                )
            bound = upper
        for c in range(CONV // LANES):
            kernel[c, 119:120, :] = flat[row + c : row + c + 1, :]
            ck_ref[:, c * LANES : (c + 1) * LANES] = to_low(kernel[c])
        pl.semaphore_wait(barrier, len(others))
        copies = []
        for i, s in enumerate(others):
            for j, ref in enumerate((ck_ref, tt_ref)):
                copies.append(
                    pltpu.make_async_remote_copy(
                        ref, ref, send.at[i, j], recv.at[j], device_id={"section": s}, device_id_type=MESH
                    )
                )
        for copy in copies:
            copy.start()
        for copy in copies:
            copy.wait_send()

    for s in others:

        @pl.when(section == s)
        def _():
            pl.semaphore_signal(barrier, inc=1, device_id={"section": 0}, device_id_type=MESH)
            pl.semaphore_wait(barrier, 1)
            for j, ref in enumerate((ck_ref, tt_ref)):
                pltpu.make_async_remote_copy(
                    ref, ref, send.at[0, j], recv.at[j], device_id={"section": 0}, device_id_type=MESH
                ).wait_recv()


def cnn_params(params):
    return pl.pallas_call(
        cnn_params_kernel,
        out_shape=[
            jax.ShapeDtypeStruct((LANES, CONV), BF),
            jax.ShapeDtypeStruct((TABLE_ROWS, LANES), BF),
        ],
        in_specs=[hbm()],
        out_specs=[vmem(), vmem()],
        scratch_shapes=[
            pltpu.VMEM((1, CNN_ROWS * LANES), BF),
            pltpu.VMEM((CNN_ROWS, LANES), F32),
            pltpu.VMEM((CONV // LANES, LANES, LANES), F32),
            pltpu.VMEM((TABLE_ROWS, LANES), F32),
            pltpu.SemaphoreType.DMA,
            pltpu.SemaphoreType.DMA((len(CNN) - 1, 2)),
            pltpu.SemaphoreType.DMA((2,)),
        ],
        compiler_params=pltpu.CompilerParams(
            collective_id=0, has_side_effects=True, vmem_limit_bytes=24 << 20
        ),
    )(params)


STAGES = ((128, 1), (64, 2), (16, 8))
SPOTS = CHAR_LEN + 14


def stage_bounds(lengths, blocks):
    words = lengths.shape[0] // blocks
    counts = jnp.sum(lengths.reshape(blocks, words, 1) > jnp.arange(CHAR_LEN, dtype=jnp.int32), axis=1)
    limits = jnp.array([[words // 2], [words // 8], [0]], jnp.int32)
    return jnp.sum(counts[:, None, :] > limits, axis=2).astype(jnp.int32)


def sorting(column_ref, row_ref):
    count = row_ref.shape[1]
    down = lax.broadcasted_iota(jnp.int32, (count, count), 0)
    across = lax.broadcasted_iota(jnp.int32, (count, count), 1)
    column, row = column_ref[...], row_ref[...]
    before = (column > row) | ((column == row) & (down < across))
    rank = jnp.sum(jnp.where(before, 1, 0), axis=0, keepdims=True)
    return jnp.where(down == rank, 1.0, 0.0).astype(BF)


def sorted_words(order, ids_ref, column_ref):
    ids = ids_ref[...]
    high = lax.div(ids, 16)
    low = ids - 16 * high
    ids = matmul(order, to_low(as_float(high))) * 16.0 + matmul(order, to_low(as_float(low)))
    length = matmul(order, to_low(as_float(jnp.broadcast_to(column_ref[...], (ids.shape[0], LANES)))))
    return ids, length


def stages(ends_ref, body):
    start = 0
    for k, (words, positions) in enumerate(STAGES):
        end = ends_ref[k]

        def one(i, unused, words=words, positions=positions, start=start, end=end):
            body(start + i * positions, words, positions, end)
            return unused

        lax.fori_loop(0, lax.div(jnp.maximum(end - start, 0) + positions - 1, positions), one, 0)
        start = end


def one_hot(first, words, positions, ids):
    lane = lax.broadcasted_iota(jnp.int32, (words, CHAR_LEN), 1)
    columns = [
        jnp.sum(jnp.where(lane == first + q, ids[0:words, :], 0.0), axis=1, keepdims=True) for q in range(positions)
    ]
    column = columns[0] if positions == 1 else jnp.concatenate(columns, axis=0)
    symbol = lax.broadcasted_iota(jnp.int32, (words * positions, TABLE_ROWS), 1)
    return jnp.where(column.astype(jnp.int32) == symbol, 1.0, 0.0).astype(BF)


def windows(first, words, positions, end, length, embedded, masks):
    total = None
    for j in range(7):
        term = embedded[pl.ds(first + j, positions), 0:words, :] * masks[j]
        total = term if total is None else total + term
    shape = (positions, words, LANES)
    lane = lax.broadcasted_iota(jnp.int32, shape, 2)
    position = first + lax.broadcasted_iota(jnp.int32, shape, 0)
    room = jnp.broadcast_to(length[0:words, :][None], shape)
    out = (lane >= 112) & (lane < 119) & ((as_float(position + lane - 111) > room) | (position >= end))
    return (total + jnp.where(out | (lane == 119), 1.0, 0.0).astype(BF)).reshape(positions * words, LANES)


def lane_masks():
    lane = lax.broadcasted_iota(jnp.int32, (1, 1, LANES), 2)
    return [
        jnp.where((lane >= j * CHAR_DIM) & (lane < (j + 1) * CHAR_DIM), 1.0, 0.0).astype(BF)
        for j in range(7)
    ]


def embedder(ids, tt_ref, embedded):
    def embed(first, words, positions, end):
        value = to_low(matmul(one_hot(first, words, positions, ids), tt_ref[...]))
        embedded[pl.ds(first, positions), 0:words, :] = value.reshape(positions, words, LANES)

    return embed


def chars_forward_kernel(ends_ref, ids_ref, column_ref, row_ref, ck_ref, tt_ref, out_ref, embedded, best):
    embedded[...] = jnp.zeros_like(embedded)
    best[...] = jnp.full_like(best, -HUGE)
    masks = lane_masks()
    order = sorting(column_ref, row_ref)
    ids, length = sorted_words(order, ids_ref, column_ref)
    stages(ends_ref, embedder(ids, tt_ref, embedded))

    def pool(first, words, positions, end):
        rows = windows(first, words, positions, end, length, embedded, masks)
        for c in range(0, CONV, 512):
            pre = jnp.max(matmul(rows, ck_ref[:, c : c + 512]).reshape(positions, words, 512), axis=0)
            best[0:words, c : c + 512] = jnp.maximum(best[0:words, c : c + 512], pre)

    stages(ends_ref, pool)
    out_ref[...] = to_low(matmul_tn(order, to_low(jnp.maximum(best[...], 0.0))))


def chars_backward_kernel(
    all_ends_ref, ids_ref, column_ref, row_ref, ck_ref, tt_ref, grad_ref,
    out_ref, embedded, best, share, backs, sums,
):
    block = pl.program_id(0)
    ends_ref = [all_ends_ref[block, k] for k in range(len(STAGES))]
    embedded[...] = jnp.zeros_like(embedded)
    backs[...] = jnp.zeros_like(backs)
    best[...] = jnp.full_like(best, -HUGE)
    share[...] = jnp.zeros_like(share)
    table_rows = pl.ds(CONV, TABLE_ROWS)

    @pl.when(block == 0)
    def _():
        sums[...] = jnp.zeros_like(sums)
        out_ref[table_rows, :] = jnp.zeros((TABLE_ROWS, LANES), F32)

    masks = lane_masks()
    order = sorting(column_ref, row_ref)
    ids, length = sorted_words(order, ids_ref, column_ref)
    stages(ends_ref, embedder(ids, tt_ref, embedded))

    def count(first, words, positions, end):
        rows = windows(first, words, positions, end, length, embedded, masks)
        for c in range(0, CONV, 512):
            part = slice(c, c + 512)
            pre = matmul(rows, ck_ref[:, part])
            top, hits = best[0:words, part], share[0:words, part]
            for q in range(positions):
                here = pre[q * words : (q + 1) * words]
                hits = jnp.where(here > top, 1.0, hits + jnp.where(here == top, 1.0, 0.0))
                top = jnp.maximum(top, here)
            best[0:words, part], share[0:words, part] = top, hits

    stages(ends_ref, count)
    share[...] = matmul(order, grad_ref[...]) / share[...]
    best[...] = jnp.where(best[...] > 0.0, best[...], 3e38)

    def spread(first, words, positions, end):
        rows = windows(first, words, positions, end, length, embedded, masks)
        back = jnp.zeros((words * positions, LANES), F32)
        for c in range(0, CONV, 512):
            part = slice(c, c + 512)
            pre = matmul(rows, ck_ref[:, part]).reshape(positions, words, 512)
            hit = pre == best[0:words, part][None]
            grad = to_low(jnp.where(hit, jnp.broadcast_to(share[0:words, part][None], pre.shape), 0.0))
            grad = grad.reshape(positions * words, 512)
            sums[:, part] += matmul_tn(rows, grad)
            back = back + matmul_nt(grad, ck_ref[:, part])
        backs[pl.ds(first + 6, positions), 0:words, :] = to_low(back).reshape(positions, words, LANES)

    stages(ends_ref, spread)

    def gather(first, words, positions, end):
        shape = (positions, words, LANES)
        lane = lax.broadcasted_iota(jnp.int32, shape, 2)
        position = first + lax.broadcasted_iota(jnp.int32, shape, 0)
        total = jnp.zeros(shape, F32)
        for j in range(7):
            here = (lane >= j * CHAR_DIM) & (lane < (j + 1) * CHAR_DIM) & (position < end)
            total = jnp.where(here, as_float(backs[pl.ds(first + 6 - j, positions), 0:words, :]), total)
        hot = one_hot(first, words, positions, ids)
        out_ref[table_rows, :] += matmul_tn(hot, to_low(total).reshape(positions * words, LANES))

    stages(ends_ref, gather)

    @pl.when(block == pl.num_programs(0) - 1)
    def _():
        for c in range(CONV // LANES):
            out_ref[c * LANES : (c + 1) * LANES, :] = sums[:, c * LANES : (c + 1) * LANES]


def chars_forward(ends, ids, column, row, ck, tt):
    words = ids.shape[0]
    return pl.pallas_call(
        chars_forward_kernel,
        out_shape=jax.ShapeDtypeStruct((words, CONV), BF),
        in_specs=[pl.BlockSpec(memory_space=pltpu.SMEM)] + [vmem()] * 5,
        out_specs=vmem(),
        scratch_shapes=[
            pltpu.VMEM((SPOTS, words, LANES), BF),
            pltpu.VMEM((words, CONV), F32),
        ],
        compiler_params=pltpu.CompilerParams(vmem_limit_bytes=32 << 20),
    )(ends, ids, column, row, ck, tt)


def chars_backward(ends, ids, column, row, ck, tt, grad):
    words = ids.shape[0] // len(CNN)
    return pl.pallas_call(
        chars_backward_kernel,
        grid=(len(CNN),),
        out_shape=jax.ShapeDtypeStruct((CNN_GRADS, LANES), F32),
        in_specs=[
            pl.BlockSpec(memory_space=pltpu.SMEM),
            pl.BlockSpec((words, CHAR_LEN), lambda i: (i, 0)),
            pl.BlockSpec((words, 1), lambda i: (i, 0)),
            pl.BlockSpec((1, words), lambda i: (0, i)),
            pl.BlockSpec((LANES, CONV), lambda i: (0, 0)),
            pl.BlockSpec((TABLE_ROWS, LANES), lambda i: (0, 0)),
            pl.BlockSpec((words, CONV), lambda i: (i, 0)),
        ],
        out_specs=pl.BlockSpec((CNN_GRADS, LANES), lambda i: (0, 0)),
        scratch_shapes=[
            pltpu.VMEM((SPOTS, words, LANES), BF),
            pltpu.VMEM((words, CONV), F32),
            pltpu.VMEM((words, CONV), F32),
            pltpu.VMEM((SPOTS, words, LANES), BF),
            pltpu.VMEM((LANES, CONV), F32),
        ],
        compiler_params=pltpu.CompilerParams(vmem_limit_bytes=40 << 20),
    )(ends, ids, column, row, ck, tt, grad)


def cnn_gradient(grads):
    table_grad = grads[CONV:]
    kernel_grad = jnp.swapaxes(grads[:CONV].reshape(-1, LANES, LANES), 0, 1).reshape(LANES, CONV)
    pieces = [
        sum(table_grad[:CHARS, g * CHAR_DIM : (g + 1) * CHAR_DIM] for g in range(7)).reshape(-1)
    ]
    offset = 0
    for number in range(7):
        channels = channel_steps[number] * CH_UNIT
        pieces.append(
            kernel_grad[: (number + 1) * CHAR_DIM, offset : offset + channels].reshape(-1)
        )
        offset += channels
    pieces.append(kernel_grad[119])
    return jnp.concatenate(pieces)


def sigmoid(value):
    return 1.0 / (1.0 + jnp.exp(-value))


def highway_layer_kernel(row, x_ref, part_ref, w_ref, bl_ref, br_ref, next_ref, left_ref, right_ref):
    both = matmul(x_ref[...], w_ref[0])
    left = both[:, :HW_CHUNK] + bl_ref[row : row + 1, :]
    right = both[:, HW_CHUNK:] + br_ref[row : row + 1, :]
    left_ref[...] = left
    right_ref[...] = right
    gate = sigmoid(right)
    next_ref[...] = to_low(gate * as_float(part_ref[...]) + (1.0 - gate) * jnp.maximum(left, 0.0))


def highway_layer(row, x, w, vec):
    group = x.shape[0]
    steps = CONV // HW_CHUNK
    part = pl.BlockSpec((group, HW_CHUNK), lambda i: (0, i))
    return pl.pallas_call(
        functools.partial(highway_layer_kernel, row),
        grid=(steps,),
        out_shape=[
            jax.ShapeDtypeStruct((group, CONV), BF),
            jax.ShapeDtypeStruct((group, CONV), F32),
            jax.ShapeDtypeStruct((group, CONV), F32),
        ],
        in_specs=[
            pl.BlockSpec((group, CONV), lambda i: (0, 0)),
            part,
            pl.BlockSpec((1,) + HW_SHAPE[1:], lambda i: (i, 0, 0)),
            pl.BlockSpec((8, HW_CHUNK), lambda i: (0, i)),
            pl.BlockSpec((8, HW_CHUNK), lambda i: (0, i + steps)),
        ],
        out_specs=[part, part, part],
        compiler_params=pltpu.CompilerParams(vmem_limit_bytes=40 << 20),
    )(x, x, w, vec, vec)


def highway_forward(w0, w1, wp, vec, wide_in):
    x1, left0, right0 = highway_layer(0, wide_in, w0, vec)
    x2, left1, right1 = highway_layer(1, x1, w1, vec)
    projected = to_low(matmul(x2, wp) + vec[2, :D])
    return (projected, x1, x2, left0, right0, left1, right1)


def highway_back_kernel(last, up_ref, wp_ref, x_ref, left_ref, right_ref, w_ref, grad_ref, out_ref, total):
    i = pl.program_id(0)
    flowing = matmul_nt(up_ref[...], wp_ref[...]) if wp_ref is not None else up_ref[...]
    gate = sigmoid(right_ref[...])
    left = left_ref[...]
    nonlinear = jnp.maximum(left, 0.0)
    closed = flowing * (1.0 - gate)
    grad_left = to_low(jnp.where(left > 0.0, closed, 0.0))
    grad_right = to_low(closed * (as_float(x_ref[...]) - nonlinear) * gate)
    grad_ref[0] = grad_left
    grad_ref[1] = grad_right
    back = matmul_nt(jnp.concatenate([grad_left, grad_right], axis=1), w_ref[0])

    @pl.when(i == 0)
    def _():
        total[...] = back

    @pl.when(i > 0)
    def _():
        total[...] += back

    here = pl.ds(pl.multiple_of(i * HW_CHUNK, HW_CHUNK), HW_CHUNK)
    total[:, here] += flowing * gate

    @pl.when(i == pl.num_programs(0) - 1)
    def _():
        out_ref[...] = to_low(total[...]) if last else total[...]


def highway_back(last, up, wp, x, left, right, w):
    group = x.shape[0]
    steps = CONV // HW_CHUNK
    part = pl.BlockSpec((group, HW_CHUNK), lambda i: (0, i))
    if wp is None:
        kernel = lambda up_ref, *refs: highway_back_kernel(last, up_ref, None, *refs)
        sources, specs = [up], [part]
    else:
        kernel = functools.partial(highway_back_kernel, last)
        sources = [up, wp]
        specs = [pl.BlockSpec((group, D), lambda i: (0, 0)), pl.BlockSpec((HW_CHUNK, D), lambda i: (i, 0))]
    return pl.pallas_call(
        kernel,
        grid=(steps,),
        out_shape=[
            jax.ShapeDtypeStruct((2, group, CONV), BF),
            jax.ShapeDtypeStruct((group, CONV), BF if last else F32),
        ],
        in_specs=specs
        + [
            part,
            part,
            part,
            pl.BlockSpec((1,) + HW_SHAPE[1:], lambda i: (i, 0, 0)),
        ],
        out_specs=[
            pl.BlockSpec((2, group, HW_CHUNK), lambda i: (0, 0, i)),
            pl.BlockSpec((group, CONV), lambda i: (0, 0)),
        ],
        scratch_shapes=[pltpu.VMEM((group, CONV), F32)],
        compiler_params=pltpu.CompilerParams(vmem_limit_bytes=40 << 20),
    )(*sources, x, left, right, w)


def highway_backward(w0, w1, wp, wide_in, x1, left0, right0, left1, right1, upstream):
    grad1, flowing = highway_back(False, upstream, wp, x1, left1, right1, w1)
    grad0, grad_pooled = highway_back(True, flowing, None, wide_in, left0, right0, w0)
    return (grad_pooled, grad0, grad1)


def layer_norm(residual):
    centered = residual - jnp.mean(residual, axis=-1, keepdims=True)
    inverse = lax.rsqrt(jnp.mean(centered * centered, axis=-1, keepdims=True) + layer_eps)
    return centered * inverse, inverse


def norm_backward(upstream, scaled, inverse, gain):
    weighted = upstream * gain
    first_mean = jnp.mean(weighted, axis=-1, keepdims=True)
    cross_mean = jnp.mean(weighted * scaled, axis=-1, keepdims=True)
    return inverse * (weighted - first_mean - scaled * cross_mean)


def encoder_kernel(
    x_ref, cot_ref, wqkv_ref, wo_ref, wu_ref, wd_ref, vec_ref, vec3_ref,
    layer_ref, back_ref, joined_ref, mixed_ref, att_ref, normed_ref, act_ref, inner_ref, branch_ref, sums_ref,
    qkv, probs, slope, scaled, carry,
):
    rows = x_ref.shape[0]
    pairs = HEADS // 2
    scale = HEAD_DIM ** (-0.5)
    lane = lax.broadcasted_iota(jnp.int32, (1, LANES), 1)
    halves = [jnp.where(lane < HEAD_DIM, 1.0, 0.0).astype(BF), jnp.where(lane < HEAD_DIM, 0.0, 1.0).astype(BF)]

    def heads(body):
        def one(i, unused):
            sequence, pair = lax.div(i, pairs), lax.rem(i, pairs)
            body(
                pl.ds(pl.multiple_of(sequence * SEQ_LEN, SEQ_LEN), SEQ_LEN),
                [pl.ds(pl.multiple_of(pair * LANES + k * D, LANES), LANES) for k in range(3)],
                i,
            )
            return unused

        lax.fori_loop(0, rows // SEQ_LEN * pairs, one, 0)

    def pieces(width, body):
        def one(i, unused):
            body(pl.ds(pl.multiple_of(i * width, width), width))
            return unused

        return lambda count: lax.fori_loop(0, count, one, 0)

    @pl.when(lax.axis_index("section") >= 2)
    def _():
        for k, bias in enumerate((vec_ref[0:1, 0:D], None, vec_ref[1:2, 0:D])):
            part = matmul(x_ref[...], wqkv_ref[:, k * D : (k + 1) * D])
            qkv[:, k * D : (k + 1) * D] = to_low(part if bias is None else part + bias)

        def attend(here, columns, i):
            query, key, value = (qkv[here, columns[k]] for k in range(3))
            out = []
            for half in range(2):
                scores = matmul_nt(query * halves[half], key) * scale
                exponent = jnp.exp(scores - jnp.max(scores, axis=-1, keepdims=True))
                soft = exponent / jnp.sum(exponent, axis=-1, keepdims=True)
                probs[2 * i + half] = soft
                out.append(matmul(to_low(soft), value))
            mixed_ref[here, columns[0]] = to_low(jnp.where(lane < HEAD_DIM, out[0], out[1]))

        heads(attend)
        residual = as_float(x_ref[...]) + matmul(mixed_ref[...], wo_ref[...]) + vec_ref[2:3, 0:D]
        scaled1, inverse1 = layer_norm(residual)
        scaled[...] = scaled1
        normed_ref[...] = to_low(scaled1 * vec_ref[3:4, 0:D] + vec_ref[4:5, 0:D])

        def up(part):
            inner = matmul(normed_ref[...], wu_ref[:, part]) + vec3_ref[0:1, part]
            phi = 0.5 * (1.0 + lax.erf(inner * 0.7071067811865476))
            act_ref[:, part] = to_low(inner * phi)
            slope[:, part] = phi + inner * jnp.exp(-0.5 * inner * inner) * 0.3989422804014327

        pieces(512, up)(FF // 512)
        residual = as_float(normed_ref[...]) + matmul(act_ref[...], wd_ref[...]) + vec3_ref[1:2, 0:D]
        scaled2, inverse2 = layer_norm(residual)
        gain2 = vec3_ref[2:3, 0:D]
        layer_ref[...] = to_low(scaled2 * gain2 + vec3_ref[3:4, 0:D])
        upstream = as_float(cot_ref[...])
        sums_ref[2:3, :] = jnp.sum(upstream * scaled2, axis=0, keepdims=True)
        sums_ref[3:4, :] = jnp.sum(upstream, axis=0, keepdims=True)
        carry[...] = norm_backward(upstream, scaled2, inverse2, gain2)
        branch_ref[...] = to_low(carry[...])

        def down(part):
            inner_ref[:, part] = to_low(matmul_nt(branch_ref[...], wd_ref[part, :]) * slope[:, part])

        pieces(512, down)(FF // 512)
        upstream = as_float(to_low(carry[...] + matmul_nt(inner_ref[...], wu_ref[...])))
        sums_ref[0:1, :] = jnp.sum(upstream * scaled[...], axis=0, keepdims=True)
        sums_ref[1:2, :] = jnp.sum(upstream, axis=0, keepdims=True)
        carry[...] = norm_backward(upstream, scaled[...], inverse1, vec_ref[3:4, 0:D])
        att_ref[...] = to_low(carry[...])
        back_ref[...] = to_low(matmul_nt(att_ref[...], wo_ref[...]))

        def attend_back(here, columns, i):
            query, key, value = (qkv[here, columns[k]] for k in range(3))
            grad = back_ref[here, columns[0]]
            totals = [0.0, 0.0, 0.0]
            for half in range(2):
                grad_half = grad * halves[half]
                soft = probs[2 * i + half]
                grad_soft = matmul_nt(grad_half, value)
                flow = to_low(soft * (grad_soft - jnp.sum(grad_soft * soft, axis=-1, keepdims=True)))
                totals[0] += matmul(flow, key * halves[half])
                totals[1] += matmul_tn(flow, query * halves[half])
                totals[2] += matmul_tn(to_low(soft), grad_half)
            joined_ref[here, columns[0]] = to_low(totals[0] * scale)
            joined_ref[here, columns[1]] = to_low(totals[1] * scale)
            joined_ref[here, columns[2]] = to_low(totals[2])

        heads(attend_back)
        back_ref[...] = to_low(carry[...] + matmul_nt(joined_ref[...], wqkv_ref[...]))


def encoder(x, cot, wqkv, wo, wu, wd, vec, vec3):
    rows = x.shape[0]
    widths = [D, D, 3 * D, D, D, D, FF, FF, D]
    return pl.pallas_call(
        encoder_kernel,
        out_shape=[jax.ShapeDtypeStruct((rows, w), BF) for w in widths] + [jax.ShapeDtypeStruct((8, D), F32)],
        in_specs=[vmem()] * 8,
        out_specs=[vmem()] * 10,
        scratch_shapes=[
            pltpu.VMEM((rows, 3 * D), BF),
            pltpu.VMEM((rows // SEQ_LEN * HEADS, SEQ_LEN, SEQ_LEN), F32),
            pltpu.VMEM((rows, FF), F32),
            pltpu.VMEM((rows, D), F32),
            pltpu.VMEM((rows, D), F32),
        ],
        compiler_params=pltpu.CompilerParams(vmem_limit_bytes=56 << 20),
    )(x, cot, wqkv, wo, wu, wd, vec, vec3)


def side_rows_kernel(*refs):
    section = lax.axis_index("section")
    own, other, (out_hbm, flat, out_ref, *targets, sem) = refs[:9], refs[9:18], refs[18:]
    x_ref, mixed_ref, joined_ref, att_ref, normed_ref, act_ref, inner_ref, branch_ref, sums_ref = targets

    def fetch(*places):
        copies = []
        for i in places:
            rows = own[i].shape[0]
            for k, source in enumerate((own[i], other[i])):
                copies.append(pltpu.make_async_copy(source, targets[i].at[pl.ds(k * rows, rows)], sem.at[k, i]))
        for copy in copies:
            copy.start()
        for copy in copies:
            copy.wait()

    def product(left_ref, right_ref, row):
        count, width = left_ref.shape[1], right_ref.shape[1]
        parts = width // LANES
        for k in range(count // D):
            for c in range(0, width, 256):
                block = matmul_tn(left_ref[:, k * D : (k + 1) * D], right_ref[:, c : c + 256])
                for t in range(2):
                    flat[pl.ds(row + k * D * parts + c // LANES + t, D, stride=parts), :] = block[:, t * LANES : (t + 1) * LANES]
        return row + count * parts

    def line(row, values):
        for c in range(values.shape[1] // LANES):
            flat[row + c : row + c + 1, :] = values[:, c * LANES : (c + 1) * LANES]
        return row + values.shape[1] // LANES

    def summed(ref, first, last):
        return jnp.sum(as_float(ref[:, first:last]), axis=0, keepdims=True)

    def write(row):
        full = out_ref.shape[0]
        flat[row:full, :] = jnp.zeros((full - row, LANES), F32)
        out_ref[...] = to_low(flat[...])
        copy = pltpu.make_async_copy(out_ref, out_hbm, sem.at[0, 0])
        copy.start()
        copy.wait()

    @pl.when(section == 2)
    def _():
        fetch(0, 1, 2, 3, 8)
        row = product(x_ref, joined_ref, 0)
        row = line(row, summed(joined_ref, 0, D))
        row = line(row, summed(joined_ref, 2 * D, 3 * D))
        row = product(mixed_ref, att_ref, row)
        row = line(row, summed(att_ref, 0, D))
        row = line(row, sums_ref[0:1, :] + sums_ref[8:9, :])
        write(line(row, sums_ref[1:2, :] + sums_ref[9:10, :]))

    @pl.when(section == 3)
    def _():
        fetch(4, 5, 6, 7, 8)
        row = product(normed_ref, inner_ref, 0)
        row = line(row, summed(inner_ref, 0, FF))
        row = product(act_ref, branch_ref, row)
        row = line(row, summed(branch_ref, 0, D))
        row = line(row, sums_ref[2:3, :] + sums_ref[10:11, :])
        write(line(row, sums_ref[3:4, :] + sums_ref[11:12, :]))


def side_rows(own, other):
    size = (SIDE_SHARE + SIDE_ROWS * SIDE_CHUNKS, LANES)
    return pl.pallas_call(
        side_rows_kernel,
        out_shape=jax.ShapeDtypeStruct(size, BF),
        in_specs=[hbm()] * (2 * len(own)),
        out_specs=hbm(),
        scratch_shapes=[pltpu.VMEM(size, F32), pltpu.VMEM(size, BF)]
        + [pltpu.VMEM((2 * value.shape[0], value.shape[1]), value.dtype) for value in own]
        + [pltpu.SemaphoreType.DMA((2, len(own)))],
        compiler_params=pltpu.CompilerParams(vmem_limit_bytes=50 << 20),
    )(*own, *other)


def stack_kernel(x0_ref, x1_ref, x2_ref, xt_hbm, x2t_hbm, low, turned, sem):
    group = x0_ref.shape[0]

    @pl.when(lax.axis_index("section") == 1)
    def _():
        turned[CONV:STACK, :] = jnp.where(
            lax.broadcasted_iota(jnp.int32, (STACK - CONV, group), 0) == 0, 1.0, 0.0
        ).astype(BF)
        targets = (xt_hbm.at[pl.ds(0, STACK)], xt_hbm.at[pl.ds(STACK, STACK)], x2t_hbm)
        for source, target in zip((x0_ref, x1_ref, x2_ref), targets, strict=True):
            copy = pltpu.make_async_copy(source, low, sem)
            copy.start()
            copy.wait()
            for c in range(0, CONV, 512):
                turned[c : c + 512, :] = low[:, c : c + 512].T
            copy = pltpu.make_async_copy(turned, target, sem)
            copy.start()
            copy.wait()


def stack_highways(x0, x1, x2):
    group = x0.shape[0]
    return pl.pallas_call(
        stack_kernel,
        out_shape=[jax.ShapeDtypeStruct((2 * STACK, group), BF), jax.ShapeDtypeStruct((STACK, group), BF)],
        in_specs=[hbm()] * 3,
        out_specs=[hbm()] * 2,
        scratch_shapes=[
            pltpu.VMEM((group, CONV), BF),
            pltpu.VMEM((STACK, group), BF),
            pltpu.SemaphoreType.DMA,
        ],
        compiler_params=pltpu.CompilerParams(vmem_limit_bytes=24 << 20),
    )(x0, x1, x2)


SLICE = 592
CHUNK = 256
N_CHUNK = 2 * CONV // CHUNK
STACK = CONV + 16
LAG = 3
SLOTS = 4
FRONT = 80
Z = 4


def reduce_kernel(
    share, xt_hbm, x2t_hbm, g0_hbm, g1_hbm, gp_hbm, out_ref, land_ref,
    xt_ref, x2t_ref, g_ref, gp_ref, load, tile, flat, y_out, y_in, z_out, z_in, y_send, y_recv, z_send, z_recv, sem,
):
    section = lax.axis_index("section")
    b = lax.axis_index("batch")
    y, z = lax.rem(b, 2), lax.div(b, 2)
    steps = Z * N_CHUNK

    def owner(step):
        o = lax.rem(step, Z)
        up = jnp.where(z == 0, 3 - o, jnp.where(o == 0, 3, jnp.where(o == 1, 0, jnp.where(o == 2, 2, 1))))
        down = jnp.where(z == 3, o, jnp.where(o == 0, 0, jnp.where(o == 1, 3, jnp.where(o == 2, 1, 2))))
        return jnp.where(z < 2, up, down)

    def product(part, j):
        column = pl.multiple_of(j * CHUNK, CHUNK)

        @pl.when((part != 3) & (part != 7))
        def _():
            row = pl.multiple_of((35 * part + jnp.where(part >= 4, 1, 0)) * 16, 16)
            col = pl.multiple_of(column + jnp.where(part >= 4, 2 * CONV, 0), CHUNK)
            tile[...] = matmul(xt_ref[pl.ds(row, SLICE), :], g_ref[:, pl.ds(col, CHUNK)])

        second = pl.ds(pl.multiple_of(column + 2 * CONV, CHUNK), CHUNK)

        @pl.when(part == 3)
        def _():
            tile[0:384, :] = matmul(xt_ref[1680:STACK, :], g_ref[:, pl.ds(column, CHUNK)])
            tile[384:SLICE, :] = matmul(xt_ref[STACK : STACK + SLICE - 384, :], g_ref[:, second])

        @pl.when(part == 7)
        def _():
            tile[0:192, :] = matmul(xt_ref[2 * STACK - 192 : 2 * STACK, :], g_ref[:, second])

            @pl.when(j < 15)
            def _():
                row = pl.multiple_of(lax.rem(j, 5) * 400, 16)
                col = pl.multiple_of(lax.div(j, 5) * 256, 256)
                tile[192:SLICE, :] = matmul(x2t_ref[pl.ds(row, 400), :], gp_ref[:, pl.ds(col, 256)])

            @pl.when(j == 15)
            def _():
                for p in range(3):
                    tile[192 + 64 * p : 256 + 64 * p, :] = matmul(
                        x2t_ref[2000:STACK, :], gp_ref[:, p * 256 : (p + 1) * 256]
                    )
                tile[384:SLICE, :] = jnp.zeros((SLICE - 384, CHUNK), F32)

    def y_copy(part, j, slot):
        place = part * N_CHUNK + j
        return pltpu.make_async_remote_copy(
            y_out.at[slot], y_in.at[place], y_send.at[slot], y_recv.at[place],
            device_id={"batch": b + 1 - 2 * y}, device_id_type=MESH,
        )

    def z_copy(part, j, o, down):
        place = part * N_CHUNK + j
        side = 0 if down else 1
        return pltpu.make_async_remote_copy(
            z_out.at[o], land_ref.at[side, place], z_send.at[o], z_recv.at[side, place],
            device_id={"batch": b - 2 if down else b + 2}, device_id_type=MESH,
        )

    def send_y(step):
        part, j, slot = owner(step), lax.div(step, Z), lax.rem(step, SLOTS)
        product(2 * part + 1 - y, j)

        @pl.when(step >= SLOTS)
        def _():
            y_copy(part, j, slot).wait_send()

        y_out[slot] = to_low(tile[...])
        y_copy(part, j, slot).start()

    def arriving(side, place, buffer):
        pltpu.make_async_remote_copy(
            z_out.at[0], land_ref.at[side, place], z_send.at[0], z_recv.at[side, place],
            device_id={"batch": b}, device_id_type=MESH,
        ).wait_recv()
        pltpu.make_async_copy(land_ref.at[side, place], z_in.at[buffer], sem.at[buffer]).start()

    def arrived(side, place, buffer):
        pltpu.make_async_copy(land_ref.at[side, place], z_in.at[buffer], sem.at[buffer]).wait()
        tile[...] += as_float(z_in[buffer])

    def keep(j):
        base = FRONT - 16 * b + jnp.where(b >= 4, 32, 0) + j * (CHUNK // LANES)

        def rows(first, count, start, column, stride):
            flat[pl.ds(start, count, stride=stride), :] = tile[first : first + count, column : column + LANES]

        @pl.when((b != 3) & (b != 7))
        def _():
            for c in range(CHUNK // LANES):
                rows(0, SLICE, base + c, c * LANES, 32)

        @pl.when(b == 3)
        def _():
            for c in range(CHUNK // LANES):
                rows(0, 369, base + c, c * LANES, 32)
                rows(384, SLICE - 384, FRONT + 11760 + j * (CHUNK // LANES) + c, c * LANES, 32)

        @pl.when(b == 7)
        def _():
            for c in range(CHUNK // LANES):
                rows(0, 177, base + c, c * LANES, 32)

            @pl.when(j < 15)
            def _():
                start = FRONT + 5584 + lax.rem(j, 5) * (400 * 6) + lax.div(j, 5) * 2
                for c in range(2):
                    rows(192, 400, start + c, c * LANES, 6)

            @pl.when(j == 15)
            def _():
                for p in range(3):
                    for c in range(2):
                        rows(192 + 64 * p, 64, FRONT + 5584 + 2000 * 6 + 2 * p + c, c * LANES, 6)

    def combine(part, j, o):
        place = part * N_CHUNK + j
        above = (part <= z) & (z < Z - 1)
        below = (part >= z) & (z > 0)

        @pl.when(above)
        def _():
            arriving(0, place, 0)

        @pl.when(below)
        def _():
            arriving(1, place, 1)

        product(2 * part + y, j)
        y_copy(part, j, 0).wait_recv()
        tile[...] += as_float(y_in[place])

        @pl.when(above)
        def _():
            arrived(0, place, 0)

        @pl.when(below)
        def _():
            arrived(1, place, 1)

        @pl.when(part == z)
        def _():
            keep(j)

        @pl.when(part != z)
        def _():
            @pl.when(j > 0)
            def _():
                z_copy(part, j, o, True).wait_send()

            z_out[o] = to_low(tile[...])

            @pl.when(part < z)
            def _():
                z_copy(part, j, o, True).start()

            @pl.when(part > z)
            def _():
                z_copy(part, j, o, False).start()

    @pl.when(section == 1)
    def _():
        loads = [
            pltpu.make_async_copy(source, target, load.at[i])
            for i, (source, target) in enumerate(
                [(xt_hbm, xt_ref), (x2t_hbm, x2t_ref), (gp_hbm, gp_ref)]
                + [
                    (source.at[half], g_ref.at[:, pl.ds((2 * layer + half) * CONV, CONV)])
                    for layer, source in enumerate((g0_hbm, g1_hbm))
                    for half in range(2)
                ]
            )
        ]
        for copy in loads:
            copy.start()
        barrier = pltpu.get_barrier_semaphore()
        pl.semaphore_signal(barrier, inc=1, device_id={"batch": b + 1 - 2 * y}, device_id_type=MESH)

        @pl.when(z > 0)
        def _():
            pl.semaphore_signal(barrier, inc=1, device_id={"batch": b - 2}, device_id_type=MESH)

        @pl.when(z < Z - 1)
        def _():
            pl.semaphore_signal(barrier, inc=1, device_id={"batch": b + 2}, device_id_type=MESH)

        pl.semaphore_wait(barrier, 1 + jnp.where(z > 0, 1, 0) + jnp.where(z < Z - 1, 1, 0))
        for copy in loads:
            copy.wait()
        def step_body(step, carry):
            @pl.when(step < steps)
            def _():
                send_y(step)

            late = step - LAG
            part, o = owner(jnp.maximum(late, 0)), lax.rem(jnp.maximum(late, 0), Z)
            hops = jnp.where(part < z, 3 - z, jnp.where(part > z, z, jnp.maximum(z, 3 - z)))
            j = lax.div(jnp.maximum(late, 0), Z) - hops

            @pl.when((late >= 0) & (j >= 0) & (j < N_CHUNK))
            def _():
                combine(part, j, o)

            return carry

        lax.fori_loop(0, steps + LAG + (Z - 1) * Z, step_body, 0)
        for slot in range(SLOTS):
            y_copy(0, 0, slot).wait_send()
        for o in range(Z - 1):
            z_copy(0, 0, o, True).wait_send()
        copy = pltpu.make_async_copy(flat.at[pl.ds(FRONT, share)], out_ref, sem.at[0])
        copy.start()
        copy.wait()


def reduce_highways(xt, x2t, g0, g1, gp, share):
    chunk = (SLICE, CHUNK)
    return pl.pallas_call(
        functools.partial(reduce_kernel, share),
        out_shape=[
            jax.ShapeDtypeStruct((share, LANES), F32),
            jax.ShapeDtypeStruct((2, Z * N_CHUNK) + chunk, BF),
        ],
        in_specs=[hbm()] * 5,
        out_specs=[hbm(), hbm()],
        scratch_shapes=[
            pltpu.VMEM(xt.shape, BF),
            pltpu.VMEM(x2t.shape, BF),
            pltpu.VMEM((gp.shape[0], 4 * CONV), BF),
            pltpu.VMEM(gp.shape, BF),
            pltpu.SemaphoreType.DMA((7,)),
            pltpu.VMEM(chunk, F32),
            pltpu.VMEM((FRONT + SLICE * 32, LANES), F32),
            pltpu.VMEM((SLOTS,) + chunk, BF),
            pltpu.VMEM((Z * N_CHUNK,) + chunk, BF),
            pltpu.VMEM((Z - 1,) + chunk, BF),
            pltpu.VMEM((2,) + chunk, BF),
            pltpu.SemaphoreType.DMA((SLOTS,)),
            pltpu.SemaphoreType.DMA((Z * N_CHUNK,)),
            pltpu.SemaphoreType.DMA((Z - 1,)),
            pltpu.SemaphoreType.DMA((2, Z * N_CHUNK)),
            pltpu.SemaphoreType.DMA((2,)),
        ],
        compiler_params=pltpu.CompilerParams(
            collective_id=1, has_side_effects=True, vmem_limit_bytes=60 << 20
        ),
    )(xt, x2t, g0, g1, gp)


SIDE_ROWS = 1200
SIDE_CHUNKS = 16
SIDE_REST = 1040
SIDE_SHARE = 17936


def side_kernel(
    share, row_ref, out_ref, own, y_in, z_in, z_out, total,
    y_send, y_recv, z_send, z_recv, l_send, l_recv, sem,
):
    section = lax.axis_index("section")
    b = lax.axis_index("batch")
    y, z = lax.rem(b, 2), lax.div(b, 2)

    def count(half):
        return jnp.where((section == 2) & (half == 1), 1, SIDE_CHUNKS)

    def rows(half, i):
        return pl.ds(pl.multiple_of(half * share + i * SIDE_ROWS, 16), SIDE_ROWS)

    def y_copy(i):
        return pltpu.make_async_remote_copy(
            row_ref.at[rows(1 - y, i)], y_in.at[i], y_send.at[i], y_recv.at[i],
            device_id={"batch": b + 1 - 2 * y}, device_id_type=MESH,
        )

    def z_copy(i):
        return pltpu.make_async_remote_copy(
            z_out.at[i], z_in.at[i], z_send.at[i], z_recv.at[i],
            device_id={"batch": b - 2}, device_id_type=MESH,
        )

    def rest_copy():
        return pltpu.make_async_remote_copy(
            total.at[pl.ds(share, SIDE_REST)], total.at[pl.ds(0, SIDE_REST)], l_send, l_recv,
            device_id={"batch": 2}, device_id_type=MESH,
        )

    def write():
        copy = pltpu.make_async_copy(total.at[pl.ds(0, share)], out_ref, sem)
        copy.start()
        copy.wait()

    @pl.when(section != 1)
    def _():
        total[...] = jnp.zeros_like(total)

    @pl.when(section == 0)
    def _():
        write()

    @pl.when(section >= 2)
    def _():
        barrier = pltpu.get_barrier_semaphore()

        pl.semaphore_signal(barrier, inc=1, device_id={"batch": b + 1 - 2 * y}, device_id_type=MESH)
        pairs = [(z > 0, b - 2), (z < Z - 1, b + 2), (b == 1, 2), (b == 2, 1)]
        for condition, other in pairs:

            @pl.when(condition)
            def _():
                pl.semaphore_signal(barrier, inc=1, device_id={"batch": other}, device_id_type=MESH)

        pl.semaphore_wait(barrier, 1 + sum(jnp.where(condition, 1, 0) for condition, _ in pairs))

        def send(i, carry):
            y_copy(i).start()
            return carry

        def combine(i, carry):
            copy = pltpu.make_async_copy(row_ref.at[rows(y, i)], own, sem)
            copy.start()
            copy.wait()
            y_copy(i).wait_recv()
            here = pl.ds(pl.multiple_of(i * SIDE_ROWS, 16), SIDE_ROWS)

            @pl.when(z == Z - 1)
            def _():
                z_out[i] = to_low(as_float(own[...]) + as_float(y_in[i]))

            @pl.when(z < Z - 1)
            def _():
                z_copy(i).wait_recv()

                @pl.when(z > 0)
                def _():
                    z_out[i] = to_low(as_float(own[...]) + as_float(y_in[i]) + as_float(z_in[i]))

                @pl.when(z == 0)
                def _():
                    total[here] = as_float(own[...]) + as_float(y_in[i]) + as_float(z_in[i])

            @pl.when(z > 0)
            def _():
                z_copy(i).start()

            return carry

        def drain(i, carry):
            y_copy(i).wait_send()
            return carry

        def drain_z(i, carry):
            z_copy(i).wait_send()
            return carry

        lax.fori_loop(0, count(1 - y), send, 0)
        lax.fori_loop(0, count(y), combine, 0)

        @pl.when((section == 3) & (b == 1))
        def _():
            rest_copy().start()
            rest_copy().wait_send()

        @pl.when((section == 3) & (b == 2))
        def _():
            rest_copy().wait_recv()

        write()
        lax.fori_loop(0, count(1 - y), drain, 0)

        @pl.when(z > 0)
        def _():
            lax.fori_loop(0, count(y), drain_z, 0)


def reduce_sides(row, share):
    chunk = (SIDE_ROWS, LANES)
    dma = pltpu.SemaphoreType.DMA
    return pl.pallas_call(
        functools.partial(side_kernel, share),
        out_shape=jax.ShapeDtypeStruct((share, LANES), F32),
        in_specs=[hbm()],
        out_specs=hbm(),
        scratch_shapes=[
            pltpu.VMEM(chunk, BF),
            pltpu.VMEM((SIDE_CHUNKS,) + chunk, BF),
            pltpu.VMEM((SIDE_CHUNKS,) + chunk, BF),
            pltpu.VMEM((SIDE_CHUNKS,) + chunk, BF),
            pltpu.VMEM((SIDE_CHUNKS * SIDE_ROWS, LANES), F32),
            dma((SIDE_CHUNKS,)),
            dma((SIDE_CHUNKS,)),
            dma((SIDE_CHUNKS,)),
            dma((SIDE_CHUNKS,)),
            dma,
            dma,
            dma,
        ],
        compiler_params=pltpu.CompilerParams(
            collective_id=2, has_side_effects=True, vmem_limit_bytes=60 << 20
        ),
    )(row)


CNN_GRADS = (CONV // LANES) * LANES + TABLE_ROWS


def cnn_sum_kernel(in_ref, out_ref, low, y_in, z_in, send, recv):
    section = lax.axis_index("section")
    b = lax.axis_index("batch")
    y, z = lax.rem(b, 2), lax.div(b, 2)
    barrier = pltpu.get_barrier_semaphore()

    def along(target, other, i):
        return pltpu.make_async_remote_copy(
            low, target, send, recv.at[i], device_id={"batch": other}, device_id_type=MESH
        )

    @pl.when(section == 0)
    def _():
        pairs = [(y == 0, b + 1), (y == 1, b - 1), ((y == 0) & (z > 0), b - 2), ((y == 0) & (z < Z - 1), b + 2)]
        for condition, other in pairs:

            @pl.when(condition)
            def _():
                pl.semaphore_signal(barrier, inc=1, device_id={"batch": other}, device_id_type=MESH)

        pl.semaphore_wait(barrier, sum(jnp.where(condition, 1, 0) for condition, _ in pairs))
        out_ref[...] = in_ref[...]

        @pl.when(y == 1)
        def _():
            low[...] = to_low(out_ref[...])
            along(y_in, b - 1, 0).start()
            along(y_in, b - 1, 0).wait_send()

        @pl.when(y == 0)
        def _():
            along(y_in, b + 1, 0).wait_recv()
            out_ref[...] += as_float(y_in[...])

            @pl.when(z < Z - 1)
            def _():
                along(z_in, b + 2, 1).wait_recv()
                out_ref[...] += as_float(z_in[...])

            @pl.when(z > 0)
            def _():
                low[...] = to_low(out_ref[...])
                along(z_in, b - 2, 1).start()
                along(z_in, b - 2, 1).wait_send()


def cnn_sum(grads):
    low = pltpu.VMEM((CNN_GRADS, LANES), BF)
    dma = pltpu.SemaphoreType.DMA
    return pl.pallas_call(
        cnn_sum_kernel,
        out_shape=jax.ShapeDtypeStruct((CNN_GRADS, LANES), F32),
        in_specs=[vmem()],
        out_specs=vmem(),
        scratch_shapes=[
            low,
            low,
            low,
            dma,
            dma((2,)),
        ],
        compiler_params=pltpu.CompilerParams(
            collective_id=3, has_side_effects=True, vmem_limit_bytes=24 << 20
        ),
    )(grads)


PIECES = 19


def assemble_kernel(cnn_ref, highways_ref, side_ref, out_ref, buffer, fetch, store):
    section = lax.axis_index("section")
    rows = out_ref.shape[0] // PIECES

    def part(i):
        return pl.ds(i * rows, rows)

    def put(source):
        for i in range(PIECES):
            pltpu.make_async_copy(source.at[part(i)], buffer.at[part(i)], fetch.at[i]).start()

    @pl.when(section == 1)
    def _():
        put(highways_ref)

    @pl.when(section != 1)
    def _():
        put(side_ref)

    for i in range(PIECES):
        pltpu.make_async_copy(side_ref.at[part(i)], buffer.at[part(i)], fetch.at[i]).wait()
        pltpu.make_async_copy(buffer.at[part(i)], out_ref.at[part(i)], store.at[i]).start()
    for i in range(PIECES):
        pltpu.make_async_copy(buffer.at[part(i)], out_ref.at[part(i)], store.at[i]).wait()

    @pl.when((section == 0) & (lax.axis_index("batch") == 0))
    def _():
        head = buffer.at[pl.ds(0, CNN_ROWS)]
        for copy in (
            pltpu.make_async_copy(cnn_ref, head, fetch.at[0]),
            pltpu.make_async_copy(head, out_ref.at[pl.ds(0, CNN_ROWS)], store.at[0]),
        ):
            copy.start()
            copy.wait()


def assemble(cnn, highways, side):
    return pl.pallas_call(
        assemble_kernel,
        out_shape=jax.ShapeDtypeStruct(side.shape, F32),
        in_specs=[hbm()] * 3,
        out_specs=hbm(),
        scratch_shapes=[
            pltpu.VMEM(side.shape, F32),
            pltpu.SemaphoreType.DMA((PIECES,)),
            pltpu.SemaphoreType.DMA((PIECES,)),
        ],
        compiler_params=pltpu.CompilerParams(vmem_limit_bytes=60 << 20),
    )(cnn, highways, side)


def on_section(numbers, function, *operands):
    shapes = jax.eval_shape(function, *operands)
    leaves, tree = jax.tree.flatten(shapes)

    def idle(*unused):
        return jax.tree.unflatten(
            tree,
            pl.pallas_call(
                lambda *refs: None,
                out_shape=[jax.ShapeDtypeStruct(s.shape, s.dtype) for s in leaves],
                out_specs=[hbm()] * len(leaves),
            )(),
        )

    section = lax.axis_index("section")
    here = sum(jnp.where(section == n, 1, 0) for n in numbers) > 0
    return lax.cond(here, function, idle, *operands)


def shards(char_ids, word_lengths, params, cotangent):
    section = lax.axis_index("section")
    n_batch = lax.axis_size("batch")
    words_all = lax.all_gather(
        jnp.concatenate([char_ids, word_lengths[:, None]], axis=1), "section", axis=0, tiled=True
    )
    params, words_all = lax.optimization_barrier((params, words_all))
    ck, tt = cnn_params(params)
    group = words_all.shape[0]
    quarter, words, half = group // 4, group // len(CNN), group // 2
    ids_all, column_all = words_all[:, :CHAR_LEN], words_all[:, CHAR_LEN:]
    row_all = column_all.T
    ends_all = stage_bounds(column_all, len(CNN))
    place = jnp.maximum(section - 1, 0)

    def mine(array, axis=0):
        return lax.dynamic_slice_in_dim(array, place * words, words, axis)

    pooled_part = on_section(
        CNN, chars_forward, ends_all[place], mine(ids_all), mine(column_all), mine(row_all, 1), ck, tt
    )
    pooled, cot, w0, w1, wp, vec = start_highways(params, pooled_part, cotangent)
    params, pooled = lax.optimization_barrier((params, pooled))
    encoder_weights = start_encoder(params)
    pooled, encoder_weights = lax.optimization_barrier((pooled, encoder_weights))
    projected, x1, x2, *kept = on_section((1,), highway_forward, w0, w1, wp, vec, pooled)
    (encoder_in,) = hand_over(
        6, [(1, 2, 0, 0, half, 0, 0), (1, 3, 0, half, half, 0, 0)], [projected], [((half, D), BF)]
    )
    x2, encoder_in = lax.optimization_barrier((x2, encoder_in))
    xt, x2t = stack_highways(pooled, x1, x2)
    encoder_in, xt = lax.optimization_barrier((encoder_in, xt))
    layer, back, joined, mixed, att, normed, activated, inner, branch, sums = on_section(
        (2, 3), encoder, encoder_in, cot, *encoder_weights
    )
    items = [(2, 1, 0, 0, half, 0, 0), (3, 1, 0, 0, half, 0, half)]
    items += [(2 + s // 2, s, 1, s % 2 * quarter, quarter, 1, 0) for s in range(4)]
    items += [(3 if k < 4 else 2, 2 if k < 4 else 3, 2 + k, 0, half, 2 + k, 0) for k in range(8)]
    items += [(2, 3, 10, 0, 8, 10, 0), (3, 2, 10, 0, 8, 10, 0)]
    own_rows = [encoder_in, mixed, joined, att, normed, activated, inner, branch, sums]
    grad_highway, layer_out, *other_rows = hand_over(
        7,
        items,
        [back, layer, *own_rows],
        [((group, D), BF), ((quarter, D), BF)] + [(value.shape, value.dtype) for value in own_rows],
    )
    grad_pooled, grad0, grad1 = on_section(
        (1,), highway_backward, w0, w1, wp, pooled, x1, *kept, grad_highway
    )
    (grad_part,) = hand_over(8, [(1, 0, 0, 0, group, 0, 0)], [grad_pooled], [((group, CONV), BF)])
    other_rows, grad_part = lax.optimization_barrier((other_rows, grad_part))
    side = side_rows(own_rows, other_rows)
    share = params.shape[1] // n_batch // LANES
    by_kernels = n_batch == 2 * Z and share == SIDE_SHARE
    if by_kernels:
        sides = reduce_sides(side, share)
        xt, sides = lax.optimization_barrier((xt, sides))
        highways, _ = reduce_highways(xt, x2t, grad0, grad1, grad_highway, share)
        grad_part, highways = lax.optimization_barrier((grad_part, highways))
    cnn_part = on_section((0,), chars_backward, ends_all, ids_all, column_all, row_all, ck, tt, grad_part)
    if not by_kernels:
        return (layer_out, summed_rows(params.shape[1], cnn_part, pooled, x1, x2, grad0, grad1, grad_highway, side))
    cnn_total = cnn_sum(cnn_part)

    def first_row(grads):
        flat = cnn_gradient(grads)
        return jnp.pad(flat, (0, CNN_ROWS * LANES - flat.shape[0])).reshape(-1, LANES)

    cnn_row = on_section((0,), first_row, cnn_total)
    total = assemble(cnn_row, highways, sides)
    return (layer_out, total.reshape(1, -1))


def summed_rows(size, cnn_part, pooled, x1, x2, grad0, grad1, grad_highway, side):
    first = lax.axis_index("batch") == 0
    cnn_flat = cnn_gradient(lax.psum(jnp.where(lax.axis_index("section") == 0, cnn_part, 0.0), ("section", "batch")))

    def wide(flat):
        return jnp.pad(as_float(flat), (0, size - flat.shape[0]))

    def highways():
        ones = jnp.ones((1, pooled.shape[0]), BF)
        pieces = []
        both = [jnp.concatenate([grad[0], grad[1]], axis=1) for grad in (grad0, grad1)]
        for x, g in ((pooled, both[0]), (x1, both[1]), (x2, grad_highway)):
            pieces += [matmul_tn(x, g).reshape(-1), matmul(ones, g).reshape(-1)]
        return wide(jnp.concatenate(pieces))

    row = lax.switch(
        lax.axis_index("section"),
        [
            lambda: wide(jnp.where(first, cnn_flat, 0.0)),
            highways,
            lambda: wide(side.reshape(-1)),
            lambda: wide(side.reshape(-1)),
        ],
    )
    return lax.psum_scatter(row, "batch", scatter_dimension=0, tiled=True).reshape(1, -1)


def solution(mesh):
    return jax.shard_map(
        shards,
        mesh=mesh,
        in_specs=(
            P(("section", "batch"), None),
            P(("section", "batch")),
            P("section", None),
            P(("section", "batch"), None),
        ),
        out_specs=(P(("section", "batch"), None), P("section", "batch")),
        check_vma=False,
    )
```

```python
import functools
import math

import jax
import jax.numpy as jnp
from jax import lax
from jax.experimental import pallas as pl
from jax.experimental.pallas import tpu as pltpu
from jax.sharding import PartitionSpec as P

D = 768
HEADS = 12
HEAD_DIM = 64
FF = 3072
CHAR_DIM = 16
CHARS = 262
CHAR_LEN = 50
CH_UNIT = 32
SEQ_LEN = 192
CONV = 64 * CH_UNIT
LANES = 128
MESH = pl.DeviceIdType.MESH
BF = jnp.bfloat16
F32 = jnp.float32
HUGE = 1e30
CNN = (0, 2, 3)

HW_CHUNK = 256
HW_SHAPE = (CONV // HW_CHUNK, CONV, 2 * HW_CHUNK)
channel_steps = (1, 1, 2, 4, 8, 16, 32)
layer_eps = 1e-12

HW_BIAS0 = CONV * 2 * CONV
HW_W1 = HW_BIAS0 + 2 * CONV
HW_BIAS1 = HW_W1 + CONV * 2 * CONV
PROJ_W = HW_BIAS1 + 2 * CONV
PROJ_B = PROJ_W + CONV * D
Q_BIAS = D * 3 * D
V_BIAS = Q_BIAS + D
OUT_W = V_BIAS + D
OUT_B = OUT_W + D * D
UP_B = D * FF
DOWN_W = UP_B + FF
DOWN_B = DOWN_W + FF * D
TABLE = CHARS * CHAR_DIM
CNN_FLAT = TABLE + sum((n + 1) * CHAR_DIM * c * CH_UNIT for n, c in enumerate(channel_steps)) + CONV


def hbm():
    return pl.BlockSpec(memory_space=pltpu.HBM)


def vmem():
    return pl.BlockSpec(memory_space=pltpu.VMEM)


def as_float(array_in):
    return array_in.astype(F32)


def to_low(array_in):
    return array_in.astype(BF)


def matmul(left_in, right_in):
    return jnp.dot(left_in, right_in, preferred_element_type=F32)


def matmul_tn(left_in, right_in):
    return lax.dot_general(left_in, right_in, (((0,), (0,)), ((), ())), preferred_element_type=F32)


def matmul_nt(left_in, right_in):
    return lax.dot_general(left_in, right_in, (((1,), (1,)), ((), ())), preferred_element_type=F32)


class Transfers:
    def __init__(self, items):
        self.items = items

    def copy(self, i, operands, outputs, send, recv):
        source, target, operand, first, rows, output, there = self.items[i]
        from_ref = operands[operand].at[pl.ds(first, rows)]
        to_ref = outputs[output].at[pl.ds(there, rows)]
        if source == target:
            return pltpu.make_async_copy(from_ref, to_ref, send.at[i])
        return pltpu.make_async_remote_copy(
            from_ref, to_ref, send.at[i], recv.at[i], device_id={"section": target}, device_id_type=MESH
        )

    def partners(self, s):
        pairs = {(item[0], item[1]) for item in self.items if item[0] != item[1]}
        return sorted({b for a, b in pairs if a == s} | {a for a, b in pairs if b == s})

    def run(self, operands, outputs, send, recv, work=None):
        section = lax.axis_index("section")
        for s in range(4):
            mine = [i for i, item in enumerate(self.items) if s in item[:2]]
            work_here = (work or {}).get(s)
            if not mine and work_here is None:
                continue

            @pl.when(section == s)
            def _(s=s, mine=mine, work_here=work_here):
                partners = self.partners(s)
                barrier = pltpu.get_barrier_semaphore()
                for other in partners:
                    pl.semaphore_signal(barrier, inc=1, device_id={"section": other}, device_id_type=MESH)
                if work_here is not None:
                    work_here()
                if partners:
                    pl.semaphore_wait(barrier, len(partners))
                outgoing = [i for i in mine if self.items[i][0] == s]
                for i in outgoing:
                    self.copy(i, operands, outputs, send, recv).start()
                for i in mine:
                    copy = self.copy(i, operands, outputs, send, recv)
                    if self.items[i][0] == self.items[i][1]:
                        copy.wait()
                    elif i in outgoing:
                        copy.wait_send()
                    else:
                        copy.wait_recv()


def hand_over(collective_id, items, operands, out_shapes):
    transfers = Transfers(items)

    def kernel(*refs):
        n, m = len(operands), len(out_shapes)
        transfers.run(refs[:n], refs[n : n + m], *refs[n + m :])

    return pl.pallas_call(
        kernel,
        out_shape=[jax.ShapeDtypeStruct(*shape) for shape in out_shapes],
        in_specs=[hbm()] * len(operands),
        out_specs=[hbm()] * len(out_shapes),
        scratch_shapes=[pltpu.SemaphoreType.DMA((len(items),))] * 2,
        compiler_params=pltpu.CompilerParams(collective_id=collective_id, has_side_effects=True),
    )(*operands)


def cut_tools(p_ref, raw, sems):
    def matrix(offset, target, rows):
        count, columns = target.shape

        def body(in_ref, out_ref):
            out_ref[...] = in_ref[...].reshape(rows, columns)

        pltpu.emit_pipeline(
            body,
            grid=(count // rows,),
            in_specs=[pl.BlockSpec((1, rows * columns), lambda i: (0, i))],
            out_specs=[pl.BlockSpec((rows, columns), lambda i: (i, 0))],
        )(p_ref.at[:, pl.ds(offset, count * columns)], target)

    def vectors(entries, vec):
        copies = []
        for row, (offset, size) in enumerate(entries):
            copy = pltpu.make_async_copy(
                p_ref.at[:, pl.ds(offset, size)], raw.at[row, :, pl.ds(0, size)], sems.at[row]
            )
            copy.start()
            copies.append(copy)
        for copy in copies:
            copy.wait()
        for row, (offset, size) in enumerate(entries):
            vec[row : row + 1, 0:size] = as_float(raw[row, :, 0:size])

    def chunks(offset, target, rows):
        def body(in_ref, out_ref):
            value = in_ref[...].reshape(rows, 2 * CONV)
            for c in range(CONV // HW_CHUNK):
                for half in range(2):
                    start = half * CONV + c * HW_CHUNK
                    out_ref[c, :, half * HW_CHUNK : (half + 1) * HW_CHUNK] = value[:, start : start + HW_CHUNK]

        pltpu.emit_pipeline(
            body,
            grid=(CONV // rows,),
            in_specs=[pl.BlockSpec((1, rows * 2 * CONV), lambda i: (0, i))],
            out_specs=[pl.BlockSpec((CONV // HW_CHUNK, rows, 2 * HW_CHUNK), lambda i: (0, i, 0))],
        )(p_ref.at[:, pl.ds(offset, CONV * 2 * CONV)], target)

    return matrix, vectors, chunks


def vector_store(vec, target, sem):
    copy = pltpu.make_async_copy(vec, target, sem)
    copy.start()
    copy.wait()


def start_highways(params, pooled_part, cotangent):
    words, quarter = pooled_part.shape[0], cotangent.shape[0]
    items = [(s, 1, 0, 0, words, 0, i * words) for i, s in enumerate(CNN)]
    items += [(s, 2 + s // 2, 1, 0, quarter, 1, s % 2 * quarter) for s in range(4)]
    transfers = Transfers(items)

    def kernel(pooled_ref, cot_ref, p_ref, pooled, cot, w0, w1, wp, vec_ref, vec, raw, sems, send, recv):
        matrix, vectors, chunks = cut_tools(p_ref, raw, sems)

        def work():
            vectors([(HW_BIAS0, 2 * CONV), (HW_BIAS1, 2 * CONV), (PROJ_B, D)], vec)
            vector_store(vec, vec_ref, sems.at[0])
            chunks(0, w0, 256)
            chunks(HW_W1, w1, 256)
            matrix(PROJ_W, wp, 512)

        transfers.run((pooled_ref, cot_ref), (pooled, cot), send, recv, {1: work})

    shapes = [(words * len(CNN), CONV), (2 * quarter, D), HW_SHAPE, HW_SHAPE, (CONV, D)]
    return pl.pallas_call(
        kernel,
        out_shape=[jax.ShapeDtypeStruct(s, BF) for s in shapes] + [jax.ShapeDtypeStruct((8, 2 * CONV), F32)],
        in_specs=[hbm()] * 3,
        out_specs=[hbm()] * 6,
        scratch_shapes=[
            pltpu.VMEM((8, 2 * CONV), F32),
            pltpu.VMEM((5, 1, 2 * CONV), BF),
            pltpu.SemaphoreType.DMA((5,)),
            pltpu.SemaphoreType.DMA((len(items),)),
            pltpu.SemaphoreType.DMA((len(items),)),
        ],
        compiler_params=pltpu.CompilerParams(
            collective_id=4, has_side_effects=True, vmem_limit_bytes=40 << 20
        ),
    )(pooled_part, cotangent, params)


def start_encoder(params):
    shapes = [(D, 3 * D), (D, D), (D, FF), (FF, D)]
    owners = (2, 2, 3, 3)
    items = [(s, 5 - s, i, 0, shape[0], i, 0) for i, (s, shape) in enumerate(zip(owners, shapes, strict=True))]
    items += [(2, 3, 4, 0, 8, 4, 0), (3, 2, 5, 0, 8, 5, 0)]
    transfers = Transfers(items)

    def kernel(p_ref, wqkv, wo, wu, wd, vec2, vec3, vec, raw, sems, send, recv):
        matrix, vectors, _ = cut_tools(p_ref, raw, sems)

        def work2():
            vectors([(Q_BIAS, D), (V_BIAS, D), (OUT_B, D), (OUT_B + D, D), (OUT_B + 2 * D, D)], vec)
            vector_store(vec, vec2, sems.at[0])
            matrix(0, wqkv, 256)
            matrix(OUT_W, wo, 384)

        def work3():
            vectors([(UP_B, FF), (DOWN_B, D), (DOWN_B + D, D), (DOWN_B + 2 * D, D)], vec)
            vector_store(vec, vec3, sems.at[0])
            matrix(0, wu, 256)
            matrix(DOWN_W, wd, 512)

        outputs = (wqkv, wo, wu, wd, vec2, vec3)
        transfers.run(outputs, outputs, send, recv, {2: work2, 3: work3})

    return pl.pallas_call(
        kernel,
        out_shape=[jax.ShapeDtypeStruct(s, BF) for s in shapes] + [jax.ShapeDtypeStruct((8, 2 * CONV), F32)] * 2,
        in_specs=[hbm()],
        out_specs=[hbm()] * 6,
        scratch_shapes=[
            pltpu.VMEM((8, 2 * CONV), F32),
            pltpu.VMEM((5, 1, 2 * CONV), BF),
            pltpu.SemaphoreType.DMA((5,)),
            pltpu.SemaphoreType.DMA((len(items),)),
            pltpu.SemaphoreType.DMA((len(items),)),
        ],
        compiler_params=pltpu.CompilerParams(
            collective_id=5, has_side_effects=True, vmem_limit_bytes=40 << 20
        ),
    )(params)


CNN_ROWS = 1600
TABLE_ROWS = 384


def cnn_params_kernel(p_ref, ck_ref, tt_ref, raw, flat, kernel, table, sem, send, recv):
    section = lax.axis_index("section")
    others = [s for s in CNN if s]
    lane = lax.broadcasted_iota(jnp.int32, (1, LANES), 1)
    barrier = pltpu.get_barrier_semaphore()

    @pl.when(section == 0)
    def _():
        copy = pltpu.make_async_copy(p_ref.at[:, pl.ds(0, CNN_ROWS * LANES)], raw, sem)
        copy.start()
        for s in others:
            pl.semaphore_signal(barrier, inc=1, device_id={"section": s}, device_id_type=MESH)
        copy.wait()
        flat[...] = as_float(raw[...]).reshape(CNN_ROWS, LANES)
        table[...] = jnp.zeros_like(table)
        head = flat[0:40, :]
        for b in range(8):
            mixed = jnp.zeros_like(head)
            for g in range(7):
                rolled = head if g == b else pltpu.roll(head, (g - b) * CHAR_DIM % LANES, 1)
                mixed = jnp.where((lane >= g * CHAR_DIM) & (lane < (g + 1) * CHAR_DIM), rolled, mixed)
            table[pl.ds(b, 33, stride=8), :] = mixed[0:33]
        tt_ref[...] = to_low(table[...])
        rolled = pltpu.roll(flat[...], 32, 1)
        flat[...] = rolled
        count = CNN_ROWS - 40
        flat[0:count, :] = jnp.where(
            lane < 32, flat[32 : 32 + count, :], flat[33 : 33 + count, :]
        )
        kernel[...] = jnp.zeros_like(kernel)
        first, second, third = flat[0:8, :], flat[4:12, :], flat[12:36, :]
        narrow = lax.broadcasted_iota(jnp.int32, (8, LANES), 0) < 4
        for b in range(4):
            one = first if b == 0 else pltpu.roll(first, -b * 32 % LANES, 1)
            two = second if b == 1 else pltpu.roll(second, (32 - b * 32) % LANES, 1)
            kernel[0, pl.ds(b, 8, stride=4), :] = jnp.where(
                lane < 32, jnp.where(narrow, one, 0.0), jnp.where(lane < 64, two, 0.0)
            )
        for b in range(2):
            three = third if b == 1 else pltpu.roll(third, 64, 1)
            kernel[0, pl.ds(b, 24, stride=2), :] = jnp.where(
                lane >= 64, three, kernel[0, pl.ds(b, 24, stride=2), :]
            )
        row, tile = 36, 1
        for number in range(3, 7):
            parts = channel_steps[number] * CH_UNIT // LANES
            depth = (number + 1) * CHAR_DIM
            for c in range(parts):
                kernel[tile, 0:depth, :] = flat[pl.ds(row + c, depth, stride=parts), :]
                tile += 1
            row += depth * parts
        bound = 0
        for number in range(7):
            upper = bound + channel_steps[number] * CH_UNIT
            for c in range(bound // LANES, -(-upper // LANES)):
                kernel[c, 112 + number : 113 + number, :] = jnp.where(
                    (lane + c * LANES >= bound) & (lane + c * LANES < upper), -HUGE, 0.0
                )
            bound = upper
        for c in range(CONV // LANES):
            kernel[c, 119:120, :] = flat[row + c : row + c + 1, :]
            ck_ref[:, c * LANES : (c + 1) * LANES] = to_low(kernel[c])
        pl.semaphore_wait(barrier, len(others))
        copies = []
        for i, s in enumerate(others):
            for j, ref in enumerate((ck_ref, tt_ref)):
                copies.append(
                    pltpu.make_async_remote_copy(
                        ref, ref, send.at[i, j], recv.at[j], device_id={"section": s}, device_id_type=MESH
                    )
                )
        for copy in copies:
            copy.start()
        for copy in copies:
            copy.wait_send()

    for s in others:

        @pl.when(section == s)
        def _():
            pl.semaphore_signal(barrier, inc=1, device_id={"section": 0}, device_id_type=MESH)
            pl.semaphore_wait(barrier, 1)
            for j, ref in enumerate((ck_ref, tt_ref)):
                pltpu.make_async_remote_copy(
                    ref, ref, send.at[0, j], recv.at[j], device_id={"section": 0}, device_id_type=MESH
                ).wait_recv()


def cnn_params(params):
    return pl.pallas_call(
        cnn_params_kernel,
        out_shape=[
            jax.ShapeDtypeStruct((LANES, CONV), BF),
            jax.ShapeDtypeStruct((TABLE_ROWS, LANES), BF),
        ],
        in_specs=[hbm()],
        out_specs=[vmem(), vmem()],
        scratch_shapes=[
            pltpu.VMEM((1, CNN_ROWS * LANES), BF),
            pltpu.VMEM((CNN_ROWS, LANES), F32),
            pltpu.VMEM((CONV // LANES, LANES, LANES), F32),
            pltpu.VMEM((TABLE_ROWS, LANES), F32),
            pltpu.SemaphoreType.DMA,
            pltpu.SemaphoreType.DMA((len(CNN) - 1, 2)),
            pltpu.SemaphoreType.DMA((2,)),
        ],
        compiler_params=pltpu.CompilerParams(
            collective_id=0, has_side_effects=True, vmem_limit_bytes=24 << 20
        ),
    )(params)


STAGES = ((128, 1), (64, 2), (16, 8))
SPOTS = CHAR_LEN + 14


def stage_bounds(lengths, blocks):
    words = lengths.shape[0] // blocks
    counts = jnp.sum(lengths.reshape(blocks, words, 1) > jnp.arange(CHAR_LEN, dtype=jnp.int32), axis=1)
    limits = jnp.array([[words // 2], [words // 8], [0]], jnp.int32)
    return jnp.sum(counts[:, None, :] > limits, axis=2).astype(jnp.int32)


def sorting(column_ref, row_ref):
    count = row_ref.shape[1]
    down = lax.broadcasted_iota(jnp.int32, (count, count), 0)
    across = lax.broadcasted_iota(jnp.int32, (count, count), 1)
    column, row = column_ref[...], row_ref[...]
    before = (column > row) | ((column == row) & (down < across))
    rank = jnp.sum(jnp.where(before, 1, 0), axis=0, keepdims=True)
    return jnp.where(down == rank, 1.0, 0.0).astype(BF)


def sorted_words(order, ids_ref, column_ref):
    ids = ids_ref[...]
    high = lax.div(ids, 16)
    low = ids - 16 * high
    ids = matmul(order, to_low(as_float(high))) * 16.0 + matmul(order, to_low(as_float(low)))
    length = matmul(order, to_low(as_float(jnp.broadcast_to(column_ref[...], (ids.shape[0], LANES)))))
    return ids, length


def stages(ends_ref, body):
    start = 0
    for k, (words, positions) in enumerate(STAGES):
        end = ends_ref[k]

        def one(i, unused, words=words, positions=positions, start=start, end=end):
            body(start + i * positions, words, positions, end)
            return unused

        lax.fori_loop(0, lax.div(jnp.maximum(end - start, 0) + positions - 1, positions), one, 0)
        start = end


def one_hot(first, words, positions, ids):
    lane = lax.broadcasted_iota(jnp.int32, (words, CHAR_LEN), 1)
    columns = [
        jnp.sum(jnp.where(lane == first + q, ids[0:words, :], 0.0), axis=1, keepdims=True) for q in range(positions)
    ]
    column = columns[0] if positions == 1 else jnp.concatenate(columns, axis=0)
    symbol = lax.broadcasted_iota(jnp.int32, (words * positions, TABLE_ROWS), 1)
    return jnp.where(column.astype(jnp.int32) == symbol, 1.0, 0.0).astype(BF)


def windows(first, words, positions, end, length, embedded, masks):
    total = None
    for j in range(7):
        term = embedded[pl.ds(first + j, positions), 0:words, :] * masks[j]
        total = term if total is None else total + term
    shape = (positions, words, LANES)
    lane = lax.broadcasted_iota(jnp.int32, shape, 2)
    position = first + lax.broadcasted_iota(jnp.int32, shape, 0)
    room = jnp.broadcast_to(length[0:words, :][None], shape)
    out = (lane >= 112) & (lane < 119) & ((as_float(position + lane - 111) > room) | (position >= end))
    return (total + jnp.where(out | (lane == 119), 1.0, 0.0).astype(BF)).reshape(positions * words, LANES)


def lane_masks():
    lane = lax.broadcasted_iota(jnp.int32, (1, 1, LANES), 2)
    return [
        jnp.where((lane >= j * CHAR_DIM) & (lane < (j + 1) * CHAR_DIM), 1.0, 0.0).astype(BF)
        for j in range(7)
    ]


def embedder(ids, tt_ref, embedded):
    def embed(first, words, positions, end):
        value = to_low(matmul(one_hot(first, words, positions, ids), tt_ref[...]))
        embedded[pl.ds(first, positions), 0:words, :] = value.reshape(positions, words, LANES)

    return embed


def chars_forward_kernel(ends_ref, ids_ref, column_ref, row_ref, ck_ref, tt_ref, out_ref, embedded, best):
    embedded[...] = jnp.zeros_like(embedded)
    best[...] = jnp.full_like(best, -HUGE)
    masks = lane_masks()
    order = sorting(column_ref, row_ref)
    ids, length = sorted_words(order, ids_ref, column_ref)
    stages(ends_ref, embedder(ids, tt_ref, embedded))

    def pool(first, words, positions, end):
        rows = windows(first, words, positions, end, length, embedded, masks)
        for c in range(0, CONV, 512):
            pre = jnp.max(matmul(rows, ck_ref[:, c : c + 512]).reshape(positions, words, 512), axis=0)
            best[0:words, c : c + 512] = jnp.maximum(best[0:words, c : c + 512], pre)

    stages(ends_ref, pool)
    out_ref[...] = to_low(matmul_tn(order, to_low(jnp.maximum(best[...], 0.0))))


def chars_backward_kernel(
    all_ends_ref, ids_ref, column_ref, row_ref, ck_ref, tt_ref, grad_ref,
    out_ref, embedded, best, share, backs, sums,
):
    block = pl.program_id(0)
    ends_ref = [all_ends_ref[block, k] for k in range(len(STAGES))]
    embedded[...] = jnp.zeros_like(embedded)
    backs[...] = jnp.zeros_like(backs)
    best[...] = jnp.full_like(best, -HUGE)
    share[...] = jnp.zeros_like(share)
    table_rows = pl.ds(CONV, TABLE_ROWS)

    @pl.when(block == 0)
    def _():
        sums[...] = jnp.zeros_like(sums)
        out_ref[table_rows, :] = jnp.zeros((TABLE_ROWS, LANES), F32)

    masks = lane_masks()
    order = sorting(column_ref, row_ref)
    ids, length = sorted_words(order, ids_ref, column_ref)
    stages(ends_ref, embedder(ids, tt_ref, embedded))

    def count(first, words, positions, end):
        rows = windows(first, words, positions, end, length, embedded, masks)
        for c in range(0, CONV, 512):
            part = slice(c, c + 512)
            pre = matmul(rows, ck_ref[:, part])
            top, hits = best[0:words, part], share[0:words, part]
            for q in range(positions):
                here = pre[q * words : (q + 1) * words]
                hits = jnp.where(here > top, 1.0, hits + jnp.where(here == top, 1.0, 0.0))
                top = jnp.maximum(top, here)
            best[0:words, part], share[0:words, part] = top, hits

    stages(ends_ref, count)
    share[...] = matmul(order, grad_ref[...]) / share[...]
    best[...] = jnp.where(best[...] > 0.0, best[...], 3e38)

    def spread(first, words, positions, end):
        rows = windows(first, words, positions, end, length, embedded, masks)
        back = jnp.zeros((words * positions, LANES), F32)
        for c in range(0, CONV, 512):
            part = slice(c, c + 512)
            pre = matmul(rows, ck_ref[:, part]).reshape(positions, words, 512)
            hit = pre == best[0:words, part][None]
            grad = to_low(jnp.where(hit, jnp.broadcast_to(share[0:words, part][None], pre.shape), 0.0))
            grad = grad.reshape(positions * words, 512)
            sums[:, part] += matmul_tn(rows, grad)
            back = back + matmul_nt(grad, ck_ref[:, part])
        backs[pl.ds(first + 6, positions), 0:words, :] = to_low(back).reshape(positions, words, LANES)

    stages(ends_ref, spread)

    def gather(first, words, positions, end):
        shape = (positions, words, LANES)
        lane = lax.broadcasted_iota(jnp.int32, shape, 2)
        position = first + lax.broadcasted_iota(jnp.int32, shape, 0)
        total = jnp.zeros(shape, F32)
        for j in range(7):
            here = (lane >= j * CHAR_DIM) & (lane < (j + 1) * CHAR_DIM) & (position < end)
            total = jnp.where(here, as_float(backs[pl.ds(first + 6 - j, positions), 0:words, :]), total)
        hot = one_hot(first, words, positions, ids)
        out_ref[table_rows, :] += matmul_tn(hot, to_low(total).reshape(positions * words, LANES))

    stages(ends_ref, gather)

    @pl.when(block == pl.num_programs(0) - 1)
    def _():
        for c in range(CONV // LANES):
            out_ref[c * LANES : (c + 1) * LANES, :] = sums[:, c * LANES : (c + 1) * LANES]


def chars_forward(ends, ids, column, row, ck, tt):
    words = ids.shape[0]
    return pl.pallas_call(
        chars_forward_kernel,
        out_shape=jax.ShapeDtypeStruct((words, CONV), BF),
        in_specs=[pl.BlockSpec(memory_space=pltpu.SMEM)] + [vmem()] * 5,
        out_specs=vmem(),
        scratch_shapes=[
            pltpu.VMEM((SPOTS, words, LANES), BF),
            pltpu.VMEM((words, CONV), F32),
        ],
        compiler_params=pltpu.CompilerParams(vmem_limit_bytes=32 << 20),
    )(ends, ids, column, row, ck, tt)


def chars_backward(ends, ids, column, row, ck, tt, grad):
    words = ids.shape[0] // len(CNN)
    return pl.pallas_call(
        chars_backward_kernel,
        grid=(len(CNN),),
        out_shape=jax.ShapeDtypeStruct((CNN_GRADS, LANES), F32),
        in_specs=[
            pl.BlockSpec(memory_space=pltpu.SMEM),
            pl.BlockSpec((words, CHAR_LEN), lambda i: (i, 0)),
            pl.BlockSpec((words, 1), lambda i: (i, 0)),
            pl.BlockSpec((1, words), lambda i: (0, i)),
            pl.BlockSpec((LANES, CONV), lambda i: (0, 0)),
            pl.BlockSpec((TABLE_ROWS, LANES), lambda i: (0, 0)),
            pl.BlockSpec((words, CONV), lambda i: (i, 0)),
        ],
        out_specs=pl.BlockSpec((CNN_GRADS, LANES), lambda i: (0, 0)),
        scratch_shapes=[
            pltpu.VMEM((SPOTS, words, LANES), BF),
            pltpu.VMEM((words, CONV), F32),
            pltpu.VMEM((words, CONV), F32),
            pltpu.VMEM((SPOTS, words, LANES), BF),
            pltpu.VMEM((LANES, CONV), F32),
        ],
        compiler_params=pltpu.CompilerParams(vmem_limit_bytes=40 << 20),
    )(ends, ids, column, row, ck, tt, grad)


def cnn_gradient(grads):
    table_grad = grads[CONV:]
    kernel_grad = jnp.swapaxes(grads[:CONV].reshape(-1, LANES, LANES), 0, 1).reshape(LANES, CONV)
    pieces = [
        sum(table_grad[:CHARS, g * CHAR_DIM : (g + 1) * CHAR_DIM] for g in range(7)).reshape(-1)
    ]
    offset = 0
    for number in range(7):
        channels = channel_steps[number] * CH_UNIT
        pieces.append(
            kernel_grad[: (number + 1) * CHAR_DIM, offset : offset + channels].reshape(-1)
        )
        offset += channels
    pieces.append(kernel_grad[119])
    return jnp.concatenate(pieces)


def sigmoid(value):
    return 1.0 / (1.0 + jnp.exp(-value))


def highway_layer_kernel(row, x_ref, part_ref, w_ref, bl_ref, br_ref, next_ref, left_ref, right_ref):
    both = matmul(x_ref[...], w_ref[0])
    left = both[:, :HW_CHUNK] + bl_ref[row : row + 1, :]
    right = both[:, HW_CHUNK:] + br_ref[row : row + 1, :]
    left_ref[...] = left
    right_ref[...] = right
    gate = sigmoid(right)
    next_ref[...] = to_low(gate * as_float(part_ref[...]) + (1.0 - gate) * jnp.maximum(left, 0.0))


def highway_layer(row, x, w, vec):
    group = x.shape[0]
    steps = CONV // HW_CHUNK
    part = pl.BlockSpec((group, HW_CHUNK), lambda i: (0, i))
    return pl.pallas_call(
        functools.partial(highway_layer_kernel, row),
        grid=(steps,),
        out_shape=[
            jax.ShapeDtypeStruct((group, CONV), BF),
            jax.ShapeDtypeStruct((group, CONV), F32),
            jax.ShapeDtypeStruct((group, CONV), F32),
        ],
        in_specs=[
            pl.BlockSpec((group, CONV), lambda i: (0, 0)),
            part,
            pl.BlockSpec((1,) + HW_SHAPE[1:], lambda i: (i, 0, 0)),
            pl.BlockSpec((8, HW_CHUNK), lambda i: (0, i)),
            pl.BlockSpec((8, HW_CHUNK), lambda i: (0, i + steps)),
        ],
        out_specs=[part, part, part],
        compiler_params=pltpu.CompilerParams(vmem_limit_bytes=40 << 20),
    )(x, x, w, vec, vec)


def highway_forward(w0, w1, wp, vec, wide_in):
    x1, left0, right0 = highway_layer(0, wide_in, w0, vec)
    x2, left1, right1 = highway_layer(1, x1, w1, vec)
    projected = to_low(matmul(x2, wp) + vec[2, :D])
    return (projected, x1, x2, left0, right0, left1, right1)


def highway_back_kernel(last, up_ref, wp_ref, x_ref, left_ref, right_ref, w_ref, grad_ref, out_ref, total):
    i = pl.program_id(0)
    flowing = matmul_nt(up_ref[...], wp_ref[...]) if wp_ref is not None else up_ref[...]
    gate = sigmoid(right_ref[...])
    left = left_ref[...]
    nonlinear = jnp.maximum(left, 0.0)
    closed = flowing * (1.0 - gate)
    grad_left = to_low(jnp.where(left > 0.0, closed, 0.0))
    grad_right = to_low(closed * (as_float(x_ref[...]) - nonlinear) * gate)
    grad_ref[0] = grad_left
    grad_ref[1] = grad_right
    back = matmul_nt(jnp.concatenate([grad_left, grad_right], axis=1), w_ref[0])

    @pl.when(i == 0)
    def _():
        total[...] = back

    @pl.when(i > 0)
    def _():
        total[...] += back

    here = pl.ds(pl.multiple_of(i * HW_CHUNK, HW_CHUNK), HW_CHUNK)
    total[:, here] += flowing * gate

    @pl.when(i == pl.num_programs(0) - 1)
    def _():
        out_ref[...] = to_low(total[...]) if last else total[...]


def highway_back(last, up, wp, x, left, right, w):
    group = x.shape[0]
    steps = CONV // HW_CHUNK
    part = pl.BlockSpec((group, HW_CHUNK), lambda i: (0, i))
    if wp is None:
        kernel = lambda up_ref, *refs: highway_back_kernel(last, up_ref, None, *refs)
        sources, specs = [up], [part]
    else:
        kernel = functools.partial(highway_back_kernel, last)
        sources = [up, wp]
        specs = [pl.BlockSpec((group, D), lambda i: (0, 0)), pl.BlockSpec((HW_CHUNK, D), lambda i: (i, 0))]
    return pl.pallas_call(
        kernel,
        grid=(steps,),
        out_shape=[
            jax.ShapeDtypeStruct((2, group, CONV), BF),
            jax.ShapeDtypeStruct((group, CONV), BF if last else F32),
        ],
        in_specs=specs
        + [
            part,
            part,
            part,
            pl.BlockSpec((1,) + HW_SHAPE[1:], lambda i: (i, 0, 0)),
        ],
        out_specs=[
            pl.BlockSpec((2, group, HW_CHUNK), lambda i: (0, 0, i)),
            pl.BlockSpec((group, CONV), lambda i: (0, 0)),
        ],
        scratch_shapes=[pltpu.VMEM((group, CONV), F32)],
        compiler_params=pltpu.CompilerParams(vmem_limit_bytes=40 << 20),
    )(*sources, x, left, right, w)


def highway_backward(w0, w1, wp, wide_in, x1, left0, right0, left1, right1, upstream):
    grad1, flowing = highway_back(False, upstream, wp, x1, left1, right1, w1)
    grad0, grad_pooled = highway_back(True, flowing, None, wide_in, left0, right0, w0)
    return (grad_pooled, grad0, grad1)


def layer_norm(residual):
    centered = residual - jnp.mean(residual, axis=-1, keepdims=True)
    inverse = lax.rsqrt(jnp.mean(centered * centered, axis=-1, keepdims=True) + layer_eps)
    return centered * inverse, inverse


def norm_backward(upstream, scaled, inverse, gain):
    weighted = upstream * gain
    first_mean = jnp.mean(weighted, axis=-1, keepdims=True)
    cross_mean = jnp.mean(weighted * scaled, axis=-1, keepdims=True)
    return inverse * (weighted - first_mean - scaled * cross_mean)


def encoder_kernel(
    x_ref, cot_ref, wqkv_ref, wo_ref, wu_ref, wd_ref, vec_ref, vec3_ref,
    layer_ref, back_ref, joined_ref, mixed_ref, att_ref, normed_ref, act_ref, inner_ref, branch_ref, sums_ref,
    qkv, probs, slope, scaled, carry,
):
    rows = x_ref.shape[0]
    pairs = HEADS // 2
    scale = HEAD_DIM ** (-0.5)
    lane = lax.broadcasted_iota(jnp.int32, (1, LANES), 1)
    halves = [jnp.where(lane < HEAD_DIM, 1.0, 0.0).astype(BF), jnp.where(lane < HEAD_DIM, 0.0, 1.0).astype(BF)]

    def heads(body):
        def one(i, unused):
            sequence, pair = lax.div(i, pairs), lax.rem(i, pairs)
            body(
                pl.ds(pl.multiple_of(sequence * SEQ_LEN, SEQ_LEN), SEQ_LEN),
                [pl.ds(pl.multiple_of(pair * LANES + k * D, LANES), LANES) for k in range(3)],
                i,
            )
            return unused

        lax.fori_loop(0, rows // SEQ_LEN * pairs, one, 0)

    def pieces(width, body):
        def one(i, unused):
            body(pl.ds(pl.multiple_of(i * width, width), width))
            return unused

        return lambda count: lax.fori_loop(0, count, one, 0)

    @pl.when(lax.axis_index("section") >= 2)
    def _():
        for k, bias in enumerate((vec_ref[0:1, 0:D], None, vec_ref[1:2, 0:D])):
            part = matmul(x_ref[...], wqkv_ref[:, k * D : (k + 1) * D])
            qkv[:, k * D : (k + 1) * D] = to_low(part if bias is None else part + bias)

        def attend(here, columns, i):
            query, key, value = (qkv[here, columns[k]] for k in range(3))
            out = []
            for half in range(2):
                scores = matmul_nt(query * halves[half], key) * scale
                exponent = jnp.exp(scores - jnp.max(scores, axis=-1, keepdims=True))
                soft = exponent / jnp.sum(exponent, axis=-1, keepdims=True)
                probs[2 * i + half] = soft
                out.append(matmul(to_low(soft), value))
            mixed_ref[here, columns[0]] = to_low(jnp.where(lane < HEAD_DIM, out[0], out[1]))

        heads(attend)
        residual = as_float(x_ref[...]) + matmul(mixed_ref[...], wo_ref[...]) + vec_ref[2:3, 0:D]
        scaled1, inverse1 = layer_norm(residual)
        scaled[...] = scaled1
        normed_ref[...] = to_low(scaled1 * vec_ref[3:4, 0:D] + vec_ref[4:5, 0:D])

        def up(part):
            inner = matmul(normed_ref[...], wu_ref[:, part]) + vec3_ref[0:1, part]
            phi = 0.5 * (1.0 + lax.erf(inner * 0.7071067811865476))
            act_ref[:, part] = to_low(inner * phi)
            slope[:, part] = phi + inner * jnp.exp(-0.5 * inner * inner) * 0.3989422804014327

        pieces(512, up)(FF // 512)
        residual = as_float(normed_ref[...]) + matmul(act_ref[...], wd_ref[...]) + vec3_ref[1:2, 0:D]
        scaled2, inverse2 = layer_norm(residual)
        gain2 = vec3_ref[2:3, 0:D]
        layer_ref[...] = to_low(scaled2 * gain2 + vec3_ref[3:4, 0:D])
        upstream = as_float(cot_ref[...])
        sums_ref[2:3, :] = jnp.sum(upstream * scaled2, axis=0, keepdims=True)
        sums_ref[3:4, :] = jnp.sum(upstream, axis=0, keepdims=True)
        carry[...] = norm_backward(upstream, scaled2, inverse2, gain2)
        branch_ref[...] = to_low(carry[...])

        def down(part):
            inner_ref[:, part] = to_low(matmul_nt(branch_ref[...], wd_ref[part, :]) * slope[:, part])

        pieces(512, down)(FF // 512)
        upstream = as_float(to_low(carry[...] + matmul_nt(inner_ref[...], wu_ref[...])))
        sums_ref[0:1, :] = jnp.sum(upstream * scaled[...], axis=0, keepdims=True)
        sums_ref[1:2, :] = jnp.sum(upstream, axis=0, keepdims=True)
        carry[...] = norm_backward(upstream, scaled[...], inverse1, vec_ref[3:4, 0:D])
        att_ref[...] = to_low(carry[...])
        back_ref[...] = to_low(matmul_nt(att_ref[...], wo_ref[...]))

        def attend_back(here, columns, i):
            query, key, value = (qkv[here, columns[k]] for k in range(3))
            grad = back_ref[here, columns[0]]
            totals = [0.0, 0.0, 0.0]
            for half in range(2):
                grad_half = grad * halves[half]
                soft = probs[2 * i + half]
                grad_soft = matmul_nt(grad_half, value)
                flow = to_low(soft * (grad_soft - jnp.sum(grad_soft * soft, axis=-1, keepdims=True)))
                totals[0] += matmul(flow, key * halves[half])
                totals[1] += matmul_tn(flow, query * halves[half])
                totals[2] += matmul_tn(to_low(soft), grad_half)
            joined_ref[here, columns[0]] = to_low(totals[0] * scale)
            joined_ref[here, columns[1]] = to_low(totals[1] * scale)
            joined_ref[here, columns[2]] = to_low(totals[2])

        heads(attend_back)
        back_ref[...] = to_low(carry[...] + matmul_nt(joined_ref[...], wqkv_ref[...]))


def encoder(x, cot, wqkv, wo, wu, wd, vec, vec3):
    rows = x.shape[0]
    widths = [D, D, 3 * D, D, D, D, FF, FF, D]
    return pl.pallas_call(
        encoder_kernel,
        out_shape=[jax.ShapeDtypeStruct((rows, w), BF) for w in widths] + [jax.ShapeDtypeStruct((8, D), F32)],
        in_specs=[vmem()] * 8,
        out_specs=[vmem()] * 10,
        scratch_shapes=[
            pltpu.VMEM((rows, 3 * D), BF),
            pltpu.VMEM((rows // SEQ_LEN * HEADS, SEQ_LEN, SEQ_LEN), F32),
            pltpu.VMEM((rows, FF), F32),
            pltpu.VMEM((rows, D), F32),
            pltpu.VMEM((rows, D), F32),
        ],
        compiler_params=pltpu.CompilerParams(vmem_limit_bytes=56 << 20),
    )(x, cot, wqkv, wo, wu, wd, vec, vec3)


def side_rows_kernel(*refs):
    section = lax.axis_index("section")
    own, other, (out_hbm, flat, out_ref, *targets, sem) = refs[:9], refs[9:18], refs[18:]
    x_ref, mixed_ref, joined_ref, att_ref, normed_ref, act_ref, inner_ref, branch_ref, sums_ref = targets

    def fetch(*places):
        copies = []
        for i in places:
            rows = own[i].shape[0]
            for k, source in enumerate((own[i], other[i])):
                copies.append(pltpu.make_async_copy(source, targets[i].at[pl.ds(k * rows, rows)], sem.at[k, i]))
        for copy in copies:
            copy.start()
        for copy in copies:
            copy.wait()

    def product(left_ref, right_ref, row):
        count, width = left_ref.shape[1], right_ref.shape[1]
        parts = width // LANES
        for k in range(count // D):
            for c in range(0, width, 256):
                block = matmul_tn(left_ref[:, k * D : (k + 1) * D], right_ref[:, c : c + 256])
                for t in range(2):
                    flat[pl.ds(row + k * D * parts + c // LANES + t, D, stride=parts), :] = block[:, t * LANES : (t + 1) * LANES]
        return row + count * parts

    def line(row, values):
        for c in range(values.shape[1] // LANES):
            flat[row + c : row + c + 1, :] = values[:, c * LANES : (c + 1) * LANES]
        return row + values.shape[1] // LANES

    def summed(ref, first, last):
        return jnp.sum(as_float(ref[:, first:last]), axis=0, keepdims=True)

    def write(row):
        full = out_ref.shape[0]
        flat[row:full, :] = jnp.zeros((full - row, LANES), F32)
        out_ref[...] = to_low(flat[...])
        copy = pltpu.make_async_copy(out_ref, out_hbm, sem.at[0, 0])
        copy.start()
        copy.wait()

    @pl.when(section == 2)
    def _():
        fetch(0, 1, 2, 3, 8)
        row = product(x_ref, joined_ref, 0)
        row = line(row, summed(joined_ref, 0, D))
        row = line(row, summed(joined_ref, 2 * D, 3 * D))
        row = product(mixed_ref, att_ref, row)
        row = line(row, summed(att_ref, 0, D))
        row = line(row, sums_ref[0:1, :] + sums_ref[8:9, :])
        write(line(row, sums_ref[1:2, :] + sums_ref[9:10, :]))

    @pl.when(section == 3)
    def _():
        fetch(4, 5, 6, 7, 8)
        row = product(normed_ref, inner_ref, 0)
        row = line(row, summed(inner_ref, 0, FF))
        row = product(act_ref, branch_ref, row)
        row = line(row, summed(branch_ref, 0, D))
        row = line(row, sums_ref[2:3, :] + sums_ref[10:11, :])
        write(line(row, sums_ref[3:4, :] + sums_ref[11:12, :]))


def side_rows(own, other):
    size = (SIDE_SHARE + SIDE_ROWS * SIDE_CHUNKS, LANES)
    return pl.pallas_call(
        side_rows_kernel,
        out_shape=jax.ShapeDtypeStruct(size, BF),
        in_specs=[hbm()] * (2 * len(own)),
        out_specs=hbm(),
        scratch_shapes=[pltpu.VMEM(size, F32), pltpu.VMEM(size, BF)]
        + [pltpu.VMEM((2 * value.shape[0], value.shape[1]), value.dtype) for value in own]
        + [pltpu.SemaphoreType.DMA((2, len(own)))],
        compiler_params=pltpu.CompilerParams(vmem_limit_bytes=50 << 20),
    )(*own, *other)


def stack_kernel(x0_ref, x1_ref, x2_ref, xt_hbm, x2t_hbm, low, turned, sem):
    group = x0_ref.shape[0]

    @pl.when(lax.axis_index("section") == 1)
    def _():
        turned[CONV:STACK, :] = jnp.where(
            lax.broadcasted_iota(jnp.int32, (STACK - CONV, group), 0) == 0, 1.0, 0.0
        ).astype(BF)
        targets = (xt_hbm.at[pl.ds(0, STACK)], xt_hbm.at[pl.ds(STACK, STACK)], x2t_hbm)
        for source, target in zip((x0_ref, x1_ref, x2_ref), targets, strict=True):
            copy = pltpu.make_async_copy(source, low, sem)
            copy.start()
            copy.wait()
            for c in range(0, CONV, 512):
                turned[c : c + 512, :] = low[:, c : c + 512].T
            copy = pltpu.make_async_copy(turned, target, sem)
            copy.start()
            copy.wait()


def stack_highways(x0, x1, x2):
    group = x0.shape[0]
    return pl.pallas_call(
        stack_kernel,
        out_shape=[jax.ShapeDtypeStruct((2 * STACK, group), BF), jax.ShapeDtypeStruct((STACK, group), BF)],
        in_specs=[hbm()] * 3,
        out_specs=[hbm()] * 2,
        scratch_shapes=[
            pltpu.VMEM((group, CONV), BF),
            pltpu.VMEM((STACK, group), BF),
            pltpu.SemaphoreType.DMA,
        ],
        compiler_params=pltpu.CompilerParams(vmem_limit_bytes=24 << 20),
    )(x0, x1, x2)


SIDE_ROWS = 1200
SIDE_CHUNKS = 16
SIDE_REST = 1040
SIDE_SHARE = 17936


def side_part(
    share, row_ref, out_ref, own, y_in, z_in, z_out, total,
    y_send, y_recv, z_send, z_recv, l_send, l_recv, sem,
):
    section = lax.axis_index("section")
    b = lax.axis_index("batch")
    y, z = lax.rem(b, 2), lax.div(b, 2)

    def count(half):
        return jnp.where((section == 2) & (half == 1), 1, SIDE_CHUNKS)

    def rows(half, i):
        return pl.ds(pl.multiple_of(half * share + i * SIDE_ROWS, 16), SIDE_ROWS)

    def y_copy(i):
        return pltpu.make_async_remote_copy(
            row_ref.at[rows(1 - y, i)], y_in.at[i], y_send.at[i], y_recv.at[i],
            device_id={"batch": b + 1 - 2 * y}, device_id_type=MESH,
        )

    def z_copy(i):
        return pltpu.make_async_remote_copy(
            z_out.at[i], z_in.at[i], z_send.at[i], z_recv.at[i],
            device_id={"batch": b - 2}, device_id_type=MESH,
        )

    def rest_copy():
        return pltpu.make_async_remote_copy(
            total.at[pl.ds(share, SIDE_REST)], total.at[pl.ds(0, SIDE_REST)], l_send, l_recv,
            device_id={"batch": 2}, device_id_type=MESH,
        )

    def write():
        copy = pltpu.make_async_copy(total.at[pl.ds(0, share)], out_ref, sem)
        copy.start()
        copy.wait()

    @pl.when(section != 1)
    def _():
        total[...] = jnp.zeros_like(total)

    @pl.when(section == 0)
    def _():
        write()

    @pl.when(section >= 2)
    def _():
        barrier = pltpu.get_barrier_semaphore()

        @pl.when(section == 3)
        def _():
            pl.semaphore_signal(barrier, inc=1, device_id={"section": 1}, device_id_type=MESH)

        pl.semaphore_signal(barrier, inc=1, device_id={"batch": b + 1 - 2 * y}, device_id_type=MESH)
        pairs = [(z > 0, b - 2), (z < Z - 1, b + 2), (b == 1, 2), (b == 2, 1)]
        for condition, other in pairs:

            @pl.when(condition)
            def _():
                pl.semaphore_signal(barrier, inc=1, device_id={"batch": other}, device_id_type=MESH)

        pl.semaphore_wait(barrier, 1 + sum(jnp.where(condition, 1, 0) for condition, _ in pairs))

        def send(i, carry):
            y_copy(i).start()
            return carry

        def combine(i, carry):
            copy = pltpu.make_async_copy(row_ref.at[rows(y, i)], own, sem)
            copy.start()
            copy.wait()
            y_copy(i).wait_recv()
            here = pl.ds(pl.multiple_of(i * SIDE_ROWS, 16), SIDE_ROWS)

            @pl.when(z == Z - 1)
            def _():
                z_out[i] = to_low(as_float(own[...]) + as_float(y_in[i]))

            @pl.when(z < Z - 1)
            def _():
                z_copy(i).wait_recv()

                @pl.when(z > 0)
                def _():
                    z_out[i] = to_low(as_float(own[...]) + as_float(y_in[i]) + as_float(z_in[i]))

                @pl.when(z == 0)
                def _():
                    total[here] = as_float(own[...]) + as_float(y_in[i]) + as_float(z_in[i])

            @pl.when(z > 0)
            def _():
                z_copy(i).start()

            return carry

        def drain(i, carry):
            y_copy(i).wait_send()
            return carry

        def drain_z(i, carry):
            z_copy(i).wait_send()
            return carry

        lax.fori_loop(0, count(1 - y), send, 0)
        lax.fori_loop(0, count(y), combine, 0)

        @pl.when((section == 3) & (b == 1))
        def _():
            rest_copy().start()
            rest_copy().wait_send()

        @pl.when((section == 3) & (b == 2))
        def _():
            rest_copy().wait_recv()

        write()
        lax.fori_loop(0, count(1 - y), drain, 0)

        @pl.when(z > 0)
        def _():
            lax.fori_loop(0, count(y), drain_z, 0)


SLICE = 592
CHUNK = 256
N_CHUNK = 2 * CONV // CHUNK
N_FAR = 5
N_NEAR = N_CHUNK - N_FAR
STACK = CONV + 16
LAG = 3
SLOTS = 4
FRONT = 80
Z = 4


def reduce_kernel(
    share, xt_hbm, x2t_hbm, g0_hbm, g1_hbm, gp_hbm, row_ref, out_ref, land_ref, far_ref,
    xt_ref, x2t_ref, g_ref, gp_ref, load, tile, flat, y_out, y_in, z_out, z_in, x_out, ret,
    y_send, y_recv, z_send, z_recv, x_send, x_recv, r_send, r_recv, hello, sem, *side_scratch,
):
    own, side_y, side_z, side_out, *side_sems = side_scratch
    side_part(share, row_ref, out_ref, own, side_y, side_z, side_out, flat, *side_sems)
    section = lax.axis_index("section")
    b = lax.axis_index("batch")
    y, z = lax.rem(b, 2), lax.div(b, 2)
    def owner(step):
        o = lax.rem(step, Z)
        up = jnp.where(z == 0, 3 - o, jnp.where(o == 0, 3, jnp.where(o == 1, 0, jnp.where(o == 2, 2, 1))))
        down = jnp.where(z == 3, o, jnp.where(o == 0, 0, jnp.where(o == 1, 3, jnp.where(o == 2, 1, 2))))
        return jnp.where(z < 2, up, down)

    def product(part, j):
        column = pl.multiple_of(j * CHUNK, CHUNK)

        @pl.when((part != 3) & (part != 7))
        def _():
            row = pl.multiple_of((35 * part + jnp.where(part >= 4, 1, 0)) * 16, 16)
            col = pl.multiple_of(column + jnp.where(part >= 4, 2 * CONV, 0), CHUNK)
            tile[...] = matmul(xt_ref[pl.ds(row, SLICE), :], g_ref[:, pl.ds(col, CHUNK)])

        second = pl.ds(pl.multiple_of(column + 2 * CONV, CHUNK), CHUNK)

        @pl.when(part == 3)
        def _():
            tile[0:384, :] = matmul(xt_ref[1680:STACK, :], g_ref[:, pl.ds(column, CHUNK)])
            tile[384:SLICE, :] = matmul(xt_ref[STACK : STACK + SLICE - 384, :], g_ref[:, second])

        @pl.when(part == 7)
        def _():
            tile[0:192, :] = matmul(xt_ref[2 * STACK - 192 : 2 * STACK, :], g_ref[:, second])

            @pl.when(j < 15)
            def _():
                row = pl.multiple_of(lax.rem(j, 5) * 400, 16)
                col = pl.multiple_of(lax.div(j, 5) * 256, 256)
                tile[192:SLICE, :] = matmul(x2t_ref[pl.ds(row, 400), :], gp_ref[:, pl.ds(col, 256)])

            @pl.when(j == 15)
            def _():
                for p in range(3):
                    tile[192 + 64 * p : 256 + 64 * p, :] = matmul(
                        x2t_ref[2000:STACK, :], gp_ref[:, p * 256 : (p + 1) * 256]
                    )
                tile[384:SLICE, :] = jnp.zeros((SLICE - 384, CHUNK), F32)

    def y_copy(part, j, slot):
        place = part * N_NEAR + j
        return pltpu.make_async_remote_copy(
            y_out.at[slot], y_in.at[place], y_send.at[slot], y_recv.at[place],
            device_id={"batch": b + 1 - 2 * y}, device_id_type=MESH,
        )

    def z_copy(part, j, o, down):
        place = part * N_CHUNK + j
        side = 0 if down else 1
        return pltpu.make_async_remote_copy(
            z_out.at[o], land_ref.at[side, place], z_send.at[o], z_recv.at[side, place],
            device_id={"batch": b - 2 if down else b + 2}, device_id_type=MESH,
        )

    def y_relay(part, j, slot):
        place = part * N_NEAR + j
        return pltpu.make_async_remote_copy(
            far_ref.at[(2 * part + 1 - y) * N_FAR + j], y_in.at[place], y_send.at[slot], y_recv.at[place],
            device_id={"batch": b + 1 - 2 * y}, device_id_type=MESH,
        )

    def x_copy(part, j, slot):
        place = part * N_FAR + j
        return pltpu.make_async_remote_copy(
            x_out.at[slot], far_ref.at[place], x_send.at[slot], x_recv.at[place],
            device_id={"section": 3}, device_id_type=MESH,
        )

    def back_copy(j):
        return pltpu.make_async_remote_copy(
            z_out.at[Z - 1], ret.at[j], r_send, r_recv.at[j], device_id={"section": 1}, device_id_type=MESH
        )

    def send_y(step, relay):
        part, j, slot = owner(step), lax.div(step, Z), lax.rem(step, SLOTS)
        copy = (y_relay if relay else y_copy)(part, j, slot)
        if relay:
            x_copy(2 * part + 1 - y, j, 0).wait_recv()
        else:
            product(2 * part + 1 - y, j)

        @pl.when(step >= SLOTS)
        def _():
            copy.wait_send()

        if not relay:
            y_out[slot] = to_low(tile[...])
        copy.start()

    def send_x(step):
        part, j, slot = lax.rem(step, 2 * Z), lax.div(step, 2 * Z), lax.rem(step, SLOTS)
        product(part, N_NEAR + j)

        @pl.when(step >= SLOTS)
        def _():
            x_copy(part, j, slot).wait_send()

        x_out[slot] = to_low(tile[...])
        x_copy(part, j, slot).start()

    def arriving(side, place, buffer):
        pltpu.make_async_remote_copy(
            z_out.at[0], land_ref.at[side, place], z_send.at[0], z_recv.at[side, place],
            device_id={"batch": b}, device_id_type=MESH,
        ).wait_recv()
        pltpu.make_async_copy(land_ref.at[side, place], z_in.at[buffer], sem.at[buffer]).start()

    def arrived(side, place, buffer):
        pltpu.make_async_copy(land_ref.at[side, place], z_in.at[buffer], sem.at[buffer]).wait()
        tile[...] += as_float(z_in[buffer])

    def keep(j):
        base = FRONT - 16 * b + jnp.where(b >= 4, 32, 0) + j * (CHUNK // LANES)

        def rows(first, count, start, column, stride):
            flat[pl.ds(start, count, stride=stride), :] = tile[first : first + count, column : column + LANES]

        @pl.when((b != 3) & (b != 7))
        def _():
            for c in range(CHUNK // LANES):
                rows(0, SLICE, base + c, c * LANES, 32)

        @pl.when(b == 3)
        def _():
            for c in range(CHUNK // LANES):
                rows(0, 369, base + c, c * LANES, 32)
                rows(384, SLICE - 384, FRONT + 11760 + j * (CHUNK // LANES) + c, c * LANES, 32)

        @pl.when(b == 7)
        def _():
            for c in range(CHUNK // LANES):
                rows(0, 177, base + c, c * LANES, 32)

            @pl.when(j < 15)
            def _():
                start = FRONT + 5584 + lax.rem(j, 5) * (400 * 6) + lax.div(j, 5) * 2
                for c in range(2):
                    rows(192, 400, start + c, c * LANES, 6)

            @pl.when(j == 15)
            def _():
                for p in range(3):
                    for c in range(2):
                        rows(192 + 64 * p, 64, FRONT + 5584 + 2000 * 6 + 2 * p + c, c * LANES, 6)

    def combine(part, j, o, relay):
        place = part * N_CHUNK + j
        above = (part <= z) & (z < Z - 1)
        below = (part >= z) & (z > 0)

        @pl.when(above)
        def _():
            arriving(0, place, 0)

        @pl.when(below)
        def _():
            arriving(1, place, 1)

        if relay:
            x_copy(2 * part + y, j, 0).wait_recv()
            copy = pltpu.make_async_copy(far_ref.at[(2 * part + y) * N_FAR + j], z_in.at[2], sem.at[2])
            copy.start()
            copy.wait()
            tile[...] = as_float(z_in[2])
        else:
            product(2 * part + y, j)
        y_copy(part, j, 0).wait_recv()
        tile[...] += as_float(y_in[part * N_NEAR + j])

        @pl.when(above)
        def _():
            arrived(0, place, 0)

        @pl.when(below)
        def _():
            arrived(1, place, 1)

        @pl.when(part == z)
        def _():
            if relay:

                @pl.when(j == 0)
                def _():
                    pl.semaphore_wait(hello, 1)

                @pl.when(j > 0)
                def _():
                    back_copy(j - 1).wait_send()

                z_out[Z - 1] = to_low(tile[...])
                back_copy(j).start()
            else:
                keep(j)

        @pl.when(part != z)
        def _():
            @pl.when(j > 0)
            def _():
                z_copy(part, j, o, True).wait_send()

            z_out[o] = to_low(tile[...])

            @pl.when(part < z)
            def _():
                z_copy(part, j, o, True).start()

            @pl.when(part > z)
            def _():
                z_copy(part, j, o, False).start()

    def rounds(chunks, relay):
        steps = Z * chunks

        def step_body(step, carry):
            @pl.when(step < steps)
            def _():
                send_y(step, relay)

            if not relay:

                @pl.when(step < 2 * Z * N_FAR)
                def _():
                    send_x(step)

            late = step - LAG
            part, o = owner(jnp.maximum(late, 0)), lax.rem(jnp.maximum(late, 0), Z)
            hops = jnp.where(part < z, 3 - z, jnp.where(part > z, z, jnp.maximum(z, 3 - z)))
            j = lax.div(jnp.maximum(late, 0), Z) - hops

            @pl.when((late >= 0) & (j >= 0) & (j < chunks))
            def _():
                combine(part, j, o, relay)

            return carry

        lax.fori_loop(0, steps + LAG + (Z - 1) * Z, step_body, 0)
        for slot in range(SLOTS):
            (y_relay if relay else y_copy)(0, 0, slot).wait_send()
        for o in range(Z - 1):
            z_copy(0, 0, o, True).wait_send()

    @pl.when(section == 1)
    def _():
        loads = [
            pltpu.make_async_copy(source, target, load.at[i])
            for i, (source, target) in enumerate(
                [(xt_hbm, xt_ref), (x2t_hbm, x2t_ref), (gp_hbm, gp_ref)]
                + [
                    (source.at[half], g_ref.at[:, pl.ds((2 * layer + half) * CONV, CONV)])
                    for layer, source in enumerate((g0_hbm, g1_hbm))
                    for half in range(2)
                ]
            )
        ]
        for copy in loads:
            copy.start()
        barrier = pltpu.get_barrier_semaphore()
        pl.semaphore_signal(barrier, inc=1, device_id={"batch": b + 1 - 2 * y}, device_id_type=MESH)

        @pl.when(z > 0)
        def _():
            pl.semaphore_signal(barrier, inc=1, device_id={"batch": b - 2}, device_id_type=MESH)

        @pl.when(z < Z - 1)
        def _():
            pl.semaphore_signal(barrier, inc=1, device_id={"batch": b + 2}, device_id_type=MESH)

        pl.semaphore_wait(barrier, 2 + jnp.where(z > 0, 1, 0) + jnp.where(z < Z - 1, 1, 0))
        pl.semaphore_signal(hello, inc=1, device_id={"section": 3}, device_id_type=MESH)
        for copy in loads:
            copy.wait()
        rounds(N_NEAR, False)
        for slot in range(SLOTS):
            x_copy(0, 0, slot).wait_send()

        def back(j, carry):
            back_copy(j).wait_recv()
            tile[...] = as_float(ret[j])
            keep(N_NEAR + j)
            return carry

        lax.fori_loop(0, N_FAR, back, 0)
        copy = pltpu.make_async_copy(flat.at[pl.ds(FRONT, share)], out_ref, sem.at[0])
        copy.start()
        copy.wait()

    @pl.when(section == 3)
    def _():
        rounds(N_FAR, True)
        back_copy(N_FAR - 1).wait_send()


def reduce_all(xt, x2t, g0, g1, gp, row, share):
    chunk = (SLICE, CHUNK)
    side = (SIDE_ROWS, LANES)
    dma = pltpu.SemaphoreType.DMA
    places = Z * N_CHUNK
    return pl.pallas_call(
        functools.partial(reduce_kernel, share),
        out_shape=[
            jax.ShapeDtypeStruct((share, LANES), F32),
            jax.ShapeDtypeStruct((2, places) + chunk, BF),
            jax.ShapeDtypeStruct((2 * Z * N_FAR,) + chunk, BF),
        ],
        in_specs=[hbm()] * 6,
        out_specs=[hbm()] * 3,
        scratch_shapes=[
            pltpu.VMEM(xt.shape, BF),
            pltpu.VMEM(x2t.shape, BF),
            pltpu.VMEM((gp.shape[0], 4 * CONV), BF),
            pltpu.VMEM(gp.shape, BF),
            dma((7,)),
            pltpu.VMEM(chunk, F32),
            pltpu.VMEM((SIDE_CHUNKS * SIDE_ROWS, LANES), F32),
            pltpu.VMEM((SLOTS,) + chunk, BF),
            pltpu.VMEM((Z * N_NEAR,) + chunk, BF),
            pltpu.VMEM((Z,) + chunk, BF),
            pltpu.VMEM((3,) + chunk, BF),
            pltpu.VMEM((SLOTS,) + chunk, BF),
            pltpu.VMEM((N_FAR,) + chunk, BF),
            dma((SLOTS,)),
            dma((Z * N_NEAR,)),
            dma((Z - 1,)),
            dma((2, places)),
            dma((SLOTS,)),
            dma((2 * Z * N_FAR,)),
            dma,
            dma((N_FAR,)),
            pltpu.SemaphoreType.REGULAR,
            dma((3,)),
            pltpu.VMEM(side, BF),
            pltpu.VMEM((SIDE_CHUNKS,) + side, BF),
            pltpu.VMEM((SIDE_CHUNKS,) + side, BF),
            pltpu.VMEM((SIDE_CHUNKS,) + side, BF),
            dma((SIDE_CHUNKS,)),
            dma((SIDE_CHUNKS,)),
            dma((SIDE_CHUNKS,)),
            dma((SIDE_CHUNKS,)),
            dma,
            dma,
            dma,
        ],
        compiler_params=pltpu.CompilerParams(
            collective_id=1, has_side_effects=True, vmem_limit_bytes=60 << 20
        ),
    )(xt, x2t, g0, g1, gp, row)


CNN_GRADS = (CONV // LANES) * LANES + TABLE_ROWS


def cnn_sum_kernel(in_ref, out_ref, low, y_in, z_in, send, recv):
    section = lax.axis_index("section")
    b = lax.axis_index("batch")
    y, z = lax.rem(b, 2), lax.div(b, 2)
    barrier = pltpu.get_barrier_semaphore()

    def along(target, other, i):
        return pltpu.make_async_remote_copy(
            low, target, send, recv.at[i], device_id={"batch": other}, device_id_type=MESH
        )

    @pl.when(section == 0)
    def _():
        pairs = [(y == 0, b + 1), (y == 1, b - 1), ((y == 0) & (z > 0), b - 2), ((y == 0) & (z < Z - 1), b + 2)]
        for condition, other in pairs:

            @pl.when(condition)
            def _():
                pl.semaphore_signal(barrier, inc=1, device_id={"batch": other}, device_id_type=MESH)

        pl.semaphore_wait(barrier, sum(jnp.where(condition, 1, 0) for condition, _ in pairs))
        out_ref[...] = in_ref[...]

        @pl.when(y == 1)
        def _():
            low[...] = to_low(out_ref[...])
            along(y_in, b - 1, 0).start()
            along(y_in, b - 1, 0).wait_send()

        @pl.when(y == 0)
        def _():
            along(y_in, b + 1, 0).wait_recv()
            out_ref[...] += as_float(y_in[...])

            @pl.when(z < Z - 1)
            def _():
                along(z_in, b + 2, 1).wait_recv()
                out_ref[...] += as_float(z_in[...])

            @pl.when(z > 0)
            def _():
                low[...] = to_low(out_ref[...])
                along(z_in, b - 2, 1).start()
                along(z_in, b - 2, 1).wait_send()


def cnn_sum(grads):
    low = pltpu.VMEM((CNN_GRADS, LANES), BF)
    dma = pltpu.SemaphoreType.DMA
    return pl.pallas_call(
        cnn_sum_kernel,
        out_shape=jax.ShapeDtypeStruct((CNN_GRADS, LANES), F32),
        in_specs=[vmem()],
        out_specs=vmem(),
        scratch_shapes=[
            low,
            low,
            low,
            dma,
            dma((2,)),
        ],
        compiler_params=pltpu.CompilerParams(
            collective_id=3, has_side_effects=True, vmem_limit_bytes=24 << 20
        ),
    )(grads)


PIECES = 19


def assemble_kernel(cnn_ref, total_ref, out_ref, buffer, fetch, store):
    section = lax.axis_index("section")
    rows = out_ref.shape[0] // PIECES

    def part(i):
        return pl.ds(i * rows, rows)

    for i in range(PIECES):
        pltpu.make_async_copy(total_ref.at[part(i)], buffer.at[part(i)], fetch.at[i]).start()
    for i in range(PIECES):
        pltpu.make_async_copy(total_ref.at[part(i)], buffer.at[part(i)], fetch.at[i]).wait()
        pltpu.make_async_copy(buffer.at[part(i)], out_ref.at[part(i)], store.at[i]).start()
    for i in range(PIECES):
        pltpu.make_async_copy(buffer.at[part(i)], out_ref.at[part(i)], store.at[i]).wait()

    @pl.when((section == 0) & (lax.axis_index("batch") == 0))
    def _():
        head = buffer.at[pl.ds(0, CNN_ROWS)]
        for copy in (
            pltpu.make_async_copy(cnn_ref, head, fetch.at[0]),
            pltpu.make_async_copy(head, out_ref.at[pl.ds(0, CNN_ROWS)], store.at[0]),
        ):
            copy.start()
            copy.wait()


def assemble(cnn, total):
    return pl.pallas_call(
        assemble_kernel,
        out_shape=jax.ShapeDtypeStruct(total.shape, F32),
        in_specs=[hbm()] * 2,
        out_specs=hbm(),
        scratch_shapes=[
            pltpu.VMEM(total.shape, F32),
            pltpu.SemaphoreType.DMA((PIECES,)),
            pltpu.SemaphoreType.DMA((PIECES,)),
        ],
        compiler_params=pltpu.CompilerParams(vmem_limit_bytes=60 << 20),
    )(cnn, total)


def on_section(numbers, function, *operands):
    shapes = jax.eval_shape(function, *operands)
    leaves, tree = jax.tree.flatten(shapes)

    def idle(*unused):
        return jax.tree.unflatten(
            tree,
            pl.pallas_call(
                lambda *refs: None,
                out_shape=[jax.ShapeDtypeStruct(s.shape, s.dtype) for s in leaves],
                out_specs=[hbm()] * len(leaves),
            )(),
        )

    section = lax.axis_index("section")
    here = sum(jnp.where(section == n, 1, 0) for n in numbers) > 0
    return lax.cond(here, function, idle, *operands)


def shards(char_ids, word_lengths, params, cotangent):
    section = lax.axis_index("section")
    n_batch = lax.axis_size("batch")
    words_all = lax.all_gather(
        jnp.concatenate([char_ids, word_lengths[:, None]], axis=1), "section", axis=0, tiled=True
    )
    params, words_all = lax.optimization_barrier((params, words_all))
    ck, tt = cnn_params(params)
    group = words_all.shape[0]
    quarter, words, half = group // 4, group // len(CNN), group // 2
    ids_all, column_all = words_all[:, :CHAR_LEN], words_all[:, CHAR_LEN:]
    row_all = column_all.T
    ends_all = stage_bounds(column_all, len(CNN))
    place = jnp.maximum(section - 1, 0)

    def mine(array, axis=0):
        return lax.dynamic_slice_in_dim(array, place * words, words, axis)

    pooled_part = on_section(
        CNN, chars_forward, ends_all[place], mine(ids_all), mine(column_all), mine(row_all, 1), ck, tt
    )
    pooled, cot, w0, w1, wp, vec = start_highways(params, pooled_part, cotangent)
    params, pooled = lax.optimization_barrier((params, pooled))
    encoder_weights = start_encoder(params)
    pooled, encoder_weights = lax.optimization_barrier((pooled, encoder_weights))
    projected, x1, x2, *kept = on_section((1,), highway_forward, w0, w1, wp, vec, pooled)
    (encoder_in,) = hand_over(
        6, [(1, 2, 0, 0, half, 0, 0), (1, 3, 0, half, half, 0, 0)], [projected], [((half, D), BF)]
    )
    x2, encoder_in = lax.optimization_barrier((x2, encoder_in))
    xt, x2t = stack_highways(pooled, x1, x2)
    encoder_in, xt = lax.optimization_barrier((encoder_in, xt))
    layer, back, joined, mixed, att, normed, activated, inner, branch, sums = on_section(
        (2, 3), encoder, encoder_in, cot, *encoder_weights
    )
    items = [(2, 1, 0, 0, half, 0, 0), (3, 1, 0, 0, half, 0, half)]
    items += [(2 + s // 2, s, 1, s % 2 * quarter, quarter, 1, 0) for s in range(4)]
    items += [(3 if k < 4 else 2, 2 if k < 4 else 3, 2 + k, 0, half, 2 + k, 0) for k in range(8)]
    items += [(2, 3, 10, 0, 8, 10, 0), (3, 2, 10, 0, 8, 10, 0)]
    own_rows = [encoder_in, mixed, joined, att, normed, activated, inner, branch, sums]
    grad_highway, layer_out, *other_rows = hand_over(
        7,
        items,
        [back, layer, *own_rows],
        [((group, D), BF), ((quarter, D), BF)] + [(value.shape, value.dtype) for value in own_rows],
    )
    grad_pooled, grad0, grad1 = on_section(
        (1,), highway_backward, w0, w1, wp, pooled, x1, *kept, grad_highway
    )
    (grad_part,) = hand_over(8, [(1, 0, 0, 0, group, 0, 0)], [grad_pooled], [((group, CONV), BF)])
    other_rows, grad_part = lax.optimization_barrier((other_rows, grad_part))
    side = side_rows(own_rows, other_rows)
    share = params.shape[1] // n_batch // LANES
    by_kernels = n_batch == 2 * Z and share == SIDE_SHARE
    if by_kernels:
        total, *_ = reduce_all(xt, x2t, grad0, grad1, grad_highway, side, share)
        grad_part, total = lax.optimization_barrier((grad_part, total))
    cnn_part = on_section((0,), chars_backward, ends_all, ids_all, column_all, row_all, ck, tt, grad_part)
    if not by_kernels:
        return (layer_out, summed_rows(params.shape[1], cnn_part, pooled, x1, x2, grad0, grad1, grad_highway, side))
    cnn_total = cnn_sum(cnn_part)

    def first_row(grads):
        flat = cnn_gradient(grads)
        return jnp.pad(flat, (0, CNN_ROWS * LANES - flat.shape[0])).reshape(-1, LANES)

    cnn_row = on_section((0,), first_row, cnn_total)
    total = assemble(cnn_row, total)
    return (layer_out, total.reshape(1, -1))


def summed_rows(size, cnn_part, pooled, x1, x2, grad0, grad1, grad_highway, side):
    first = lax.axis_index("batch") == 0
    cnn_flat = cnn_gradient(lax.psum(jnp.where(lax.axis_index("section") == 0, cnn_part, 0.0), ("section", "batch")))

    def wide(flat):
        return jnp.pad(as_float(flat), (0, size - flat.shape[0]))

    def highways():
        ones = jnp.ones((1, pooled.shape[0]), BF)
        pieces = []
        both = [jnp.concatenate([grad[0], grad[1]], axis=1) for grad in (grad0, grad1)]
        for x, g in ((pooled, both[0]), (x1, both[1]), (x2, grad_highway)):
            pieces += [matmul_tn(x, g).reshape(-1), matmul(ones, g).reshape(-1)]
        return wide(jnp.concatenate(pieces))

    row = lax.switch(
        lax.axis_index("section"),
        [
            lambda: wide(jnp.where(first, cnn_flat, 0.0)),
            highways,
            lambda: wide(side.reshape(-1)),
            lambda: wide(side.reshape(-1)),
        ],
    )
    return lax.psum_scatter(row, "batch", scatter_dimension=0, tiled=True).reshape(1, -1)


def solution(mesh):
    return jax.shard_map(
        shards,
        mesh=mesh,
        in_specs=(
            P(("section", "batch"), None),
            P(("section", "batch")),
            P("section", None),
            P(("section", "batch"), None),
        ),
        out_specs=(P(("section", "batch"), None), P("section", "batch")),
        check_vma=False,
    )
```

```python
import functools
import math

import jax
import jax.numpy as jnp
from jax import lax
from jax.experimental import pallas as pl
from jax.experimental.pallas import tpu as pltpu
from jax.sharding import PartitionSpec as P

D = 768
HEADS = 12
HEAD_DIM = 64
FF = 3072
CHAR_DIM = 16
CHARS = 262
CHAR_LEN = 50
CH_UNIT = 32
SEQ_LEN = 192
CONV = 64 * CH_UNIT
LANES = 128
MESH = pl.DeviceIdType.MESH
BF = jnp.bfloat16
F32 = jnp.float32
HUGE = 1e30
CNN = (0, 2, 3)

HW_CHUNK = 512
HW_SHAPE = (CONV // HW_CHUNK, CONV, 2 * HW_CHUNK)
channel_steps = (1, 1, 2, 4, 8, 16, 32)
layer_eps = 1e-12

HW_BIAS0 = CONV * 2 * CONV
HW_W1 = HW_BIAS0 + 2 * CONV
HW_BIAS1 = HW_W1 + CONV * 2 * CONV
PROJ_W = HW_BIAS1 + 2 * CONV
PROJ_B = PROJ_W + CONV * D
Q_BIAS = D * 3 * D
V_BIAS = Q_BIAS + D
OUT_W = V_BIAS + D
OUT_B = OUT_W + D * D
UP_B = D * FF
DOWN_W = UP_B + FF
DOWN_B = DOWN_W + FF * D
TABLE = CHARS * CHAR_DIM
CNN_FLAT = TABLE + sum((n + 1) * CHAR_DIM * c * CH_UNIT for n, c in enumerate(channel_steps)) + CONV


def hbm():
    return pl.BlockSpec(memory_space=pltpu.HBM)


def vmem():
    return pl.BlockSpec(memory_space=pltpu.VMEM)


def as_float(array_in):
    return array_in.astype(F32)


def to_low(array_in):
    return array_in.astype(BF)


def matmul(left_in, right_in):
    return jnp.dot(left_in, right_in, preferred_element_type=F32)


def matmul_tn(left_in, right_in):
    return lax.dot_general(left_in, right_in, (((0,), (0,)), ((), ())), preferred_element_type=F32)


def matmul_nt(left_in, right_in):
    return lax.dot_general(left_in, right_in, (((1,), (1,)), ((), ())), preferred_element_type=F32)


class Transfers:
    def __init__(self, items):
        self.items = items

    def copy(self, i, operands, outputs, send, recv):
        source, target, operand, first, rows, output, there = self.items[i]
        from_ref = operands[operand].at[pl.ds(first, rows)]
        to_ref = outputs[output].at[pl.ds(there, rows)]
        if source == target:
            return pltpu.make_async_copy(from_ref, to_ref, send.at[i])
        return pltpu.make_async_remote_copy(
            from_ref, to_ref, send.at[i], recv.at[i], device_id={"section": target}, device_id_type=MESH
        )

    def partners(self, s):
        pairs = {(item[0], item[1]) for item in self.items if item[0] != item[1]}
        return sorted({b for a, b in pairs if a == s} | {a for a, b in pairs if b == s})

    def run(self, operands, outputs, send, recv, work=None):
        section = lax.axis_index("section")
        for s in range(4):
            mine = [i for i, item in enumerate(self.items) if s in item[:2]]
            work_here = (work or {}).get(s)
            if not mine and work_here is None:
                continue

            @pl.when(section == s)
            def _(s=s, mine=mine, work_here=work_here):
                partners = self.partners(s)
                barrier = pltpu.get_barrier_semaphore()
                for other in partners:
                    pl.semaphore_signal(barrier, inc=1, device_id={"section": other}, device_id_type=MESH)
                if work_here is not None:
                    work_here()
                if partners:
                    pl.semaphore_wait(barrier, len(partners))
                outgoing = [i for i in mine if self.items[i][0] == s]
                for i in outgoing:
                    self.copy(i, operands, outputs, send, recv).start()
                for i in mine:
                    copy = self.copy(i, operands, outputs, send, recv)
                    if self.items[i][0] == self.items[i][1]:
                        copy.wait()
                    elif i in outgoing:
                        copy.wait_send()
                    else:
                        copy.wait_recv()


def hand_over(collective_id, items, operands, out_shapes):
    transfers = Transfers(items)

    def kernel(*refs):
        n, m = len(operands), len(out_shapes)
        transfers.run(refs[:n], refs[n : n + m], *refs[n + m :])

    return pl.pallas_call(
        kernel,
        out_shape=[jax.ShapeDtypeStruct(*shape) for shape in out_shapes],
        in_specs=[hbm()] * len(operands),
        out_specs=[hbm()] * len(out_shapes),
        scratch_shapes=[pltpu.SemaphoreType.DMA((len(items),))] * 2,
        compiler_params=pltpu.CompilerParams(collective_id=collective_id, has_side_effects=True),
    )(*operands)


def cut_tools(p_ref, raw, sems):
    def matrix(offset, target, rows):
        count, columns = target.shape

        def body(in_ref, out_ref):
            out_ref[...] = in_ref[...].reshape(rows, columns)

        pltpu.emit_pipeline(
            body,
            grid=(count // rows,),
            in_specs=[pl.BlockSpec((1, rows * columns), lambda i: (0, i))],
            out_specs=[pl.BlockSpec((rows, columns), lambda i: (i, 0))],
        )(p_ref.at[:, pl.ds(offset, count * columns)], target)

    def vectors(entries, vec):
        copies = []
        for row, (offset, size) in enumerate(entries):
            copy = pltpu.make_async_copy(
                p_ref.at[:, pl.ds(offset, size)], raw.at[row, :, pl.ds(0, size)], sems.at[row]
            )
            copy.start()
            copies.append(copy)
        for copy in copies:
            copy.wait()
        for row, (offset, size) in enumerate(entries):
            vec[row : row + 1, 0:size] = as_float(raw[row, :, 0:size])

    def chunks(offset, target, rows):
        parts = 4
        count = rows // parts

        def body(*refs):
            out_ref = refs[-1]
            for k, in_ref in enumerate(refs[:-1]):
                value = in_ref[...].reshape(count, 2 * CONV)
                for c in range(CONV // HW_CHUNK):
                    for half in range(2):
                        start = half * CONV + c * HW_CHUNK
                        out_ref[c, k * count : (k + 1) * count, half * HW_CHUNK : (half + 1) * HW_CHUNK] = value[
                            :, start : start + HW_CHUNK
                        ]

        pltpu.emit_pipeline(
            body,
            grid=(CONV // rows,),
            in_specs=[
                pl.BlockSpec(
                    (1, count * 2 * CONV), lambda i, k=k: (0, i * parts + k), pipeline_mode=pl.Buffered(3)
                )
                for k in range(parts)
            ],
            out_specs=[pl.BlockSpec((CONV // HW_CHUNK, rows, 2 * HW_CHUNK), lambda i: (0, i, 0))],
        )(*([p_ref.at[:, pl.ds(offset, CONV * 2 * CONV)]] * parts), target)

    return matrix, vectors, chunks


def vector_store(vec, target, sem):
    copy = pltpu.make_async_copy(vec, target, sem)
    copy.start()
    copy.wait()


def start_highways(params, pooled_part, cotangent):
    words, quarter = pooled_part.shape[0], cotangent.shape[0]
    items = [(s, 1, 0, 0, words, 0, i * words) for i, s in enumerate(CNN)]
    items += [(s, 2 + s // 2, 1, 0, quarter, 1, s % 2 * quarter) for s in range(4)]
    transfers = Transfers(items)

    def kernel(pooled_ref, cot_ref, p_ref, pooled, cot, w0, w1, wp, vec_ref, vec, raw, sems, send, recv):
        matrix, vectors, chunks = cut_tools(p_ref, raw, sems)

        def work():
            vectors([(HW_BIAS0, 2 * CONV), (HW_BIAS1, 2 * CONV), (PROJ_B, D)], vec)
            vector_store(vec, vec_ref, sems.at[0])
            chunks(0, w0, 256)
            chunks(HW_W1, w1, 256)
            matrix(PROJ_W, wp, 512)

        transfers.run((pooled_ref, cot_ref), (pooled, cot), send, recv, {1: work})

    shapes = [(words * len(CNN), CONV), (2 * quarter, D), HW_SHAPE, HW_SHAPE, (CONV, D)]
    return pl.pallas_call(
        kernel,
        out_shape=[jax.ShapeDtypeStruct(s, BF) for s in shapes] + [jax.ShapeDtypeStruct((8, 2 * CONV), F32)],
        in_specs=[hbm()] * 3,
        out_specs=[hbm()] * 6,
        scratch_shapes=[
            pltpu.VMEM((8, 2 * CONV), F32),
            pltpu.VMEM((5, 1, 2 * CONV), BF),
            pltpu.SemaphoreType.DMA((5,)),
            pltpu.SemaphoreType.DMA((len(items),)),
            pltpu.SemaphoreType.DMA((len(items),)),
        ],
        compiler_params=pltpu.CompilerParams(
            collective_id=4, has_side_effects=True, vmem_limit_bytes=40 << 20
        ),
    )(pooled_part, cotangent, params)


def start_encoder(params):
    shapes = [(D, 3 * D), (D, D), (D, FF), (FF, D)]
    owners = (2, 2, 3, 3)
    items = [(s, 5 - s, i, 0, shape[0], i, 0) for i, (s, shape) in enumerate(zip(owners, shapes, strict=True))]
    items += [(2, 3, 4, 0, 8, 4, 0), (3, 2, 5, 0, 8, 5, 0)]
    transfers = Transfers(items)

    def kernel(p_ref, wqkv, wo, wu, wd, vec2, vec3, vec, raw, sems, send, recv):
        matrix, vectors, _ = cut_tools(p_ref, raw, sems)

        def work2():
            vectors([(Q_BIAS, D), (V_BIAS, D), (OUT_B, D), (OUT_B + D, D), (OUT_B + 2 * D, D)], vec)
            vector_store(vec, vec2, sems.at[0])
            matrix(0, wqkv, 256)
            matrix(OUT_W, wo, 384)

        def work3():
            vectors([(UP_B, FF), (DOWN_B, D), (DOWN_B + D, D), (DOWN_B + 2 * D, D)], vec)
            vector_store(vec, vec3, sems.at[0])
            matrix(0, wu, 256)
            matrix(DOWN_W, wd, 512)

        outputs = (wqkv, wo, wu, wd, vec2, vec3)
        transfers.run(outputs, outputs, send, recv, {2: work2, 3: work3})

    return pl.pallas_call(
        kernel,
        out_shape=[jax.ShapeDtypeStruct(s, BF) for s in shapes] + [jax.ShapeDtypeStruct((8, 2 * CONV), F32)] * 2,
        in_specs=[hbm()],
        out_specs=[hbm()] * 6,
        scratch_shapes=[
            pltpu.VMEM((8, 2 * CONV), F32),
            pltpu.VMEM((5, 1, 2 * CONV), BF),
            pltpu.SemaphoreType.DMA((5,)),
            pltpu.SemaphoreType.DMA((len(items),)),
            pltpu.SemaphoreType.DMA((len(items),)),
        ],
        compiler_params=pltpu.CompilerParams(
            collective_id=5, has_side_effects=True, vmem_limit_bytes=40 << 20
        ),
    )(params)


CNN_ROWS = 1600
TABLE_ROWS = 384


def cnn_params_kernel(p_ref, ck_ref, tt_ref, raw, flat, kernel, table, sem, send, recv):
    section = lax.axis_index("section")
    others = [s for s in CNN if s]
    lane = lax.broadcasted_iota(jnp.int32, (1, LANES), 1)
    barrier = pltpu.get_barrier_semaphore()

    @pl.when(section == 0)
    def _():
        copy = pltpu.make_async_copy(p_ref.at[:, pl.ds(0, CNN_ROWS * LANES)], raw, sem)
        copy.start()
        for s in others:
            pl.semaphore_signal(barrier, inc=1, device_id={"section": s}, device_id_type=MESH)
        copy.wait()
        flat[...] = as_float(raw[...]).reshape(CNN_ROWS, LANES)
        table[...] = jnp.zeros_like(table)
        head = flat[0:40, :]
        for b in range(8):
            mixed = jnp.zeros_like(head)
            for g in range(7):
                rolled = head if g == b else pltpu.roll(head, (g - b) * CHAR_DIM % LANES, 1)
                mixed = jnp.where((lane >= g * CHAR_DIM) & (lane < (g + 1) * CHAR_DIM), rolled, mixed)
            table[pl.ds(b, 33, stride=8), :] = mixed[0:33]
        tt_ref[...] = to_low(table[...])
        rolled = pltpu.roll(flat[...], 32, 1)
        flat[...] = rolled
        count = CNN_ROWS - 40
        flat[0:count, :] = jnp.where(
            lane < 32, flat[32 : 32 + count, :], flat[33 : 33 + count, :]
        )
        kernel[...] = jnp.zeros_like(kernel)
        first, second, third = flat[0:8, :], flat[4:12, :], flat[12:36, :]
        narrow = lax.broadcasted_iota(jnp.int32, (8, LANES), 0) < 4
        for b in range(4):
            one = first if b == 0 else pltpu.roll(first, -b * 32 % LANES, 1)
            two = second if b == 1 else pltpu.roll(second, (32 - b * 32) % LANES, 1)
            kernel[0, pl.ds(b, 8, stride=4), :] = jnp.where(
                lane < 32, jnp.where(narrow, one, 0.0), jnp.where(lane < 64, two, 0.0)
            )
        for b in range(2):
            three = third if b == 1 else pltpu.roll(third, 64, 1)
            kernel[0, pl.ds(b, 24, stride=2), :] = jnp.where(
                lane >= 64, three, kernel[0, pl.ds(b, 24, stride=2), :]
            )
        row, tile = 36, 1
        for number in range(3, 7):
            parts = channel_steps[number] * CH_UNIT // LANES
            depth = (number + 1) * CHAR_DIM
            for c in range(parts):
                kernel[tile, 0:depth, :] = flat[pl.ds(row + c, depth, stride=parts), :]
                tile += 1
            row += depth * parts
        bound = 0
        for number in range(7):
            upper = bound + channel_steps[number] * CH_UNIT
            for c in range(bound // LANES, -(-upper // LANES)):
                kernel[c, 112 + number : 113 + number, :] = jnp.where(
                    (lane + c * LANES >= bound) & (lane + c * LANES < upper), -HUGE, 0.0
                )
            bound = upper
        for c in range(CONV // LANES):
            kernel[c, 119:120, :] = flat[row + c : row + c + 1, :]
            ck_ref[:, c * LANES : (c + 1) * LANES] = to_low(kernel[c])
        pl.semaphore_wait(barrier, len(others))
        copies = []
        for i, s in enumerate(others):
            for j, ref in enumerate((ck_ref, tt_ref)):
                copies.append(
                    pltpu.make_async_remote_copy(
                        ref, ref, send.at[i, j], recv.at[j], device_id={"section": s}, device_id_type=MESH
                    )
                )
        for copy in copies:
            copy.start()
        for copy in copies:
            copy.wait_send()

    for s in others:

        @pl.when(section == s)
        def _():
            pl.semaphore_signal(barrier, inc=1, device_id={"section": 0}, device_id_type=MESH)
            pl.semaphore_wait(barrier, 1)
            for j, ref in enumerate((ck_ref, tt_ref)):
                pltpu.make_async_remote_copy(
                    ref, ref, send.at[0, j], recv.at[j], device_id={"section": 0}, device_id_type=MESH
                ).wait_recv()


def cnn_params(params):
    return pl.pallas_call(
        cnn_params_kernel,
        out_shape=[
            jax.ShapeDtypeStruct((LANES, CONV), BF),
            jax.ShapeDtypeStruct((TABLE_ROWS, LANES), BF),
        ],
        in_specs=[hbm()],
        out_specs=[vmem(), vmem()],
        scratch_shapes=[
            pltpu.VMEM((1, CNN_ROWS * LANES), BF),
            pltpu.VMEM((CNN_ROWS, LANES), F32),
            pltpu.VMEM((CONV // LANES, LANES, LANES), F32),
            pltpu.VMEM((TABLE_ROWS, LANES), F32),
            pltpu.SemaphoreType.DMA,
            pltpu.SemaphoreType.DMA((len(CNN) - 1, 2)),
            pltpu.SemaphoreType.DMA((2,)),
        ],
        compiler_params=pltpu.CompilerParams(
            collective_id=0, has_side_effects=True, vmem_limit_bytes=24 << 20
        ),
    )(params)


STAGES = ((128, 1), (64, 2), (16, 8))
SPOTS = CHAR_LEN + 14


def stage_bounds(lengths, blocks):
    words = lengths.shape[0] // blocks
    counts = jnp.sum(lengths.reshape(blocks, words, 1) > jnp.arange(CHAR_LEN, dtype=jnp.int32), axis=1)
    limits = jnp.array([[words // 2], [words // 8], [0]], jnp.int32)
    return jnp.sum(counts[:, None, :] > limits, axis=2).astype(jnp.int32)


def sorting(column_ref, row_ref):
    count = row_ref.shape[1]
    down = lax.broadcasted_iota(jnp.int32, (count, count), 0)
    across = lax.broadcasted_iota(jnp.int32, (count, count), 1)
    column, row = column_ref[...], row_ref[...]
    before = (column > row) | ((column == row) & (down < across))
    rank = jnp.sum(jnp.where(before, 1, 0), axis=0, keepdims=True)
    return jnp.where(down == rank, 1.0, 0.0).astype(BF)


def sorted_words(order, ids_ref, column_ref):
    ids = ids_ref[...]
    high = lax.div(ids, 16)
    low = ids - 16 * high
    ids = matmul(order, to_low(as_float(high))) * 16.0 + matmul(order, to_low(as_float(low)))
    length = matmul(order, to_low(as_float(jnp.broadcast_to(column_ref[...], (ids.shape[0], LANES)))))
    return ids, length


def stages(ends_ref, body):
    start = 0
    for k, (words, positions) in enumerate(STAGES):
        end = ends_ref[k]

        def one(i, unused, words=words, positions=positions, start=start, end=end):
            body(start + i * positions, words, positions, end)
            return unused

        lax.fori_loop(0, lax.div(jnp.maximum(end - start, 0) + positions - 1, positions), one, 0)
        start = end


def one_hot(first, words, positions, ids):
    lane = lax.broadcasted_iota(jnp.int32, (words, CHAR_LEN), 1)
    columns = [
        jnp.sum(jnp.where(lane == first + q, ids[0:words, :], 0.0), axis=1, keepdims=True) for q in range(positions)
    ]
    column = columns[0] if positions == 1 else jnp.concatenate(columns, axis=0)
    symbol = lax.broadcasted_iota(jnp.int32, (words * positions, TABLE_ROWS), 1)
    return jnp.where(column.astype(jnp.int32) == symbol, 1.0, 0.0).astype(BF)


def windows(first, words, positions, end, length, embedded, masks):
    total = None
    for j in range(7):
        term = embedded[pl.ds(first + j, positions), 0:words, :] * masks[j]
        total = term if total is None else total + term
    shape = (positions, words, LANES)
    lane = lax.broadcasted_iota(jnp.int32, shape, 2)
    position = first + lax.broadcasted_iota(jnp.int32, shape, 0)
    room = jnp.broadcast_to(length[0:words, :][None], shape)
    out = (lane >= 112) & (lane < 119) & ((as_float(position + lane - 111) > room) | (position >= end))
    return (total + jnp.where(out | (lane == 119), 1.0, 0.0).astype(BF)).reshape(positions * words, LANES)


def lane_masks():
    lane = lax.broadcasted_iota(jnp.int32, (1, 1, LANES), 2)
    return [
        jnp.where((lane >= j * CHAR_DIM) & (lane < (j + 1) * CHAR_DIM), 1.0, 0.0).astype(BF)
        for j in range(7)
    ]


def embedder(ids, tt_ref, embedded):
    def embed(first, words, positions, end):
        value = to_low(matmul(one_hot(first, words, positions, ids), tt_ref[...]))
        embedded[pl.ds(first, positions), 0:words, :] = value.reshape(positions, words, LANES)

    return embed


def chars_forward_kernel(ends_ref, ids_ref, column_ref, row_ref, ck_ref, tt_ref, out_ref, embedded, best):
    embedded[...] = jnp.zeros_like(embedded)
    best[...] = jnp.full_like(best, -HUGE)
    masks = lane_masks()
    order = sorting(column_ref, row_ref)
    ids, length = sorted_words(order, ids_ref, column_ref)
    stages(ends_ref, embedder(ids, tt_ref, embedded))

    def pool(first, words, positions, end):
        rows = windows(first, words, positions, end, length, embedded, masks)
        for c in range(0, CONV, 512):
            pre = jnp.max(matmul(rows, ck_ref[:, c : c + 512]).reshape(positions, words, 512), axis=0)
            best[0:words, c : c + 512] = jnp.maximum(best[0:words, c : c + 512], pre)

    stages(ends_ref, pool)
    out_ref[...] = to_low(matmul_tn(order, to_low(jnp.maximum(best[...], 0.0))))


def chars_backward_kernel(
    all_ends_ref, ids_ref, column_ref, row_ref, ck_ref, tt_ref, grad_ref,
    out_ref, embedded, best, share, backs, sums,
):
    block = pl.program_id(0)
    ends_ref = [all_ends_ref[block, k] for k in range(len(STAGES))]
    embedded[...] = jnp.zeros_like(embedded)
    backs[...] = jnp.zeros_like(backs)
    best[...] = jnp.full_like(best, -HUGE)
    share[...] = jnp.zeros_like(share)
    table_rows = pl.ds(CONV, TABLE_ROWS)

    @pl.when(block == 0)
    def _():
        sums[...] = jnp.zeros_like(sums)
        out_ref[table_rows, :] = jnp.zeros((TABLE_ROWS, LANES), F32)

    masks = lane_masks()
    order = sorting(column_ref, row_ref)
    ids, length = sorted_words(order, ids_ref, column_ref)
    stages(ends_ref, embedder(ids, tt_ref, embedded))

    def count(first, words, positions, end):
        rows = windows(first, words, positions, end, length, embedded, masks)
        for c in range(0, CONV, 512):
            part = slice(c, c + 512)
            pre = matmul(rows, ck_ref[:, part])
            top, hits = best[0:words, part], share[0:words, part]
            for q in range(positions):
                here = pre[q * words : (q + 1) * words]
                hits = jnp.where(here > top, 1.0, hits + jnp.where(here == top, 1.0, 0.0))
                top = jnp.maximum(top, here)
            best[0:words, part], share[0:words, part] = top, hits

    stages(ends_ref, count)
    share[...] = matmul(order, grad_ref[...]) / share[...]
    best[...] = jnp.where(best[...] > 0.0, best[...], 3e38)

    def spread(first, words, positions, end):
        rows = windows(first, words, positions, end, length, embedded, masks)
        back = jnp.zeros((words * positions, LANES), F32)
        for c in range(0, CONV, 512):
            part = slice(c, c + 512)
            pre = matmul(rows, ck_ref[:, part]).reshape(positions, words, 512)
            hit = pre == best[0:words, part][None]
            grad = to_low(jnp.where(hit, jnp.broadcast_to(share[0:words, part][None], pre.shape), 0.0))
            grad = grad.reshape(positions * words, 512)
            sums[:, part] += matmul_tn(rows, grad)
            back = back + matmul_nt(grad, ck_ref[:, part])
        backs[pl.ds(first + 6, positions), 0:words, :] = to_low(back).reshape(positions, words, LANES)

    stages(ends_ref, spread)

    def gather(first, words, positions, end):
        shape = (positions, words, LANES)
        lane = lax.broadcasted_iota(jnp.int32, shape, 2)
        position = first + lax.broadcasted_iota(jnp.int32, shape, 0)
        total = jnp.zeros(shape, F32)
        for j in range(7):
            here = (lane >= j * CHAR_DIM) & (lane < (j + 1) * CHAR_DIM) & (position < end)
            total = jnp.where(here, as_float(backs[pl.ds(first + 6 - j, positions), 0:words, :]), total)
        hot = one_hot(first, words, positions, ids)
        out_ref[table_rows, :] += matmul_tn(hot, to_low(total).reshape(positions * words, LANES))

    stages(ends_ref, gather)

    @pl.when(block == pl.num_programs(0) - 1)
    def _():
        for c in range(CONV // LANES):
            out_ref[c * LANES : (c + 1) * LANES, :] = sums[:, c * LANES : (c + 1) * LANES]


def chars_forward(ends, ids, column, row, ck, tt):
    words = ids.shape[0]
    return pl.pallas_call(
        chars_forward_kernel,
        out_shape=jax.ShapeDtypeStruct((words, CONV), BF),
        in_specs=[pl.BlockSpec(memory_space=pltpu.SMEM)] + [vmem()] * 5,
        out_specs=vmem(),
        scratch_shapes=[
            pltpu.VMEM((SPOTS, words, LANES), BF),
            pltpu.VMEM((words, CONV), F32),
        ],
        compiler_params=pltpu.CompilerParams(vmem_limit_bytes=32 << 20),
    )(ends, ids, column, row, ck, tt)


def chars_backward(ends, ids, column, row, ck, tt, grad):
    words = ids.shape[0] // len(CNN)
    return pl.pallas_call(
        chars_backward_kernel,
        grid=(len(CNN),),
        out_shape=jax.ShapeDtypeStruct((CNN_GRADS, LANES), F32),
        in_specs=[
            pl.BlockSpec(memory_space=pltpu.SMEM),
            pl.BlockSpec((words, CHAR_LEN), lambda i: (i, 0)),
            pl.BlockSpec((words, 1), lambda i: (i, 0)),
            pl.BlockSpec((1, words), lambda i: (0, i)),
            pl.BlockSpec((LANES, CONV), lambda i: (0, 0)),
            pl.BlockSpec((TABLE_ROWS, LANES), lambda i: (0, 0)),
            pl.BlockSpec((words, CONV), lambda i: (i, 0)),
        ],
        out_specs=pl.BlockSpec((CNN_GRADS, LANES), lambda i: (0, 0)),
        scratch_shapes=[
            pltpu.VMEM((SPOTS, words, LANES), BF),
            pltpu.VMEM((words, CONV), F32),
            pltpu.VMEM((words, CONV), F32),
            pltpu.VMEM((SPOTS, words, LANES), BF),
            pltpu.VMEM((LANES, CONV), F32),
        ],
        compiler_params=pltpu.CompilerParams(vmem_limit_bytes=40 << 20),
    )(ends, ids, column, row, ck, tt, grad)


def cnn_gradient(grads):
    table_grad = grads[CONV:]
    kernel_grad = jnp.swapaxes(grads[:CONV].reshape(-1, LANES, LANES), 0, 1).reshape(LANES, CONV)
    pieces = [
        sum(table_grad[:CHARS, g * CHAR_DIM : (g + 1) * CHAR_DIM] for g in range(7)).reshape(-1)
    ]
    offset = 0
    for number in range(7):
        channels = channel_steps[number] * CH_UNIT
        pieces.append(
            kernel_grad[: (number + 1) * CHAR_DIM, offset : offset + channels].reshape(-1)
        )
        offset += channels
    pieces.append(kernel_grad[119])
    return jnp.concatenate(pieces)


def sigmoid(value):
    return 1.0 / (1.0 + jnp.exp(-value))


def highway_layer_kernel(row, x_ref, part_ref, w_ref, bl_ref, br_ref, next_ref, left_ref, right_ref):
    both = matmul(x_ref[...], w_ref[0])
    left = both[:, :HW_CHUNK] + bl_ref[row : row + 1, :]
    right = both[:, HW_CHUNK:] + br_ref[row : row + 1, :]
    left_ref[...] = left
    right_ref[...] = right
    gate = sigmoid(right)
    next_ref[...] = to_low(gate * as_float(part_ref[...]) + (1.0 - gate) * jnp.maximum(left, 0.0))


def highway_layer(row, x, w, vec):
    group = x.shape[0]
    steps = CONV // HW_CHUNK
    part = pl.BlockSpec((group, HW_CHUNK), lambda i: (0, i))
    return pl.pallas_call(
        functools.partial(highway_layer_kernel, row),
        grid=(steps,),
        out_shape=[
            jax.ShapeDtypeStruct((group, CONV), BF),
            jax.ShapeDtypeStruct((group, CONV), F32),
            jax.ShapeDtypeStruct((group, CONV), F32),
        ],
        in_specs=[
            pl.BlockSpec((group, CONV), lambda i: (0, 0)),
            part,
            pl.BlockSpec((1,) + HW_SHAPE[1:], lambda i: (i, 0, 0)),
            pl.BlockSpec((8, HW_CHUNK), lambda i: (0, i)),
            pl.BlockSpec((8, HW_CHUNK), lambda i: (0, i + steps)),
        ],
        out_specs=[part, part, part],
        compiler_params=pltpu.CompilerParams(vmem_limit_bytes=40 << 20),
    )(x, x, w, vec, vec)


def highway_forward(w0, w1, wp, vec, wide_in):
    x1, left0, right0 = highway_layer(0, wide_in, w0, vec)
    x2, left1, right1 = highway_layer(1, x1, w1, vec)
    projected = to_low(matmul(x2, wp) + vec[2, :D])
    return (projected, x1, x2, left0, right0, left1, right1)


def highway_back_kernel(last, up_ref, wp_ref, x_ref, left_ref, right_ref, w_ref, grad_ref, out_ref, total):
    i = pl.program_id(0)
    flowing = matmul_nt(up_ref[...], wp_ref[...]) if wp_ref is not None else up_ref[...]
    gate = sigmoid(right_ref[...])
    left = left_ref[...]
    nonlinear = jnp.maximum(left, 0.0)
    closed = flowing * (1.0 - gate)
    grad_left = to_low(jnp.where(left > 0.0, closed, 0.0))
    grad_right = to_low(closed * (as_float(x_ref[...]) - nonlinear) * gate)
    grad_ref[0] = grad_left
    grad_ref[1] = grad_right
    back = matmul_nt(jnp.concatenate([grad_left, grad_right], axis=1), w_ref[0])

    @pl.when(i == 0)
    def _():
        total[...] = back

    @pl.when(i > 0)
    def _():
        total[...] += back

    here = pl.ds(pl.multiple_of(i * HW_CHUNK, HW_CHUNK), HW_CHUNK)
    total[:, here] += flowing * gate

    @pl.when(i == pl.num_programs(0) - 1)
    def _():
        out_ref[...] = to_low(total[...]) if last else total[...]


def highway_back(last, up, wp, x, left, right, w):
    group = x.shape[0]
    steps = CONV // HW_CHUNK
    part = pl.BlockSpec((group, HW_CHUNK), lambda i: (0, i))
    if wp is None:
        kernel = lambda up_ref, *refs: highway_back_kernel(last, up_ref, None, *refs)
        sources, specs = [up], [part]
    else:
        kernel = functools.partial(highway_back_kernel, last)
        sources = [up, wp]
        specs = [pl.BlockSpec((group, D), lambda i: (0, 0)), pl.BlockSpec((HW_CHUNK, D), lambda i: (i, 0))]
    return pl.pallas_call(
        kernel,
        grid=(steps,),
        out_shape=[
            jax.ShapeDtypeStruct((2, group, CONV), BF),
            jax.ShapeDtypeStruct((group, CONV), BF if last else F32),
        ],
        in_specs=specs
        + [
            part,
            part,
            part,
            pl.BlockSpec((1,) + HW_SHAPE[1:], lambda i: (i, 0, 0)),
        ],
        out_specs=[
            pl.BlockSpec((2, group, HW_CHUNK), lambda i: (0, 0, i)),
            pl.BlockSpec((group, CONV), lambda i: (0, 0)),
        ],
        scratch_shapes=[pltpu.VMEM((group, CONV), F32)],
        compiler_params=pltpu.CompilerParams(vmem_limit_bytes=40 << 20),
    )(*sources, x, left, right, w)


def highway_backward(w0, w1, wp, wide_in, x1, left0, right0, left1, right1, upstream):
    grad1, flowing = highway_back(False, upstream, wp, x1, left1, right1, w1)
    grad0, grad_pooled = highway_back(True, flowing, None, wide_in, left0, right0, w0)
    return (grad_pooled, grad0, grad1)


def layer_norm(residual):
    centered = residual - jnp.mean(residual, axis=-1, keepdims=True)
    inverse = lax.rsqrt(jnp.mean(centered * centered, axis=-1, keepdims=True) + layer_eps)
    return centered * inverse, inverse


def norm_backward(upstream, scaled, inverse, gain):
    weighted = upstream * gain
    first_mean = jnp.mean(weighted, axis=-1, keepdims=True)
    cross_mean = jnp.mean(weighted * scaled, axis=-1, keepdims=True)
    return inverse * (weighted - first_mean - scaled * cross_mean)


def encoder_kernel(
    x_ref, cot_ref, wqkv_ref, wo_ref, wu_ref, wd_ref, vec_ref, vec3_ref,
    layer_ref, back_ref, joined_ref, mixed_ref, att_ref, normed_ref, act_ref, inner_ref, branch_ref, sums_ref,
    qkv, probs, slope, scaled, carry,
):
    rows = x_ref.shape[0]
    pairs = HEADS // 2
    scale = HEAD_DIM ** (-0.5)
    lane = lax.broadcasted_iota(jnp.int32, (1, LANES), 1)
    halves = [jnp.where(lane < HEAD_DIM, 1.0, 0.0).astype(BF), jnp.where(lane < HEAD_DIM, 0.0, 1.0).astype(BF)]

    def heads(body):
        def one(i, unused):
            sequence, pair = lax.div(i, pairs), lax.rem(i, pairs)
            body(
                pl.ds(pl.multiple_of(sequence * SEQ_LEN, SEQ_LEN), SEQ_LEN),
                [pl.ds(pl.multiple_of(pair * LANES + k * D, LANES), LANES) for k in range(3)],
                i,
            )
            return unused

        lax.fori_loop(0, rows // SEQ_LEN * pairs, one, 0)

    def pieces(width, body):
        def one(i, unused):
            body(pl.ds(pl.multiple_of(i * width, width), width))
            return unused

        return lambda count: lax.fori_loop(0, count, one, 0)

    @pl.when(lax.axis_index("section") >= 2)
    def _():
        for k, bias in enumerate((vec_ref[0:1, 0:D], None, vec_ref[1:2, 0:D])):
            part = matmul(x_ref[...], wqkv_ref[:, k * D : (k + 1) * D])
            qkv[:, k * D : (k + 1) * D] = to_low(part if bias is None else part + bias)

        def attend(here, columns, i):
            query, key, value = (qkv[here, columns[k]] for k in range(3))
            out = []
            for half in range(2):
                scores = matmul_nt(query * halves[half], key) * scale
                exponent = jnp.exp(scores - jnp.max(scores, axis=-1, keepdims=True))
                soft = exponent / jnp.sum(exponent, axis=-1, keepdims=True)
                probs[2 * i + half] = soft
                out.append(matmul(to_low(soft), value))
            mixed_ref[here, columns[0]] = to_low(jnp.where(lane < HEAD_DIM, out[0], out[1]))

        heads(attend)
        residual = as_float(x_ref[...]) + matmul(mixed_ref[...], wo_ref[...]) + vec_ref[2:3, 0:D]
        scaled1, inverse1 = layer_norm(residual)
        scaled[...] = scaled1
        normed_ref[...] = to_low(scaled1 * vec_ref[3:4, 0:D] + vec_ref[4:5, 0:D])

        def up(part):
            inner = matmul(normed_ref[...], wu_ref[:, part]) + vec3_ref[0:1, part]
            phi = 0.5 * (1.0 + lax.erf(inner * 0.7071067811865476))
            act_ref[:, part] = to_low(inner * phi)
            slope[:, part] = phi + inner * jnp.exp(-0.5 * inner * inner) * 0.3989422804014327

        pieces(512, up)(FF // 512)
        residual = as_float(normed_ref[...]) + matmul(act_ref[...], wd_ref[...]) + vec3_ref[1:2, 0:D]
        scaled2, inverse2 = layer_norm(residual)
        gain2 = vec3_ref[2:3, 0:D]
        layer_ref[...] = to_low(scaled2 * gain2 + vec3_ref[3:4, 0:D])
        upstream = as_float(cot_ref[...])
        sums_ref[2:3, :] = jnp.sum(upstream * scaled2, axis=0, keepdims=True)
        sums_ref[3:4, :] = jnp.sum(upstream, axis=0, keepdims=True)
        carry[...] = norm_backward(upstream, scaled2, inverse2, gain2)
        branch_ref[...] = to_low(carry[...])

        def down(part):
            inner_ref[:, part] = to_low(matmul_nt(branch_ref[...], wd_ref[part, :]) * slope[:, part])

        pieces(512, down)(FF // 512)
        upstream = as_float(to_low(carry[...] + matmul_nt(inner_ref[...], wu_ref[...])))
        sums_ref[0:1, :] = jnp.sum(upstream * scaled[...], axis=0, keepdims=True)
        sums_ref[1:2, :] = jnp.sum(upstream, axis=0, keepdims=True)
        carry[...] = norm_backward(upstream, scaled[...], inverse1, vec_ref[3:4, 0:D])
        att_ref[...] = to_low(carry[...])
        back_ref[...] = to_low(matmul_nt(att_ref[...], wo_ref[...]))

        def attend_back(here, columns, i):
            query, key, value = (qkv[here, columns[k]] for k in range(3))
            grad = back_ref[here, columns[0]]
            totals = [0.0, 0.0, 0.0]
            for half in range(2):
                grad_half = grad * halves[half]
                soft = probs[2 * i + half]
                grad_soft = matmul_nt(grad_half, value)
                flow = to_low(soft * (grad_soft - jnp.sum(grad_soft * soft, axis=-1, keepdims=True)))
                totals[0] += matmul(flow, key * halves[half])
                totals[1] += matmul_tn(flow, query * halves[half])
                totals[2] += matmul_tn(to_low(soft), grad_half)
            joined_ref[here, columns[0]] = to_low(totals[0] * scale)
            joined_ref[here, columns[1]] = to_low(totals[1] * scale)
            joined_ref[here, columns[2]] = to_low(totals[2])

        heads(attend_back)
        back_ref[...] = to_low(carry[...] + matmul_nt(joined_ref[...], wqkv_ref[...]))


def encoder(x, cot, wqkv, wo, wu, wd, vec, vec3):
    rows = x.shape[0]
    widths = [D, D, 3 * D, D, D, D, FF, FF, D]
    return pl.pallas_call(
        encoder_kernel,
        out_shape=[jax.ShapeDtypeStruct((rows, w), BF) for w in widths] + [jax.ShapeDtypeStruct((8, D), F32)],
        in_specs=[vmem()] * 8,
        out_specs=[vmem()] * 10,
        scratch_shapes=[
            pltpu.VMEM((rows, 3 * D), BF),
            pltpu.VMEM((rows // SEQ_LEN * HEADS, SEQ_LEN, SEQ_LEN), F32),
            pltpu.VMEM((rows, FF), F32),
            pltpu.VMEM((rows, D), F32),
            pltpu.VMEM((rows, D), F32),
        ],
        compiler_params=pltpu.CompilerParams(vmem_limit_bytes=56 << 20),
    )(x, cot, wqkv, wo, wu, wd, vec, vec3)


def side_rows_kernel(*refs):
    section = lax.axis_index("section")
    own, other, (out_hbm, flat, out_ref, *targets, sem) = refs[:9], refs[9:18], refs[18:]
    x_ref, mixed_ref, joined_ref, att_ref, normed_ref, act_ref, inner_ref, branch_ref, sums_ref = targets

    def fetch(*places):
        copies = []
        for i in places:
            rows = own[i].shape[0]
            for k, source in enumerate((own[i], other[i])):
                copies.append(pltpu.make_async_copy(source, targets[i].at[pl.ds(k * rows, rows)], sem.at[k, i]))
        for copy in copies:
            copy.start()
        for copy in copies:
            copy.wait()

    def product(left_ref, right_ref, row):
        count, width = left_ref.shape[1], right_ref.shape[1]
        parts = width // LANES
        for k in range(count // D):
            for c in range(0, width, 256):
                block = matmul_tn(left_ref[:, k * D : (k + 1) * D], right_ref[:, c : c + 256])
                for t in range(2):
                    flat[pl.ds(row + k * D * parts + c // LANES + t, D, stride=parts), :] = block[:, t * LANES : (t + 1) * LANES]
        return row + count * parts

    def line(row, values):
        for c in range(values.shape[1] // LANES):
            flat[row + c : row + c + 1, :] = values[:, c * LANES : (c + 1) * LANES]
        return row + values.shape[1] // LANES

    def summed(ref, first, last):
        return jnp.sum(as_float(ref[:, first:last]), axis=0, keepdims=True)

    def write(row):
        full = out_ref.shape[0]
        flat[row:full, :] = jnp.zeros((full - row, LANES), F32)
        out_ref[...] = to_low(flat[...])
        copy = pltpu.make_async_copy(out_ref, out_hbm, sem.at[0, 0])
        copy.start()
        copy.wait()

    @pl.when(section == 2)
    def _():
        fetch(0, 1, 2, 3, 8)
        row = product(x_ref, joined_ref, 0)
        row = line(row, summed(joined_ref, 0, D))
        row = line(row, summed(joined_ref, 2 * D, 3 * D))
        row = product(mixed_ref, att_ref, row)
        row = line(row, summed(att_ref, 0, D))
        row = line(row, sums_ref[0:1, :] + sums_ref[8:9, :])
        write(line(row, sums_ref[1:2, :] + sums_ref[9:10, :]))

    @pl.when(section == 3)
    def _():
        fetch(4, 5, 6, 7, 8)
        row = product(normed_ref, inner_ref, 0)
        row = line(row, summed(inner_ref, 0, FF))
        row = product(act_ref, branch_ref, row)
        row = line(row, summed(branch_ref, 0, D))
        row = line(row, sums_ref[2:3, :] + sums_ref[10:11, :])
        write(line(row, sums_ref[3:4, :] + sums_ref[11:12, :]))


def side_rows(own, other):
    size = (SIDE_SHARE + SIDE_ROWS * SIDE_CHUNKS, LANES)
    return pl.pallas_call(
        side_rows_kernel,
        out_shape=jax.ShapeDtypeStruct(size, BF),
        in_specs=[hbm()] * (2 * len(own)),
        out_specs=hbm(),
        scratch_shapes=[pltpu.VMEM(size, F32), pltpu.VMEM(size, BF)]
        + [pltpu.VMEM((2 * value.shape[0], value.shape[1]), value.dtype) for value in own]
        + [pltpu.SemaphoreType.DMA((2, len(own)))],
        compiler_params=pltpu.CompilerParams(vmem_limit_bytes=50 << 20),
    )(*own, *other)


def stack_kernel(x0_ref, x1_ref, x2_ref, xt_hbm, x2t_hbm, low, turned, sem):
    group = x0_ref.shape[0]

    @pl.when(lax.axis_index("section") == 1)
    def _():
        turned[CONV:STACK, :] = jnp.where(
            lax.broadcasted_iota(jnp.int32, (STACK - CONV, group), 0) == 0, 1.0, 0.0
        ).astype(BF)
        targets = (xt_hbm.at[pl.ds(0, STACK)], xt_hbm.at[pl.ds(STACK, STACK)], x2t_hbm)
        for source, target in zip((x0_ref, x1_ref, x2_ref), targets, strict=True):
            copy = pltpu.make_async_copy(source, low, sem)
            copy.start()
            copy.wait()
            for c in range(0, CONV, 512):
                turned[c : c + 512, :] = low[:, c : c + 512].T
            copy = pltpu.make_async_copy(turned, target, sem)
            copy.start()
            copy.wait()


def stack_highways(x0, x1, x2):
    group = x0.shape[0]
    return pl.pallas_call(
        stack_kernel,
        out_shape=[jax.ShapeDtypeStruct((2 * STACK, group), BF), jax.ShapeDtypeStruct((STACK, group), BF)],
        in_specs=[hbm()] * 3,
        out_specs=[hbm()] * 2,
        scratch_shapes=[
            pltpu.VMEM((group, CONV), BF),
            pltpu.VMEM((STACK, group), BF),
            pltpu.SemaphoreType.DMA,
        ],
        compiler_params=pltpu.CompilerParams(vmem_limit_bytes=24 << 20),
    )(x0, x1, x2)


SIDE_ROWS = 1200
SIDE_CHUNKS = 16
SIDE_REST = 1040
SIDE_SHARE = 17936


def side_part(
    share, row_ref, out_ref, own, y_in, z_in, z_out, total,
    y_send, y_recv, z_send, z_recv, l_send, l_recv, sem, turn,
):
    section = lax.axis_index("section")
    b = lax.axis_index("batch")
    y, z = lax.rem(b, 2), lax.div(b, 2)

    def count(half):
        return jnp.where((section == 2) & (half == 1), 1, SIDE_CHUNKS)

    def rows(half, i):
        return pl.ds(pl.multiple_of(half * share + i * SIDE_ROWS, 16), SIDE_ROWS)

    def y_copy(i):
        return pltpu.make_async_remote_copy(
            row_ref.at[rows(1 - y, i)], y_in.at[i], y_send.at[i], y_recv.at[i],
            device_id={"batch": b + 1 - 2 * y}, device_id_type=MESH,
        )

    def z_copy(i):
        return pltpu.make_async_remote_copy(
            z_out.at[i], z_in.at[i], z_send.at[i], z_recv.at[i],
            device_id={"batch": b - 2}, device_id_type=MESH,
        )

    def rest_copy():
        return pltpu.make_async_remote_copy(
            total.at[pl.ds(share, SIDE_REST)], total.at[pl.ds(0, SIDE_REST)], l_send, l_recv,
            device_id={"batch": 2}, device_id_type=MESH,
        )

    def write():
        copy = pltpu.make_async_copy(total.at[pl.ds(0, share)], out_ref, sem)
        copy.start()
        copy.wait()

    @pl.when(section != 1)
    def _():
        total[...] = jnp.zeros_like(total)

    @pl.when(section == 0)
    def _():
        write()

    @pl.when(section >= 2)
    def _():
        barrier = pltpu.get_barrier_semaphore()

        @pl.when(section == 3)
        def _():
            pl.semaphore_signal(barrier, inc=1, device_id={"section": 1}, device_id_type=MESH)

        pl.semaphore_signal(barrier, inc=1, device_id={"batch": b + 1 - 2 * y}, device_id_type=MESH)
        pairs = [(z > 0, b - 2), (z < Z - 1, b + 2), (b == 1, 2), (b == 2, 1)]
        for condition, other in pairs:

            @pl.when(condition)
            def _():
                pl.semaphore_signal(barrier, inc=1, device_id={"batch": other}, device_id_type=MESH)

        pl.semaphore_signal(barrier, inc=1, device_id={"section": 5 - section}, device_id_type=MESH)
        pl.semaphore_wait(barrier, 2 + sum(jnp.where(condition, 1, 0) for condition, _ in pairs))

        def send(i, carry):
            y_copy(i).start()
            return carry

        def combine(i, carry):
            copy = pltpu.make_async_copy(row_ref.at[rows(y, i)], own, sem)
            copy.start()
            copy.wait()
            y_copy(i).wait_recv()
            here = pl.ds(pl.multiple_of(i * SIDE_ROWS, 16), SIDE_ROWS)

            @pl.when(z == Z - 1)
            def _():
                z_out[i] = to_low(as_float(own[...]) + as_float(y_in[i]))

            @pl.when(z < Z - 1)
            def _():
                z_copy(i).wait_recv()

                @pl.when(z > 0)
                def _():
                    z_out[i] = to_low(as_float(own[...]) + as_float(y_in[i]) + as_float(z_in[i]))

                @pl.when(z == 0)
                def _():
                    total[here] = as_float(own[...]) + as_float(y_in[i]) + as_float(z_in[i])

            @pl.when(z > 0)
            def _():
                z_copy(i).start()

            return carry

        def drain(i, carry):
            y_copy(i).wait_send()
            return carry

        def drain_z(i, carry):
            z_copy(i).wait_send()
            return carry

        @pl.when(section == 2)
        def _():
            pl.semaphore_wait(turn, 1)

        lax.fori_loop(0, count(1 - y), send, 0)
        lax.fori_loop(0, count(y), combine, 0)

        @pl.when(section == 3)
        def _():
            pl.semaphore_signal(turn, inc=1, device_id={"section": 2}, device_id_type=MESH)

        @pl.when((section == 3) & (b == 1))
        def _():
            rest_copy().start()
            rest_copy().wait_send()

        @pl.when((section == 3) & (b == 2))
        def _():
            rest_copy().wait_recv()

        write()
        lax.fori_loop(0, count(1 - y), drain, 0)

        @pl.when(z > 0)
        def _():
            lax.fori_loop(0, count(y), drain_z, 0)


SLICE = 592
CHUNK = 256
N_CHUNK = 2 * CONV // CHUNK
N_FAR = 4
N_NEAR = N_CHUNK - N_FAR
STACK = CONV + 16
LAG = 3
SLOTS = 4
FRONT = 80
Z = 4


def reduce_kernel(
    share, xt_hbm, x2t_hbm, g0_hbm, g1_hbm, gp_hbm, row_ref, out_ref, land_ref, far_ref,
    xt_ref, x2t_ref, g_ref, gp_ref, load, tile, flat, y_out, y_in, z_out, z_in, x_out, ret,
    y_send, y_recv, z_send, z_recv, x_send, x_recv, r_send, r_recv, hello, sem, *side_scratch,
):
    own, side_y, side_z, side_out, *side_sems = side_scratch
    side_part(share, row_ref, out_ref, own, side_y, side_z, side_out, flat, *side_sems)
    section = lax.axis_index("section")
    b = lax.axis_index("batch")
    y, z = lax.rem(b, 2), lax.div(b, 2)
    def owner(step):
        o = lax.rem(step, Z)
        up = jnp.where(z == 0, 3 - o, jnp.where(o == 0, 3, jnp.where(o == 1, 0, jnp.where(o == 2, 2, 1))))
        down = jnp.where(z == 3, o, jnp.where(o == 0, 0, jnp.where(o == 1, 3, jnp.where(o == 2, 1, 2))))
        return jnp.where(z < 2, up, down)

    def product(part, j):
        column = pl.multiple_of(j * CHUNK, CHUNK)

        @pl.when((part != 3) & (part != 7))
        def _():
            row = pl.multiple_of((35 * part + jnp.where(part >= 4, 1, 0)) * 16, 16)
            col = pl.multiple_of(column + jnp.where(part >= 4, 2 * CONV, 0), CHUNK)
            tile[...] = matmul(xt_ref[pl.ds(row, SLICE), :], g_ref[:, pl.ds(col, CHUNK)])

        second = pl.ds(pl.multiple_of(column + 2 * CONV, CHUNK), CHUNK)

        @pl.when(part == 3)
        def _():
            tile[0:384, :] = matmul(xt_ref[1680:STACK, :], g_ref[:, pl.ds(column, CHUNK)])
            tile[384:SLICE, :] = matmul(xt_ref[STACK : STACK + SLICE - 384, :], g_ref[:, second])

        @pl.when(part == 7)
        def _():
            tile[0:192, :] = matmul(xt_ref[2 * STACK - 192 : 2 * STACK, :], g_ref[:, second])

            @pl.when(j < 15)
            def _():
                row = pl.multiple_of(lax.rem(j, 5) * 400, 16)
                col = pl.multiple_of(lax.div(j, 5) * 256, 256)
                tile[192:SLICE, :] = matmul(x2t_ref[pl.ds(row, 400), :], gp_ref[:, pl.ds(col, 256)])

            @pl.when(j == 15)
            def _():
                for p in range(3):
                    tile[192 + 64 * p : 256 + 64 * p, :] = matmul(
                        x2t_ref[2000:STACK, :], gp_ref[:, p * 256 : (p + 1) * 256]
                    )
                tile[384:SLICE, :] = jnp.zeros((SLICE - 384, CHUNK), F32)

    def y_copy(part, j, slot):
        place = part * N_NEAR + j
        return pltpu.make_async_remote_copy(
            y_out.at[slot], y_in.at[place], y_send.at[slot], y_recv.at[place],
            device_id={"batch": b + 1 - 2 * y}, device_id_type=MESH,
        )

    def z_copy(part, j, o, down):
        place = part * N_CHUNK + j
        side = 0 if down else 1
        return pltpu.make_async_remote_copy(
            z_out.at[o], land_ref.at[side, place], z_send.at[o], z_recv.at[side, place],
            device_id={"batch": b - 2 if down else b + 2}, device_id_type=MESH,
        )

    def y_relay(part, j, slot):
        place = part * N_NEAR + j
        return pltpu.make_async_remote_copy(
            far_ref.at[(2 * part + 1 - y) * N_FAR + j], y_in.at[place], y_send.at[slot], y_recv.at[place],
            device_id={"batch": b + 1 - 2 * y}, device_id_type=MESH,
        )

    def x_copy(part, j, slot):
        place = part * N_FAR + j
        return pltpu.make_async_remote_copy(
            x_out.at[slot], far_ref.at[place], x_send.at[slot], x_recv.at[place],
            device_id={"section": 3}, device_id_type=MESH,
        )

    def back_copy(j):
        return pltpu.make_async_remote_copy(
            z_out.at[Z - 1], ret.at[j], r_send, r_recv.at[j], device_id={"section": 1}, device_id_type=MESH
        )

    def send_y(step, relay):
        part, j, slot = owner(step), lax.div(step, Z), lax.rem(step, SLOTS)
        copy = (y_relay if relay else y_copy)(part, j, slot)
        if relay:
            x_copy(2 * part + 1 - y, j, 0).wait_recv()
        else:
            product(2 * part + 1 - y, j)

        @pl.when(step >= SLOTS)
        def _():
            copy.wait_send()

        if not relay:
            y_out[slot] = to_low(tile[...])
        copy.start()

    def send_x(step):
        part, j, slot = lax.rem(step, 2 * Z), lax.div(step, 2 * Z), lax.rem(step, SLOTS)
        product(part, N_NEAR + j)

        @pl.when(step >= SLOTS)
        def _():
            x_copy(part, j, slot).wait_send()

        x_out[slot] = to_low(tile[...])
        x_copy(part, j, slot).start()

    def arriving(side, place, buffer):
        pltpu.make_async_remote_copy(
            z_out.at[0], land_ref.at[side, place], z_send.at[0], z_recv.at[side, place],
            device_id={"batch": b}, device_id_type=MESH,
        ).wait_recv()
        pltpu.make_async_copy(land_ref.at[side, place], z_in.at[buffer], sem.at[buffer]).start()

    def arrived(side, place, buffer):
        pltpu.make_async_copy(land_ref.at[side, place], z_in.at[buffer], sem.at[buffer]).wait()
        tile[...] += as_float(z_in[buffer])

    def keep(j):
        base = FRONT - 16 * b + jnp.where(b >= 4, 32, 0) + j * (CHUNK // LANES)

        def rows(first, count, start, column, stride):
            flat[pl.ds(start, count, stride=stride), :] = tile[first : first + count, column : column + LANES]

        @pl.when((b != 3) & (b != 7))
        def _():
            for c in range(CHUNK // LANES):
                rows(0, SLICE, base + c, c * LANES, 32)

        @pl.when(b == 3)
        def _():
            for c in range(CHUNK // LANES):
                rows(0, 369, base + c, c * LANES, 32)
                rows(384, SLICE - 384, FRONT + 11760 + j * (CHUNK // LANES) + c, c * LANES, 32)

        @pl.when(b == 7)
        def _():
            for c in range(CHUNK // LANES):
                rows(0, 177, base + c, c * LANES, 32)

            @pl.when(j < 15)
            def _():
                start = FRONT + 5584 + lax.rem(j, 5) * (400 * 6) + lax.div(j, 5) * 2
                for c in range(2):
                    rows(192, 400, start + c, c * LANES, 6)

            @pl.when(j == 15)
            def _():
                for p in range(3):
                    for c in range(2):
                        rows(192 + 64 * p, 64, FRONT + 5584 + 2000 * 6 + 2 * p + c, c * LANES, 6)

    def combine(part, j, o, relay):
        place = part * N_CHUNK + j
        above = (part <= z) & (z < Z - 1)
        below = (part >= z) & (z > 0)

        @pl.when(above)
        def _():
            arriving(0, place, 0)

        @pl.when(below)
        def _():
            arriving(1, place, 1)

        if relay:
            x_copy(2 * part + y, j, 0).wait_recv()
            copy = pltpu.make_async_copy(far_ref.at[(2 * part + y) * N_FAR + j], z_in.at[2], sem.at[2])
            copy.start()
            copy.wait()
            tile[...] = as_float(z_in[2])
        else:
            product(2 * part + y, j)
        y_copy(part, j, 0).wait_recv()
        tile[...] += as_float(y_in[part * N_NEAR + j])

        @pl.when(above)
        def _():
            arrived(0, place, 0)

        @pl.when(below)
        def _():
            arrived(1, place, 1)

        @pl.when(part == z)
        def _():
            if relay:

                @pl.when(j == 0)
                def _():
                    pl.semaphore_wait(hello, 1)

                @pl.when(j > 0)
                def _():
                    back_copy(j - 1).wait_send()

                z_out[Z - 1] = to_low(tile[...])
                back_copy(j).start()
            else:
                keep(j)

        @pl.when(part != z)
        def _():
            @pl.when(j > 0)
            def _():
                z_copy(part, j, o, True).wait_send()

            z_out[o] = to_low(tile[...])

            @pl.when(part < z)
            def _():
                z_copy(part, j, o, True).start()

            @pl.when(part > z)
            def _():
                z_copy(part, j, o, False).start()

    def rounds(chunks, relay):
        steps = Z * chunks

        def step_body(step, carry):
            @pl.when(step < steps)
            def _():
                send_y(step, relay)

            if not relay:

                @pl.when(step < 2 * Z * N_FAR)
                def _():
                    send_x(step)

            late = step - LAG
            part, o = owner(jnp.maximum(late, 0)), lax.rem(jnp.maximum(late, 0), Z)
            hops = jnp.where(part < z, 3 - z, jnp.where(part > z, z, jnp.maximum(z, 3 - z)))
            j = lax.div(jnp.maximum(late, 0), Z) - hops

            @pl.when((late >= 0) & (j >= 0) & (j < chunks))
            def _():
                combine(part, j, o, relay)

            return carry

        lax.fori_loop(0, steps + LAG + (Z - 1) * Z, step_body, 0)
        for slot in range(SLOTS):
            (y_relay if relay else y_copy)(0, 0, slot).wait_send()
        for o in range(Z - 1):
            z_copy(0, 0, o, True).wait_send()

    @pl.when(section == 1)
    def _():
        loads = [
            pltpu.make_async_copy(source, target, load.at[i])
            for i, (source, target) in enumerate(
                [(xt_hbm, xt_ref), (x2t_hbm, x2t_ref), (gp_hbm, gp_ref)]
                + [
                    (source.at[half], g_ref.at[:, pl.ds((2 * layer + half) * CONV, CONV)])
                    for layer, source in enumerate((g0_hbm, g1_hbm))
                    for half in range(2)
                ]
            )
        ]
        for copy in loads:
            copy.start()
        barrier = pltpu.get_barrier_semaphore()
        pl.semaphore_signal(barrier, inc=1, device_id={"batch": b + 1 - 2 * y}, device_id_type=MESH)

        @pl.when(z > 0)
        def _():
            pl.semaphore_signal(barrier, inc=1, device_id={"batch": b - 2}, device_id_type=MESH)

        @pl.when(z < Z - 1)
        def _():
            pl.semaphore_signal(barrier, inc=1, device_id={"batch": b + 2}, device_id_type=MESH)

        pl.semaphore_wait(barrier, 2 + jnp.where(z > 0, 1, 0) + jnp.where(z < Z - 1, 1, 0))
        pl.semaphore_signal(hello, inc=1, device_id={"section": 3}, device_id_type=MESH)
        for copy in loads:
            copy.wait()
        rounds(N_NEAR, False)
        for slot in range(SLOTS):
            x_copy(0, 0, slot).wait_send()

        def back(j, carry):
            back_copy(j).wait_recv()
            tile[...] = as_float(ret[j])
            keep(N_NEAR + j)
            return carry

        lax.fori_loop(0, N_FAR, back, 0)
        copy = pltpu.make_async_copy(flat.at[pl.ds(FRONT, share)], out_ref, sem.at[0])
        copy.start()
        copy.wait()

    @pl.when(section == 3)
    def _():
        rounds(N_FAR, True)
        back_copy(N_FAR - 1).wait_send()


def reduce_all(xt, x2t, g0, g1, gp, row, share):
    chunk = (SLICE, CHUNK)
    side = (SIDE_ROWS, LANES)
    dma = pltpu.SemaphoreType.DMA
    places = Z * N_CHUNK
    return pl.pallas_call(
        functools.partial(reduce_kernel, share),
        out_shape=[
            jax.ShapeDtypeStruct((share, LANES), F32),
            jax.ShapeDtypeStruct((2, places) + chunk, BF),
            jax.ShapeDtypeStruct((2 * Z * N_FAR,) + chunk, BF),
        ],
        in_specs=[hbm()] * 6,
        out_specs=[hbm()] * 3,
        scratch_shapes=[
            pltpu.VMEM(xt.shape, BF),
            pltpu.VMEM(x2t.shape, BF),
            pltpu.VMEM((gp.shape[0], 4 * CONV), BF),
            pltpu.VMEM(gp.shape, BF),
            dma((7,)),
            pltpu.VMEM(chunk, F32),
            pltpu.VMEM((SIDE_CHUNKS * SIDE_ROWS, LANES), F32),
            pltpu.VMEM((SLOTS,) + chunk, BF),
            pltpu.VMEM((Z * N_NEAR,) + chunk, BF),
            pltpu.VMEM((Z,) + chunk, BF),
            pltpu.VMEM((3,) + chunk, BF),
            pltpu.VMEM((SLOTS,) + chunk, BF),
            pltpu.VMEM((N_FAR,) + chunk, BF),
            dma((SLOTS,)),
            dma((Z * N_NEAR,)),
            dma((Z - 1,)),
            dma((2, places)),
            dma((SLOTS,)),
            dma((2 * Z * N_FAR,)),
            dma,
            dma((N_FAR,)),
            pltpu.SemaphoreType.REGULAR,
            dma((3,)),
            pltpu.VMEM(side, BF),
            pltpu.VMEM((SIDE_CHUNKS,) + side, BF),
            pltpu.VMEM((SIDE_CHUNKS,) + side, BF),
            pltpu.VMEM((SIDE_CHUNKS,) + side, BF),
            dma((SIDE_CHUNKS,)),
            dma((SIDE_CHUNKS,)),
            dma((SIDE_CHUNKS,)),
            dma((SIDE_CHUNKS,)),
            dma,
            dma,
            dma,
            pltpu.SemaphoreType.REGULAR,
        ],
        compiler_params=pltpu.CompilerParams(
            collective_id=1, has_side_effects=True, vmem_limit_bytes=60 << 20
        ),
    )(xt, x2t, g0, g1, gp, row)


CNN_GRADS = (CONV // LANES) * LANES + TABLE_ROWS


def cnn_sum_kernel(in_ref, out_ref, low, y_in, z_in, send, recv):
    section = lax.axis_index("section")
    b = lax.axis_index("batch")
    y, z = lax.rem(b, 2), lax.div(b, 2)
    barrier = pltpu.get_barrier_semaphore()

    def along(target, other, i):
        return pltpu.make_async_remote_copy(
            low, target, send, recv.at[i], device_id={"batch": other}, device_id_type=MESH
        )

    @pl.when(section == 0)
    def _():
        pairs = [(y == 0, b + 1), (y == 1, b - 1), ((y == 0) & (z > 0), b - 2), ((y == 0) & (z < Z - 1), b + 2)]
        for condition, other in pairs:

            @pl.when(condition)
            def _():
                pl.semaphore_signal(barrier, inc=1, device_id={"batch": other}, device_id_type=MESH)

        pl.semaphore_wait(barrier, sum(jnp.where(condition, 1, 0) for condition, _ in pairs))
        out_ref[...] = in_ref[...]

        @pl.when(y == 1)
        def _():
            low[...] = to_low(out_ref[...])
            along(y_in, b - 1, 0).start()
            along(y_in, b - 1, 0).wait_send()

        @pl.when(y == 0)
        def _():
            along(y_in, b + 1, 0).wait_recv()
            out_ref[...] += as_float(y_in[...])

            @pl.when(z < Z - 1)
            def _():
                along(z_in, b + 2, 1).wait_recv()
                out_ref[...] += as_float(z_in[...])

            @pl.when(z > 0)
            def _():
                low[...] = to_low(out_ref[...])
                along(z_in, b - 2, 1).start()
                along(z_in, b - 2, 1).wait_send()


def cnn_sum(grads):
    low = pltpu.VMEM((CNN_GRADS, LANES), BF)
    dma = pltpu.SemaphoreType.DMA
    return pl.pallas_call(
        cnn_sum_kernel,
        out_shape=jax.ShapeDtypeStruct((CNN_GRADS, LANES), F32),
        in_specs=[vmem()],
        out_specs=vmem(),
        scratch_shapes=[
            low,
            low,
            low,
            dma,
            dma((2,)),
        ],
        compiler_params=pltpu.CompilerParams(
            collective_id=3, has_side_effects=True, vmem_limit_bytes=24 << 20
        ),
    )(grads)


PIECES = 19


def assemble_kernel(cnn_ref, total_ref, out_ref, buffer, fetch, store):
    section = lax.axis_index("section")
    rows = out_ref.shape[0] // PIECES

    def part(i):
        return pl.ds(i * rows, rows)

    for i in range(PIECES):
        pltpu.make_async_copy(total_ref.at[part(i)], buffer.at[part(i)], fetch.at[i]).start()
    for i in range(PIECES):
        pltpu.make_async_copy(total_ref.at[part(i)], buffer.at[part(i)], fetch.at[i]).wait()
        pltpu.make_async_copy(buffer.at[part(i)], out_ref.at[part(i)], store.at[i]).start()
    for i in range(PIECES):
        pltpu.make_async_copy(buffer.at[part(i)], out_ref.at[part(i)], store.at[i]).wait()

    @pl.when((section == 0) & (lax.axis_index("batch") == 0))
    def _():
        head = buffer.at[pl.ds(0, CNN_ROWS)]
        for copy in (
            pltpu.make_async_copy(cnn_ref, head, fetch.at[0]),
            pltpu.make_async_copy(head, out_ref.at[pl.ds(0, CNN_ROWS)], store.at[0]),
        ):
            copy.start()
            copy.wait()


def assemble(cnn, total):
    return pl.pallas_call(
        assemble_kernel,
        out_shape=jax.ShapeDtypeStruct(total.shape, F32),
        in_specs=[hbm()] * 2,
        out_specs=hbm(),
        scratch_shapes=[
            pltpu.VMEM(total.shape, F32),
            pltpu.SemaphoreType.DMA((PIECES,)),
            pltpu.SemaphoreType.DMA((PIECES,)),
        ],
        compiler_params=pltpu.CompilerParams(vmem_limit_bytes=60 << 20),
    )(cnn, total)


def on_section(numbers, function, *operands):
    shapes = jax.eval_shape(function, *operands)
    leaves, tree = jax.tree.flatten(shapes)

    def idle(*unused):
        return jax.tree.unflatten(
            tree,
            pl.pallas_call(
                lambda *refs: None,
                out_shape=[jax.ShapeDtypeStruct(s.shape, s.dtype) for s in leaves],
                out_specs=[hbm()] * len(leaves),
            )(),
        )

    section = lax.axis_index("section")
    here = sum(jnp.where(section == n, 1, 0) for n in numbers) > 0
    return lax.cond(here, function, idle, *operands)


def shards(char_ids, word_lengths, params, cotangent):
    section = lax.axis_index("section")
    n_batch = lax.axis_size("batch")
    words_all = lax.all_gather(
        jnp.concatenate([char_ids, word_lengths[:, None]], axis=1), "section", axis=0, tiled=True
    )
    params, words_all = lax.optimization_barrier((params, words_all))
    ck, tt = cnn_params(params)
    group = words_all.shape[0]
    quarter, words, half = group // 4, group // len(CNN), group // 2
    ids_all, column_all = words_all[:, :CHAR_LEN], words_all[:, CHAR_LEN:]
    row_all = column_all.T
    ends_all = stage_bounds(column_all, len(CNN))
    place = jnp.maximum(section - 1, 0)

    def mine(array, axis=0):
        return lax.dynamic_slice_in_dim(array, place * words, words, axis)

    pooled_part = on_section(
        CNN, chars_forward, ends_all[place], mine(ids_all), mine(column_all), mine(row_all, 1), ck, tt
    )
    pooled, cot, w0, w1, wp, vec = start_highways(params, pooled_part, cotangent)
    params, pooled = lax.optimization_barrier((params, pooled))
    encoder_weights = start_encoder(params)
    pooled, encoder_weights = lax.optimization_barrier((pooled, encoder_weights))
    projected, x1, x2, *kept = on_section((1,), highway_forward, w0, w1, wp, vec, pooled)
    (encoder_in,) = hand_over(
        6, [(1, 2, 0, 0, half, 0, 0), (1, 3, 0, half, half, 0, 0)], [projected], [((half, D), BF)]
    )
    x2, encoder_in = lax.optimization_barrier((x2, encoder_in))
    xt, x2t = stack_highways(pooled, x1, x2)
    encoder_in, xt = lax.optimization_barrier((encoder_in, xt))
    layer, back, joined, mixed, att, normed, activated, inner, branch, sums = on_section(
        (2, 3), encoder, encoder_in, cot, *encoder_weights
    )
    items = [(2, 1, 0, 0, half, 0, 0), (3, 1, 0, 0, half, 0, half)]
    items += [(2 + s // 2, s, 1, s % 2 * quarter, quarter, 1, 0) for s in range(4)]
    items += [(3 if k < 4 else 2, 2 if k < 4 else 3, 2 + k, 0, half, 2 + k, 0) for k in range(8)]
    items += [(2, 3, 10, 0, 8, 10, 0), (3, 2, 10, 0, 8, 10, 0)]
    own_rows = [encoder_in, mixed, joined, att, normed, activated, inner, branch, sums]
    grad_highway, layer_out, *other_rows = hand_over(
        7,
        items,
        [back, layer, *own_rows],
        [((group, D), BF), ((quarter, D), BF)] + [(value.shape, value.dtype) for value in own_rows],
    )
    grad_pooled, grad0, grad1 = on_section(
        (1,), highway_backward, w0, w1, wp, pooled, x1, *kept, grad_highway
    )
    (grad_part,) = hand_over(8, [(1, 0, 0, 0, group, 0, 0)], [grad_pooled], [((group, CONV), BF)])
    other_rows, grad_part = lax.optimization_barrier((other_rows, grad_part))
    side = side_rows(own_rows, other_rows)
    share = params.shape[1] // n_batch // LANES
    by_kernels = n_batch == 2 * Z and share == SIDE_SHARE
    if by_kernels:
        total, *_ = reduce_all(xt, x2t, grad0, grad1, grad_highway, side, share)
        grad_part, total = lax.optimization_barrier((grad_part, total))
    cnn_part = on_section((0,), chars_backward, ends_all, ids_all, column_all, row_all, ck, tt, grad_part)
    if not by_kernels:
        return (layer_out, summed_rows(params.shape[1], cnn_part, pooled, x1, x2, grad0, grad1, grad_highway, side))
    cnn_total = cnn_sum(cnn_part)

    def first_row(grads):
        flat = cnn_gradient(grads)
        return jnp.pad(flat, (0, CNN_ROWS * LANES - flat.shape[0])).reshape(-1, LANES)

    cnn_row = on_section((0,), first_row, cnn_total)
    total = assemble(cnn_row, total)
    return (layer_out, total.reshape(1, -1))


def summed_rows(size, cnn_part, pooled, x1, x2, grad0, grad1, grad_highway, side):
    first = lax.axis_index("batch") == 0
    cnn_flat = cnn_gradient(lax.psum(jnp.where(lax.axis_index("section") == 0, cnn_part, 0.0), ("section", "batch")))

    def wide(flat):
        return jnp.pad(as_float(flat), (0, size - flat.shape[0]))

    def highways():
        ones = jnp.ones((1, pooled.shape[0]), BF)
        pieces = []
        both = [jnp.concatenate([grad[0], grad[1]], axis=1) for grad in (grad0, grad1)]
        for x, g in ((pooled, both[0]), (x1, both[1]), (x2, grad_highway)):
            pieces += [matmul_tn(x, g).reshape(-1), matmul(ones, g).reshape(-1)]
        return wide(jnp.concatenate(pieces))

    row = lax.switch(
        lax.axis_index("section"),
        [
            lambda: wide(jnp.where(first, cnn_flat, 0.0)),
            highways,
            lambda: wide(side.reshape(-1)),
            lambda: wide(side.reshape(-1)),
        ],
    )
    return lax.psum_scatter(row, "batch", scatter_dimension=0, tiled=True).reshape(1, -1)


def solution(mesh):
    return jax.shard_map(
        shards,
        mesh=mesh,
        in_specs=(
            P(("section", "batch"), None),
            P(("section", "batch")),
            P("section", None),
            P(("section", "batch"), None),
        ),
        out_specs=(P(("section", "batch"), None), P("section", "batch")),
        check_vma=False,
    )
```

```python
import functools
import math

import jax
import jax.numpy as jnp
from jax import lax
from jax.experimental import pallas as pl
from jax.experimental.pallas import tpu as pltpu
from jax.sharding import PartitionSpec as P

D = 768
HEADS = 12
HEAD_DIM = 64
FF = 3072
CHAR_DIM = 16
CHARS = 262
CHAR_LEN = 50
CH_UNIT = 32
SEQ_LEN = 192
CONV = 64 * CH_UNIT
LANES = 128
MESH = pl.DeviceIdType.MESH
BF = jnp.bfloat16
F32 = jnp.float32
HUGE = 1e30
CNN = (0, 2, 3)

HW_CHUNK = 512
HW_SHAPE = (CONV // HW_CHUNK, CONV, 2 * HW_CHUNK)
channel_steps = (1, 1, 2, 4, 8, 16, 32)
layer_eps = 1e-12

HW_BIAS0 = CONV * 2 * CONV
HW_W1 = HW_BIAS0 + 2 * CONV
HW_BIAS1 = HW_W1 + CONV * 2 * CONV
PROJ_W = HW_BIAS1 + 2 * CONV
PROJ_B = PROJ_W + CONV * D
Q_BIAS = D * 3 * D
V_BIAS = Q_BIAS + D
OUT_W = V_BIAS + D
OUT_B = OUT_W + D * D
UP_B = D * FF
DOWN_W = UP_B + FF
DOWN_B = DOWN_W + FF * D
TABLE = CHARS * CHAR_DIM
CNN_FLAT = TABLE + sum((n + 1) * CHAR_DIM * c * CH_UNIT for n, c in enumerate(channel_steps)) + CONV


def hbm():
    return pl.BlockSpec(memory_space=pltpu.HBM)


def vmem():
    return pl.BlockSpec(memory_space=pltpu.VMEM)


def as_float(array_in):
    return array_in.astype(F32)


def to_low(array_in):
    return array_in.astype(BF)


def matmul(left_in, right_in):
    return jnp.dot(left_in, right_in, preferred_element_type=F32)


def matmul_tn(left_in, right_in):
    return lax.dot_general(left_in, right_in, (((0,), (0,)), ((), ())), preferred_element_type=F32)


def matmul_nt(left_in, right_in):
    return lax.dot_general(left_in, right_in, (((1,), (1,)), ((), ())), preferred_element_type=F32)


class Transfers:
    def __init__(self, items):
        self.items = items

    def copy(self, i, operands, outputs, send, recv):
        source, target, operand, first, rows, output, there = self.items[i]
        from_ref = operands[operand].at[pl.ds(first, rows)]
        to_ref = outputs[output].at[pl.ds(there, rows)]
        if source == target:
            return pltpu.make_async_copy(from_ref, to_ref, send.at[i])
        return pltpu.make_async_remote_copy(
            from_ref, to_ref, send.at[i], recv.at[i], device_id={"section": target}, device_id_type=MESH
        )

    def partners(self, s):
        pairs = {(item[0], item[1]) for item in self.items if item[0] != item[1]}
        return sorted({b for a, b in pairs if a == s} | {a for a, b in pairs if b == s})

    def run(self, operands, outputs, send, recv, work=None):
        section = lax.axis_index("section")
        for s in range(4):
            mine = [i for i, item in enumerate(self.items) if s in item[:2]]
            work_here = (work or {}).get(s)
            if not mine and work_here is None:
                continue

            @pl.when(section == s)
            def _(s=s, mine=mine, work_here=work_here):
                partners = self.partners(s)
                barrier = pltpu.get_barrier_semaphore()
                for other in partners:
                    pl.semaphore_signal(barrier, inc=1, device_id={"section": other}, device_id_type=MESH)
                if work_here is not None:
                    work_here()
                if partners:
                    pl.semaphore_wait(barrier, len(partners))
                outgoing = [i for i in mine if self.items[i][0] == s]
                for i in outgoing:
                    self.copy(i, operands, outputs, send, recv).start()
                for i in mine:
                    copy = self.copy(i, operands, outputs, send, recv)
                    if self.items[i][0] == self.items[i][1]:
                        copy.wait()
                    elif i in outgoing:
                        copy.wait_send()
                    else:
                        copy.wait_recv()


def hand_over(collective_id, items, operands, out_shapes):
    transfers = Transfers(items)

    def kernel(*refs):
        n, m = len(operands), len(out_shapes)
        transfers.run(refs[:n], refs[n : n + m], *refs[n + m :])

    return pl.pallas_call(
        kernel,
        out_shape=[jax.ShapeDtypeStruct(*shape) for shape in out_shapes],
        in_specs=[hbm()] * len(operands),
        out_specs=[hbm()] * len(out_shapes),
        scratch_shapes=[pltpu.SemaphoreType.DMA((len(items),))] * 2,
        compiler_params=pltpu.CompilerParams(collective_id=collective_id, has_side_effects=True),
    )(*operands)


def cut_tools(p_ref, raw, sems):
    def matrix(offset, target, rows):
        count, columns = target.shape

        def body(in_ref, out_ref):
            out_ref[...] = in_ref[...].reshape(rows, columns)

        pltpu.emit_pipeline(
            body,
            grid=(count // rows,),
            in_specs=[pl.BlockSpec((1, rows * columns), lambda i: (0, i))],
            out_specs=[pl.BlockSpec((rows, columns), lambda i: (i, 0))],
        )(p_ref.at[:, pl.ds(offset, count * columns)], target)

    def vectors(entries, vec):
        copies = []
        for row, (offset, size) in enumerate(entries):
            copy = pltpu.make_async_copy(
                p_ref.at[:, pl.ds(offset, size)], raw.at[row, :, pl.ds(0, size)], sems.at[row]
            )
            copy.start()
            copies.append(copy)
        for copy in copies:
            copy.wait()
        for row, (offset, size) in enumerate(entries):
            vec[row : row + 1, 0:size] = as_float(raw[row, :, 0:size])

    def chunks(offset, target, rows):
        parts = 4
        count = rows // parts

        def body(*refs):
            out_ref = refs[-1]
            for k, in_ref in enumerate(refs[:-1]):
                value = in_ref[...].reshape(count, 2 * CONV)
                for c in range(CONV // HW_CHUNK):
                    for half in range(2):
                        start = half * CONV + c * HW_CHUNK
                        out_ref[c, k * count : (k + 1) * count, half * HW_CHUNK : (half + 1) * HW_CHUNK] = value[
                            :, start : start + HW_CHUNK
                        ]

        pltpu.emit_pipeline(
            body,
            grid=(CONV // rows,),
            in_specs=[
                pl.BlockSpec(
                    (1, count * 2 * CONV), lambda i, k=k: (0, i * parts + k), pipeline_mode=pl.Buffered(3)
                )
                for k in range(parts)
            ],
            out_specs=[pl.BlockSpec((CONV // HW_CHUNK, rows, 2 * HW_CHUNK), lambda i: (0, i, 0))],
        )(*([p_ref.at[:, pl.ds(offset, CONV * 2 * CONV)]] * parts), target)

    return matrix, vectors, chunks


def vector_store(vec, target, sem):
    copy = pltpu.make_async_copy(vec, target, sem)
    copy.start()
    copy.wait()


def start_highways(params, pooled_part, cotangent):
    words, quarter = pooled_part.shape[0], cotangent.shape[0]
    items = [(s, 1, 0, 0, words, 0, i * words) for i, s in enumerate(CNN)]
    items += [(s, 2 + s // 2, 1, 0, quarter, 1, s % 2 * quarter) for s in range(4)]
    transfers = Transfers(items)

    def kernel(pooled_ref, cot_ref, p_ref, pooled, cot, w0, w1, wp, vec_ref, vec, raw, sems, send, recv):
        matrix, vectors, chunks = cut_tools(p_ref, raw, sems)

        def work():
            vectors([(HW_BIAS0, 2 * CONV), (HW_BIAS1, 2 * CONV), (PROJ_B, D)], vec)
            vector_store(vec, vec_ref, sems.at[0])
            chunks(0, w0, 256)
            chunks(HW_W1, w1, 256)
            matrix(PROJ_W, wp, 512)

        transfers.run((pooled_ref, cot_ref), (pooled, cot), send, recv, {1: work})

    shapes = [(words * len(CNN), CONV), (2 * quarter, D), HW_SHAPE, HW_SHAPE, (CONV, D)]
    return pl.pallas_call(
        kernel,
        out_shape=[jax.ShapeDtypeStruct(s, BF) for s in shapes] + [jax.ShapeDtypeStruct((8, 2 * CONV), F32)],
        in_specs=[hbm()] * 3,
        out_specs=[hbm()] * 6,
        scratch_shapes=[
            pltpu.VMEM((8, 2 * CONV), F32),
            pltpu.VMEM((5, 1, 2 * CONV), BF),
            pltpu.SemaphoreType.DMA((5,)),
            pltpu.SemaphoreType.DMA((len(items),)),
            pltpu.SemaphoreType.DMA((len(items),)),
        ],
        compiler_params=pltpu.CompilerParams(
            collective_id=4, has_side_effects=True, vmem_limit_bytes=40 << 20
        ),
    )(pooled_part, cotangent, params)


def start_encoder(params):
    shapes = [(D, 3 * D), (D, D), (D, FF), (FF, D)]
    owners = (2, 2, 3, 3)
    items = [(s, 5 - s, i, 0, shape[0], i, 0) for i, (s, shape) in enumerate(zip(owners, shapes, strict=True))]
    items += [(2, 3, 4, 0, 8, 4, 0), (3, 2, 5, 0, 8, 5, 0)]
    transfers = Transfers(items)

    def kernel(p_ref, wqkv, wo, wu, wd, vec2, vec3, vec, raw, sems, send, recv):
        matrix, vectors, _ = cut_tools(p_ref, raw, sems)

        def work2():
            vectors([(Q_BIAS, D), (V_BIAS, D), (OUT_B, D), (OUT_B + D, D), (OUT_B + 2 * D, D)], vec)
            vector_store(vec, vec2, sems.at[0])
            matrix(0, wqkv, 256)
            matrix(OUT_W, wo, 384)

        def work3():
            vectors([(UP_B, FF), (DOWN_B, D), (DOWN_B + D, D), (DOWN_B + 2 * D, D)], vec)
            vector_store(vec, vec3, sems.at[0])
            matrix(0, wu, 256)
            matrix(DOWN_W, wd, 512)

        outputs = (wqkv, wo, wu, wd, vec2, vec3)
        transfers.run(outputs, outputs, send, recv, {2: work2, 3: work3})

    return pl.pallas_call(
        kernel,
        out_shape=[jax.ShapeDtypeStruct(s, BF) for s in shapes] + [jax.ShapeDtypeStruct((8, 2 * CONV), F32)] * 2,
        in_specs=[hbm()],
        out_specs=[hbm()] * 6,
        scratch_shapes=[
            pltpu.VMEM((8, 2 * CONV), F32),
            pltpu.VMEM((5, 1, 2 * CONV), BF),
            pltpu.SemaphoreType.DMA((5,)),
            pltpu.SemaphoreType.DMA((len(items),)),
            pltpu.SemaphoreType.DMA((len(items),)),
        ],
        compiler_params=pltpu.CompilerParams(
            collective_id=5, has_side_effects=True, vmem_limit_bytes=40 << 20
        ),
    )(params)


CNN_ROWS = 1600
TABLE_ROWS = 384


def cnn_params_kernel(p_ref, ck_ref, tt_ref, raw, flat, kernel, table, sem, send, recv):
    section = lax.axis_index("section")
    others = [s for s in CNN if s]
    lane = lax.broadcasted_iota(jnp.int32, (1, LANES), 1)
    barrier = pltpu.get_barrier_semaphore()

    @pl.when(section == 0)
    def _():
        copy = pltpu.make_async_copy(p_ref.at[:, pl.ds(0, CNN_ROWS * LANES)], raw, sem)
        copy.start()
        for s in others:
            pl.semaphore_signal(barrier, inc=1, device_id={"section": s}, device_id_type=MESH)
        copy.wait()
        flat[...] = as_float(raw[...]).reshape(CNN_ROWS, LANES)
        table[...] = jnp.zeros_like(table)
        head = flat[0:40, :]
        for b in range(8):
            mixed = jnp.zeros_like(head)
            for g in range(7):
                rolled = head if g == b else pltpu.roll(head, (g - b) * CHAR_DIM % LANES, 1)
                mixed = jnp.where((lane >= g * CHAR_DIM) & (lane < (g + 1) * CHAR_DIM), rolled, mixed)
            table[pl.ds(b, 33, stride=8), :] = mixed[0:33]
        tt_ref[...] = to_low(table[...])
        rolled = pltpu.roll(flat[...], 32, 1)
        flat[...] = rolled
        count = CNN_ROWS - 40
        flat[0:count, :] = jnp.where(
            lane < 32, flat[32 : 32 + count, :], flat[33 : 33 + count, :]
        )
        kernel[...] = jnp.zeros_like(kernel)
        first, second, third = flat[0:8, :], flat[4:12, :], flat[12:36, :]
        narrow = lax.broadcasted_iota(jnp.int32, (8, LANES), 0) < 4
        for b in range(4):
            one = first if b == 0 else pltpu.roll(first, -b * 32 % LANES, 1)
            two = second if b == 1 else pltpu.roll(second, (32 - b * 32) % LANES, 1)
            kernel[0, pl.ds(b, 8, stride=4), :] = jnp.where(
                lane < 32, jnp.where(narrow, one, 0.0), jnp.where(lane < 64, two, 0.0)
            )
        for b in range(2):
            three = third if b == 1 else pltpu.roll(third, 64, 1)
            kernel[0, pl.ds(b, 24, stride=2), :] = jnp.where(
                lane >= 64, three, kernel[0, pl.ds(b, 24, stride=2), :]
            )
        row, tile = 36, 1
        for number in range(3, 7):
            parts = channel_steps[number] * CH_UNIT // LANES
            depth = (number + 1) * CHAR_DIM
            for c in range(parts):
                kernel[tile, 0:depth, :] = flat[pl.ds(row + c, depth, stride=parts), :]
                tile += 1
            row += depth * parts
        bound = 0
        for number in range(7):
            upper = bound + channel_steps[number] * CH_UNIT
            for c in range(bound // LANES, -(-upper // LANES)):
                kernel[c, 112 + number : 113 + number, :] = jnp.where(
                    (lane + c * LANES >= bound) & (lane + c * LANES < upper), -HUGE, 0.0
                )
            bound = upper
        for c in range(CONV // LANES):
            kernel[c, 119:120, :] = flat[row + c : row + c + 1, :]
            ck_ref[:, c * LANES : (c + 1) * LANES] = to_low(kernel[c])
        pl.semaphore_wait(barrier, len(others))
        copies = []
        for i, s in enumerate(others):
            for j, ref in enumerate((ck_ref, tt_ref)):
                copies.append(
                    pltpu.make_async_remote_copy(
                        ref, ref, send.at[i, j], recv.at[j], device_id={"section": s}, device_id_type=MESH
                    )
                )
        for copy in copies:
            copy.start()
        for copy in copies:
            copy.wait_send()

    for s in others:

        @pl.when(section == s)
        def _():
            pl.semaphore_signal(barrier, inc=1, device_id={"section": 0}, device_id_type=MESH)
            pl.semaphore_wait(barrier, 1)
            for j, ref in enumerate((ck_ref, tt_ref)):
                pltpu.make_async_remote_copy(
                    ref, ref, send.at[0, j], recv.at[j], device_id={"section": 0}, device_id_type=MESH
                ).wait_recv()


def cnn_params(params):
    return pl.pallas_call(
        cnn_params_kernel,
        out_shape=[
            jax.ShapeDtypeStruct((LANES, CONV), BF),
            jax.ShapeDtypeStruct((TABLE_ROWS, LANES), BF),
        ],
        in_specs=[hbm()],
        out_specs=[vmem(), vmem()],
        scratch_shapes=[
            pltpu.VMEM((1, CNN_ROWS * LANES), BF),
            pltpu.VMEM((CNN_ROWS, LANES), F32),
            pltpu.VMEM((CONV // LANES, LANES, LANES), F32),
            pltpu.VMEM((TABLE_ROWS, LANES), F32),
            pltpu.SemaphoreType.DMA,
            pltpu.SemaphoreType.DMA((len(CNN) - 1, 2)),
            pltpu.SemaphoreType.DMA((2,)),
        ],
        compiler_params=pltpu.CompilerParams(
            collective_id=0, has_side_effects=True, vmem_limit_bytes=24 << 20
        ),
    )(params)


STAGES = ((128, 1), (64, 2), (16, 8))
SPOTS = CHAR_LEN + 14


def stage_bounds(lengths, blocks):
    words = lengths.shape[0] // blocks
    counts = jnp.sum(lengths.reshape(blocks, words, 1) > jnp.arange(CHAR_LEN, dtype=jnp.int32), axis=1)
    limits = jnp.array([[words // 2], [words // 8], [0]], jnp.int32)
    return jnp.sum(counts[:, None, :] > limits, axis=2).astype(jnp.int32)


def sorting(column_ref, row_ref):
    count = row_ref.shape[1]
    down = lax.broadcasted_iota(jnp.int32, (count, count), 0)
    across = lax.broadcasted_iota(jnp.int32, (count, count), 1)
    column, row = column_ref[...], row_ref[...]
    before = (column > row) | ((column == row) & (down < across))
    rank = jnp.sum(jnp.where(before, 1, 0), axis=0, keepdims=True)
    return jnp.where(down == rank, 1.0, 0.0).astype(BF)


def sorted_words(order, ids_ref, column_ref):
    ids = ids_ref[...]
    high = lax.div(ids, 16)
    low = ids - 16 * high
    ids = matmul(order, to_low(as_float(high))) * 16.0 + matmul(order, to_low(as_float(low)))
    length = matmul(order, to_low(as_float(jnp.broadcast_to(column_ref[...], (ids.shape[0], LANES)))))
    return ids, length


def stages(ends_ref, body):
    start = 0
    for k, (words, positions) in enumerate(STAGES):
        end = ends_ref[k]

        def one(i, unused, words=words, positions=positions, start=start, end=end):
            body(start + i * positions, words, positions, end)
            return unused

        lax.fori_loop(0, lax.div(jnp.maximum(end - start, 0) + positions - 1, positions), one, 0)
        start = end


def one_hot(first, words, positions, ids):
    lane = lax.broadcasted_iota(jnp.int32, (words, CHAR_LEN), 1)
    columns = [
        jnp.sum(jnp.where(lane == first + q, ids[0:words, :], 0.0), axis=1, keepdims=True) for q in range(positions)
    ]
    column = columns[0] if positions == 1 else jnp.concatenate(columns, axis=0)
    symbol = lax.broadcasted_iota(jnp.int32, (words * positions, TABLE_ROWS), 1)
    return jnp.where(column.astype(jnp.int32) == symbol, 1.0, 0.0).astype(BF)


def windows(first, words, positions, end, length, embedded, masks):
    total = None
    for j in range(7):
        term = embedded[pl.ds(first + j, positions), 0:words, :] * masks[j]
        total = term if total is None else total + term
    shape = (positions, words, LANES)
    lane = lax.broadcasted_iota(jnp.int32, shape, 2)
    position = first + lax.broadcasted_iota(jnp.int32, shape, 0)
    room = jnp.broadcast_to(length[0:words, :][None], shape)
    out = (lane >= 112) & (lane < 119) & ((as_float(position + lane - 111) > room) | (position >= end))
    return (total + jnp.where(out | (lane == 119), 1.0, 0.0).astype(BF)).reshape(positions * words, LANES)


def lane_masks():
    lane = lax.broadcasted_iota(jnp.int32, (1, 1, LANES), 2)
    return [
        jnp.where((lane >= j * CHAR_DIM) & (lane < (j + 1) * CHAR_DIM), 1.0, 0.0).astype(BF)
        for j in range(7)
    ]


def embedder(ids, tt_ref, embedded):
    def embed(first, words, positions, end):
        value = to_low(matmul(one_hot(first, words, positions, ids), tt_ref[...]))
        embedded[pl.ds(first, positions), 0:words, :] = value.reshape(positions, words, LANES)

    return embed


def chars_forward_kernel(ends_ref, ids_ref, column_ref, row_ref, ck_ref, tt_ref, out_ref, embedded, best):
    embedded[...] = jnp.zeros_like(embedded)
    best[...] = jnp.full_like(best, -HUGE)
    masks = lane_masks()
    order = sorting(column_ref, row_ref)
    ids, length = sorted_words(order, ids_ref, column_ref)
    stages(ends_ref, embedder(ids, tt_ref, embedded))

    def pool(first, words, positions, end):
        rows = windows(first, words, positions, end, length, embedded, masks)
        for c in range(0, CONV, 512):
            pre = jnp.max(matmul(rows, ck_ref[:, c : c + 512]).reshape(positions, words, 512), axis=0)
            best[0:words, c : c + 512] = jnp.maximum(best[0:words, c : c + 512], pre)

    stages(ends_ref, pool)
    out_ref[...] = to_low(matmul_tn(order, to_low(jnp.maximum(best[...], 0.0))))


def chars_backward_kernel(
    all_ends_ref, ids_ref, column_ref, row_ref, ck_ref, tt_ref, grad_ref,
    out_ref, embedded, best, share, backs, sums,
):
    block = pl.program_id(0)
    ends_ref = [all_ends_ref[block, k] for k in range(len(STAGES))]
    embedded[...] = jnp.zeros_like(embedded)
    backs[...] = jnp.zeros_like(backs)
    best[...] = jnp.full_like(best, -HUGE)
    share[...] = jnp.zeros_like(share)
    table_rows = pl.ds(CONV, TABLE_ROWS)

    @pl.when(block == 0)
    def _():
        sums[...] = jnp.zeros_like(sums)
        out_ref[table_rows, :] = jnp.zeros((TABLE_ROWS, LANES), F32)

    masks = lane_masks()
    order = sorting(column_ref, row_ref)
    ids, length = sorted_words(order, ids_ref, column_ref)
    stages(ends_ref, embedder(ids, tt_ref, embedded))

    def count(first, words, positions, end):
        rows = windows(first, words, positions, end, length, embedded, masks)
        for c in range(0, CONV, 512):
            part = slice(c, c + 512)
            pre = matmul(rows, ck_ref[:, part])
            top, hits = best[0:words, part], share[0:words, part]
            for q in range(positions):
                here = pre[q * words : (q + 1) * words]
                hits = jnp.where(here > top, 1.0, hits + jnp.where(here == top, 1.0, 0.0))
                top = jnp.maximum(top, here)
            best[0:words, part], share[0:words, part] = top, hits

    stages(ends_ref, count)
    share[...] = matmul(order, grad_ref[...]) / share[...]
    best[...] = jnp.where(best[...] > 0.0, best[...], 3e38)

    def spread(first, words, positions, end):
        rows = windows(first, words, positions, end, length, embedded, masks)
        back = jnp.zeros((words * positions, LANES), F32)
        for c in range(0, CONV, 512):
            part = slice(c, c + 512)
            pre = matmul(rows, ck_ref[:, part]).reshape(positions, words, 512)
            hit = pre == best[0:words, part][None]
            grad = to_low(jnp.where(hit, jnp.broadcast_to(share[0:words, part][None], pre.shape), 0.0))
            grad = grad.reshape(positions * words, 512)
            sums[:, part] += matmul_tn(rows, grad)
            back = back + matmul_nt(grad, ck_ref[:, part])
        backs[pl.ds(first + 6, positions), 0:words, :] = to_low(back).reshape(positions, words, LANES)

    stages(ends_ref, spread)

    def gather(first, words, positions, end):
        shape = (positions, words, LANES)
        lane = lax.broadcasted_iota(jnp.int32, shape, 2)
        position = first + lax.broadcasted_iota(jnp.int32, shape, 0)
        total = jnp.zeros(shape, F32)
        for j in range(7):
            here = (lane >= j * CHAR_DIM) & (lane < (j + 1) * CHAR_DIM) & (position < end)
            total = jnp.where(here, as_float(backs[pl.ds(first + 6 - j, positions), 0:words, :]), total)
        hot = one_hot(first, words, positions, ids)
        out_ref[table_rows, :] += matmul_tn(hot, to_low(total).reshape(positions * words, LANES))

    stages(ends_ref, gather)

    @pl.when(block == pl.num_programs(0) - 1)
    def _():
        for c in range(CONV // LANES):
            out_ref[c * LANES : (c + 1) * LANES, :] = sums[:, c * LANES : (c + 1) * LANES]


def chars_forward(ends, ids, column, row, ck, tt):
    words = ids.shape[0]
    return pl.pallas_call(
        chars_forward_kernel,
        out_shape=jax.ShapeDtypeStruct((words, CONV), BF),
        in_specs=[pl.BlockSpec(memory_space=pltpu.SMEM)] + [vmem()] * 5,
        out_specs=vmem(),
        scratch_shapes=[
            pltpu.VMEM((SPOTS, words, LANES), BF),
            pltpu.VMEM((words, CONV), F32),
        ],
        compiler_params=pltpu.CompilerParams(vmem_limit_bytes=32 << 20),
    )(ends, ids, column, row, ck, tt)


def chars_backward(ends, ids, column, row, ck, tt, grad):
    words = ids.shape[0] // len(CNN)
    return pl.pallas_call(
        chars_backward_kernel,
        grid=(len(CNN),),
        out_shape=jax.ShapeDtypeStruct((CNN_GRADS, LANES), F32),
        in_specs=[
            pl.BlockSpec(memory_space=pltpu.SMEM),
            pl.BlockSpec((words, CHAR_LEN), lambda i: (i, 0)),
            pl.BlockSpec((words, 1), lambda i: (i, 0)),
            pl.BlockSpec((1, words), lambda i: (0, i)),
            pl.BlockSpec((LANES, CONV), lambda i: (0, 0)),
            pl.BlockSpec((TABLE_ROWS, LANES), lambda i: (0, 0)),
            pl.BlockSpec((words, CONV), lambda i: (i, 0)),
        ],
        out_specs=pl.BlockSpec((CNN_GRADS, LANES), lambda i: (0, 0)),
        scratch_shapes=[
            pltpu.VMEM((SPOTS, words, LANES), BF),
            pltpu.VMEM((words, CONV), F32),
            pltpu.VMEM((words, CONV), F32),
            pltpu.VMEM((SPOTS, words, LANES), BF),
            pltpu.VMEM((LANES, CONV), F32),
        ],
        compiler_params=pltpu.CompilerParams(vmem_limit_bytes=40 << 20),
    )(ends, ids, column, row, ck, tt, grad)


def cnn_gradient(grads):
    table_grad = grads[CONV:]
    kernel_grad = jnp.swapaxes(grads[:CONV].reshape(-1, LANES, LANES), 0, 1).reshape(LANES, CONV)
    pieces = [
        sum(table_grad[:CHARS, g * CHAR_DIM : (g + 1) * CHAR_DIM] for g in range(7)).reshape(-1)
    ]
    offset = 0
    for number in range(7):
        channels = channel_steps[number] * CH_UNIT
        pieces.append(
            kernel_grad[: (number + 1) * CHAR_DIM, offset : offset + channels].reshape(-1)
        )
        offset += channels
    pieces.append(kernel_grad[119])
    return jnp.concatenate(pieces)


def sigmoid(value):
    return 1.0 / (1.0 + jnp.exp(-value))


def highway_layer_kernel(row, x_ref, part_ref, w_ref, bl_ref, br_ref, next_ref, left_ref, right_ref):
    both = matmul(x_ref[...], w_ref[0])
    left = both[:, :HW_CHUNK] + bl_ref[row : row + 1, :]
    right = both[:, HW_CHUNK:] + br_ref[row : row + 1, :]
    left_ref[...] = left
    right_ref[...] = right
    gate = sigmoid(right)
    next_ref[...] = to_low(gate * as_float(part_ref[...]) + (1.0 - gate) * jnp.maximum(left, 0.0))


def highway_layer(row, x, w, vec):
    group = x.shape[0]
    steps = CONV // HW_CHUNK
    part = pl.BlockSpec((group, HW_CHUNK), lambda i: (0, i))
    return pl.pallas_call(
        functools.partial(highway_layer_kernel, row),
        grid=(steps,),
        out_shape=[
            jax.ShapeDtypeStruct((group, CONV), BF),
            jax.ShapeDtypeStruct((group, CONV), F32),
            jax.ShapeDtypeStruct((group, CONV), F32),
        ],
        in_specs=[
            pl.BlockSpec((group, CONV), lambda i: (0, 0)),
            part,
            pl.BlockSpec((1,) + HW_SHAPE[1:], lambda i: (i, 0, 0)),
            pl.BlockSpec((8, HW_CHUNK), lambda i: (0, i)),
            pl.BlockSpec((8, HW_CHUNK), lambda i: (0, i + steps)),
        ],
        out_specs=[part, part, part],
        compiler_params=pltpu.CompilerParams(vmem_limit_bytes=40 << 20),
    )(x, x, w, vec, vec)


def highway_forward(w0, w1, wp, vec, wide_in):
    x1, left0, right0 = highway_layer(0, wide_in, w0, vec)
    x2, left1, right1 = highway_layer(1, x1, w1, vec)
    projected = to_low(matmul(x2, wp) + vec[2, :D])
    return (projected, x1, x2, left0, right0, left1, right1)


def highway_back_kernel(last, up_ref, wp_ref, x_ref, left_ref, right_ref, w_ref, grad_ref, out_ref, total):
    i = pl.program_id(0)
    flowing = matmul_nt(up_ref[...], wp_ref[...]) if wp_ref is not None else up_ref[...]
    gate = sigmoid(right_ref[...])
    left = left_ref[...]
    nonlinear = jnp.maximum(left, 0.0)
    closed = flowing * (1.0 - gate)
    grad_left = to_low(jnp.where(left > 0.0, closed, 0.0))
    grad_right = to_low(closed * (as_float(x_ref[...]) - nonlinear) * gate)
    grad_ref[0] = grad_left
    grad_ref[1] = grad_right
    back = matmul_nt(jnp.concatenate([grad_left, grad_right], axis=1), w_ref[0])

    @pl.when(i == 0)
    def _():
        total[...] = back

    @pl.when(i > 0)
    def _():
        total[...] += back

    here = pl.ds(pl.multiple_of(i * HW_CHUNK, HW_CHUNK), HW_CHUNK)
    total[:, here] += flowing * gate

    @pl.when(i == pl.num_programs(0) - 1)
    def _():
        out_ref[...] = to_low(total[...]) if last else total[...]


def highway_back(last, up, wp, x, left, right, w):
    group = x.shape[0]
    steps = CONV // HW_CHUNK
    part = pl.BlockSpec((group, HW_CHUNK), lambda i: (0, i))
    if wp is None:
        kernel = lambda up_ref, *refs: highway_back_kernel(last, up_ref, None, *refs)
        sources, specs = [up], [part]
    else:
        kernel = functools.partial(highway_back_kernel, last)
        sources = [up, wp]
        specs = [pl.BlockSpec((group, D), lambda i: (0, 0)), pl.BlockSpec((HW_CHUNK, D), lambda i: (i, 0))]
    return pl.pallas_call(
        kernel,
        grid=(steps,),
        out_shape=[
            jax.ShapeDtypeStruct((2, group, CONV), BF),
            jax.ShapeDtypeStruct((group, CONV), BF if last else F32),
        ],
        in_specs=specs
        + [
            part,
            part,
            part,
            pl.BlockSpec((1,) + HW_SHAPE[1:], lambda i: (i, 0, 0)),
        ],
        out_specs=[
            pl.BlockSpec((2, group, HW_CHUNK), lambda i: (0, 0, i)),
            pl.BlockSpec((group, CONV), lambda i: (0, 0)),
        ],
        scratch_shapes=[pltpu.VMEM((group, CONV), F32)],
        compiler_params=pltpu.CompilerParams(vmem_limit_bytes=40 << 20),
    )(*sources, x, left, right, w)


def highway_backward(w0, w1, wp, wide_in, x1, left0, right0, left1, right1, upstream):
    grad1, flowing = highway_back(False, upstream, wp, x1, left1, right1, w1)
    grad0, grad_pooled = highway_back(True, flowing, None, wide_in, left0, right0, w0)
    return (grad_pooled, grad0, grad1)


def layer_norm(residual):
    centered = residual - jnp.mean(residual, axis=-1, keepdims=True)
    inverse = lax.rsqrt(jnp.mean(centered * centered, axis=-1, keepdims=True) + layer_eps)
    return centered * inverse, inverse


def norm_backward(upstream, scaled, inverse, gain):
    weighted = upstream * gain
    first_mean = jnp.mean(weighted, axis=-1, keepdims=True)
    cross_mean = jnp.mean(weighted * scaled, axis=-1, keepdims=True)
    return inverse * (weighted - first_mean - scaled * cross_mean)


def encoder_kernel(
    x_ref, cot_ref, wqkv_ref, wo_ref, wu_ref, wd_ref, vec_ref, vec3_ref,
    layer_ref, back_ref, joined_ref, mixed_ref, att_ref, normed_ref, act_ref, inner_ref, branch_ref, sums_ref,
    qkv, probs, slope, scaled, carry,
):
    rows = x_ref.shape[0]
    pairs = HEADS // 2
    scale = HEAD_DIM ** (-0.5)
    lane = lax.broadcasted_iota(jnp.int32, (1, LANES), 1)
    halves = [jnp.where(lane < HEAD_DIM, 1.0, 0.0).astype(BF), jnp.where(lane < HEAD_DIM, 0.0, 1.0).astype(BF)]

    def heads(body):
        def one(i, unused):
            sequence, pair = lax.div(i, pairs), lax.rem(i, pairs)
            body(
                pl.ds(pl.multiple_of(sequence * SEQ_LEN, SEQ_LEN), SEQ_LEN),
                [pl.ds(pl.multiple_of(pair * LANES + k * D, LANES), LANES) for k in range(3)],
                i,
            )
            return unused

        lax.fori_loop(0, rows // SEQ_LEN * pairs, one, 0, unroll=True)

    def pieces(width, body):
        def one(i, unused):
            body(pl.ds(pl.multiple_of(i * width, width), width))
            return unused

        return lambda count: lax.fori_loop(0, count, one, 0, unroll=True)

    @pl.when(lax.axis_index("section") >= 2)
    def _():
        for k, bias in enumerate((vec_ref[0:1, 0:D], None, vec_ref[1:2, 0:D])):
            part = matmul(x_ref[...], wqkv_ref[:, k * D : (k + 1) * D])
            qkv[:, k * D : (k + 1) * D] = to_low(part if bias is None else part + bias)

        def attend(here, columns, i):
            query, key, value = (qkv[here, columns[k]] for k in range(3))
            out = []
            for half in range(2):
                scores = matmul_nt(query * halves[half], key) * scale
                exponent = jnp.exp(scores - jnp.max(scores, axis=-1, keepdims=True))
                soft = exponent / jnp.sum(exponent, axis=-1, keepdims=True)
                probs[2 * i + half] = soft
                out.append(matmul(to_low(soft), value))
            mixed_ref[here, columns[0]] = to_low(jnp.where(lane < HEAD_DIM, out[0], out[1]))

        heads(attend)
        residual = as_float(x_ref[...]) + matmul(mixed_ref[...], wo_ref[...]) + vec_ref[2:3, 0:D]
        scaled1, inverse1 = layer_norm(residual)
        scaled[...] = scaled1
        normed_ref[...] = to_low(scaled1 * vec_ref[3:4, 0:D] + vec_ref[4:5, 0:D])

        def up(part):
            inner = matmul(normed_ref[...], wu_ref[:, part]) + vec3_ref[0:1, part]
            phi = 0.5 * (1.0 + lax.erf(inner * 0.7071067811865476))
            act_ref[:, part] = to_low(inner * phi)
            slope[:, part] = phi + inner * jnp.exp(-0.5 * inner * inner) * 0.3989422804014327

        pieces(512, up)(FF // 512)
        residual = as_float(normed_ref[...]) + matmul(act_ref[...], wd_ref[...]) + vec3_ref[1:2, 0:D]
        scaled2, inverse2 = layer_norm(residual)
        gain2 = vec3_ref[2:3, 0:D]
        layer_ref[...] = to_low(scaled2 * gain2 + vec3_ref[3:4, 0:D])
        upstream = as_float(cot_ref[...])
        sums_ref[2:3, :] = jnp.sum(upstream * scaled2, axis=0, keepdims=True)
        sums_ref[3:4, :] = jnp.sum(upstream, axis=0, keepdims=True)
        carry[...] = norm_backward(upstream, scaled2, inverse2, gain2)
        branch_ref[...] = to_low(carry[...])

        def down(part):
            inner_ref[:, part] = to_low(matmul_nt(branch_ref[...], wd_ref[part, :]) * slope[:, part])

        pieces(512, down)(FF // 512)
        upstream = as_float(to_low(carry[...] + matmul_nt(inner_ref[...], wu_ref[...])))
        sums_ref[0:1, :] = jnp.sum(upstream * scaled[...], axis=0, keepdims=True)
        sums_ref[1:2, :] = jnp.sum(upstream, axis=0, keepdims=True)
        carry[...] = norm_backward(upstream, scaled[...], inverse1, vec_ref[3:4, 0:D])
        att_ref[...] = to_low(carry[...])
        back_ref[...] = to_low(matmul_nt(att_ref[...], wo_ref[...]))

        def attend_back(here, columns, i):
            query, key, value = (qkv[here, columns[k]] for k in range(3))
            grad = back_ref[here, columns[0]]
            totals = [0.0, 0.0, 0.0]
            for half in range(2):
                grad_half = grad * halves[half]
                soft = probs[2 * i + half]
                grad_soft = matmul_nt(grad_half, value)
                flow = to_low(soft * (grad_soft - jnp.sum(grad_soft * soft, axis=-1, keepdims=True)))
                totals[0] += matmul(flow, key * halves[half])
                totals[1] += matmul_tn(flow, query * halves[half])
                totals[2] += matmul_tn(to_low(soft), grad_half)
            joined_ref[here, columns[0]] = to_low(totals[0] * scale)
            joined_ref[here, columns[1]] = to_low(totals[1] * scale)
            joined_ref[here, columns[2]] = to_low(totals[2])

        heads(attend_back)
        back_ref[...] = to_low(carry[...] + matmul_nt(joined_ref[...], wqkv_ref[...]))


def encoder(x, cot, wqkv, wo, wu, wd, vec, vec3):
    rows = x.shape[0]
    widths = [D, D, 3 * D, D, D, D, FF, FF, D]
    return pl.pallas_call(
        encoder_kernel,
        out_shape=[jax.ShapeDtypeStruct((rows, w), BF) for w in widths] + [jax.ShapeDtypeStruct((8, D), F32)],
        in_specs=[vmem()] * 8,
        out_specs=[vmem()] * 10,
        scratch_shapes=[
            pltpu.VMEM((rows, 3 * D), BF),
            pltpu.VMEM((rows // SEQ_LEN * HEADS, SEQ_LEN, SEQ_LEN), F32),
            pltpu.VMEM((rows, FF), F32),
            pltpu.VMEM((rows, D), F32),
            pltpu.VMEM((rows, D), F32),
        ],
        compiler_params=pltpu.CompilerParams(vmem_limit_bytes=56 << 20),
    )(x, cot, wqkv, wo, wu, wd, vec, vec3)


def side_rows_kernel(*refs):
    section = lax.axis_index("section")
    own, other, (out_hbm, flat, out_ref, *targets, sem) = refs[:9], refs[9:18], refs[18:]
    x_ref, mixed_ref, joined_ref, att_ref, normed_ref, act_ref, inner_ref, branch_ref, sums_ref = targets

    def fetch(*places):
        copies = []
        for i in places:
            rows = own[i].shape[0]
            for k, source in enumerate((own[i], other[i])):
                copies.append(pltpu.make_async_copy(source, targets[i].at[pl.ds(k * rows, rows)], sem.at[k, i]))
        for copy in copies:
            copy.start()
        for copy in copies:
            copy.wait()

    def product(left_ref, right_ref, row):
        count, width = left_ref.shape[1], right_ref.shape[1]
        parts = width // LANES
        for k in range(count // D):
            for c in range(0, width, 256):
                block = matmul_tn(left_ref[:, k * D : (k + 1) * D], right_ref[:, c : c + 256])
                for t in range(2):
                    flat[pl.ds(row + k * D * parts + c // LANES + t, D, stride=parts), :] = block[:, t * LANES : (t + 1) * LANES]
        return row + count * parts

    def line(row, values):
        for c in range(values.shape[1] // LANES):
            flat[row + c : row + c + 1, :] = values[:, c * LANES : (c + 1) * LANES]
        return row + values.shape[1] // LANES

    def summed(ref, first, last):
        return jnp.sum(as_float(ref[:, first:last]), axis=0, keepdims=True)

    def write(row):
        full = out_ref.shape[0]
        flat[row:full, :] = jnp.zeros((full - row, LANES), F32)
        out_ref[...] = to_low(flat[...])
        copy = pltpu.make_async_copy(out_ref, out_hbm, sem.at[0, 0])
        copy.start()
        copy.wait()

    @pl.when(section == 2)
    def _():
        fetch(0, 1, 2, 3, 8)
        row = product(x_ref, joined_ref, 0)
        row = line(row, summed(joined_ref, 0, D))
        row = line(row, summed(joined_ref, 2 * D, 3 * D))
        row = product(mixed_ref, att_ref, row)
        row = line(row, summed(att_ref, 0, D))
        row = line(row, sums_ref[0:1, :] + sums_ref[8:9, :])
        write(line(row, sums_ref[1:2, :] + sums_ref[9:10, :]))

    @pl.when(section == 3)
    def _():
        fetch(4, 5, 6, 7, 8)
        row = product(normed_ref, inner_ref, 0)
        row = line(row, summed(inner_ref, 0, FF))
        row = product(act_ref, branch_ref, row)
        row = line(row, summed(branch_ref, 0, D))
        row = line(row, sums_ref[2:3, :] + sums_ref[10:11, :])
        write(line(row, sums_ref[3:4, :] + sums_ref[11:12, :]))


def side_rows(own, other):
    size = (SIDE_SHARE + SIDE_ROWS * SIDE_CHUNKS, LANES)
    return pl.pallas_call(
        side_rows_kernel,
        out_shape=jax.ShapeDtypeStruct(size, BF),
        in_specs=[hbm()] * (2 * len(own)),
        out_specs=hbm(),
        scratch_shapes=[pltpu.VMEM(size, F32), pltpu.VMEM(size, BF)]
        + [pltpu.VMEM((2 * value.shape[0], value.shape[1]), value.dtype) for value in own]
        + [pltpu.SemaphoreType.DMA((2, len(own)))],
        compiler_params=pltpu.CompilerParams(vmem_limit_bytes=50 << 20),
    )(*own, *other)


def stack_kernel(x0_ref, x1_ref, x2_ref, xt_hbm, x2t_hbm, low, turned, sem):
    group = x0_ref.shape[0]

    @pl.when(lax.axis_index("section") == 1)
    def _():
        turned[CONV:STACK, :] = jnp.where(
            lax.broadcasted_iota(jnp.int32, (STACK - CONV, group), 0) == 0, 1.0, 0.0
        ).astype(BF)
        targets = (xt_hbm.at[pl.ds(0, STACK)], xt_hbm.at[pl.ds(STACK, STACK)], x2t_hbm)
        for source, target in zip((x0_ref, x1_ref, x2_ref), targets, strict=True):
            copy = pltpu.make_async_copy(source, low, sem)
            copy.start()
            copy.wait()
            for c in range(0, CONV, 512):
                turned[c : c + 512, :] = low[:, c : c + 512].T
            copy = pltpu.make_async_copy(turned, target, sem)
            copy.start()
            copy.wait()


def stack_highways(x0, x1, x2):
    group = x0.shape[0]
    return pl.pallas_call(
        stack_kernel,
        out_shape=[jax.ShapeDtypeStruct((2 * STACK, group), BF), jax.ShapeDtypeStruct((STACK, group), BF)],
        in_specs=[hbm()] * 3,
        out_specs=[hbm()] * 2,
        scratch_shapes=[
            pltpu.VMEM((group, CONV), BF),
            pltpu.VMEM((STACK, group), BF),
            pltpu.SemaphoreType.DMA,
        ],
        compiler_params=pltpu.CompilerParams(vmem_limit_bytes=24 << 20),
    )(x0, x1, x2)


SIDE_ROWS = 1200
SIDE_CHUNKS = 16
SIDE_REST = 1040
SIDE_SHARE = 17936


def side_part(
    share, row_ref, out_ref, own, y_in, z_in, z_out, total,
    y_send, y_recv, z_send, z_recv, l_send, l_recv, sem, turn,
):
    section = lax.axis_index("section")
    b = lax.axis_index("batch")
    y, z = lax.rem(b, 2), lax.div(b, 2)

    def count(half):
        return jnp.where((section == 2) & (half == 1), 1, SIDE_CHUNKS)

    def rows(half, i):
        return pl.ds(pl.multiple_of(half * share + i * SIDE_ROWS, 16), SIDE_ROWS)

    def y_copy(i):
        return pltpu.make_async_remote_copy(
            row_ref.at[rows(1 - y, i)], y_in.at[i], y_send.at[i], y_recv.at[i],
            device_id={"batch": b + 1 - 2 * y}, device_id_type=MESH,
        )

    def z_copy(i):
        return pltpu.make_async_remote_copy(
            z_out.at[i], z_in.at[i], z_send.at[i], z_recv.at[i],
            device_id={"batch": b - 2}, device_id_type=MESH,
        )

    def rest_copy():
        return pltpu.make_async_remote_copy(
            total.at[pl.ds(share, SIDE_REST)], total.at[pl.ds(0, SIDE_REST)], l_send, l_recv,
            device_id={"batch": 2}, device_id_type=MESH,
        )

    def write():
        copy = pltpu.make_async_copy(total.at[pl.ds(0, share)], out_ref, sem)
        copy.start()
        copy.wait()

    @pl.when(section != 1)
    def _():
        total[...] = jnp.zeros_like(total)

    @pl.when(section == 0)
    def _():
        write()

    @pl.when(section >= 2)
    def _():
        barrier = pltpu.get_barrier_semaphore()

        @pl.when(section == 3)
        def _():
            pl.semaphore_signal(barrier, inc=1, device_id={"section": 1}, device_id_type=MESH)

        pl.semaphore_signal(barrier, inc=1, device_id={"batch": b + 1 - 2 * y}, device_id_type=MESH)
        pairs = [(z > 0, b - 2), (z < Z - 1, b + 2), (b == 1, 2), (b == 2, 1)]
        for condition, other in pairs:

            @pl.when(condition)
            def _():
                pl.semaphore_signal(barrier, inc=1, device_id={"batch": other}, device_id_type=MESH)

        pl.semaphore_signal(barrier, inc=1, device_id={"section": 5 - section}, device_id_type=MESH)
        pl.semaphore_wait(barrier, 2 + sum(jnp.where(condition, 1, 0) for condition, _ in pairs))

        def send(i, carry):
            y_copy(i).start()
            return carry

        def combine(i, carry):
            copy = pltpu.make_async_copy(row_ref.at[rows(y, i)], own, sem)
            copy.start()
            copy.wait()
            y_copy(i).wait_recv()
            here = pl.ds(pl.multiple_of(i * SIDE_ROWS, 16), SIDE_ROWS)

            @pl.when(z == Z - 1)
            def _():
                z_out[i] = to_low(as_float(own[...]) + as_float(y_in[i]))

            @pl.when(z < Z - 1)
            def _():
                z_copy(i).wait_recv()

                @pl.when(z > 0)
                def _():
                    z_out[i] = to_low(as_float(own[...]) + as_float(y_in[i]) + as_float(z_in[i]))

                @pl.when(z == 0)
                def _():
                    total[here] = as_float(own[...]) + as_float(y_in[i]) + as_float(z_in[i])

            @pl.when(z > 0)
            def _():
                z_copy(i).start()

            return carry

        def drain(i, carry):
            y_copy(i).wait_send()
            return carry

        def drain_z(i, carry):
            z_copy(i).wait_send()
            return carry

        @pl.when(section == 2)
        def _():
            pl.semaphore_wait(turn, 1)

        lax.fori_loop(0, count(1 - y), send, 0)
        lax.fori_loop(0, count(y), combine, 0)

        @pl.when(section == 3)
        def _():
            pl.semaphore_signal(turn, inc=1, device_id={"section": 2}, device_id_type=MESH)

        @pl.when((section == 3) & (b == 1))
        def _():
            rest_copy().start()
            rest_copy().wait_send()

        @pl.when((section == 3) & (b == 2))
        def _():
            rest_copy().wait_recv()

        write()
        lax.fori_loop(0, count(1 - y), drain, 0)

        @pl.when(z > 0)
        def _():
            lax.fori_loop(0, count(y), drain_z, 0)


SLICE = 592
CHUNK = 256
N_CHUNK = 2 * CONV // CHUNK
N_FAR = 3
N_NEAR = N_CHUNK - N_FAR
N_TURN = 2
TURN_EVERY = 2
N_FIRST = N_NEAR - N_TURN
STACK = CONV + 16
LAG = 3
SLOTS = 4
FRONT = 80
Z = 4


def reduce_kernel(
    share, xt_hbm, x2t_hbm, g0_hbm, g1_hbm, gp_hbm, row_ref, out_ref, land_ref, far_ref,
    xt_ref, x2t_ref, g_ref, gp_ref, load, tile, flat, y_out, y_in, z_out, z_in, x_out, ret, t_out, t_in, t_send, t_recv,
    y_send, y_recv, z_send, z_recv, x_send, x_recv, r_send, r_recv, hello, sem, *side_scratch,
):
    own, side_y, side_z, side_out, *side_sems = side_scratch
    side_part(share, row_ref, out_ref, own, side_y, side_z, side_out, flat, *side_sems)
    section = lax.axis_index("section")
    b = lax.axis_index("batch")
    y, z = lax.rem(b, 2), lax.div(b, 2)
    def owner(step):
        o = lax.rem(step, Z)
        up = jnp.where(z == 0, 3 - o, jnp.where(o == 0, 3, jnp.where(o == 1, 0, jnp.where(o == 2, 2, 1))))
        down = jnp.where(z == 3, o, jnp.where(o == 0, 0, jnp.where(o == 1, 3, jnp.where(o == 2, 1, 2))))
        return jnp.where(z < 2, up, down)

    def product(part, j):
        column = pl.multiple_of(j * CHUNK, CHUNK)

        @pl.when((part != 3) & (part != 7))
        def _():
            row = pl.multiple_of((35 * part + jnp.where(part >= 4, 1, 0)) * 16, 16)
            col = pl.multiple_of(column + jnp.where(part >= 4, 2 * CONV, 0), CHUNK)
            tile[...] = matmul(xt_ref[pl.ds(row, SLICE), :], g_ref[:, pl.ds(col, CHUNK)])

        second = pl.ds(pl.multiple_of(column + 2 * CONV, CHUNK), CHUNK)

        @pl.when(part == 3)
        def _():
            tile[0:384, :] = matmul(xt_ref[1680:STACK, :], g_ref[:, pl.ds(column, CHUNK)])
            tile[384:SLICE, :] = matmul(xt_ref[STACK : STACK + SLICE - 384, :], g_ref[:, second])

        @pl.when(part == 7)
        def _():
            tile[0:192, :] = matmul(xt_ref[2 * STACK - 192 : 2 * STACK, :], g_ref[:, second])

            @pl.when(j < 15)
            def _():
                row = pl.multiple_of(lax.rem(j, 5) * 400, 16)
                col = pl.multiple_of(lax.div(j, 5) * 256, 256)
                tile[192:SLICE, :] = matmul(x2t_ref[pl.ds(row, 400), :], gp_ref[:, pl.ds(col, 256)])

            @pl.when(j == 15)
            def _():
                for p in range(3):
                    tile[192 + 64 * p : 256 + 64 * p, :] = matmul(
                        x2t_ref[2000:STACK, :], gp_ref[:, p * 256 : (p + 1) * 256]
                    )
                tile[384:SLICE, :] = jnp.zeros((SLICE - 384, CHUNK), F32)

    def y_copy(part, j, slot):
        place = part * N_NEAR + j
        return pltpu.make_async_remote_copy(
            y_out.at[slot], y_in.at[place], y_send.at[slot], y_recv.at[place],
            device_id={"batch": b + 1 - 2 * y}, device_id_type=MESH,
        )

    def z_copy(part, j, o, down):
        place = part * N_CHUNK + j
        side = 0 if down else 1
        return pltpu.make_async_remote_copy(
            z_out.at[o], land_ref.at[side, place], z_send.at[o], z_recv.at[side, place],
            device_id={"batch": b - 2 if down else b + 2}, device_id_type=MESH,
        )

    def y_relay(part, j, slot):
        place = part * N_NEAR + j
        return pltpu.make_async_remote_copy(
            far_ref.at[(2 * part + 1 - y) * N_FAR + j], y_in.at[place], y_send.at[slot], y_recv.at[place],
            device_id={"batch": b + 1 - 2 * y}, device_id_type=MESH,
        )

    def x_copy(part, j, slot):
        place = part * N_FAR + j
        return pltpu.make_async_remote_copy(
            x_out.at[slot], far_ref.at[place], x_send.at[slot], x_recv.at[place],
            device_id={"section": 3}, device_id_type=MESH,
        )

    def back_copy(j):
        return pltpu.make_async_remote_copy(
            z_out.at[Z - 1], ret.at[j], r_send, r_recv.at[j], device_id={"section": 1}, device_id_type=MESH
        )

    def turn_copy(i):
        return pltpu.make_async_remote_copy(
            t_out.at[i], t_in.at[i], t_send.at[i], t_recv.at[i],
            device_id={"batch": b + 1 - 2 * y}, device_id_type=MESH,
        )

    def combine_turned(part, p, o):
        i, mine = lax.div(p, 2), lax.rem(p, 2)
        j = N_FIRST + p
        place = part * N_CHUNK + j
        above = (part <= z) & (z < Z - 1)
        below = (part >= z) & (z > 0)

        @pl.when(above)
        def _():
            arriving(0, place, 0)

        @pl.when(below)
        def _():
            arriving(1, place, 1)

        product(2 * part + jnp.where(mine == 1, y, 1 - y), N_FIRST + i)

        @pl.when(above)
        def _():
            arrived(0, place, 0)

        @pl.when(below)
        def _():
            arrived(1, place, 1)

        @pl.when((part == z) & (mine == 0))
        def _():
            t_out[i] = to_low(tile[...])
            turn_copy(i).start()

        @pl.when((part == z) & (mine == 1))
        def _():
            turn_copy(i).wait_recv()
            tile[...] += as_float(t_in[i])
            keep(N_FIRST + i)

        @pl.when(part != z)
        def _():
            @pl.when(p > 0)
            def _():
                z_copy(part, j, Z + o, True).wait_send()

            z_out[Z + o] = to_low(tile[...])

            @pl.when(part < z)
            def _():
                z_copy(part, j, Z + o, True).start()

            @pl.when(part > z)
            def _():
                z_copy(part, j, Z + o, False).start()

    def hops_to(part):
        return jnp.where(part < z, 3 - z, jnp.where(part > z, z, jnp.maximum(z, 3 - z)))

    def send_y(step, relay):
        part, j, slot = owner(step), lax.div(step, Z), lax.rem(step, SLOTS)
        copy = (y_relay if relay else y_copy)(part, j, slot)
        if relay:
            x_copy(2 * part + 1 - y, j, 0).wait_recv()
        else:
            product(2 * part + 1 - y, j)

        @pl.when(step >= SLOTS)
        def _():
            copy.wait_send()

        if not relay:
            y_out[slot] = to_low(tile[...])
        copy.start()

    def send_x(step):
        part, j, slot = lax.rem(step, 2 * Z), lax.div(step, 2 * Z), lax.rem(step, SLOTS)
        product(part, N_NEAR + j)

        @pl.when(step >= SLOTS)
        def _():
            x_copy(part, j, slot).wait_send()

        x_out[slot] = to_low(tile[...])
        x_copy(part, j, slot).start()

    def arriving(side, place, buffer):
        pltpu.make_async_remote_copy(
            z_out.at[0], land_ref.at[side, place], z_send.at[0], z_recv.at[side, place],
            device_id={"batch": b}, device_id_type=MESH,
        ).wait_recv()
        pltpu.make_async_copy(land_ref.at[side, place], z_in.at[buffer], sem.at[buffer]).start()

    def arrived(side, place, buffer):
        pltpu.make_async_copy(land_ref.at[side, place], z_in.at[buffer], sem.at[buffer]).wait()
        tile[...] += as_float(z_in[buffer])

    def keep(j):
        base = FRONT - 16 * b + jnp.where(b >= 4, 32, 0) + j * (CHUNK // LANES)

        def rows(first, count, start, column, stride):
            flat[pl.ds(start, count, stride=stride), :] = tile[first : first + count, column : column + LANES]

        @pl.when((b != 3) & (b != 7))
        def _():
            for c in range(CHUNK // LANES):
                rows(0, SLICE, base + c, c * LANES, 32)

        @pl.when(b == 3)
        def _():
            for c in range(CHUNK // LANES):
                rows(0, 369, base + c, c * LANES, 32)
                rows(384, SLICE - 384, FRONT + 11760 + j * (CHUNK // LANES) + c, c * LANES, 32)

        @pl.when(b == 7)
        def _():
            for c in range(CHUNK // LANES):
                rows(0, 177, base + c, c * LANES, 32)

            @pl.when(j < 15)
            def _():
                start = FRONT + 5584 + lax.rem(j, 5) * (400 * 6) + lax.div(j, 5) * 2
                for c in range(2):
                    rows(192, 400, start + c, c * LANES, 6)

            @pl.when(j == 15)
            def _():
                for p in range(3):
                    for c in range(2):
                        rows(192 + 64 * p, 64, FRONT + 5584 + 2000 * 6 + 2 * p + c, c * LANES, 6)

    def combine(part, j, o, relay):
        place = part * N_CHUNK + j
        above = (part <= z) & (z < Z - 1)
        below = (part >= z) & (z > 0)

        @pl.when(above)
        def _():
            arriving(0, place, 0)

        @pl.when(below)
        def _():
            arriving(1, place, 1)

        if relay:
            x_copy(2 * part + y, j, 0).wait_recv()
            copy = pltpu.make_async_copy(far_ref.at[(2 * part + y) * N_FAR + j], z_in.at[2], sem.at[2])
            copy.start()
            copy.wait()
            tile[...] = as_float(z_in[2])
        else:
            product(2 * part + y, j)
        y_copy(part, j, 0).wait_recv()
        tile[...] += as_float(y_in[part * N_NEAR + j])

        @pl.when(above)
        def _():
            arrived(0, place, 0)

        @pl.when(below)
        def _():
            arrived(1, place, 1)

        @pl.when(part == z)
        def _():
            if relay:

                @pl.when(j == 0)
                def _():
                    pl.semaphore_wait(hello, 1)

                @pl.when(j > 0)
                def _():
                    back_copy(j - 1).wait_send()

                z_out[Z - 1] = to_low(tile[...])
                back_copy(j).start()
            else:
                keep(j)

        @pl.when(part != z)
        def _():
            @pl.when(j > 0)
            def _():
                z_copy(part, j, o, True).wait_send()

            z_out[o] = to_low(tile[...])

            @pl.when(part < z)
            def _():
                z_copy(part, j, o, True).start()

            @pl.when(part > z)
            def _():
                z_copy(part, j, o, False).start()

    def rounds(chunks, relay):
        steps = Z * chunks

        def step_body(step, carry):
            @pl.when(step < steps)
            def _():
                send_y(step, relay)

            if not relay:

                @pl.when(step < 2 * Z * N_FAR)
                def _():
                    send_x(step)

            late = step - LAG
            part, o = owner(jnp.maximum(late, 0)), lax.rem(jnp.maximum(late, 0), Z)
            j = lax.div(jnp.maximum(late, 0), Z) - hops_to(part)

            @pl.when((late >= 0) & (j >= 0) & (j < chunks))
            def _():
                combine(part, j, o, relay)

            if not relay:
                turn = lax.div(step, TURN_EVERY)
                part, o = owner(turn), lax.rem(turn, Z)
                p = lax.div(turn, Z) - hops_to(part)

                @pl.when((lax.rem(step, TURN_EVERY) == 0) & (p >= 0) & (p < 2 * N_TURN))
                def _():
                    combine_turned(part, p, o)

            return carry

        count = steps + LAG + (Z - 1) * Z
        if not relay:
            count = max(count, TURN_EVERY * Z * (2 * N_TURN + Z - 1))
        lax.fori_loop(0, count, step_body, 0)
        for slot in range(SLOTS):
            (y_relay if relay else y_copy)(0, 0, slot).wait_send()
        for o in range(Z - 1):
            z_copy(0, 0, o, True).wait_send()
            if not relay:
                z_copy(0, 0, Z + o, True).wait_send()
        if not relay:
            for i in range(N_TURN):
                turn_copy(i).wait_send()

    @pl.when(section == 1)
    def _():
        loads = [
            pltpu.make_async_copy(source, target, load.at[i])
            for i, (source, target) in enumerate(
                [(xt_hbm, xt_ref), (x2t_hbm, x2t_ref), (gp_hbm, gp_ref)]
                + [
                    (source.at[half], g_ref.at[:, pl.ds((2 * layer + half) * CONV, CONV)])
                    for layer, source in enumerate((g0_hbm, g1_hbm))
                    for half in range(2)
                ]
            )
        ]
        for copy in loads:
            copy.start()
        barrier = pltpu.get_barrier_semaphore()
        pl.semaphore_signal(barrier, inc=1, device_id={"batch": b + 1 - 2 * y}, device_id_type=MESH)

        @pl.when(z > 0)
        def _():
            pl.semaphore_signal(barrier, inc=1, device_id={"batch": b - 2}, device_id_type=MESH)

        @pl.when(z < Z - 1)
        def _():
            pl.semaphore_signal(barrier, inc=1, device_id={"batch": b + 2}, device_id_type=MESH)

        pl.semaphore_wait(barrier, 2 + jnp.where(z > 0, 1, 0) + jnp.where(z < Z - 1, 1, 0))
        pl.semaphore_signal(hello, inc=1, device_id={"section": 3}, device_id_type=MESH)
        for copy in loads:
            copy.wait()
        rounds(N_FIRST, False)
        for slot in range(SLOTS):
            x_copy(0, 0, slot).wait_send()

        def back(j, carry):
            back_copy(j).wait_recv()
            tile[...] = as_float(ret[j])
            keep(N_NEAR + j)
            return carry

        lax.fori_loop(0, N_FAR, back, 0)
        copy = pltpu.make_async_copy(flat.at[pl.ds(FRONT, share)], out_ref, sem.at[0])
        copy.start()
        copy.wait()

    @pl.when(section == 3)
    def _():
        rounds(N_FAR, True)
        back_copy(N_FAR - 1).wait_send()


def reduce_all(xt, x2t, g0, g1, gp, row, share):
    chunk = (SLICE, CHUNK)
    side = (SIDE_ROWS, LANES)
    dma = pltpu.SemaphoreType.DMA
    places = Z * N_CHUNK
    return pl.pallas_call(
        functools.partial(reduce_kernel, share),
        out_shape=[
            jax.ShapeDtypeStruct((share, LANES), F32),
            jax.ShapeDtypeStruct((2, places) + chunk, BF),
            jax.ShapeDtypeStruct((2 * Z * N_FAR,) + chunk, BF),
        ],
        in_specs=[hbm()] * 6,
        out_specs=[hbm()] * 3,
        scratch_shapes=[
            pltpu.VMEM(xt.shape, BF),
            pltpu.VMEM(x2t.shape, BF),
            pltpu.VMEM((gp.shape[0], 4 * CONV), BF),
            pltpu.VMEM(gp.shape, BF),
            dma((7,)),
            pltpu.VMEM(chunk, F32),
            pltpu.VMEM((SIDE_CHUNKS * SIDE_ROWS, LANES), F32),
            pltpu.VMEM((SLOTS,) + chunk, BF),
            pltpu.VMEM((Z * N_NEAR,) + chunk, BF),
            pltpu.VMEM((2 * Z - 1,) + chunk, BF),
            pltpu.VMEM((3,) + chunk, BF),
            pltpu.VMEM((SLOTS,) + chunk, BF),
            pltpu.VMEM((N_FAR,) + chunk, BF),
            pltpu.VMEM((N_TURN,) + chunk, BF),
            pltpu.VMEM((N_TURN,) + chunk, BF),
            dma((N_TURN,)),
            dma((N_TURN,)),
            dma((SLOTS,)),
            dma((Z * N_NEAR,)),
            dma((2 * Z - 1,)),
            dma((2, places)),
            dma((SLOTS,)),
            dma((2 * Z * N_FAR,)),
            dma,
            dma((N_FAR,)),
            pltpu.SemaphoreType.REGULAR,
            dma((3,)),
            pltpu.VMEM(side, BF),
            pltpu.VMEM((SIDE_CHUNKS,) + side, BF),
            pltpu.VMEM((SIDE_CHUNKS,) + side, BF),
            pltpu.VMEM((SIDE_CHUNKS,) + side, BF),
            dma((SIDE_CHUNKS,)),
            dma((SIDE_CHUNKS,)),
            dma((SIDE_CHUNKS,)),
            dma((SIDE_CHUNKS,)),
            dma,
            dma,
            dma,
            pltpu.SemaphoreType.REGULAR,
        ],
        compiler_params=pltpu.CompilerParams(
            collective_id=1, has_side_effects=True, vmem_limit_bytes=60 << 20
        ),
    )(xt, x2t, g0, g1, gp, row)


CNN_GRADS = (CONV // LANES) * LANES + TABLE_ROWS


def cnn_sum_kernel(in_ref, out_ref, low, y_in, z_in, send, recv):
    section = lax.axis_index("section")
    b = lax.axis_index("batch")
    y, z = lax.rem(b, 2), lax.div(b, 2)
    barrier = pltpu.get_barrier_semaphore()

    def along(target, other, i):
        return pltpu.make_async_remote_copy(
            low, target, send, recv.at[i], device_id={"batch": other}, device_id_type=MESH
        )

    @pl.when(section == 0)
    def _():
        pairs = [(y == 0, b + 1), (y == 1, b - 1), ((y == 0) & (z > 0), b - 2), ((y == 0) & (z < Z - 1), b + 2)]
        for condition, other in pairs:

            @pl.when(condition)
            def _():
                pl.semaphore_signal(barrier, inc=1, device_id={"batch": other}, device_id_type=MESH)

        pl.semaphore_wait(barrier, sum(jnp.where(condition, 1, 0) for condition, _ in pairs))
        out_ref[...] = in_ref[...]

        @pl.when(y == 1)
        def _():
            low[...] = to_low(out_ref[...])
            along(y_in, b - 1, 0).start()
            along(y_in, b - 1, 0).wait_send()

        @pl.when(y == 0)
        def _():
            along(y_in, b + 1, 0).wait_recv()
            out_ref[...] += as_float(y_in[...])

            @pl.when(z < Z - 1)
            def _():
                along(z_in, b + 2, 1).wait_recv()
                out_ref[...] += as_float(z_in[...])

            @pl.when(z > 0)
            def _():
                low[...] = to_low(out_ref[...])
                along(z_in, b - 2, 1).start()
                along(z_in, b - 2, 1).wait_send()


def cnn_sum(grads):
    low = pltpu.VMEM((CNN_GRADS, LANES), BF)
    dma = pltpu.SemaphoreType.DMA
    return pl.pallas_call(
        cnn_sum_kernel,
        out_shape=jax.ShapeDtypeStruct((CNN_GRADS, LANES), F32),
        in_specs=[vmem()],
        out_specs=vmem(),
        scratch_shapes=[
            low,
            low,
            low,
            dma,
            dma((2,)),
        ],
        compiler_params=pltpu.CompilerParams(
            collective_id=3, has_side_effects=True, vmem_limit_bytes=24 << 20
        ),
    )(grads)


PIECES = 19


def assemble_kernel(cnn_ref, total_ref, out_ref, buffer, fetch, store):
    section = lax.axis_index("section")
    rows = out_ref.shape[0] // PIECES

    def part(i):
        return pl.ds(i * rows, rows)

    for i in range(PIECES):
        pltpu.make_async_copy(total_ref.at[part(i)], buffer.at[part(i)], fetch.at[i]).start()
    for i in range(PIECES):
        pltpu.make_async_copy(total_ref.at[part(i)], buffer.at[part(i)], fetch.at[i]).wait()
        pltpu.make_async_copy(buffer.at[part(i)], out_ref.at[part(i)], store.at[i]).start()
    for i in range(PIECES):
        pltpu.make_async_copy(buffer.at[part(i)], out_ref.at[part(i)], store.at[i]).wait()

    @pl.when((section == 0) & (lax.axis_index("batch") == 0))
    def _():
        head = buffer.at[pl.ds(0, CNN_ROWS)]
        for copy in (
            pltpu.make_async_copy(cnn_ref, head, fetch.at[0]),
            pltpu.make_async_copy(head, out_ref.at[pl.ds(0, CNN_ROWS)], store.at[0]),
        ):
            copy.start()
            copy.wait()


def assemble(cnn, total):
    return pl.pallas_call(
        assemble_kernel,
        out_shape=jax.ShapeDtypeStruct(total.shape, F32),
        in_specs=[hbm()] * 2,
        out_specs=hbm(),
        scratch_shapes=[
            pltpu.VMEM(total.shape, F32),
            pltpu.SemaphoreType.DMA((PIECES,)),
            pltpu.SemaphoreType.DMA((PIECES,)),
        ],
        compiler_params=pltpu.CompilerParams(vmem_limit_bytes=60 << 20),
    )(cnn, total)


def on_section(numbers, function, *operands):
    shapes = jax.eval_shape(function, *operands)
    leaves, tree = jax.tree.flatten(shapes)

    def idle(*unused):
        return jax.tree.unflatten(
            tree,
            pl.pallas_call(
                lambda *refs: None,
                out_shape=[jax.ShapeDtypeStruct(s.shape, s.dtype) for s in leaves],
                out_specs=[hbm()] * len(leaves),
            )(),
        )

    section = lax.axis_index("section")
    here = sum(jnp.where(section == n, 1, 0) for n in numbers) > 0
    return lax.cond(here, function, idle, *operands)


def shards(char_ids, word_lengths, params, cotangent):
    section = lax.axis_index("section")
    n_batch = lax.axis_size("batch")
    words_all = lax.all_gather(
        jnp.concatenate([char_ids, word_lengths[:, None]], axis=1), "section", axis=0, tiled=True
    )
    params, words_all = lax.optimization_barrier((params, words_all))
    ck, tt = cnn_params(params)
    group = words_all.shape[0]
    quarter, words, half = group // 4, group // len(CNN), group // 2
    ids_all, column_all = words_all[:, :CHAR_LEN], words_all[:, CHAR_LEN:]
    row_all = column_all.T
    ends_all = stage_bounds(column_all, len(CNN))
    place = jnp.maximum(section - 1, 0)

    def mine(array, axis=0):
        return lax.dynamic_slice_in_dim(array, place * words, words, axis)

    pooled_part = on_section(
        CNN, chars_forward, ends_all[place], mine(ids_all), mine(column_all), mine(row_all, 1), ck, tt
    )
    pooled, cot, w0, w1, wp, vec = start_highways(params, pooled_part, cotangent)
    params, pooled = lax.optimization_barrier((params, pooled))
    encoder_weights = start_encoder(params)
    pooled, encoder_weights = lax.optimization_barrier((pooled, encoder_weights))
    projected, x1, x2, *kept = on_section((1,), highway_forward, w0, w1, wp, vec, pooled)
    (encoder_in,) = hand_over(
        6, [(1, 2, 0, 0, half, 0, 0), (1, 3, 0, half, half, 0, 0)], [projected], [((half, D), BF)]
    )
    x2, encoder_in = lax.optimization_barrier((x2, encoder_in))
    xt, x2t = stack_highways(pooled, x1, x2)
    encoder_in, xt = lax.optimization_barrier((encoder_in, xt))
    layer, back, joined, mixed, att, normed, activated, inner, branch, sums = on_section(
        (2, 3), encoder, encoder_in, cot, *encoder_weights
    )
    items = [(2, 1, 0, 0, half, 0, 0), (3, 1, 0, 0, half, 0, half)]
    items += [(2 + s // 2, s, 1, s % 2 * quarter, quarter, 1, 0) for s in range(4)]
    items += [(3 if k < 4 else 2, 2 if k < 4 else 3, 2 + k, 0, half, 2 + k, 0) for k in range(8)]
    items += [(2, 3, 10, 0, 8, 10, 0), (3, 2, 10, 0, 8, 10, 0)]
    own_rows = [encoder_in, mixed, joined, att, normed, activated, inner, branch, sums]
    grad_highway, layer_out, *other_rows = hand_over(
        7,
        items,
        [back, layer, *own_rows],
        [((group, D), BF), ((quarter, D), BF)] + [(value.shape, value.dtype) for value in own_rows],
    )
    grad_pooled, grad0, grad1 = on_section(
        (1,), highway_backward, w0, w1, wp, pooled, x1, *kept, grad_highway
    )
    (grad_part,) = hand_over(8, [(1, 0, 0, 0, group, 0, 0)], [grad_pooled], [((group, CONV), BF)])
    other_rows, grad_part = lax.optimization_barrier((other_rows, grad_part))
    side = side_rows(own_rows, other_rows)
    share = params.shape[1] // n_batch // LANES
    by_kernels = n_batch == 2 * Z and share == SIDE_SHARE
    if by_kernels:
        total, *_ = reduce_all(xt, x2t, grad0, grad1, grad_highway, side, share)
        grad_part, total = lax.optimization_barrier((grad_part, total))
    cnn_part = on_section((0,), chars_backward, ends_all, ids_all, column_all, row_all, ck, tt, grad_part)
    if not by_kernels:
        return (layer_out, summed_rows(params.shape[1], cnn_part, pooled, x1, x2, grad0, grad1, grad_highway, side))
    cnn_total = cnn_sum(cnn_part)

    def first_row(grads):
        flat = cnn_gradient(grads)
        return jnp.pad(flat, (0, CNN_ROWS * LANES - flat.shape[0])).reshape(-1, LANES)

    cnn_row = on_section((0,), first_row, cnn_total)
    total = assemble(cnn_row, total)
    return (layer_out, total.reshape(1, -1))


def summed_rows(size, cnn_part, pooled, x1, x2, grad0, grad1, grad_highway, side):
    first = lax.axis_index("batch") == 0
    cnn_flat = cnn_gradient(lax.psum(jnp.where(lax.axis_index("section") == 0, cnn_part, 0.0), ("section", "batch")))

    def wide(flat):
        return jnp.pad(as_float(flat), (0, size - flat.shape[0]))

    def highways():
        ones = jnp.ones((1, pooled.shape[0]), BF)
        pieces = []
        both = [jnp.concatenate([grad[0], grad[1]], axis=1) for grad in (grad0, grad1)]
        for x, g in ((pooled, both[0]), (x1, both[1]), (x2, grad_highway)):
            pieces += [matmul_tn(x, g).reshape(-1), matmul(ones, g).reshape(-1)]
        return wide(jnp.concatenate(pieces))

    row = lax.switch(
        lax.axis_index("section"),
        [
            lambda: wide(jnp.where(first, cnn_flat, 0.0)),
            highways,
            lambda: wide(side.reshape(-1)),
            lambda: wide(side.reshape(-1)),
        ],
    )
    return lax.psum_scatter(row, "batch", scatter_dimension=0, tiled=True).reshape(1, -1)


def solution(mesh):
    return jax.shard_map(
        shards,
        mesh=mesh,
        in_specs=(
            P(("section", "batch"), None),
            P(("section", "batch")),
            P("section", None),
            P(("section", "batch"), None),
        ),
        out_specs=(P(("section", "batch"), None), P("section", "batch")),
        check_vma=False,
    )
```

```python
import functools
import math

import jax
import jax.numpy as jnp
from jax import lax
from jax.experimental import pallas as pl
from jax.experimental.pallas import tpu as pltpu
from jax.sharding import PartitionSpec as P

D = 768
HEADS = 12
HEAD_DIM = 64
FF = 3072
CHAR_DIM = 16
CHARS = 262
CHAR_LEN = 50
CH_UNIT = 32
SEQ_LEN = 192
CONV = 64 * CH_UNIT
LANES = 128
MESH = pl.DeviceIdType.MESH
BF = jnp.bfloat16
F32 = jnp.float32
HUGE = 1e30
CNN = (0, 2, 3)

HW_CHUNK = 512
HW_SHAPE = (CONV // HW_CHUNK, CONV, 2 * HW_CHUNK)
channel_steps = (1, 1, 2, 4, 8, 16, 32)
layer_eps = 1e-12

HW_BIAS0 = CONV * 2 * CONV
HW_W1 = HW_BIAS0 + 2 * CONV
HW_BIAS1 = HW_W1 + CONV * 2 * CONV
PROJ_W = HW_BIAS1 + 2 * CONV
PROJ_B = PROJ_W + CONV * D
Q_BIAS = D * 3 * D
V_BIAS = Q_BIAS + D
OUT_W = V_BIAS + D
OUT_B = OUT_W + D * D
UP_B = D * FF
DOWN_W = UP_B + FF
DOWN_B = DOWN_W + FF * D
TABLE = CHARS * CHAR_DIM
CNN_FLAT = TABLE + sum((n + 1) * CHAR_DIM * c * CH_UNIT for n, c in enumerate(channel_steps)) + CONV


def hbm():
    return pl.BlockSpec(memory_space=pltpu.HBM)


def vmem():
    return pl.BlockSpec(memory_space=pltpu.VMEM)


def as_float(array_in):
    return array_in.astype(F32)


def to_low(array_in):
    return array_in.astype(BF)


def matmul(left_in, right_in):
    return jnp.dot(left_in, right_in, preferred_element_type=F32)


def matmul_tn(left_in, right_in):
    return lax.dot_general(left_in, right_in, (((0,), (0,)), ((), ())), preferred_element_type=F32)


def matmul_nt(left_in, right_in):
    return lax.dot_general(left_in, right_in, (((1,), (1,)), ((), ())), preferred_element_type=F32)


class Transfers:
    def __init__(self, items):
        self.items = items

    def copy(self, i, operands, outputs, send, recv):
        source, target, operand, first, rows, output, there = self.items[i]
        from_ref = operands[operand].at[pl.ds(first, rows)]
        to_ref = outputs[output].at[pl.ds(there, rows)]
        if source == target:
            return pltpu.make_async_copy(from_ref, to_ref, send.at[i])
        return pltpu.make_async_remote_copy(
            from_ref, to_ref, send.at[i], recv.at[i], device_id={"section": target}, device_id_type=MESH
        )

    def partners(self, s):
        pairs = {(item[0], item[1]) for item in self.items if item[0] != item[1]}
        return sorted({b for a, b in pairs if a == s} | {a for a, b in pairs if b == s})

    def run(self, operands, outputs, send, recv, work=None):
        section = lax.axis_index("section")
        for s in range(4):
            mine = [i for i, item in enumerate(self.items) if s in item[:2]]
            work_here = (work or {}).get(s)
            if not mine and work_here is None:
                continue

            @pl.when(section == s)
            def _(s=s, mine=mine, work_here=work_here):
                partners = self.partners(s)
                barrier = pltpu.get_barrier_semaphore()
                for other in partners:
                    pl.semaphore_signal(barrier, inc=1, device_id={"section": other}, device_id_type=MESH)
                if work_here is not None:
                    work_here()
                if partners:
                    pl.semaphore_wait(barrier, len(partners))
                outgoing = [i for i in mine if self.items[i][0] == s]
                for i in outgoing:
                    self.copy(i, operands, outputs, send, recv).start()
                for i in mine:
                    copy = self.copy(i, operands, outputs, send, recv)
                    if self.items[i][0] == self.items[i][1]:
                        copy.wait()
                    elif i in outgoing:
                        copy.wait_send()
                    else:
                        copy.wait_recv()


def hand_over(collective_id, items, operands, out_shapes):
    transfers = Transfers(items)

    def kernel(*refs):
        n, m = len(operands), len(out_shapes)
        transfers.run(refs[:n], refs[n : n + m], *refs[n + m :])

    return pl.pallas_call(
        kernel,
        out_shape=[jax.ShapeDtypeStruct(*shape) for shape in out_shapes],
        in_specs=[hbm()] * len(operands),
        out_specs=[hbm()] * len(out_shapes),
        scratch_shapes=[pltpu.SemaphoreType.DMA((len(items),))] * 2,
        compiler_params=pltpu.CompilerParams(collective_id=collective_id, has_side_effects=True),
    )(*operands)


def cut_tools(p_ref, raw, sems):
    def matrix(offset, target, rows):
        count, columns = target.shape

        def body(in_ref, out_ref):
            out_ref[...] = in_ref[...].reshape(rows, columns)

        pltpu.emit_pipeline(
            body,
            grid=(count // rows,),
            in_specs=[pl.BlockSpec((1, rows * columns), lambda i: (0, i))],
            out_specs=[pl.BlockSpec((rows, columns), lambda i: (i, 0))],
        )(p_ref.at[:, pl.ds(offset, count * columns)], target)

    def vectors(entries, vec, target, work):
        copies = []
        for row, (offset, size) in enumerate(entries):
            copy = pltpu.make_async_copy(
                p_ref.at[:, pl.ds(offset, size)], raw.at[row, :, pl.ds(0, size)], sems.at[row]
            )
            copy.start()
            copies.append(copy)
        work()
        for copy in copies:
            copy.wait()
        for row, (offset, size) in enumerate(entries):
            vec[row : row + 1, 0:size] = as_float(raw[row, :, 0:size])
        copy = pltpu.make_async_copy(vec, target, sems.at[0])
        copy.start()
        copy.wait()

    def chunks(offset, target, rows):
        parts = 4
        count = rows // parts

        def body(*refs):
            out_ref = refs[-1]
            for k, in_ref in enumerate(refs[:-1]):
                value = in_ref[...].reshape(count, 2 * CONV)
                for c in range(CONV // HW_CHUNK):
                    for half in range(2):
                        start = half * CONV + c * HW_CHUNK
                        out_ref[c, k * count : (k + 1) * count, half * HW_CHUNK : (half + 1) * HW_CHUNK] = value[
                            :, start : start + HW_CHUNK
                        ]

        pltpu.emit_pipeline(
            body,
            grid=(CONV // rows,),
            in_specs=[
                pl.BlockSpec(
                    (1, count * 2 * CONV), lambda i, k=k: (0, i * parts + k), pipeline_mode=pl.Buffered(3)
                )
                for k in range(parts)
            ],
            out_specs=[pl.BlockSpec((CONV // HW_CHUNK, rows, 2 * HW_CHUNK), lambda i: (0, i, 0))],
        )(*([p_ref.at[:, pl.ds(offset, CONV * 2 * CONV)]] * parts), target)

    return matrix, vectors, chunks


def start_highways(params, pooled_part, cotangent):
    words, quarter = pooled_part.shape[0], cotangent.shape[0]
    items = [(s, 1, 0, 0, words, 0, i * words) for i, s in enumerate(CNN)]
    items += [(s, 2 + s // 2, 1, 0, quarter, 1, s % 2 * quarter) for s in range(4)]
    transfers = Transfers(items)

    def kernel(pooled_ref, cot_ref, p_ref, pooled, cot, w0, w1, wp, vec_ref, vec, raw, sems, send, recv):
        matrix, vectors, chunks = cut_tools(p_ref, raw, sems)

        def work():
            def matrices():
                chunks(0, w0, 256)
                chunks(HW_W1, w1, 256)
                matrix(PROJ_W, wp, 512)

            vectors([(HW_BIAS0, 2 * CONV), (HW_BIAS1, 2 * CONV), (PROJ_B, D)], vec, vec_ref, matrices)

        transfers.run((pooled_ref, cot_ref), (pooled, cot), send, recv, {1: work})

    shapes = [(words * len(CNN), CONV), (2 * quarter, D), HW_SHAPE, HW_SHAPE, (CONV, D)]
    return pl.pallas_call(
        kernel,
        out_shape=[jax.ShapeDtypeStruct(s, BF) for s in shapes] + [jax.ShapeDtypeStruct((8, 2 * CONV), F32)],
        in_specs=[hbm()] * 3,
        out_specs=[hbm()] * 6,
        scratch_shapes=[
            pltpu.VMEM((8, 2 * CONV), F32),
            pltpu.VMEM((5, 1, 2 * CONV), BF),
            pltpu.SemaphoreType.DMA((5,)),
            pltpu.SemaphoreType.DMA((len(items),)),
            pltpu.SemaphoreType.DMA((len(items),)),
        ],
        compiler_params=pltpu.CompilerParams(
            collective_id=4, has_side_effects=True, vmem_limit_bytes=40 << 20
        ),
    )(pooled_part, cotangent, params)


def start_encoder(params):
    shapes = [(D, 3 * D), (D, D), (D, FF), (FF, D)]
    owners = (2, 2, 3, 3)
    items = [(s, 5 - s, i, 0, shape[0], i, 0) for i, (s, shape) in enumerate(zip(owners, shapes, strict=True))]
    items += [(2, 3, 4, 0, 8, 4, 0), (3, 2, 5, 0, 8, 5, 0)]
    transfers = Transfers(items)

    def kernel(p_ref, wqkv, wo, wu, wd, vec2, vec3, vec, raw, sems, send, recv):
        matrix, vectors, _ = cut_tools(p_ref, raw, sems)

        def work2():
            def matrices():
                matrix(0, wqkv, 256)
                matrix(OUT_W, wo, 384)

            entries = [(Q_BIAS, D), (V_BIAS, D), (OUT_B, D), (OUT_B + D, D), (OUT_B + 2 * D, D)]
            vectors(entries, vec, vec2, matrices)

        def work3():
            def matrices():
                matrix(0, wu, 256)
                matrix(DOWN_W, wd, 512)

            vectors([(UP_B, FF), (DOWN_B, D), (DOWN_B + D, D), (DOWN_B + 2 * D, D)], vec, vec3, matrices)

        outputs = (wqkv, wo, wu, wd, vec2, vec3)
        transfers.run(outputs, outputs, send, recv, {2: work2, 3: work3})

    return pl.pallas_call(
        kernel,
        out_shape=[jax.ShapeDtypeStruct(s, BF) for s in shapes] + [jax.ShapeDtypeStruct((8, 2 * CONV), F32)] * 2,
        in_specs=[hbm()],
        out_specs=[hbm()] * 6,
        scratch_shapes=[
            pltpu.VMEM((8, 2 * CONV), F32),
            pltpu.VMEM((5, 1, 2 * CONV), BF),
            pltpu.SemaphoreType.DMA((5,)),
            pltpu.SemaphoreType.DMA((len(items),)),
            pltpu.SemaphoreType.DMA((len(items),)),
        ],
        compiler_params=pltpu.CompilerParams(
            collective_id=5, has_side_effects=True, vmem_limit_bytes=40 << 20
        ),
    )(params)


CNN_ROWS = 1600
TABLE_ROWS = 384


def cnn_params_kernel(p_ref, ck_ref, tt_ref, raw, flat, kernel, table, sem, send, recv):
    section = lax.axis_index("section")
    others = [s for s in CNN if s]
    lane = lax.broadcasted_iota(jnp.int32, (1, LANES), 1)
    barrier = pltpu.get_barrier_semaphore()

    @pl.when(section == 0)
    def _():
        copy = pltpu.make_async_copy(p_ref.at[:, pl.ds(0, CNN_ROWS * LANES)], raw, sem)
        copy.start()
        for s in others:
            pl.semaphore_signal(barrier, inc=1, device_id={"section": s}, device_id_type=MESH)
        copy.wait()
        flat[...] = as_float(raw[...]).reshape(CNN_ROWS, LANES)
        table[...] = jnp.zeros_like(table)
        head = flat[0:40, :]
        for b in range(8):
            mixed = jnp.zeros_like(head)
            for g in range(7):
                rolled = head if g == b else pltpu.roll(head, (g - b) * CHAR_DIM % LANES, 1)
                mixed = jnp.where((lane >= g * CHAR_DIM) & (lane < (g + 1) * CHAR_DIM), rolled, mixed)
            table[pl.ds(b, 33, stride=8), :] = mixed[0:33]
        tt_ref[...] = to_low(table[...])
        rolled = pltpu.roll(flat[...], 32, 1)
        flat[...] = rolled
        count = CNN_ROWS - 40
        flat[0:count, :] = jnp.where(
            lane < 32, flat[32 : 32 + count, :], flat[33 : 33 + count, :]
        )
        kernel[...] = jnp.zeros_like(kernel)
        first, second, third = flat[0:8, :], flat[4:12, :], flat[12:36, :]
        narrow = lax.broadcasted_iota(jnp.int32, (8, LANES), 0) < 4
        for b in range(4):
            one = first if b == 0 else pltpu.roll(first, -b * 32 % LANES, 1)
            two = second if b == 1 else pltpu.roll(second, (32 - b * 32) % LANES, 1)
            kernel[0, pl.ds(b, 8, stride=4), :] = jnp.where(
                lane < 32, jnp.where(narrow, one, 0.0), jnp.where(lane < 64, two, 0.0)
            )
        for b in range(2):
            three = third if b == 1 else pltpu.roll(third, 64, 1)
            kernel[0, pl.ds(b, 24, stride=2), :] = jnp.where(
                lane >= 64, three, kernel[0, pl.ds(b, 24, stride=2), :]
            )
        row, tile = 36, 1
        for number in range(3, 7):
            parts = channel_steps[number] * CH_UNIT // LANES
            depth = (number + 1) * CHAR_DIM
            for c in range(parts):
                kernel[tile, 0:depth, :] = flat[pl.ds(row + c, depth, stride=parts), :]
                tile += 1
            row += depth * parts
        bound = 0
        for number in range(7):
            upper = bound + channel_steps[number] * CH_UNIT
            for c in range(bound // LANES, -(-upper // LANES)):
                kernel[c, 112 + number : 113 + number, :] = jnp.where(
                    (lane + c * LANES >= bound) & (lane + c * LANES < upper), -HUGE, 0.0
                )
            bound = upper
        for c in range(CONV // LANES):
            kernel[c, 119:120, :] = flat[row + c : row + c + 1, :]
            ck_ref[:, c * LANES : (c + 1) * LANES] = to_low(kernel[c])
        pl.semaphore_wait(barrier, len(others))
        copies = []
        for i, s in enumerate(others):
            for j, ref in enumerate((ck_ref, tt_ref)):
                copies.append(
                    pltpu.make_async_remote_copy(
                        ref, ref, send.at[i, j], recv.at[j], device_id={"section": s}, device_id_type=MESH
                    )
                )
        for copy in copies:
            copy.start()
        for copy in copies:
            copy.wait_send()

    for s in others:

        @pl.when(section == s)
        def _():
            pl.semaphore_signal(barrier, inc=1, device_id={"section": 0}, device_id_type=MESH)
            pl.semaphore_wait(barrier, 1)
            for j, ref in enumerate((ck_ref, tt_ref)):
                pltpu.make_async_remote_copy(
                    ref, ref, send.at[0, j], recv.at[j], device_id={"section": 0}, device_id_type=MESH
                ).wait_recv()


def cnn_params(params):
    return pl.pallas_call(
        cnn_params_kernel,
        out_shape=[
            jax.ShapeDtypeStruct((LANES, CONV), BF),
            jax.ShapeDtypeStruct((TABLE_ROWS, LANES), BF),
        ],
        in_specs=[hbm()],
        out_specs=[vmem(), vmem()],
        scratch_shapes=[
            pltpu.VMEM((1, CNN_ROWS * LANES), BF),
            pltpu.VMEM((CNN_ROWS, LANES), F32),
            pltpu.VMEM((CONV // LANES, LANES, LANES), F32),
            pltpu.VMEM((TABLE_ROWS, LANES), F32),
            pltpu.SemaphoreType.DMA,
            pltpu.SemaphoreType.DMA((len(CNN) - 1, 2)),
            pltpu.SemaphoreType.DMA((2,)),
        ],
        compiler_params=pltpu.CompilerParams(
            collective_id=0, has_side_effects=True, vmem_limit_bytes=24 << 20
        ),
    )(params)


STAGES = ((128, 1), (64, 2), (16, 8))
SPOTS = CHAR_LEN + 14


def stage_bounds(lengths, blocks):
    words = lengths.shape[0] // blocks
    counts = jnp.sum(lengths.reshape(blocks, words, 1) > jnp.arange(CHAR_LEN, dtype=jnp.int32), axis=1)
    limits = jnp.array([[words // 2], [words // 8], [0]], jnp.int32)
    return jnp.sum(counts[:, None, :] > limits, axis=2).astype(jnp.int32)


def sorting(column_ref, row_ref):
    count = row_ref.shape[1]
    down = lax.broadcasted_iota(jnp.int32, (count, count), 0)
    across = lax.broadcasted_iota(jnp.int32, (count, count), 1)
    column, row = column_ref[...], row_ref[...]
    before = (column > row) | ((column == row) & (down < across))
    rank = jnp.sum(jnp.where(before, 1, 0), axis=0, keepdims=True)
    return jnp.where(down == rank, 1.0, 0.0).astype(BF)


def sorted_words(order, ids_ref, column_ref):
    ids = ids_ref[...]
    high = lax.div(ids, 16)
    low = ids - 16 * high
    ids = matmul(order, to_low(as_float(high))) * 16.0 + matmul(order, to_low(as_float(low)))
    length = matmul(order, to_low(as_float(jnp.broadcast_to(column_ref[...], (ids.shape[0], LANES)))))
    return ids, length


def stages(ends_ref, body):
    start = 0
    for k, (words, positions) in enumerate(STAGES):
        end = ends_ref[k]

        def one(i, unused, words=words, positions=positions, start=start, end=end):
            body(start + i * positions, words, positions, end)
            return unused

        lax.fori_loop(0, lax.div(jnp.maximum(end - start, 0) + positions - 1, positions), one, 0)
        start = end


def one_hot(first, words, positions, ids):
    lane = lax.broadcasted_iota(jnp.int32, (words, CHAR_LEN), 1)
    columns = [
        jnp.sum(jnp.where(lane == first + q, ids[0:words, :], 0.0), axis=1, keepdims=True) for q in range(positions)
    ]
    column = columns[0] if positions == 1 else jnp.concatenate(columns, axis=0)
    symbol = lax.broadcasted_iota(jnp.int32, (words * positions, TABLE_ROWS), 1)
    return jnp.where(column.astype(jnp.int32) == symbol, 1.0, 0.0).astype(BF)


def windows(first, words, positions, end, length, embedded, masks):
    total = None
    for j in range(7):
        term = embedded[pl.ds(first + j, positions), 0:words, :] * masks[j]
        total = term if total is None else total + term
    shape = (positions, words, LANES)
    lane = lax.broadcasted_iota(jnp.int32, shape, 2)
    position = first + lax.broadcasted_iota(jnp.int32, shape, 0)
    room = jnp.broadcast_to(length[0:words, :][None], shape)
    out = (lane >= 112) & (lane < 119) & ((as_float(position + lane - 111) > room) | (position >= end))
    return (total + jnp.where(out | (lane == 119), 1.0, 0.0).astype(BF)).reshape(positions * words, LANES)


def lane_masks():
    lane = lax.broadcasted_iota(jnp.int32, (1, 1, LANES), 2)
    return [
        jnp.where((lane >= j * CHAR_DIM) & (lane < (j + 1) * CHAR_DIM), 1.0, 0.0).astype(BF)
        for j in range(7)
    ]


def embedder(ids, tt_ref, embedded):
    def embed(first, words, positions, end):
        value = to_low(matmul(one_hot(first, words, positions, ids), tt_ref[...]))
        embedded[pl.ds(first, positions), 0:words, :] = value.reshape(positions, words, LANES)

    return embed


def chars_forward_kernel(ends_ref, ids_ref, column_ref, row_ref, ck_ref, tt_ref, out_ref, embedded, best):
    embedded[...] = jnp.zeros_like(embedded)
    best[...] = jnp.full_like(best, -HUGE)
    masks = lane_masks()
    order = sorting(column_ref, row_ref)
    ids, length = sorted_words(order, ids_ref, column_ref)
    stages(ends_ref, embedder(ids, tt_ref, embedded))

    def pool(first, words, positions, end):
        rows = windows(first, words, positions, end, length, embedded, masks)
        for c in range(0, CONV, 512):
            pre = jnp.max(matmul(rows, ck_ref[:, c : c + 512]).reshape(positions, words, 512), axis=0)
            best[0:words, c : c + 512] = jnp.maximum(best[0:words, c : c + 512], pre)

    stages(ends_ref, pool)
    out_ref[...] = to_low(matmul_tn(order, to_low(jnp.maximum(best[...], 0.0))))


def chars_backward_kernel(
    all_ends_ref, ids_ref, column_ref, row_ref, ck_ref, tt_ref, grad_ref,
    out_ref, embedded, best, share, backs, sums,
):
    block = pl.program_id(0)
    ends_ref = [all_ends_ref[block, k] for k in range(len(STAGES))]
    embedded[...] = jnp.zeros_like(embedded)
    backs[...] = jnp.zeros_like(backs)
    best[...] = jnp.full_like(best, -HUGE)
    share[...] = jnp.zeros_like(share)
    table_rows = pl.ds(CONV, TABLE_ROWS)

    @pl.when(block == 0)
    def _():
        sums[...] = jnp.zeros_like(sums)
        out_ref[table_rows, :] = jnp.zeros((TABLE_ROWS, LANES), F32)

    masks = lane_masks()
    order = sorting(column_ref, row_ref)
    ids, length = sorted_words(order, ids_ref, column_ref)
    stages(ends_ref, embedder(ids, tt_ref, embedded))

    def count(first, words, positions, end):
        rows = windows(first, words, positions, end, length, embedded, masks)
        for c in range(0, CONV, 512):
            part = slice(c, c + 512)
            pre = matmul(rows, ck_ref[:, part])
            top, hits = best[0:words, part], share[0:words, part]
            for q in range(positions):
                here = pre[q * words : (q + 1) * words]
                hits = jnp.where(here > top, 1.0, hits + jnp.where(here == top, 1.0, 0.0))
                top = jnp.maximum(top, here)
            best[0:words, part], share[0:words, part] = top, hits

    stages(ends_ref, count)
    share[...] = matmul(order, grad_ref[...]) / share[...]
    best[...] = jnp.where(best[...] > 0.0, best[...], 3e38)

    def spread(first, words, positions, end):
        rows = windows(first, words, positions, end, length, embedded, masks)
        back = jnp.zeros((words * positions, LANES), F32)
        for c in range(0, CONV, 512):
            part = slice(c, c + 512)
            pre = matmul(rows, ck_ref[:, part]).reshape(positions, words, 512)
            hit = pre == best[0:words, part][None]
            grad = to_low(jnp.where(hit, jnp.broadcast_to(share[0:words, part][None], pre.shape), 0.0))
            grad = grad.reshape(positions * words, 512)
            sums[:, part] += matmul_tn(rows, grad)
            back = back + matmul_nt(grad, ck_ref[:, part])
        backs[pl.ds(first + 6, positions), 0:words, :] = to_low(back).reshape(positions, words, LANES)

    stages(ends_ref, spread)

    def gather(first, words, positions, end):
        shape = (positions, words, LANES)
        lane = lax.broadcasted_iota(jnp.int32, shape, 2)
        position = first + lax.broadcasted_iota(jnp.int32, shape, 0)
        total = jnp.zeros(shape, F32)
        for j in range(7):
            here = (lane >= j * CHAR_DIM) & (lane < (j + 1) * CHAR_DIM) & (position < end)
            total = jnp.where(here, as_float(backs[pl.ds(first + 6 - j, positions), 0:words, :]), total)
        hot = one_hot(first, words, positions, ids)
        out_ref[table_rows, :] += matmul_tn(hot, to_low(total).reshape(positions * words, LANES))

    stages(ends_ref, gather)

    @pl.when(block == pl.num_programs(0) - 1)
    def _():
        for c in range(CONV // LANES):
            out_ref[c * LANES : (c + 1) * LANES, :] = sums[:, c * LANES : (c + 1) * LANES]


def chars_forward(ends, ids, column, row, ck, tt):
    words = ids.shape[0]
    return pl.pallas_call(
        chars_forward_kernel,
        out_shape=jax.ShapeDtypeStruct((words, CONV), BF),
        in_specs=[pl.BlockSpec(memory_space=pltpu.SMEM)] + [vmem()] * 5,
        out_specs=vmem(),
        scratch_shapes=[
            pltpu.VMEM((SPOTS, words, LANES), BF),
            pltpu.VMEM((words, CONV), F32),
        ],
        compiler_params=pltpu.CompilerParams(vmem_limit_bytes=32 << 20),
    )(ends, ids, column, row, ck, tt)


def chars_backward(ends, ids, column, row, ck, tt, grad):
    words = ids.shape[0] // len(CNN)
    return pl.pallas_call(
        chars_backward_kernel,
        grid=(len(CNN),),
        out_shape=jax.ShapeDtypeStruct((CNN_GRADS, LANES), F32),
        in_specs=[
            pl.BlockSpec(memory_space=pltpu.SMEM),
            pl.BlockSpec((words, CHAR_LEN), lambda i: (i, 0)),
            pl.BlockSpec((words, 1), lambda i: (i, 0)),
            pl.BlockSpec((1, words), lambda i: (0, i)),
            pl.BlockSpec((LANES, CONV), lambda i: (0, 0)),
            pl.BlockSpec((TABLE_ROWS, LANES), lambda i: (0, 0)),
            pl.BlockSpec((words, CONV), lambda i: (i, 0)),
        ],
        out_specs=pl.BlockSpec((CNN_GRADS, LANES), lambda i: (0, 0)),
        scratch_shapes=[
            pltpu.VMEM((SPOTS, words, LANES), BF),
            pltpu.VMEM((words, CONV), F32),
            pltpu.VMEM((words, CONV), F32),
            pltpu.VMEM((SPOTS, words, LANES), BF),
            pltpu.VMEM((LANES, CONV), F32),
        ],
        compiler_params=pltpu.CompilerParams(vmem_limit_bytes=40 << 20),
    )(ends, ids, column, row, ck, tt, grad)


def cnn_gradient(grads):
    table_grad = grads[CONV:]
    kernel_grad = jnp.swapaxes(grads[:CONV].reshape(-1, LANES, LANES), 0, 1).reshape(LANES, CONV)
    pieces = [
        sum(table_grad[:CHARS, g * CHAR_DIM : (g + 1) * CHAR_DIM] for g in range(7)).reshape(-1)
    ]
    offset = 0
    for number in range(7):
        channels = channel_steps[number] * CH_UNIT
        pieces.append(
            kernel_grad[: (number + 1) * CHAR_DIM, offset : offset + channels].reshape(-1)
        )
        offset += channels
    pieces.append(kernel_grad[119])
    return jnp.concatenate(pieces)


def sigmoid(value):
    return 1.0 / (1.0 + jnp.exp(-value))


def highway_layer_kernel(row, x_ref, part_ref, w_ref, bl_ref, br_ref, next_ref, left_ref, right_ref):
    both = matmul(x_ref[...], w_ref[0])
    left = both[:, :HW_CHUNK] + bl_ref[row : row + 1, :]
    right = both[:, HW_CHUNK:] + br_ref[row : row + 1, :]
    left_ref[...] = left
    right_ref[...] = right
    gate = sigmoid(right)
    next_ref[...] = to_low(gate * as_float(part_ref[...]) + (1.0 - gate) * jnp.maximum(left, 0.0))


def highway_layer(row, x, w, vec):
    group = x.shape[0]
    steps = CONV // HW_CHUNK
    part = pl.BlockSpec((group, HW_CHUNK), lambda i: (0, i))
    return pl.pallas_call(
        functools.partial(highway_layer_kernel, row),
        grid=(steps,),
        out_shape=[
            jax.ShapeDtypeStruct((group, CONV), BF),
            jax.ShapeDtypeStruct((group, CONV), F32),
            jax.ShapeDtypeStruct((group, CONV), F32),
        ],
        in_specs=[
            pl.BlockSpec((group, CONV), lambda i: (0, 0)),
            part,
            pl.BlockSpec((1,) + HW_SHAPE[1:], lambda i: (i, 0, 0)),
            pl.BlockSpec((8, HW_CHUNK), lambda i: (0, i)),
            pl.BlockSpec((8, HW_CHUNK), lambda i: (0, i + steps)),
        ],
        out_specs=[part, part, part],
        compiler_params=pltpu.CompilerParams(vmem_limit_bytes=40 << 20),
    )(x, x, w, vec, vec)


def highway_forward(w0, w1, wp, vec, wide_in):
    x1, left0, right0 = highway_layer(0, wide_in, w0, vec)
    x2, left1, right1 = highway_layer(1, x1, w1, vec)
    projected = to_low(matmul(x2, wp) + vec[2, :D])
    return (projected, x1, x2, left0, right0, left1, right1)


def highway_back_kernel(last, up_ref, wp_ref, x_ref, left_ref, right_ref, w_ref, grad_ref, out_ref, total):
    i = pl.program_id(0)
    flowing = matmul_nt(up_ref[...], wp_ref[...]) if wp_ref is not None else up_ref[...]
    gate = sigmoid(right_ref[...])
    left = left_ref[...]
    nonlinear = jnp.maximum(left, 0.0)
    closed = flowing * (1.0 - gate)
    grad_left = to_low(jnp.where(left > 0.0, closed, 0.0))
    grad_right = to_low(closed * (as_float(x_ref[...]) - nonlinear) * gate)
    grad_ref[0] = grad_left
    grad_ref[1] = grad_right
    back = matmul_nt(jnp.concatenate([grad_left, grad_right], axis=1), w_ref[0])

    @pl.when(i == 0)
    def _():
        total[...] = back

    @pl.when(i > 0)
    def _():
        total[...] += back

    here = pl.ds(pl.multiple_of(i * HW_CHUNK, HW_CHUNK), HW_CHUNK)
    total[:, here] += flowing * gate

    @pl.when(i == pl.num_programs(0) - 1)
    def _():
        out_ref[...] = to_low(total[...]) if last else total[...]


def highway_back(last, up, wp, x, left, right, w):
    group = x.shape[0]
    steps = CONV // HW_CHUNK
    part = pl.BlockSpec((group, HW_CHUNK), lambda i: (0, i))
    if wp is None:
        kernel = lambda up_ref, *refs: highway_back_kernel(last, up_ref, None, *refs)
        sources, specs = [up], [part]
    else:
        kernel = functools.partial(highway_back_kernel, last)
        sources = [up, wp]
        specs = [pl.BlockSpec((group, D), lambda i: (0, 0)), pl.BlockSpec((HW_CHUNK, D), lambda i: (i, 0))]
    return pl.pallas_call(
        kernel,
        grid=(steps,),
        out_shape=[
            jax.ShapeDtypeStruct((2, group, CONV), BF),
            jax.ShapeDtypeStruct((group, CONV), BF if last else F32),
        ],
        in_specs=specs
        + [
            part,
            part,
            part,
            pl.BlockSpec((1,) + HW_SHAPE[1:], lambda i: (i, 0, 0)),
        ],
        out_specs=[
            pl.BlockSpec((2, group, HW_CHUNK), lambda i: (0, 0, i)),
            pl.BlockSpec((group, CONV), lambda i: (0, 0)),
        ],
        scratch_shapes=[pltpu.VMEM((group, CONV), F32)],
        compiler_params=pltpu.CompilerParams(vmem_limit_bytes=40 << 20),
    )(*sources, x, left, right, w)


def highway_backward(w0, w1, wp, wide_in, x1, left0, right0, left1, right1, upstream):
    grad1, flowing = highway_back(False, upstream, wp, x1, left1, right1, w1)
    grad0, grad_pooled = highway_back(True, flowing, None, wide_in, left0, right0, w0)
    return (grad_pooled, grad0, grad1)


def layer_norm(residual):
    centered = residual - jnp.mean(residual, axis=-1, keepdims=True)
    inverse = lax.rsqrt(jnp.mean(centered * centered, axis=-1, keepdims=True) + layer_eps)
    return centered * inverse, inverse


def norm_backward(upstream, scaled, inverse, gain):
    weighted = upstream * gain
    first_mean = jnp.mean(weighted, axis=-1, keepdims=True)
    cross_mean = jnp.mean(weighted * scaled, axis=-1, keepdims=True)
    return inverse * (weighted - first_mean - scaled * cross_mean)


def encoder_kernel(
    x_ref, cot_ref, wqkv_ref, wo_ref, wu_ref, wd_ref, vec_ref, vec3_ref,
    layer_ref, back_ref, joined_ref, mixed_ref, att_ref, normed_ref, act_ref, inner_ref, branch_ref, sums_ref,
    qkv, probs, slope, scaled, carry,
):
    rows = x_ref.shape[0]
    pairs = HEADS // 2
    scale = HEAD_DIM ** (-0.5)
    lane = lax.broadcasted_iota(jnp.int32, (1, LANES), 1)
    halves = [jnp.where(lane < HEAD_DIM, 1.0, 0.0).astype(BF), jnp.where(lane < HEAD_DIM, 0.0, 1.0).astype(BF)]

    def heads(body):
        def one(i, unused):
            sequence, pair = lax.div(i, pairs), lax.rem(i, pairs)
            body(
                pl.ds(pl.multiple_of(sequence * SEQ_LEN, SEQ_LEN), SEQ_LEN),
                [pl.ds(pl.multiple_of(pair * LANES + k * D, LANES), LANES) for k in range(3)],
                i,
            )
            return unused

        lax.fori_loop(0, rows // SEQ_LEN * pairs, one, 0, unroll=True)

    def pieces(width, body):
        def one(i, unused):
            body(pl.ds(pl.multiple_of(i * width, width), width))
            return unused

        return lambda count: lax.fori_loop(0, count, one, 0, unroll=True)

    @pl.when(lax.axis_index("section") >= 2)
    def _():
        for k, bias in enumerate((vec_ref[0:1, 0:D], None, vec_ref[1:2, 0:D])):
            part = matmul(x_ref[...], wqkv_ref[:, k * D : (k + 1) * D])
            qkv[:, k * D : (k + 1) * D] = to_low(part if bias is None else part + bias)

        def attend(here, columns, i):
            query, key, value = (qkv[here, columns[k]] for k in range(3))
            out = []
            for half in range(2):
                scores = matmul_nt(query * halves[half], key) * scale
                exponent = jnp.exp(scores - jnp.max(scores, axis=-1, keepdims=True))
                soft = exponent / jnp.sum(exponent, axis=-1, keepdims=True)
                probs[2 * i + half] = soft
                out.append(matmul(to_low(soft), value))
            mixed_ref[here, columns[0]] = to_low(jnp.where(lane < HEAD_DIM, out[0], out[1]))

        heads(attend)
        residual = as_float(x_ref[...]) + matmul(mixed_ref[...], wo_ref[...]) + vec_ref[2:3, 0:D]
        scaled1, inverse1 = layer_norm(residual)
        scaled[...] = scaled1
        normed_ref[...] = to_low(scaled1 * vec_ref[3:4, 0:D] + vec_ref[4:5, 0:D])

        def up(part):
            inner = matmul(normed_ref[...], wu_ref[:, part]) + vec3_ref[0:1, part]
            phi = 0.5 * (1.0 + lax.erf(inner * 0.7071067811865476))
            act_ref[:, part] = to_low(inner * phi)
            slope[:, part] = phi + inner * jnp.exp(-0.5 * inner * inner) * 0.3989422804014327

        pieces(512, up)(FF // 512)
        residual = as_float(normed_ref[...]) + matmul(act_ref[...], wd_ref[...]) + vec3_ref[1:2, 0:D]
        scaled2, inverse2 = layer_norm(residual)
        gain2 = vec3_ref[2:3, 0:D]
        layer_ref[...] = to_low(scaled2 * gain2 + vec3_ref[3:4, 0:D])
        upstream = as_float(cot_ref[...])
        sums_ref[2:3, :] = jnp.sum(upstream * scaled2, axis=0, keepdims=True)
        sums_ref[3:4, :] = jnp.sum(upstream, axis=0, keepdims=True)
        carry[...] = norm_backward(upstream, scaled2, inverse2, gain2)
        branch_ref[...] = to_low(carry[...])

        def down(part):
            inner_ref[:, part] = to_low(matmul_nt(branch_ref[...], wd_ref[part, :]) * slope[:, part])

        pieces(512, down)(FF // 512)
        upstream = as_float(to_low(carry[...] + matmul_nt(inner_ref[...], wu_ref[...])))
        sums_ref[0:1, :] = jnp.sum(upstream * scaled[...], axis=0, keepdims=True)
        sums_ref[1:2, :] = jnp.sum(upstream, axis=0, keepdims=True)
        carry[...] = norm_backward(upstream, scaled[...], inverse1, vec_ref[3:4, 0:D])
        att_ref[...] = to_low(carry[...])
        back_ref[...] = to_low(matmul_nt(att_ref[...], wo_ref[...]))

        def attend_back(here, columns, i):
            query, key, value = (qkv[here, columns[k]] for k in range(3))
            grad = back_ref[here, columns[0]]
            totals = [0.0, 0.0, 0.0]
            for half in range(2):
                grad_half = grad * halves[half]
                soft = probs[2 * i + half]
                grad_soft = matmul_nt(grad_half, value)
                flow = to_low(soft * (grad_soft - jnp.sum(grad_soft * soft, axis=-1, keepdims=True)))
                totals[0] += matmul(flow, key * halves[half])
                totals[1] += matmul_tn(flow, query * halves[half])
                totals[2] += matmul_tn(to_low(soft), grad_half)
            joined_ref[here, columns[0]] = to_low(totals[0] * scale)
            joined_ref[here, columns[1]] = to_low(totals[1] * scale)
            joined_ref[here, columns[2]] = to_low(totals[2])

        heads(attend_back)
        back_ref[...] = to_low(carry[...] + matmul_nt(joined_ref[...], wqkv_ref[...]))


def encoder(x, cot, wqkv, wo, wu, wd, vec, vec3):
    rows = x.shape[0]
    widths = [D, D, 3 * D, D, D, D, FF, FF, D]
    return pl.pallas_call(
        encoder_kernel,
        out_shape=[jax.ShapeDtypeStruct((rows, w), BF) for w in widths] + [jax.ShapeDtypeStruct((8, D), F32)],
        in_specs=[vmem()] * 8,
        out_specs=[vmem()] * 10,
        scratch_shapes=[
            pltpu.VMEM((rows, 3 * D), BF),
            pltpu.VMEM((rows // SEQ_LEN * HEADS, SEQ_LEN, SEQ_LEN), F32),
            pltpu.VMEM((rows, FF), F32),
            pltpu.VMEM((rows, D), F32),
            pltpu.VMEM((rows, D), F32),
        ],
        compiler_params=pltpu.CompilerParams(vmem_limit_bytes=56 << 20),
    )(x, cot, wqkv, wo, wu, wd, vec, vec3)


def side_rows_kernel(*refs):
    section = lax.axis_index("section")
    own, other, (out_hbm, flat, out_ref, *targets, sem) = refs[:9], refs[9:18], refs[18:]
    x_ref, mixed_ref, joined_ref, att_ref, normed_ref, act_ref, inner_ref, branch_ref, sums_ref = targets

    def fetch(*places):
        copies = []
        for i in places:
            rows = own[i].shape[0]
            for k, source in enumerate((own[i], other[i])):
                copies.append(pltpu.make_async_copy(source, targets[i].at[pl.ds(k * rows, rows)], sem.at[k, i]))
        for copy in copies:
            copy.start()
        for copy in copies:
            copy.wait()

    def product(left_ref, right_ref, row):
        count, width = left_ref.shape[1], right_ref.shape[1]
        parts = width // LANES
        for k in range(count // D):
            for c in range(0, width, 256):
                block = matmul_tn(left_ref[:, k * D : (k + 1) * D], right_ref[:, c : c + 256])
                for t in range(2):
                    flat[pl.ds(row + k * D * parts + c // LANES + t, D, stride=parts), :] = block[:, t * LANES : (t + 1) * LANES]
        return row + count * parts

    def line(row, values):
        for c in range(values.shape[1] // LANES):
            flat[row + c : row + c + 1, :] = values[:, c * LANES : (c + 1) * LANES]
        return row + values.shape[1] // LANES

    def summed(ref, first, last):
        return jnp.sum(as_float(ref[:, first:last]), axis=0, keepdims=True)

    def write(row):
        full = out_ref.shape[0]
        flat[row:full, :] = jnp.zeros((full - row, LANES), F32)
        out_ref[...] = to_low(flat[...])
        copy = pltpu.make_async_copy(out_ref, out_hbm, sem.at[0, 0])
        copy.start()
        copy.wait()

    @pl.when(section == 2)
    def _():
        fetch(0, 1, 2, 3, 8)
        row = product(x_ref, joined_ref, 0)
        row = line(row, summed(joined_ref, 0, D))
        row = line(row, summed(joined_ref, 2 * D, 3 * D))
        row = product(mixed_ref, att_ref, row)
        row = line(row, summed(att_ref, 0, D))
        row = line(row, sums_ref[0:1, :] + sums_ref[8:9, :])
        write(line(row, sums_ref[1:2, :] + sums_ref[9:10, :]))

    @pl.when(section == 3)
    def _():
        fetch(4, 5, 6, 7, 8)
        row = product(normed_ref, inner_ref, 0)
        row = line(row, summed(inner_ref, 0, FF))
        row = product(act_ref, branch_ref, row)
        row = line(row, summed(branch_ref, 0, D))
        row = line(row, sums_ref[2:3, :] + sums_ref[10:11, :])
        write(line(row, sums_ref[3:4, :] + sums_ref[11:12, :]))


def side_rows(own, other):
    size = (SIDE_SHARE + SIDE_ROWS * SIDE_CHUNKS, LANES)
    return pl.pallas_call(
        side_rows_kernel,
        out_shape=jax.ShapeDtypeStruct(size, BF),
        in_specs=[hbm()] * (2 * len(own)),
        out_specs=hbm(),
        scratch_shapes=[pltpu.VMEM(size, F32), pltpu.VMEM(size, BF)]
        + [pltpu.VMEM((2 * value.shape[0], value.shape[1]), value.dtype) for value in own]
        + [pltpu.SemaphoreType.DMA((2, len(own)))],
        compiler_params=pltpu.CompilerParams(vmem_limit_bytes=50 << 20),
    )(*own, *other)


def stack_kernel(x0_ref, x1_ref, x2_ref, xt_hbm, x2t_hbm, low, turned, sem):
    group = x0_ref.shape[0]

    @pl.when(lax.axis_index("section") == 1)
    def _():
        turned[CONV:STACK, :] = jnp.where(
            lax.broadcasted_iota(jnp.int32, (STACK - CONV, group), 0) == 0, 1.0, 0.0
        ).astype(BF)
        targets = (xt_hbm.at[pl.ds(0, STACK)], xt_hbm.at[pl.ds(STACK, STACK)], x2t_hbm)
        for source, target in zip((x0_ref, x1_ref, x2_ref), targets, strict=True):
            copy = pltpu.make_async_copy(source, low, sem)
            copy.start()
            copy.wait()
            for c in range(0, CONV, 512):
                turned[c : c + 512, :] = low[:, c : c + 512].T
            copy = pltpu.make_async_copy(turned, target, sem)
            copy.start()
            copy.wait()


def stack_highways(x0, x1, x2):
    group = x0.shape[0]
    return pl.pallas_call(
        stack_kernel,
        out_shape=[jax.ShapeDtypeStruct((2 * STACK, group), BF), jax.ShapeDtypeStruct((STACK, group), BF)],
        in_specs=[hbm()] * 3,
        out_specs=[hbm()] * 2,
        scratch_shapes=[
            pltpu.VMEM((group, CONV), BF),
            pltpu.VMEM((STACK, group), BF),
            pltpu.SemaphoreType.DMA,
        ],
        compiler_params=pltpu.CompilerParams(vmem_limit_bytes=24 << 20),
    )(x0, x1, x2)


SIDE_ROWS = 1200
SIDE_CHUNKS = 16
SIDE_REST = 1040
SIDE_SHARE = 17936


def side_part(
    share, row_ref, out_ref, own, y_in, z_in, z_out, total,
    y_send, y_recv, z_send, z_recv, l_send, l_recv, sem, turn,
):
    section = lax.axis_index("section")
    b = lax.axis_index("batch")
    y, z = lax.rem(b, 2), lax.div(b, 2)

    def count(half):
        return jnp.where((section == 2) & (half == 1), 1, SIDE_CHUNKS)

    def rows(half, i):
        return pl.ds(pl.multiple_of(half * share + i * SIDE_ROWS, 16), SIDE_ROWS)

    def y_copy(i):
        return pltpu.make_async_remote_copy(
            row_ref.at[rows(1 - y, i)], y_in.at[i], y_send.at[i], y_recv.at[i],
            device_id={"batch": b + 1 - 2 * y}, device_id_type=MESH,
        )

    def z_copy(i):
        return pltpu.make_async_remote_copy(
            z_out.at[i], z_in.at[i], z_send.at[i], z_recv.at[i],
            device_id={"batch": b - 2}, device_id_type=MESH,
        )

    def rest_copy():
        return pltpu.make_async_remote_copy(
            total.at[pl.ds(share, SIDE_REST)], total.at[pl.ds(0, SIDE_REST)], l_send, l_recv,
            device_id={"batch": 2}, device_id_type=MESH,
        )

    def write():
        copy = pltpu.make_async_copy(total.at[pl.ds(0, share)], out_ref, sem)
        copy.start()
        copy.wait()

    @pl.when(section != 1)
    def _():
        total[...] = jnp.zeros_like(total)

    @pl.when(section == 0)
    def _():
        write()

    @pl.when(section >= 2)
    def _():
        barrier = pltpu.get_barrier_semaphore()

        @pl.when(section == 3)
        def _():
            pl.semaphore_signal(barrier, inc=1, device_id={"section": 1}, device_id_type=MESH)

        pl.semaphore_signal(barrier, inc=1, device_id={"batch": b + 1 - 2 * y}, device_id_type=MESH)
        pairs = [(z > 0, b - 2), (z < Z - 1, b + 2), (b == 1, 2), (b == 2, 1)]
        for condition, other in pairs:

            @pl.when(condition)
            def _():
                pl.semaphore_signal(barrier, inc=1, device_id={"batch": other}, device_id_type=MESH)

        pl.semaphore_signal(barrier, inc=1, device_id={"section": 5 - section}, device_id_type=MESH)
        pl.semaphore_wait(barrier, 2 + sum(jnp.where(condition, 1, 0) for condition, _ in pairs))

        def send(i, carry):
            y_copy(i).start()
            return carry

        def combine(i, carry):
            copy = pltpu.make_async_copy(row_ref.at[rows(y, i)], own, sem)
            copy.start()
            copy.wait()
            y_copy(i).wait_recv()
            here = pl.ds(pl.multiple_of(i * SIDE_ROWS, 16), SIDE_ROWS)

            @pl.when(z == Z - 1)
            def _():
                z_out[i] = to_low(as_float(own[...]) + as_float(y_in[i]))

            @pl.when(z < Z - 1)
            def _():
                z_copy(i).wait_recv()

                @pl.when(z > 0)
                def _():
                    z_out[i] = to_low(as_float(own[...]) + as_float(y_in[i]) + as_float(z_in[i]))

                @pl.when(z == 0)
                def _():
                    total[here] = as_float(own[...]) + as_float(y_in[i]) + as_float(z_in[i])

            @pl.when(z > 0)
            def _():
                z_copy(i).start()

            return carry

        def drain(i, carry):
            y_copy(i).wait_send()
            return carry

        def drain_z(i, carry):
            z_copy(i).wait_send()
            return carry

        @pl.when(section == 2)
        def _():
            pl.semaphore_wait(turn, 1)

        lax.fori_loop(0, count(1 - y), send, 0)
        lax.fori_loop(0, count(y), combine, 0)

        @pl.when(section == 3)
        def _():
            pl.semaphore_signal(turn, inc=1, device_id={"section": 2}, device_id_type=MESH)

        @pl.when((section == 3) & (b == 1))
        def _():
            rest_copy().start()
            rest_copy().wait_send()

        @pl.when((section == 3) & (b == 2))
        def _():
            rest_copy().wait_recv()

        write()
        lax.fori_loop(0, count(1 - y), drain, 0)

        @pl.when(z > 0)
        def _():
            lax.fori_loop(0, count(y), drain_z, 0)


SLICE = 576
CHUNK = 256
N_CHUNK = 2 * CONV // CHUNK
N_FAR = 3
N_NEAR = N_CHUNK - N_FAR
N_TURN = 2
TURN_EVERY = 2
N_FIRST = N_NEAR - N_TURN
STACK = CONV + 16
LAG = 3
SLOTS = 4
FRONT = 80
Z = 4


def reduce_kernel(
    share, xt_hbm, x2t_hbm, g0_hbm, g1_hbm, gp_hbm, row_ref, out_ref, land_ref, far_ref,
    xt_ref, x2t_ref, g_ref, gp_ref, load, tile, flat, y_out, y_in, z_out, z_in, x_out, ret, t_out, t_in, t_send, t_recv,
    y_send, y_recv, z_send, z_recv, x_send, x_recv, r_send, r_recv, hello, sem, *side_scratch,
):
    own, side_y, side_z, side_out, *side_sems = side_scratch
    side_part(share, row_ref, out_ref, own, side_y, side_z, side_out, flat, *side_sems)
    section = lax.axis_index("section")
    b = lax.axis_index("batch")
    y, z = lax.rem(b, 2), lax.div(b, 2)
    def owner(step):
        o = lax.rem(step, Z)
        up = jnp.where(z == 0, 3 - o, jnp.where(o == 0, 3, jnp.where(o == 1, 0, jnp.where(o == 2, 2, 1))))
        down = jnp.where(z == 3, o, jnp.where(o == 0, 0, jnp.where(o == 1, 3, jnp.where(o == 2, 1, 2))))
        return jnp.where(z < 2, up, down)

    def product(part, j):
        column = pl.multiple_of(j * CHUNK, CHUNK)

        @pl.when((part != 3) & (part != 7))
        def _():
            row = pl.multiple_of((35 * part + jnp.where(part >= 4, 1, 0)) * 16, 16)
            col = pl.multiple_of(column + jnp.where(part >= 4, 2 * CONV, 0), CHUNK)
            tile[...] = matmul(xt_ref[pl.ds(row, SLICE), :], g_ref[:, pl.ds(col, CHUNK)])

        second = pl.ds(pl.multiple_of(column + 2 * CONV, CHUNK), CHUNK)

        @pl.when(part == 3)
        def _():
            tile[0:384, :] = matmul(xt_ref[1680:STACK, :], g_ref[:, pl.ds(column, CHUNK)])
            tile[384:SLICE, :] = matmul(xt_ref[STACK : STACK + SLICE - 384, :], g_ref[:, second])
            tile[376:384, :] = matmul(xt_ref[STACK + 192 : STACK + 208, :], g_ref[:, second])[0:8]

        @pl.when(part == 7)
        def _():
            tile[0:192, :] = matmul(xt_ref[2 * STACK - 192 : 2 * STACK, :], g_ref[:, second])

            @pl.when(j < 3)
            def _():
                third = pl.ds(pl.multiple_of(j * 256, 256), 256)
                tile[184:192, :] = matmul(x2t_ref[CONV:STACK, :], gp_ref[:, third])[0:8]

            @pl.when(j < 15)
            def _():
                row = pl.multiple_of(lax.rem(j, 5) * 384, 16)
                col = pl.multiple_of(lax.div(j, 5) * 256, 256)
                tile[192:SLICE, :] = matmul(x2t_ref[pl.ds(row, 384), :], gp_ref[:, pl.ds(col, 256)])

            @pl.when(j == 15)
            def _():
                for p in range(3):
                    tile[192 + 128 * p : 320 + 128 * p, :] = matmul(
                        x2t_ref[1920:CONV, :], gp_ref[:, p * 256 : (p + 1) * 256]
                    )

    def y_copy(part, j, slot):
        place = part * N_NEAR + j
        return pltpu.make_async_remote_copy(
            y_out.at[slot], y_in.at[place], y_send.at[slot], y_recv.at[place],
            device_id={"batch": b + 1 - 2 * y}, device_id_type=MESH,
        )

    def z_copy(part, j, o, down):
        place = part * N_CHUNK + j
        side = 0 if down else 1
        return pltpu.make_async_remote_copy(
            z_out.at[o], land_ref.at[side, place], z_send.at[o], z_recv.at[side, place],
            device_id={"batch": b - 2 if down else b + 2}, device_id_type=MESH,
        )

    def y_relay(part, j, slot):
        place = part * N_NEAR + j
        return pltpu.make_async_remote_copy(
            far_ref.at[(2 * part + 1 - y) * N_FAR + j], y_in.at[place], y_send.at[slot], y_recv.at[place],
            device_id={"batch": b + 1 - 2 * y}, device_id_type=MESH,
        )

    def x_copy(part, j, slot):
        place = part * N_FAR + j
        return pltpu.make_async_remote_copy(
            x_out.at[slot], far_ref.at[place], x_send.at[slot], x_recv.at[place],
            device_id={"section": 3}, device_id_type=MESH,
        )

    def back_copy(j):
        return pltpu.make_async_remote_copy(
            z_out.at[Z - 1], ret.at[j], r_send, r_recv.at[j], device_id={"section": 1}, device_id_type=MESH
        )

    def turn_copy(i):
        return pltpu.make_async_remote_copy(
            t_out.at[i], t_in.at[i], t_send.at[i], t_recv.at[i],
            device_id={"batch": b + 1 - 2 * y}, device_id_type=MESH,
        )

    def combine_turned(part, p, o):
        i, mine = lax.div(p, 2), lax.rem(p, 2)
        j = N_FIRST + p
        place = part * N_CHUNK + j
        above = (part <= z) & (z < Z - 1)
        below = (part >= z) & (z > 0)

        @pl.when(above)
        def _():
            arriving(0, place, 0)

        @pl.when(below)
        def _():
            arriving(1, place, 1)

        product(2 * part + jnp.where(mine == 1, y, 1 - y), N_FIRST + i)

        @pl.when(above)
        def _():
            arrived(0, place, 0)

        @pl.when(below)
        def _():
            arrived(1, place, 1)

        @pl.when((part == z) & (mine == 0))
        def _():
            t_out[i] = to_low(tile[...])
            turn_copy(i).start()

        @pl.when((part == z) & (mine == 1))
        def _():
            turn_copy(i).wait_recv()
            tile[...] += as_float(t_in[i])
            keep(N_FIRST + i)

        @pl.when(part != z)
        def _():
            @pl.when(p > 0)
            def _():
                z_copy(part, j, Z + o, True).wait_send()

            z_out[Z + o] = to_low(tile[...])

            @pl.when(part < z)
            def _():
                z_copy(part, j, Z + o, True).start()

            @pl.when(part > z)
            def _():
                z_copy(part, j, Z + o, False).start()

    def hops_to(part):
        return jnp.where(part < z, 3 - z, jnp.where(part > z, z, jnp.maximum(z, 3 - z)))

    def send_y(step, relay):
        part, j, slot = owner(step), lax.div(step, Z), lax.rem(step, SLOTS)
        copy = (y_relay if relay else y_copy)(part, j, slot)
        if relay:
            x_copy(2 * part + 1 - y, j, 0).wait_recv()
        else:
            product(2 * part + 1 - y, j)

        @pl.when(step >= SLOTS)
        def _():
            copy.wait_send()

        if not relay:
            y_out[slot] = to_low(tile[...])
        copy.start()

    def send_x(step):
        part, j, slot = lax.rem(step, 2 * Z), lax.div(step, 2 * Z), lax.rem(step, SLOTS)
        product(part, N_NEAR + j)

        @pl.when(step >= SLOTS)
        def _():
            x_copy(part, j, slot).wait_send()

        x_out[slot] = to_low(tile[...])
        x_copy(part, j, slot).start()

    def arriving(side, place, buffer):
        pltpu.make_async_remote_copy(
            z_out.at[0], land_ref.at[side, place], z_send.at[0], z_recv.at[side, place],
            device_id={"batch": b}, device_id_type=MESH,
        ).wait_recv()
        pltpu.make_async_copy(land_ref.at[side, place], z_in.at[buffer], sem.at[buffer]).start()

    def arrived(side, place, buffer):
        pltpu.make_async_copy(land_ref.at[side, place], z_in.at[buffer], sem.at[buffer]).wait()
        tile[...] += as_float(z_in[buffer])

    def keep(j):
        base = FRONT - 16 * b + jnp.where(b >= 4, 32, 0) + j * (CHUNK // LANES)

        def rows(first, count, start, column, stride):
            flat[pl.ds(start, count, stride=stride), :] = tile[first : first + count, column : column + LANES]

        @pl.when((b != 3) & (b != 7))
        def _():
            for c in range(CHUNK // LANES):
                rows(0, SLICE, base + c, c * LANES, 32)

        def row_at(first, start, column):
            flat[pl.ds(start, 1), :] = tile[first : first + 1, column : column + LANES]

        @pl.when(b == 3)
        def _():
            for c in range(CHUNK // LANES):
                start = FRONT + 11760 + j * (CHUNK // LANES) + c
                rows(0, 369, base + c, c * LANES, 32)
                rows(384, SLICE - 384, start, c * LANES, 32)
                row_at(376, start + 192 * 32, c * LANES)

        @pl.when(b == 7)
        def _():
            for c in range(CHUNK // LANES):
                rows(0, 177, base + c, c * LANES, 32)

            @pl.when(j < 3)
            def _():
                for c in range(2):
                    row_at(184, FRONT + 5584 + CONV * 6 + 2 * j + c, c * LANES)

            @pl.when(j < 15)
            def _():
                start = FRONT + 5584 + lax.rem(j, 5) * (384 * 6) + lax.div(j, 5) * 2
                for c in range(2):
                    rows(192, 384, start + c, c * LANES, 6)

            @pl.when(j == 15)
            def _():
                for p in range(3):
                    for c in range(2):
                        rows(192 + 128 * p, 128, FRONT + 5584 + 1920 * 6 + 2 * p + c, c * LANES, 6)

    def combine(part, j, o, relay):
        place = part * N_CHUNK + j
        above = (part <= z) & (z < Z - 1)
        below = (part >= z) & (z > 0)

        @pl.when(above)
        def _():
            arriving(0, place, 0)

        @pl.when(below)
        def _():
            arriving(1, place, 1)

        if relay:
            x_copy(2 * part + y, j, 0).wait_recv()
            copy = pltpu.make_async_copy(far_ref.at[(2 * part + y) * N_FAR + j], z_in.at[2], sem.at[2])
            copy.start()
            copy.wait()
            tile[...] = as_float(z_in[2])
        else:
            product(2 * part + y, j)
        y_copy(part, j, 0).wait_recv()
        tile[...] += as_float(y_in[part * N_NEAR + j])

        @pl.when(above)
        def _():
            arrived(0, place, 0)

        @pl.when(below)
        def _():
            arrived(1, place, 1)

        @pl.when(part == z)
        def _():
            if relay:

                @pl.when(j == 0)
                def _():
                    pl.semaphore_wait(hello, 1)

                @pl.when(j > 0)
                def _():
                    back_copy(j - 1).wait_send()

                z_out[Z - 1] = to_low(tile[...])
                back_copy(j).start()
            else:
                keep(j)

        @pl.when(part != z)
        def _():
            @pl.when(j > 0)
            def _():
                z_copy(part, j, o, True).wait_send()

            z_out[o] = to_low(tile[...])

            @pl.when(part < z)
            def _():
                z_copy(part, j, o, True).start()

            @pl.when(part > z)
            def _():
                z_copy(part, j, o, False).start()

    def rounds(chunks, relay):
        steps = Z * chunks

        def step_body(step, carry):
            @pl.when(step < steps)
            def _():
                send_y(step, relay)

            if not relay:

                @pl.when(step < 2 * Z * N_FAR)
                def _():
                    send_x(step)

            late = step - LAG
            part, o = owner(jnp.maximum(late, 0)), lax.rem(jnp.maximum(late, 0), Z)
            j = lax.div(jnp.maximum(late, 0), Z) - hops_to(part)

            @pl.when((late >= 0) & (j >= 0) & (j < chunks))
            def _():
                combine(part, j, o, relay)

            if not relay:
                turn = lax.div(step, TURN_EVERY)
                part, o = owner(turn), lax.rem(turn, Z)
                p = lax.div(turn, Z) - hops_to(part)

                @pl.when((lax.rem(step, TURN_EVERY) == 0) & (p >= 0) & (p < 2 * N_TURN))
                def _():
                    combine_turned(part, p, o)

            return carry

        count = steps + LAG + (Z - 1) * Z
        if not relay:
            count = max(count, TURN_EVERY * Z * (2 * N_TURN + Z - 1))
        lax.fori_loop(0, count, step_body, 0)
        for slot in range(SLOTS):
            (y_relay if relay else y_copy)(0, 0, slot).wait_send()
        for o in range(Z - 1):
            z_copy(0, 0, o, True).wait_send()
            if not relay:
                z_copy(0, 0, Z + o, True).wait_send()
        if not relay:
            for i in range(N_TURN):
                turn_copy(i).wait_send()

    @pl.when(section == 1)
    def _():
        loads = [
            pltpu.make_async_copy(source, target, load.at[i])
            for i, (source, target) in enumerate(
                [(xt_hbm, xt_ref), (x2t_hbm, x2t_ref), (gp_hbm, gp_ref)]
                + [
                    (source.at[half], g_ref.at[:, pl.ds((2 * layer + half) * CONV, CONV)])
                    for layer, source in enumerate((g0_hbm, g1_hbm))
                    for half in range(2)
                ]
            )
        ]
        for copy in loads:
            copy.start()
        barrier = pltpu.get_barrier_semaphore()
        pl.semaphore_signal(barrier, inc=1, device_id={"batch": b + 1 - 2 * y}, device_id_type=MESH)

        @pl.when(z > 0)
        def _():
            pl.semaphore_signal(barrier, inc=1, device_id={"batch": b - 2}, device_id_type=MESH)

        @pl.when(z < Z - 1)
        def _():
            pl.semaphore_signal(barrier, inc=1, device_id={"batch": b + 2}, device_id_type=MESH)

        pl.semaphore_wait(barrier, 2 + jnp.where(z > 0, 1, 0) + jnp.where(z < Z - 1, 1, 0))
        pl.semaphore_signal(hello, inc=1, device_id={"section": 3}, device_id_type=MESH)
        for copy in loads:
            copy.wait()
        flat[FRONT + share - 64 : FRONT + share, :] = jnp.zeros((64, LANES), F32)
        rounds(N_FIRST, False)
        for slot in range(SLOTS):
            x_copy(0, 0, slot).wait_send()

        def back(j, carry):
            back_copy(j).wait_recv()
            tile[...] = as_float(ret[j])
            keep(N_NEAR + j)
            return carry

        lax.fori_loop(0, N_FAR, back, 0)
        copy = pltpu.make_async_copy(flat.at[pl.ds(FRONT, share)], out_ref, sem.at[0])
        copy.start()
        copy.wait()

    @pl.when(section == 3)
    def _():
        rounds(N_FAR, True)
        back_copy(N_FAR - 1).wait_send()


def reduce_all(xt, x2t, g0, g1, gp, row, share):
    chunk = (SLICE, CHUNK)
    side = (SIDE_ROWS, LANES)
    dma = pltpu.SemaphoreType.DMA
    places = Z * N_CHUNK
    return pl.pallas_call(
        functools.partial(reduce_kernel, share),
        out_shape=[
            jax.ShapeDtypeStruct((share, LANES), F32),
            jax.ShapeDtypeStruct((2, places) + chunk, BF),
            jax.ShapeDtypeStruct((2 * Z * N_FAR,) + chunk, BF),
        ],
        in_specs=[hbm()] * 6,
        out_specs=[hbm()] * 3,
        scratch_shapes=[
            pltpu.VMEM(xt.shape, BF),
            pltpu.VMEM(x2t.shape, BF),
            pltpu.VMEM((gp.shape[0], 4 * CONV), BF),
            pltpu.VMEM(gp.shape, BF),
            dma((7,)),
            pltpu.VMEM(chunk, F32),
            pltpu.VMEM((SIDE_CHUNKS * SIDE_ROWS, LANES), F32),
            pltpu.VMEM((SLOTS,) + chunk, BF),
            pltpu.VMEM((Z * N_NEAR,) + chunk, BF),
            pltpu.VMEM((2 * Z - 1,) + chunk, BF),
            pltpu.VMEM((3,) + chunk, BF),
            pltpu.VMEM((SLOTS,) + chunk, BF),
            pltpu.VMEM((N_FAR,) + chunk, BF),
            pltpu.VMEM((N_TURN,) + chunk, BF),
            pltpu.VMEM((N_TURN,) + chunk, BF),
            dma((N_TURN,)),
            dma((N_TURN,)),
            dma((SLOTS,)),
            dma((Z * N_NEAR,)),
            dma((2 * Z - 1,)),
            dma((2, places)),
            dma((SLOTS,)),
            dma((2 * Z * N_FAR,)),
            dma,
            dma((N_FAR,)),
            pltpu.SemaphoreType.REGULAR,
            dma((3,)),
            pltpu.VMEM(side, BF),
            pltpu.VMEM((SIDE_CHUNKS,) + side, BF),
            pltpu.VMEM((SIDE_CHUNKS,) + side, BF),
            pltpu.VMEM((SIDE_CHUNKS,) + side, BF),
            dma((SIDE_CHUNKS,)),
            dma((SIDE_CHUNKS,)),
            dma((SIDE_CHUNKS,)),
            dma((SIDE_CHUNKS,)),
            dma,
            dma,
            dma,
            pltpu.SemaphoreType.REGULAR,
        ],
        compiler_params=pltpu.CompilerParams(
            collective_id=1, has_side_effects=True, vmem_limit_bytes=60 << 20
        ),
    )(xt, x2t, g0, g1, gp, row)


CNN_GRADS = (CONV // LANES) * LANES + TABLE_ROWS


def cnn_sum_kernel(in_ref, out_ref, low, y_in, z_in, send, recv):
    section = lax.axis_index("section")
    b = lax.axis_index("batch")
    y, z = lax.rem(b, 2), lax.div(b, 2)
    barrier = pltpu.get_barrier_semaphore()

    def along(target, other, i):
        return pltpu.make_async_remote_copy(
            low, target, send, recv.at[i], device_id={"batch": other}, device_id_type=MESH
        )

    @pl.when(section == 0)
    def _():
        pairs = [(y == 0, b + 1), (y == 1, b - 1), ((y == 0) & (z > 0), b - 2), ((y == 0) & (z < Z - 1), b + 2)]
        for condition, other in pairs:

            @pl.when(condition)
            def _():
                pl.semaphore_signal(barrier, inc=1, device_id={"batch": other}, device_id_type=MESH)

        pl.semaphore_wait(barrier, sum(jnp.where(condition, 1, 0) for condition, _ in pairs))
        out_ref[...] = in_ref[...]

        @pl.when(y == 1)
        def _():
            low[...] = to_low(out_ref[...])
            along(y_in, b - 1, 0).start()
            along(y_in, b - 1, 0).wait_send()

        @pl.when(y == 0)
        def _():
            along(y_in, b + 1, 0).wait_recv()
            out_ref[...] += as_float(y_in[...])

            @pl.when(z < Z - 1)
            def _():
                along(z_in, b + 2, 1).wait_recv()
                out_ref[...] += as_float(z_in[...])

            @pl.when(z > 0)
            def _():
                low[...] = to_low(out_ref[...])
                along(z_in, b - 2, 1).start()
                along(z_in, b - 2, 1).wait_send()


def cnn_sum(grads):
    low = pltpu.VMEM((CNN_GRADS, LANES), BF)
    dma = pltpu.SemaphoreType.DMA
    return pl.pallas_call(
        cnn_sum_kernel,
        out_shape=jax.ShapeDtypeStruct((CNN_GRADS, LANES), F32),
        in_specs=[vmem()],
        out_specs=vmem(),
        scratch_shapes=[
            low,
            low,
            low,
            dma,
            dma((2,)),
        ],
        compiler_params=pltpu.CompilerParams(
            collective_id=3, has_side_effects=True, vmem_limit_bytes=24 << 20
        ),
    )(grads)


PIECES = 19


def assemble_kernel(cnn_ref, total_ref, out_ref, buffer, fetch, store):
    section = lax.axis_index("section")
    rows = out_ref.shape[0] // PIECES

    def part(i):
        return pl.ds(i * rows, rows)

    for i in range(PIECES):
        pltpu.make_async_copy(total_ref.at[part(i)], buffer.at[part(i)], fetch.at[i]).start()
    for i in range(PIECES):
        pltpu.make_async_copy(total_ref.at[part(i)], buffer.at[part(i)], fetch.at[i]).wait()
        pltpu.make_async_copy(buffer.at[part(i)], out_ref.at[part(i)], store.at[i]).start()
    for i in range(PIECES):
        pltpu.make_async_copy(buffer.at[part(i)], out_ref.at[part(i)], store.at[i]).wait()

    @pl.when((section == 0) & (lax.axis_index("batch") == 0))
    def _():
        head = buffer.at[pl.ds(0, CNN_ROWS)]
        for copy in (
            pltpu.make_async_copy(cnn_ref, head, fetch.at[0]),
            pltpu.make_async_copy(head, out_ref.at[pl.ds(0, CNN_ROWS)], store.at[0]),
        ):
            copy.start()
            copy.wait()


def assemble(cnn, total):
    return pl.pallas_call(
        assemble_kernel,
        out_shape=jax.ShapeDtypeStruct(total.shape, F32),
        in_specs=[hbm()] * 2,
        out_specs=hbm(),
        scratch_shapes=[
            pltpu.VMEM(total.shape, F32),
            pltpu.SemaphoreType.DMA((PIECES,)),
            pltpu.SemaphoreType.DMA((PIECES,)),
        ],
        compiler_params=pltpu.CompilerParams(vmem_limit_bytes=60 << 20),
    )(cnn, total)


def on_section(numbers, function, *operands):
    shapes = jax.eval_shape(function, *operands)
    leaves, tree = jax.tree.flatten(shapes)

    def idle(*unused):
        return jax.tree.unflatten(
            tree,
            pl.pallas_call(
                lambda *refs: None,
                out_shape=[jax.ShapeDtypeStruct(s.shape, s.dtype) for s in leaves],
                out_specs=[hbm()] * len(leaves),
            )(),
        )

    section = lax.axis_index("section")
    here = sum(jnp.where(section == n, 1, 0) for n in numbers) > 0
    return lax.cond(here, function, idle, *operands)


def shards(char_ids, word_lengths, params, cotangent):
    section = lax.axis_index("section")
    n_batch = lax.axis_size("batch")
    words_all = lax.all_gather(
        jnp.concatenate([char_ids, word_lengths[:, None]], axis=1), "section", axis=0, tiled=True
    )
    params, words_all = lax.optimization_barrier((params, words_all))
    ck, tt = cnn_params(params)
    group = words_all.shape[0]
    quarter, words, half = group // 4, group // len(CNN), group // 2
    ids_all, column_all = words_all[:, :CHAR_LEN], words_all[:, CHAR_LEN:]
    row_all = column_all.T
    ends_all = stage_bounds(column_all, len(CNN))
    place = jnp.maximum(section - 1, 0)

    def mine(array, axis=0):
        return lax.dynamic_slice_in_dim(array, place * words, words, axis)

    pooled_part = on_section(
        CNN, chars_forward, ends_all[place], mine(ids_all), mine(column_all), mine(row_all, 1), ck, tt
    )
    pooled, cot, w0, w1, wp, vec = start_highways(params, pooled_part, cotangent)
    params, pooled = lax.optimization_barrier((params, pooled))
    encoder_weights = start_encoder(params)
    pooled, encoder_weights = lax.optimization_barrier((pooled, encoder_weights))
    projected, x1, x2, *kept = on_section((1,), highway_forward, w0, w1, wp, vec, pooled)
    (encoder_in,) = hand_over(
        6, [(1, 2, 0, 0, half, 0, 0), (1, 3, 0, half, half, 0, 0)], [projected], [((half, D), BF)]
    )
    x2, encoder_in = lax.optimization_barrier((x2, encoder_in))
    xt, x2t = stack_highways(pooled, x1, x2)
    encoder_in, xt = lax.optimization_barrier((encoder_in, xt))
    layer, back, joined, mixed, att, normed, activated, inner, branch, sums = on_section(
        (2, 3), encoder, encoder_in, cot, *encoder_weights
    )
    items = [(2, 1, 0, 0, half, 0, 0), (3, 1, 0, 0, half, 0, half)]
    items += [(2 + s // 2, s, 1, s % 2 * quarter, quarter, 1, 0) for s in range(4)]
    items += [(3 if k < 4 else 2, 2 if k < 4 else 3, 2 + k, 0, half, 2 + k, 0) for k in range(8)]
    items += [(2, 3, 10, 0, 8, 10, 0), (3, 2, 10, 0, 8, 10, 0)]
    own_rows = [encoder_in, mixed, joined, att, normed, activated, inner, branch, sums]
    grad_highway, layer_out, *other_rows = hand_over(
        7,
        items,
        [back, layer, *own_rows],
        [((group, D), BF), ((quarter, D), BF)] + [(value.shape, value.dtype) for value in own_rows],
    )
    grad_pooled, grad0, grad1 = on_section(
        (1,), highway_backward, w0, w1, wp, pooled, x1, *kept, grad_highway
    )
    (grad_part,) = hand_over(8, [(1, 0, 0, 0, group, 0, 0)], [grad_pooled], [((group, CONV), BF)])
    other_rows, grad_part = lax.optimization_barrier((other_rows, grad_part))
    side = side_rows(own_rows, other_rows)
    share = params.shape[1] // n_batch // LANES
    by_kernels = n_batch == 2 * Z and share == SIDE_SHARE
    if by_kernels:
        total, *_ = reduce_all(xt, x2t, grad0, grad1, grad_highway, side, share)
        grad_part, total = lax.optimization_barrier((grad_part, total))
    cnn_part = on_section((0,), chars_backward, ends_all, ids_all, column_all, row_all, ck, tt, grad_part)
    if not by_kernels:
        return (layer_out, summed_rows(params.shape[1], cnn_part, pooled, x1, x2, grad0, grad1, grad_highway, side))
    cnn_total = cnn_sum(cnn_part)

    def first_row(grads):
        flat = cnn_gradient(grads)
        return jnp.pad(flat, (0, CNN_ROWS * LANES - flat.shape[0])).reshape(-1, LANES)

    cnn_row = on_section((0,), first_row, cnn_total)
    total = assemble(cnn_row, total)
    return (layer_out, total.reshape(1, -1))


def summed_rows(size, cnn_part, pooled, x1, x2, grad0, grad1, grad_highway, side):
    first = lax.axis_index("batch") == 0
    cnn_flat = cnn_gradient(lax.psum(jnp.where(lax.axis_index("section") == 0, cnn_part, 0.0), ("section", "batch")))

    def wide(flat):
        return jnp.pad(as_float(flat), (0, size - flat.shape[0]))

    def highways():
        ones = jnp.ones((1, pooled.shape[0]), BF)
        pieces = []
        both = [jnp.concatenate([grad[0], grad[1]], axis=1) for grad in (grad0, grad1)]
        for x, g in ((pooled, both[0]), (x1, both[1]), (x2, grad_highway)):
            pieces += [matmul_tn(x, g).reshape(-1), matmul(ones, g).reshape(-1)]
        return wide(jnp.concatenate(pieces))

    row = lax.switch(
        lax.axis_index("section"),
        [
            lambda: wide(jnp.where(first, cnn_flat, 0.0)),
            highways,
            lambda: wide(side.reshape(-1)),
            lambda: wide(side.reshape(-1)),
        ],
    )
    return lax.psum_scatter(row, "batch", scatter_dimension=0, tiled=True).reshape(1, -1)


def solution(mesh):
    return jax.shard_map(
        shards,
        mesh=mesh,
        in_specs=(
            P(("section", "batch"), None),
            P(("section", "batch")),
            P("section", None),
            P(("section", "batch"), None),
        ),
        out_specs=(P(("section", "batch"), None), P("section", "batch")),
        check_vma=False,
    )
```

```python
import functools
import math

import jax
import jax.numpy as jnp
from jax import lax
from jax.experimental import pallas as pl
from jax.experimental.pallas import tpu as pltpu
from jax.sharding import PartitionSpec as P

D = 768
HEADS = 12
HEAD_DIM = 64
FF = 3072
CHAR_DIM = 16
CHARS = 262
CHAR_LEN = 50
CH_UNIT = 32
SEQ_LEN = 192
CONV = 64 * CH_UNIT
LANES = 128
MESH = pl.DeviceIdType.MESH
BF = jnp.bfloat16
F32 = jnp.float32
HUGE = 1e30
CNN = (0, 2, 3)

HW_CHUNK = 512
HW_SHAPE = (CONV // HW_CHUNK, CONV, 2 * HW_CHUNK)
channel_steps = (1, 1, 2, 4, 8, 16, 32)
layer_eps = 1e-12

HW_BIAS0 = CONV * 2 * CONV
HW_W1 = HW_BIAS0 + 2 * CONV
HW_BIAS1 = HW_W1 + CONV * 2 * CONV
PROJ_W = HW_BIAS1 + 2 * CONV
PROJ_B = PROJ_W + CONV * D
Q_BIAS = D * 3 * D
V_BIAS = Q_BIAS + D
OUT_W = V_BIAS + D
OUT_B = OUT_W + D * D
UP_B = D * FF
DOWN_W = UP_B + FF
DOWN_B = DOWN_W + FF * D
TABLE = CHARS * CHAR_DIM
CNN_FLAT = TABLE + sum((n + 1) * CHAR_DIM * c * CH_UNIT for n, c in enumerate(channel_steps)) + CONV


def hbm():
    return pl.BlockSpec(memory_space=pltpu.HBM)


def vmem():
    return pl.BlockSpec(memory_space=pltpu.VMEM)


def as_float(array_in):
    return array_in.astype(F32)


def to_low(array_in):
    return array_in.astype(BF)


def matmul(left_in, right_in):
    return jnp.dot(left_in, right_in, preferred_element_type=F32)


def matmul_tn(left_in, right_in):
    return lax.dot_general(left_in, right_in, (((0,), (0,)), ((), ())), preferred_element_type=F32)


def matmul_nt(left_in, right_in):
    return lax.dot_general(left_in, right_in, (((1,), (1,)), ((), ())), preferred_element_type=F32)


class Transfers:
    def __init__(self, items, late=()):
        self.items, self.late = items, tuple(late)
        self.held = {items[i][0] for i in self.late}

    def copy(self, i, operands, outputs, send, recv):
        source, target, operand, first, rows, output, there = self.items[i]
        from_ref = operands[operand].at[pl.ds(first, rows)]
        to_ref = outputs[output].at[pl.ds(there, rows)]
        if source == target:
            return pltpu.make_async_copy(from_ref, to_ref, send.at[i])
        return pltpu.make_async_remote_copy(
            from_ref, to_ref, send.at[i], recv.at[i], device_id={"section": target}, device_id_type=MESH
        )

    def partners(self, s):
        pairs = {(item[0], item[1]) for item in self.items if item[0] != item[1]}
        return sorted({b for a, b in pairs if a == s} | {a for a, b in pairs if b == s})

    def run(self, operands, outputs, send, recv, work=None):
        section = lax.axis_index("section")
        for s in range(4):
            mine = [i for i, item in enumerate(self.items) if s in item[:2]]
            work_here = (work or {}).get(s)
            if not mine and work_here is None:
                continue

            @pl.when(section == s)
            def _(s=s, mine=mine, work_here=work_here):
                partners = self.partners(s)
                barrier = pltpu.get_barrier_semaphore()
                for other in partners:
                    pl.semaphore_signal(barrier, inc=1, device_id={"section": other}, device_id_type=MESH)
                if work_here is not None:
                    work_here()
                if partners:
                    pl.semaphore_wait(barrier, len(partners))
                outgoing = [i for i in mine if self.items[i][0] == s]
                first = [i for i in outgoing if i not in self.late]
                for i in first:
                    self.copy(i, operands, outputs, send, recv).start()
                if s in self.held:
                    self.copy(first[0], operands, outputs, send, recv).wait_send()
                for i in outgoing:
                    if i in self.late:
                        self.copy(i, operands, outputs, send, recv).start()
                if s in self.held:
                    mine = [i for i in mine if i != first[0]]
                for i in mine:
                    copy = self.copy(i, operands, outputs, send, recv)
                    if self.items[i][0] == self.items[i][1]:
                        copy.wait()
                    elif i in outgoing:
                        copy.wait_send()
                    else:
                        copy.wait_recv()


def hand_over(collective_id, items, operands, out_shapes, late=()):
    transfers = Transfers(items, late)

    def kernel(*refs):
        n, m = len(operands), len(out_shapes)
        transfers.run(refs[:n], refs[n : n + m], *refs[n + m :])

    return pl.pallas_call(
        kernel,
        out_shape=[jax.ShapeDtypeStruct(*shape) for shape in out_shapes],
        in_specs=[hbm()] * len(operands),
        out_specs=[hbm()] * len(out_shapes),
        scratch_shapes=[pltpu.SemaphoreType.DMA((len(items),))] * 2,
        compiler_params=pltpu.CompilerParams(collective_id=collective_id, has_side_effects=True),
    )(*operands)


def cut_tools(p_ref, raw, sems):
    def matrix(offset, target, rows):
        count, columns = target.shape

        def body(in_ref, out_ref):
            out_ref[...] = in_ref[...].reshape(rows, columns)

        pltpu.emit_pipeline(
            body,
            grid=(count // rows,),
            in_specs=[pl.BlockSpec((1, rows * columns), lambda i: (0, i))],
            out_specs=[pl.BlockSpec((rows, columns), lambda i: (i, 0))],
        )(p_ref.at[:, pl.ds(offset, count * columns)], target)

    def vectors(entries, vec, target, work):
        copies = []
        for row, (offset, size) in enumerate(entries):
            copy = pltpu.make_async_copy(
                p_ref.at[:, pl.ds(offset, size)], raw.at[row, :, pl.ds(0, size)], sems.at[row]
            )
            copy.start()
            copies.append(copy)
        work()
        for copy in copies:
            copy.wait()
        for row, (offset, size) in enumerate(entries):
            vec[row : row + 1, 0:size] = as_float(raw[row, :, 0:size])
        copy = pltpu.make_async_copy(vec, target, sems.at[0])
        copy.start()
        copy.wait()

    def chunks(offset, target, rows):
        parts = 4
        count = rows // parts

        def body(*refs):
            out_ref = refs[-1]
            for k, in_ref in enumerate(refs[:-1]):
                value = in_ref[...].reshape(count, 2 * CONV)
                for c in range(CONV // HW_CHUNK):
                    for half in range(2):
                        start = half * CONV + c * HW_CHUNK
                        out_ref[c, k * count : (k + 1) * count, half * HW_CHUNK : (half + 1) * HW_CHUNK] = value[
                            :, start : start + HW_CHUNK
                        ]

        pltpu.emit_pipeline(
            body,
            grid=(CONV // rows,),
            in_specs=[
                pl.BlockSpec(
                    (1, count * 2 * CONV), lambda i, k=k: (0, i * parts + k), pipeline_mode=pl.Buffered(3)
                )
                for k in range(parts)
            ],
            out_specs=[pl.BlockSpec((CONV // HW_CHUNK, rows, 2 * HW_CHUNK), lambda i: (0, i, 0))],
        )(*([p_ref.at[:, pl.ds(offset, CONV * 2 * CONV)]] * parts), target)

    return matrix, vectors, chunks


def start_highways(params, pooled_part, cotangent):
    words, quarter = pooled_part.shape[0], cotangent.shape[0]
    items = [(s, 1, 0, 0, words, 0, i * words) for i, s in enumerate(CNN)]
    items += [(s, 2 + s // 2, 1, 0, quarter, 1, s % 2 * quarter) for s in range(4)]
    transfers = Transfers(items)

    def kernel(pooled_ref, cot_ref, p_ref, pooled, cot, w0, w1, wp, vec_ref, vec, raw, sems, send, recv):
        matrix, vectors, chunks = cut_tools(p_ref, raw, sems)

        def work():
            def matrices():
                chunks(0, w0, 256)
                chunks(HW_W1, w1, 256)
                matrix(PROJ_W, wp, 512)

            vectors([(HW_BIAS0, 2 * CONV), (HW_BIAS1, 2 * CONV), (PROJ_B, D)], vec, vec_ref, matrices)

        transfers.run((pooled_ref, cot_ref), (pooled, cot), send, recv, {1: work})

    shapes = [(words * len(CNN), CONV), (2 * quarter, D), HW_SHAPE, HW_SHAPE, (CONV, D)]
    return pl.pallas_call(
        kernel,
        out_shape=[jax.ShapeDtypeStruct(s, BF) for s in shapes] + [jax.ShapeDtypeStruct((8, 2 * CONV), F32)],
        in_specs=[hbm()] * 3,
        out_specs=[hbm()] * 6,
        scratch_shapes=[
            pltpu.VMEM((8, 2 * CONV), F32),
            pltpu.VMEM((5, 1, 2 * CONV), BF),
            pltpu.SemaphoreType.DMA((5,)),
            pltpu.SemaphoreType.DMA((len(items),)),
            pltpu.SemaphoreType.DMA((len(items),)),
        ],
        compiler_params=pltpu.CompilerParams(
            collective_id=4, has_side_effects=True, vmem_limit_bytes=40 << 20
        ),
    )(pooled_part, cotangent, params)


def start_encoder(params):
    shapes = [(D, 3 * D), (D, D), (D, FF), (FF, D)]
    owners = (2, 2, 3, 3)
    items = [(s, 5 - s, i, 0, shape[0], i, 0) for i, (s, shape) in enumerate(zip(owners, shapes, strict=True))]
    items += [(2, 3, 4, 0, 8, 4, 0), (3, 2, 5, 0, 8, 5, 0)]
    transfers = Transfers(items)

    def kernel(p_ref, wqkv, wo, wu, wd, vec2, vec3, vec, raw, sems, send, recv):
        matrix, vectors, _ = cut_tools(p_ref, raw, sems)

        def work2():
            def matrices():
                matrix(0, wqkv, 256)
                matrix(OUT_W, wo, 384)

            entries = [(Q_BIAS, D), (V_BIAS, D), (OUT_B, D), (OUT_B + D, D), (OUT_B + 2 * D, D)]
            vectors(entries, vec, vec2, matrices)

        def work3():
            def matrices():
                matrix(0, wu, 256)
                matrix(DOWN_W, wd, 512)

            vectors([(UP_B, FF), (DOWN_B, D), (DOWN_B + D, D), (DOWN_B + 2 * D, D)], vec, vec3, matrices)

        outputs = (wqkv, wo, wu, wd, vec2, vec3)
        transfers.run(outputs, outputs, send, recv, {2: work2, 3: work3})

    return pl.pallas_call(
        kernel,
        out_shape=[jax.ShapeDtypeStruct(s, BF) for s in shapes] + [jax.ShapeDtypeStruct((8, 2 * CONV), F32)] * 2,
        in_specs=[hbm()],
        out_specs=[hbm()] * 6,
        scratch_shapes=[
            pltpu.VMEM((8, 2 * CONV), F32),
            pltpu.VMEM((5, 1, 2 * CONV), BF),
            pltpu.SemaphoreType.DMA((5,)),
            pltpu.SemaphoreType.DMA((len(items),)),
            pltpu.SemaphoreType.DMA((len(items),)),
        ],
        compiler_params=pltpu.CompilerParams(
            collective_id=5, has_side_effects=True, vmem_limit_bytes=40 << 20
        ),
    )(params)


CNN_ROWS = 1600
TABLE_ROWS = 384


def cnn_params_kernel(p_ref, ck_ref, tt_ref, raw, flat, kernel, table, sem, send, recv):
    section = lax.axis_index("section")
    others = [s for s in CNN if s]
    lane = lax.broadcasted_iota(jnp.int32, (1, LANES), 1)
    barrier = pltpu.get_barrier_semaphore()

    @pl.when(section == 0)
    def _():
        copy = pltpu.make_async_copy(p_ref.at[:, pl.ds(0, CNN_ROWS * LANES)], raw, sem)
        copy.start()
        for s in others:
            pl.semaphore_signal(barrier, inc=1, device_id={"section": s}, device_id_type=MESH)
        copy.wait()
        flat[...] = as_float(raw[...]).reshape(CNN_ROWS, LANES)
        table[...] = jnp.zeros_like(table)
        head = flat[0:40, :]
        for b in range(8):
            mixed = jnp.zeros_like(head)
            for g in range(7):
                rolled = head if g == b else pltpu.roll(head, (g - b) * CHAR_DIM % LANES, 1)
                mixed = jnp.where((lane >= g * CHAR_DIM) & (lane < (g + 1) * CHAR_DIM), rolled, mixed)
            table[pl.ds(b, 33, stride=8), :] = mixed[0:33]
        tt_ref[...] = to_low(table[...])
        rolled = pltpu.roll(flat[...], 32, 1)
        flat[...] = rolled
        count = CNN_ROWS - 40
        flat[0:count, :] = jnp.where(
            lane < 32, flat[32 : 32 + count, :], flat[33 : 33 + count, :]
        )
        kernel[...] = jnp.zeros_like(kernel)
        first, second, third = flat[0:8, :], flat[4:12, :], flat[12:36, :]
        narrow = lax.broadcasted_iota(jnp.int32, (8, LANES), 0) < 4
        for b in range(4):
            one = first if b == 0 else pltpu.roll(first, -b * 32 % LANES, 1)
            two = second if b == 1 else pltpu.roll(second, (32 - b * 32) % LANES, 1)
            kernel[0, pl.ds(b, 8, stride=4), :] = jnp.where(
                lane < 32, jnp.where(narrow, one, 0.0), jnp.where(lane < 64, two, 0.0)
            )
        for b in range(2):
            three = third if b == 1 else pltpu.roll(third, 64, 1)
            kernel[0, pl.ds(b, 24, stride=2), :] = jnp.where(
                lane >= 64, three, kernel[0, pl.ds(b, 24, stride=2), :]
            )
        row, tile = 36, 1
        for number in range(3, 7):
            parts = channel_steps[number] * CH_UNIT // LANES
            depth = (number + 1) * CHAR_DIM
            for c in range(parts):
                kernel[tile, 0:depth, :] = flat[pl.ds(row + c, depth, stride=parts), :]
                tile += 1
            row += depth * parts
        bound = 0
        for number in range(7):
            upper = bound + channel_steps[number] * CH_UNIT
            for c in range(bound // LANES, -(-upper // LANES)):
                kernel[c, 112 + number : 113 + number, :] = jnp.where(
                    (lane + c * LANES >= bound) & (lane + c * LANES < upper), -HUGE, 0.0
                )
            bound = upper
        for c in range(CONV // LANES):
            kernel[c, 119:120, :] = flat[row + c : row + c + 1, :]
            ck_ref[:, c * LANES : (c + 1) * LANES] = to_low(kernel[c])
        pl.semaphore_wait(barrier, len(others))
        copies = []
        for i, s in enumerate(others):
            for j, ref in enumerate((ck_ref, tt_ref)):
                copies.append(
                    pltpu.make_async_remote_copy(
                        ref, ref, send.at[i, j], recv.at[j], device_id={"section": s}, device_id_type=MESH
                    )
                )
        for copy in copies:
            copy.start()
        for copy in copies:
            copy.wait_send()

    for s in others:

        @pl.when(section == s)
        def _():
            pl.semaphore_signal(barrier, inc=1, device_id={"section": 0}, device_id_type=MESH)
            pl.semaphore_wait(barrier, 1)
            for j, ref in enumerate((ck_ref, tt_ref)):
                pltpu.make_async_remote_copy(
                    ref, ref, send.at[0, j], recv.at[j], device_id={"section": 0}, device_id_type=MESH
                ).wait_recv()


def cnn_params(params):
    return pl.pallas_call(
        cnn_params_kernel,
        out_shape=[
            jax.ShapeDtypeStruct((LANES, CONV), BF),
            jax.ShapeDtypeStruct((TABLE_ROWS, LANES), BF),
        ],
        in_specs=[hbm()],
        out_specs=[vmem(), vmem()],
        scratch_shapes=[
            pltpu.VMEM((1, CNN_ROWS * LANES), BF),
            pltpu.VMEM((CNN_ROWS, LANES), F32),
            pltpu.VMEM((CONV // LANES, LANES, LANES), F32),
            pltpu.VMEM((TABLE_ROWS, LANES), F32),
            pltpu.SemaphoreType.DMA,
            pltpu.SemaphoreType.DMA((len(CNN) - 1, 2)),
            pltpu.SemaphoreType.DMA((2,)),
        ],
        compiler_params=pltpu.CompilerParams(
            collective_id=0, has_side_effects=True, vmem_limit_bytes=24 << 20
        ),
    )(params)


STAGES = ((128, 1), (64, 2), (16, 8))
SPOTS = CHAR_LEN + 14


def stage_bounds(lengths, blocks):
    words = lengths.shape[0] // blocks
    counts = jnp.sum(lengths.reshape(blocks, words, 1) > jnp.arange(CHAR_LEN, dtype=jnp.int32), axis=1)
    limits = jnp.array([[words // 2], [words // 8], [0]], jnp.int32)
    return jnp.sum(counts[:, None, :] > limits, axis=2).astype(jnp.int32)


def sorting(column_ref, row_ref):
    count = row_ref.shape[1]
    down = lax.broadcasted_iota(jnp.int32, (count, count), 0)
    across = lax.broadcasted_iota(jnp.int32, (count, count), 1)
    column, row = column_ref[...], row_ref[...]
    before = (column > row) | ((column == row) & (down < across))
    rank = jnp.sum(jnp.where(before, 1, 0), axis=0, keepdims=True)
    return jnp.where(down == rank, 1.0, 0.0).astype(BF)


def sorted_words(order, ids_ref, column_ref):
    ids = ids_ref[...]
    high = lax.div(ids, 16)
    low = ids - 16 * high
    ids = matmul(order, to_low(as_float(high))) * 16.0 + matmul(order, to_low(as_float(low)))
    length = matmul(order, to_low(as_float(jnp.broadcast_to(column_ref[...], (ids.shape[0], LANES)))))
    return ids, length


def stages(ends_ref, body):
    start = 0
    for k, (words, positions) in enumerate(STAGES):
        end = ends_ref[k]

        def one(i, unused, words=words, positions=positions, start=start, end=end):
            body(start + i * positions, words, positions, end)
            return unused

        lax.fori_loop(0, lax.div(jnp.maximum(end - start, 0) + positions - 1, positions), one, 0)
        start = end


def one_hot(first, words, positions, ids):
    lane = lax.broadcasted_iota(jnp.int32, (words, CHAR_LEN), 1)
    columns = [
        jnp.sum(jnp.where(lane == first + q, ids[0:words, :], 0.0), axis=1, keepdims=True) for q in range(positions)
    ]
    column = columns[0] if positions == 1 else jnp.concatenate(columns, axis=0)
    symbol = lax.broadcasted_iota(jnp.int32, (words * positions, TABLE_ROWS), 1)
    return jnp.where(column.astype(jnp.int32) == symbol, 1.0, 0.0).astype(BF)


def windows(first, words, positions, end, length, embedded, masks):
    total = None
    for j in range(7):
        term = embedded[pl.ds(first + j, positions), 0:words, :] * masks[j]
        total = term if total is None else total + term
    shape = (positions, words, LANES)
    lane = lax.broadcasted_iota(jnp.int32, shape, 2)
    position = first + lax.broadcasted_iota(jnp.int32, shape, 0)
    room = jnp.broadcast_to(length[0:words, :][None], shape)
    out = (lane >= 112) & (lane < 119) & ((as_float(position + lane - 111) > room) | (position >= end))
    return (total + jnp.where(out | (lane == 119), 1.0, 0.0).astype(BF)).reshape(positions * words, LANES)


def lane_masks():
    lane = lax.broadcasted_iota(jnp.int32, (1, 1, LANES), 2)
    return [
        jnp.where((lane >= j * CHAR_DIM) & (lane < (j + 1) * CHAR_DIM), 1.0, 0.0).astype(BF)
        for j in range(7)
    ]


def embedder(ids, tt_ref, embedded):
    def embed(first, words, positions, end):
        value = to_low(matmul(one_hot(first, words, positions, ids), tt_ref[...]))
        embedded[pl.ds(first, positions), 0:words, :] = value.reshape(positions, words, LANES)

    return embed


def chars_forward_kernel(ends_ref, ids_ref, column_ref, row_ref, ck_ref, tt_ref, out_ref, embedded, best):
    embedded[...] = jnp.zeros_like(embedded)
    best[...] = jnp.full_like(best, -HUGE)
    masks = lane_masks()
    order = sorting(column_ref, row_ref)
    ids, length = sorted_words(order, ids_ref, column_ref)
    stages(ends_ref, embedder(ids, tt_ref, embedded))

    def pool(first, words, positions, end):
        rows = windows(first, words, positions, end, length, embedded, masks)
        for c in range(0, CONV, 512):
            pre = jnp.max(matmul(rows, ck_ref[:, c : c + 512]).reshape(positions, words, 512), axis=0)
            best[0:words, c : c + 512] = jnp.maximum(best[0:words, c : c + 512], pre)

    stages(ends_ref, pool)
    out_ref[...] = to_low(matmul_tn(order, to_low(jnp.maximum(best[...], 0.0))))


def chars_backward_kernel(
    all_ends_ref, ids_ref, column_ref, row_ref, ck_ref, tt_ref, grad_ref,
    out_ref, embedded, best, share, backs, sums,
):
    block = pl.program_id(0)
    ends_ref = [all_ends_ref[block, k] for k in range(len(STAGES))]
    embedded[...] = jnp.zeros_like(embedded)
    backs[...] = jnp.zeros_like(backs)
    best[...] = jnp.full_like(best, -HUGE)
    share[...] = jnp.zeros_like(share)
    table_rows = pl.ds(CONV, TABLE_ROWS)

    @pl.when(block == 0)
    def _():
        sums[...] = jnp.zeros_like(sums)
        out_ref[table_rows, :] = jnp.zeros((TABLE_ROWS, LANES), F32)

    masks = lane_masks()
    order = sorting(column_ref, row_ref)
    ids, length = sorted_words(order, ids_ref, column_ref)
    stages(ends_ref, embedder(ids, tt_ref, embedded))

    def count(first, words, positions, end):
        rows = windows(first, words, positions, end, length, embedded, masks)
        for c in range(0, CONV, 512):
            part = slice(c, c + 512)
            pre = matmul(rows, ck_ref[:, part])
            top, hits = best[0:words, part], share[0:words, part]
            for q in range(positions):
                here = pre[q * words : (q + 1) * words]
                hits = jnp.where(here > top, 1.0, hits + jnp.where(here == top, 1.0, 0.0))
                top = jnp.maximum(top, here)
            best[0:words, part], share[0:words, part] = top, hits

    stages(ends_ref, count)
    share[...] = matmul(order, grad_ref[...]) / share[...]
    best[...] = jnp.where(best[...] > 0.0, best[...], 3e38)

    def spread(first, words, positions, end):
        rows = windows(first, words, positions, end, length, embedded, masks)
        back = jnp.zeros((words * positions, LANES), F32)
        for c in range(0, CONV, 512):
            part = slice(c, c + 512)
            pre = matmul(rows, ck_ref[:, part]).reshape(positions, words, 512)
            hit = pre == best[0:words, part][None]
            grad = to_low(jnp.where(hit, jnp.broadcast_to(share[0:words, part][None], pre.shape), 0.0))
            grad = grad.reshape(positions * words, 512)
            sums[:, part] += matmul_tn(rows, grad)
            back = back + matmul_nt(grad, ck_ref[:, part])
        backs[pl.ds(first + 6, positions), 0:words, :] = to_low(back).reshape(positions, words, LANES)

    stages(ends_ref, spread)

    def gather(first, words, positions, end):
        shape = (positions, words, LANES)
        lane = lax.broadcasted_iota(jnp.int32, shape, 2)
        position = first + lax.broadcasted_iota(jnp.int32, shape, 0)
        total = jnp.zeros(shape, F32)
        for j in range(7):
            here = (lane >= j * CHAR_DIM) & (lane < (j + 1) * CHAR_DIM) & (position < end)
            total = jnp.where(here, as_float(backs[pl.ds(first + 6 - j, positions), 0:words, :]), total)
        hot = one_hot(first, words, positions, ids)
        out_ref[table_rows, :] += matmul_tn(hot, to_low(total).reshape(positions * words, LANES))

    stages(ends_ref, gather)

    @pl.when(block == pl.num_programs(0) - 1)
    def _():
        for c in range(CONV // LANES):
            out_ref[c * LANES : (c + 1) * LANES, :] = sums[:, c * LANES : (c + 1) * LANES]


def chars_forward(ends, ids, column, row, ck, tt):
    words = ids.shape[0]
    return pl.pallas_call(
        chars_forward_kernel,
        out_shape=jax.ShapeDtypeStruct((words, CONV), BF),
        in_specs=[pl.BlockSpec(memory_space=pltpu.SMEM)] + [vmem()] * 5,
        out_specs=vmem(),
        scratch_shapes=[
            pltpu.VMEM((SPOTS, words, LANES), BF),
            pltpu.VMEM((words, CONV), F32),
        ],
        compiler_params=pltpu.CompilerParams(vmem_limit_bytes=32 << 20),
    )(ends, ids, column, row, ck, tt)


def chars_backward(ends, ids, column, row, ck, tt, grad):
    words = ids.shape[0] // len(CNN)
    return pl.pallas_call(
        chars_backward_kernel,
        grid=(len(CNN),),
        out_shape=jax.ShapeDtypeStruct((CNN_GRADS, LANES), F32),
        in_specs=[
            pl.BlockSpec(memory_space=pltpu.SMEM),
            pl.BlockSpec((words, CHAR_LEN), lambda i: (i, 0)),
            pl.BlockSpec((words, 1), lambda i: (i, 0)),
            pl.BlockSpec((1, words), lambda i: (0, i)),
            pl.BlockSpec((LANES, CONV), lambda i: (0, 0)),
            pl.BlockSpec((TABLE_ROWS, LANES), lambda i: (0, 0)),
            pl.BlockSpec((words, CONV), lambda i: (i, 0)),
        ],
        out_specs=pl.BlockSpec((CNN_GRADS, LANES), lambda i: (0, 0)),
        scratch_shapes=[
            pltpu.VMEM((SPOTS, words, LANES), BF),
            pltpu.VMEM((words, CONV), F32),
            pltpu.VMEM((words, CONV), F32),
            pltpu.VMEM((SPOTS, words, LANES), BF),
            pltpu.VMEM((LANES, CONV), F32),
        ],
        compiler_params=pltpu.CompilerParams(vmem_limit_bytes=40 << 20),
    )(ends, ids, column, row, ck, tt, grad)


def cnn_gradient(grads):
    table_grad = grads[CONV:]
    kernel_grad = jnp.swapaxes(grads[:CONV].reshape(-1, LANES, LANES), 0, 1).reshape(LANES, CONV)
    pieces = [
        sum(table_grad[:CHARS, g * CHAR_DIM : (g + 1) * CHAR_DIM] for g in range(7)).reshape(-1)
    ]
    offset = 0
    for number in range(7):
        channels = channel_steps[number] * CH_UNIT
        pieces.append(
            kernel_grad[: (number + 1) * CHAR_DIM, offset : offset + channels].reshape(-1)
        )
        offset += channels
    pieces.append(kernel_grad[119])
    return jnp.concatenate(pieces)


def sigmoid(value):
    return 1.0 / (1.0 + jnp.exp(-value))


def highway_layer_kernel(row, x_ref, part_ref, w_ref, bl_ref, br_ref, next_ref, left_ref, right_ref):
    both = matmul(x_ref[...], w_ref[0])
    left = both[:, :HW_CHUNK] + bl_ref[row : row + 1, :]
    right = both[:, HW_CHUNK:] + br_ref[row : row + 1, :]
    left_ref[...] = left
    right_ref[...] = right
    gate = sigmoid(right)
    next_ref[...] = to_low(gate * as_float(part_ref[...]) + (1.0 - gate) * jnp.maximum(left, 0.0))


def highway_layer(row, x, w, vec):
    group = x.shape[0]
    steps = CONV // HW_CHUNK
    part = pl.BlockSpec((group, HW_CHUNK), lambda i: (0, i))
    return pl.pallas_call(
        functools.partial(highway_layer_kernel, row),
        grid=(steps,),
        out_shape=[
            jax.ShapeDtypeStruct((group, CONV), BF),
            jax.ShapeDtypeStruct((group, CONV), F32),
            jax.ShapeDtypeStruct((group, CONV), F32),
        ],
        in_specs=[
            pl.BlockSpec((group, CONV), lambda i: (0, 0)),
            part,
            pl.BlockSpec((1,) + HW_SHAPE[1:], lambda i: (i, 0, 0)),
            pl.BlockSpec((8, HW_CHUNK), lambda i: (0, i)),
            pl.BlockSpec((8, HW_CHUNK), lambda i: (0, i + steps)),
        ],
        out_specs=[part, part, part],
        compiler_params=pltpu.CompilerParams(vmem_limit_bytes=40 << 20),
    )(x, x, w, vec, vec)


def highway_forward(w0, w1, wp, vec, wide_in):
    x1, left0, right0 = highway_layer(0, wide_in, w0, vec)
    x2, left1, right1 = highway_layer(1, x1, w1, vec)
    projected = to_low(matmul(x2, wp) + vec[2, :D])
    return (projected, x1, x2, left0, right0, left1, right1)


def highway_back_kernel(last, up_ref, wp_ref, x_ref, left_ref, right_ref, w_ref, grad_ref, out_ref, total):
    i = pl.program_id(0)
    flowing = matmul_nt(up_ref[...], wp_ref[...]) if wp_ref is not None else up_ref[...]
    gate = sigmoid(right_ref[...])
    left = left_ref[...]
    nonlinear = jnp.maximum(left, 0.0)
    closed = flowing * (1.0 - gate)
    grad_left = to_low(jnp.where(left > 0.0, closed, 0.0))
    grad_right = to_low(closed * (as_float(x_ref[...]) - nonlinear) * gate)
    grad_ref[0] = grad_left
    grad_ref[1] = grad_right
    back = matmul_nt(jnp.concatenate([grad_left, grad_right], axis=1), w_ref[0])

    @pl.when(i == 0)
    def _():
        total[...] = back

    @pl.when(i > 0)
    def _():
        total[...] += back

    here = pl.ds(pl.multiple_of(i * HW_CHUNK, HW_CHUNK), HW_CHUNK)
    total[:, here] += flowing * gate

    @pl.when(i == pl.num_programs(0) - 1)
    def _():
        out_ref[...] = to_low(total[...]) if last else total[...]


def highway_back(last, up, wp, x, left, right, w):
    group = x.shape[0]
    steps = CONV // HW_CHUNK
    part = pl.BlockSpec((group, HW_CHUNK), lambda i: (0, i))
    if wp is None:
        kernel = lambda up_ref, *refs: highway_back_kernel(last, up_ref, None, *refs)
        sources, specs = [up], [part]
    else:
        kernel = functools.partial(highway_back_kernel, last)
        sources = [up, wp]
        specs = [pl.BlockSpec((group, D), lambda i: (0, 0)), pl.BlockSpec((HW_CHUNK, D), lambda i: (i, 0))]
    return pl.pallas_call(
        kernel,
        grid=(steps,),
        out_shape=[
            jax.ShapeDtypeStruct((2, group, CONV), BF),
            jax.ShapeDtypeStruct((group, CONV), BF if last else F32),
        ],
        in_specs=specs
        + [
            part,
            part,
            part,
            pl.BlockSpec((1,) + HW_SHAPE[1:], lambda i: (i, 0, 0)),
        ],
        out_specs=[
            pl.BlockSpec((2, group, HW_CHUNK), lambda i: (0, 0, i)),
            pl.BlockSpec((group, CONV), lambda i: (0, 0)),
        ],
        scratch_shapes=[pltpu.VMEM((group, CONV), F32)],
        compiler_params=pltpu.CompilerParams(vmem_limit_bytes=40 << 20),
    )(*sources, x, left, right, w)


def highway_backward(w0, w1, wp, wide_in, x1, left0, right0, left1, right1, upstream):
    grad1, flowing = highway_back(False, upstream, wp, x1, left1, right1, w1)
    grad0, grad_pooled = highway_back(True, flowing, None, wide_in, left0, right0, w0)
    return (grad_pooled, grad0, grad1)


def layer_norm(residual):
    centered = residual - jnp.mean(residual, axis=-1, keepdims=True)
    inverse = lax.rsqrt(jnp.mean(centered * centered, axis=-1, keepdims=True) + layer_eps)
    return centered * inverse, inverse


def norm_backward(upstream, scaled, inverse, gain):
    weighted = upstream * gain
    first_mean = jnp.mean(weighted, axis=-1, keepdims=True)
    cross_mean = jnp.mean(weighted * scaled, axis=-1, keepdims=True)
    return inverse * (weighted - first_mean - scaled * cross_mean)


def encoder_kernel(
    x_ref, cot_ref, wqkv_ref, wo_ref, wu_ref, wd_ref, vec_ref, vec3_ref,
    layer_ref, back_ref, joined_ref, mixed_ref, att_ref, normed_ref, act_ref, inner_ref, branch_ref, sums_ref,
    qkv, probs, slope, scaled, carry,
):
    rows = x_ref.shape[0]
    pairs = HEADS // 2
    scale = HEAD_DIM ** (-0.5)
    lane = lax.broadcasted_iota(jnp.int32, (1, LANES), 1)
    halves = [jnp.where(lane < HEAD_DIM, 1.0, 0.0).astype(BF), jnp.where(lane < HEAD_DIM, 0.0, 1.0).astype(BF)]

    def heads(body):
        def one(i, unused):
            sequence, pair = lax.div(i, pairs), lax.rem(i, pairs)
            body(
                pl.ds(pl.multiple_of(sequence * SEQ_LEN, SEQ_LEN), SEQ_LEN),
                [pl.ds(pl.multiple_of(pair * LANES + k * D, LANES), LANES) for k in range(3)],
                i,
            )
            return unused

        lax.fori_loop(0, rows // SEQ_LEN * pairs, one, 0, unroll=True)

    def pieces(width, body):
        def one(i, unused):
            body(pl.ds(pl.multiple_of(i * width, width), width))
            return unused

        return lambda count: lax.fori_loop(0, count, one, 0, unroll=True)

    @pl.when(lax.axis_index("section") >= 2)
    def _():
        for k, bias in enumerate((vec_ref[0:1, 0:D], None, vec_ref[1:2, 0:D])):
            part = matmul(x_ref[...], wqkv_ref[:, k * D : (k + 1) * D])
            qkv[:, k * D : (k + 1) * D] = to_low(part if bias is None else part + bias)

        def attend(here, columns, i):
            query, key, value = (qkv[here, columns[k]] for k in range(3))
            out = []
            for half in range(2):
                scores = matmul_nt(query * halves[half], key) * scale
                exponent = jnp.exp(scores - jnp.max(scores, axis=-1, keepdims=True))
                soft = exponent / jnp.sum(exponent, axis=-1, keepdims=True)
                probs[2 * i + half] = soft
                out.append(matmul(to_low(soft), value))
            mixed_ref[here, columns[0]] = to_low(jnp.where(lane < HEAD_DIM, out[0], out[1]))

        heads(attend)
        residual = as_float(x_ref[...]) + matmul(mixed_ref[...], wo_ref[...]) + vec_ref[2:3, 0:D]
        scaled1, inverse1 = layer_norm(residual)
        scaled[...] = scaled1
        normed_ref[...] = to_low(scaled1 * vec_ref[3:4, 0:D] + vec_ref[4:5, 0:D])

        def up(part):
            inner = matmul(normed_ref[...], wu_ref[:, part]) + vec3_ref[0:1, part]
            phi = 0.5 * (1.0 + lax.erf(inner * 0.7071067811865476))
            act_ref[:, part] = to_low(inner * phi)
            slope[:, part] = phi + inner * jnp.exp(-0.5 * inner * inner) * 0.3989422804014327

        pieces(512, up)(FF // 512)
        residual = as_float(normed_ref[...]) + matmul(act_ref[...], wd_ref[...]) + vec3_ref[1:2, 0:D]
        scaled2, inverse2 = layer_norm(residual)
        gain2 = vec3_ref[2:3, 0:D]
        layer_ref[...] = to_low(scaled2 * gain2 + vec3_ref[3:4, 0:D])
        upstream = as_float(cot_ref[...])
        sums_ref[2:3, :] = jnp.sum(upstream * scaled2, axis=0, keepdims=True)
        sums_ref[3:4, :] = jnp.sum(upstream, axis=0, keepdims=True)
        carry[...] = norm_backward(upstream, scaled2, inverse2, gain2)
        branch_ref[...] = to_low(carry[...])

        def down(part):
            inner_ref[:, part] = to_low(matmul_nt(branch_ref[...], wd_ref[part, :]) * slope[:, part])

        pieces(512, down)(FF // 512)
        upstream = as_float(to_low(carry[...] + matmul_nt(inner_ref[...], wu_ref[...])))
        sums_ref[0:1, :] = jnp.sum(upstream * scaled[...], axis=0, keepdims=True)
        sums_ref[1:2, :] = jnp.sum(upstream, axis=0, keepdims=True)
        carry[...] = norm_backward(upstream, scaled[...], inverse1, vec_ref[3:4, 0:D])
        att_ref[...] = to_low(carry[...])
        back_ref[...] = to_low(matmul_nt(att_ref[...], wo_ref[...]))

        def attend_back(here, columns, i):
            query, key, value = (qkv[here, columns[k]] for k in range(3))
            grad = back_ref[here, columns[0]]
            totals = [0.0, 0.0, 0.0]
            for half in range(2):
                grad_half = grad * halves[half]
                soft = probs[2 * i + half]
                grad_soft = matmul_nt(grad_half, value)
                flow = to_low(soft * (grad_soft - jnp.sum(grad_soft * soft, axis=-1, keepdims=True)))
                totals[0] += matmul(flow, key * halves[half])
                totals[1] += matmul_tn(flow, query * halves[half])
                totals[2] += matmul_tn(to_low(soft), grad_half)
            joined_ref[here, columns[0]] = to_low(totals[0] * scale)
            joined_ref[here, columns[1]] = to_low(totals[1] * scale)
            joined_ref[here, columns[2]] = to_low(totals[2])

        heads(attend_back)
        back_ref[...] = to_low(carry[...] + matmul_nt(joined_ref[...], wqkv_ref[...]))


def encoder(x, cot, wqkv, wo, wu, wd, vec, vec3):
    rows = x.shape[0]
    widths = [D, D, 3 * D, D, D, D, FF, FF, D]
    return pl.pallas_call(
        encoder_kernel,
        out_shape=[jax.ShapeDtypeStruct((rows, w), BF) for w in widths] + [jax.ShapeDtypeStruct((8, D), F32)],
        in_specs=[vmem()] * 8,
        out_specs=[vmem()] * 10,
        scratch_shapes=[
            pltpu.VMEM((rows, 3 * D), BF),
            pltpu.VMEM((rows // SEQ_LEN * HEADS, SEQ_LEN, SEQ_LEN), F32),
            pltpu.VMEM((rows, FF), F32),
            pltpu.VMEM((rows, D), F32),
            pltpu.VMEM((rows, D), F32),
        ],
        compiler_params=pltpu.CompilerParams(vmem_limit_bytes=56 << 20),
    )(x, cot, wqkv, wo, wu, wd, vec, vec3)


def side_rows_kernel(*refs):
    section = lax.axis_index("section")
    own, other, (out_hbm, flat, out_ref, *targets, sem) = refs[:9], refs[9:18], refs[18:]
    x_ref, mixed_ref, joined_ref, att_ref, normed_ref, act_ref, inner_ref, branch_ref, sums_ref = targets

    def fetch(*places):
        copies = []
        for i in places:
            rows = own[i].shape[0]
            for k, source in enumerate((own[i], other[i])):
                copies.append(pltpu.make_async_copy(source, targets[i].at[pl.ds(k * rows, rows)], sem.at[k, i]))
        for copy in copies:
            copy.start()
        for copy in copies:
            copy.wait()

    def product(left_ref, right_ref, row):
        count, width = left_ref.shape[1], right_ref.shape[1]
        parts = width // LANES
        for k in range(count // D):
            for c in range(0, width, 256):
                block = matmul_tn(left_ref[:, k * D : (k + 1) * D], right_ref[:, c : c + 256])
                for t in range(2):
                    flat[pl.ds(row + k * D * parts + c // LANES + t, D, stride=parts), :] = block[:, t * LANES : (t + 1) * LANES]
        return row + count * parts

    def line(row, values):
        for c in range(values.shape[1] // LANES):
            flat[row + c : row + c + 1, :] = values[:, c * LANES : (c + 1) * LANES]
        return row + values.shape[1] // LANES

    def summed(ref, first, last):
        return jnp.sum(as_float(ref[:, first:last]), axis=0, keepdims=True)

    def write(row):
        full = out_ref.shape[0]
        flat[row:full, :] = jnp.zeros((full - row, LANES), F32)
        out_ref[...] = to_low(flat[...])
        copy = pltpu.make_async_copy(out_ref, out_hbm, sem.at[0, 0])
        copy.start()
        copy.wait()

    @pl.when(section == 2)
    def _():
        fetch(0, 1, 2, 3, 8)
        row = product(x_ref, joined_ref, 0)
        row = line(row, summed(joined_ref, 0, D))
        row = line(row, summed(joined_ref, 2 * D, 3 * D))
        row = product(mixed_ref, att_ref, row)
        row = line(row, summed(att_ref, 0, D))
        row = line(row, sums_ref[0:1, :] + sums_ref[8:9, :])
        write(line(row, sums_ref[1:2, :] + sums_ref[9:10, :]))

    @pl.when(section == 3)
    def _():
        fetch(4, 5, 6, 7, 8)
        row = product(normed_ref, inner_ref, 0)
        row = line(row, summed(inner_ref, 0, FF))
        row = product(act_ref, branch_ref, row)
        row = line(row, summed(branch_ref, 0, D))
        row = line(row, sums_ref[2:3, :] + sums_ref[10:11, :])
        write(line(row, sums_ref[3:4, :] + sums_ref[11:12, :]))


def side_rows(own, other):
    size = (SIDE_SHARE + SIDE_ROWS * SIDE_CHUNKS, LANES)
    return pl.pallas_call(
        side_rows_kernel,
        out_shape=jax.ShapeDtypeStruct(size, BF),
        in_specs=[hbm()] * (2 * len(own)),
        out_specs=hbm(),
        scratch_shapes=[pltpu.VMEM(size, F32), pltpu.VMEM(size, BF)]
        + [pltpu.VMEM((2 * value.shape[0], value.shape[1]), value.dtype) for value in own]
        + [pltpu.SemaphoreType.DMA((2, len(own)))],
        compiler_params=pltpu.CompilerParams(vmem_limit_bytes=50 << 20),
    )(*own, *other)


def stack_kernel(x0_ref, x1_ref, x2_ref, xt_hbm, x2t_hbm, low, turned, sem):
    group = x0_ref.shape[0]

    @pl.when(lax.axis_index("section") == 1)
    def _():
        turned[CONV:STACK, :] = jnp.where(
            lax.broadcasted_iota(jnp.int32, (STACK - CONV, group), 0) == 0, 1.0, 0.0
        ).astype(BF)
        targets = (xt_hbm.at[pl.ds(0, STACK)], xt_hbm.at[pl.ds(STACK, STACK)], x2t_hbm)
        for source, target in zip((x0_ref, x1_ref, x2_ref), targets, strict=True):
            copy = pltpu.make_async_copy(source, low, sem)
            copy.start()
            copy.wait()
            for c in range(0, CONV, 512):
                turned[c : c + 512, :] = low[:, c : c + 512].T
            copy = pltpu.make_async_copy(turned, target, sem)
            copy.start()
            copy.wait()


def stack_highways(x0, x1, x2):
    group = x0.shape[0]
    return pl.pallas_call(
        stack_kernel,
        out_shape=[jax.ShapeDtypeStruct((2 * STACK, group), BF), jax.ShapeDtypeStruct((STACK, group), BF)],
        in_specs=[hbm()] * 3,
        out_specs=[hbm()] * 2,
        scratch_shapes=[
            pltpu.VMEM((group, CONV), BF),
            pltpu.VMEM((STACK, group), BF),
            pltpu.SemaphoreType.DMA,
        ],
        compiler_params=pltpu.CompilerParams(vmem_limit_bytes=24 << 20),
    )(x0, x1, x2)


SIDE_ROWS = 1200
SIDE_CHUNKS = 16
SIDE_REST = 1040
SIDE_SHARE = 17936


def side_part(
    share, row_ref, out_ref, own, y_in, z_in, z_out, total,
    y_send, y_recv, z_send, z_recv, l_send, l_recv, sem, turn,
):
    section = lax.axis_index("section")
    b = lax.axis_index("batch")
    y, z = lax.rem(b, 2), lax.div(b, 2)

    def count(half):
        return jnp.where((section == 2) & (half == 1), 1, SIDE_CHUNKS)

    def rows(half, i):
        return pl.ds(pl.multiple_of(half * share + i * SIDE_ROWS, 16), SIDE_ROWS)

    def y_copy(i):
        return pltpu.make_async_remote_copy(
            row_ref.at[rows(1 - y, i)], y_in.at[i], y_send.at[i], y_recv.at[i],
            device_id={"batch": b + 1 - 2 * y}, device_id_type=MESH,
        )

    def z_copy(i):
        return pltpu.make_async_remote_copy(
            z_out.at[i], z_in.at[i], z_send.at[i], z_recv.at[i],
            device_id={"batch": b - 2}, device_id_type=MESH,
        )

    def rest_copy():
        return pltpu.make_async_remote_copy(
            total.at[pl.ds(share, SIDE_REST)], total.at[pl.ds(0, SIDE_REST)], l_send, l_recv,
            device_id={"batch": 2}, device_id_type=MESH,
        )

    def write():
        copy = pltpu.make_async_copy(total.at[pl.ds(0, share)], out_ref, sem)
        copy.start()
        copy.wait()

    @pl.when(section != 1)
    def _():
        total[...] = jnp.zeros_like(total)

    @pl.when(section == 0)
    def _():
        write()

    @pl.when(section >= 2)
    def _():
        barrier = pltpu.get_barrier_semaphore()

        @pl.when(section == 3)
        def _():
            pl.semaphore_signal(barrier, inc=1, device_id={"section": 1}, device_id_type=MESH)

        pl.semaphore_signal(barrier, inc=1, device_id={"batch": b + 1 - 2 * y}, device_id_type=MESH)
        pairs = [(z > 0, b - 2), (z < Z - 1, b + 2), (b == 1, 2), (b == 2, 1)]
        for condition, other in pairs:

            @pl.when(condition)
            def _():
                pl.semaphore_signal(barrier, inc=1, device_id={"batch": other}, device_id_type=MESH)

        pl.semaphore_signal(barrier, inc=1, device_id={"section": 5 - section}, device_id_type=MESH)
        pl.semaphore_wait(barrier, 2 + sum(jnp.where(condition, 1, 0) for condition, _ in pairs))

        def send(i, carry):
            y_copy(i).start()
            return carry

        def combine(i, carry):
            copy = pltpu.make_async_copy(row_ref.at[rows(y, i)], own, sem)
            copy.start()
            copy.wait()
            y_copy(i).wait_recv()
            here = pl.ds(pl.multiple_of(i * SIDE_ROWS, 16), SIDE_ROWS)

            @pl.when(z == Z - 1)
            def _():
                z_out[i] = to_low(as_float(own[...]) + as_float(y_in[i]))

            @pl.when(z < Z - 1)
            def _():
                z_copy(i).wait_recv()

                @pl.when(z > 0)
                def _():
                    z_out[i] = to_low(as_float(own[...]) + as_float(y_in[i]) + as_float(z_in[i]))

                @pl.when(z == 0)
                def _():
                    total[here] = as_float(own[...]) + as_float(y_in[i]) + as_float(z_in[i])

            @pl.when(z > 0)
            def _():
                z_copy(i).start()

            return carry

        def drain(i, carry):
            y_copy(i).wait_send()
            return carry

        def drain_z(i, carry):
            z_copy(i).wait_send()
            return carry

        @pl.when(section == 2)
        def _():
            pl.semaphore_wait(turn, 1)

        lax.fori_loop(0, count(1 - y), send, 0)
        lax.fori_loop(0, count(y), combine, 0)

        @pl.when(section == 3)
        def _():
            pl.semaphore_signal(turn, inc=1, device_id={"section": 2}, device_id_type=MESH)

        @pl.when((section == 3) & (b == 1))
        def _():
            rest_copy().start()
            rest_copy().wait_send()

        @pl.when((section == 3) & (b == 2))
        def _():
            rest_copy().wait_recv()

        write()
        lax.fori_loop(0, count(1 - y), drain, 0)

        @pl.when(z > 0)
        def _():
            lax.fori_loop(0, count(y), drain_z, 0)


SLICE = 576
CHUNK = 256
N_CHUNK = 2 * CONV // CHUNK
N_FAR = 3
N_NEAR = N_CHUNK - N_FAR
N_TURN = 2
TURN_EVERY = 2
N_FIRST = N_NEAR - N_TURN
STACK = CONV + 16
LAG = 3
SLOTS = 4
FRONT = 80
Z = 4


def reduce_kernel(
    share, xt_hbm, x2t_hbm, g0_hbm, g1_hbm, gp_hbm, row_ref, out_ref, land_ref, far_ref,
    xt_ref, x2t_ref, g_ref, gp_ref, load, tile, flat, y_out, y_in, z_out, z_in, x_out, ret, t_out, t_in, t_send, t_recv,
    y_send, y_recv, z_send, z_recv, x_send, x_recv, r_send, r_recv, hello, sem, *side_scratch,
):
    own, side_y, side_z, side_out, *side_sems = side_scratch
    side_part(share, row_ref, out_ref, own, side_y, side_z, side_out, flat, *side_sems)
    section = lax.axis_index("section")
    b = lax.axis_index("batch")
    y, z = lax.rem(b, 2), lax.div(b, 2)
    def owner(step):
        o = lax.rem(step, Z)
        up = jnp.where(z == 0, 3 - o, jnp.where(o == 0, 3, jnp.where(o == 1, 0, jnp.where(o == 2, 2, 1))))
        down = jnp.where(z == 3, o, jnp.where(o == 0, 0, jnp.where(o == 1, 3, jnp.where(o == 2, 1, 2))))
        return jnp.where(z < 2, up, down)

    def product(part, j):
        column = pl.multiple_of(j * CHUNK, CHUNK)

        @pl.when((part != 3) & (part != 7))
        def _():
            row = pl.multiple_of((35 * part + jnp.where(part >= 4, 1, 0)) * 16, 16)
            col = pl.multiple_of(column + jnp.where(part >= 4, 2 * CONV, 0), CHUNK)
            tile[...] = matmul(xt_ref[pl.ds(row, SLICE), :], g_ref[:, pl.ds(col, CHUNK)])

        second = pl.ds(pl.multiple_of(column + 2 * CONV, CHUNK), CHUNK)

        @pl.when(part == 3)
        def _():
            tile[0:384, :] = matmul(xt_ref[1680:STACK, :], g_ref[:, pl.ds(column, CHUNK)])
            tile[384:SLICE, :] = matmul(xt_ref[STACK : STACK + SLICE - 384, :], g_ref[:, second])
            tile[376:384, :] = matmul(xt_ref[STACK + 192 : STACK + 208, :], g_ref[:, second])[0:8]

        @pl.when(part == 7)
        def _():
            tile[0:192, :] = matmul(xt_ref[2 * STACK - 192 : 2 * STACK, :], g_ref[:, second])

            @pl.when(j < 3)
            def _():
                third = pl.ds(pl.multiple_of(j * 256, 256), 256)
                tile[184:192, :] = matmul(x2t_ref[CONV:STACK, :], gp_ref[:, third])[0:8]

            @pl.when(j < 15)
            def _():
                row = pl.multiple_of(lax.rem(j, 5) * 384, 16)
                col = pl.multiple_of(lax.div(j, 5) * 256, 256)
                tile[192:SLICE, :] = matmul(x2t_ref[pl.ds(row, 384), :], gp_ref[:, pl.ds(col, 256)])

            @pl.when(j == 15)
            def _():
                for p in range(3):
                    tile[192 + 128 * p : 320 + 128 * p, :] = matmul(
                        x2t_ref[1920:CONV, :], gp_ref[:, p * 256 : (p + 1) * 256]
                    )

    def y_copy(part, j, slot):
        place = part * N_NEAR + j
        return pltpu.make_async_remote_copy(
            y_out.at[slot], y_in.at[place], y_send.at[slot], y_recv.at[place],
            device_id={"batch": b + 1 - 2 * y}, device_id_type=MESH,
        )

    def z_copy(part, j, o, down):
        place = part * N_CHUNK + j
        side = 0 if down else 1
        return pltpu.make_async_remote_copy(
            z_out.at[o], land_ref.at[side, place], z_send.at[o], z_recv.at[side, place],
            device_id={"batch": b - 2 if down else b + 2}, device_id_type=MESH,
        )

    def y_relay(part, j, slot):
        place = part * N_NEAR + j
        return pltpu.make_async_remote_copy(
            far_ref.at[(2 * part + 1 - y) * N_FAR + j], y_in.at[place], y_send.at[slot], y_recv.at[place],
            device_id={"batch": b + 1 - 2 * y}, device_id_type=MESH,
        )

    def x_copy(part, j, slot):
        place = part * N_FAR + j
        return pltpu.make_async_remote_copy(
            x_out.at[slot], far_ref.at[place], x_send.at[slot], x_recv.at[place],
            device_id={"section": 3}, device_id_type=MESH,
        )

    def back_copy(j):
        return pltpu.make_async_remote_copy(
            z_out.at[Z - 1], ret.at[j], r_send, r_recv.at[j], device_id={"section": 1}, device_id_type=MESH
        )

    def turn_copy(i):
        return pltpu.make_async_remote_copy(
            t_out.at[i], t_in.at[i], t_send.at[i], t_recv.at[i],
            device_id={"batch": b + 1 - 2 * y}, device_id_type=MESH,
        )

    def combine_turned(part, p, o):
        i, mine = lax.div(p, 2), lax.rem(p, 2)
        j = N_FIRST + p
        place = part * N_CHUNK + j
        above = (part <= z) & (z < Z - 1)
        below = (part >= z) & (z > 0)

        @pl.when(above)
        def _():
            arriving(0, place, 0)

        @pl.when(below)
        def _():
            arriving(1, place, 1)

        product(2 * part + jnp.where(mine == 1, y, 1 - y), N_FIRST + i)

        @pl.when(above)
        def _():
            arrived(0, place, 0)

        @pl.when(below)
        def _():
            arrived(1, place, 1)

        @pl.when((part == z) & (mine == 0))
        def _():
            t_out[i] = to_low(tile[...])
            turn_copy(i).start()

        @pl.when((part == z) & (mine == 1))
        def _():
            turn_copy(i).wait_recv()
            tile[...] += as_float(t_in[i])
            keep(N_FIRST + i)

        @pl.when(part != z)
        def _():
            @pl.when(p > 0)
            def _():
                z_copy(part, j, Z + o, True).wait_send()

            z_out[Z + o] = to_low(tile[...])

            @pl.when(part < z)
            def _():
                z_copy(part, j, Z + o, True).start()

            @pl.when(part > z)
            def _():
                z_copy(part, j, Z + o, False).start()

    def hops_to(part):
        return jnp.where(part < z, 3 - z, jnp.where(part > z, z, jnp.maximum(z, 3 - z)))

    def send_y(step, relay):
        part, j, slot = owner(step), lax.div(step, Z), lax.rem(step, SLOTS)
        copy = (y_relay if relay else y_copy)(part, j, slot)
        if relay:
            x_copy(2 * part + 1 - y, j, 0).wait_recv()
        else:
            product(2 * part + 1 - y, j)

        @pl.when(step >= SLOTS)
        def _():
            copy.wait_send()

        if not relay:
            y_out[slot] = to_low(tile[...])
        copy.start()

    def send_x(step):
        part, j, slot = lax.rem(step, 2 * Z), lax.div(step, 2 * Z), lax.rem(step, SLOTS)
        product(part, N_NEAR + j)

        @pl.when(step >= SLOTS)
        def _():
            x_copy(part, j, slot).wait_send()

        x_out[slot] = to_low(tile[...])
        x_copy(part, j, slot).start()

    def arriving(side, place, buffer):
        pltpu.make_async_remote_copy(
            z_out.at[0], land_ref.at[side, place], z_send.at[0], z_recv.at[side, place],
            device_id={"batch": b}, device_id_type=MESH,
        ).wait_recv()
        pltpu.make_async_copy(land_ref.at[side, place], z_in.at[buffer], sem.at[buffer]).start()

    def arrived(side, place, buffer):
        pltpu.make_async_copy(land_ref.at[side, place], z_in.at[buffer], sem.at[buffer]).wait()
        tile[...] += as_float(z_in[buffer])

    def keep(j):
        base = FRONT - 16 * b + jnp.where(b >= 4, 32, 0) + j * (CHUNK // LANES)

        def rows(first, count, start, column, stride):
            flat[pl.ds(start, count, stride=stride), :] = tile[first : first + count, column : column + LANES]

        @pl.when((b != 3) & (b != 7))
        def _():
            for c in range(CHUNK // LANES):
                rows(0, SLICE, base + c, c * LANES, 32)

        def row_at(first, start, column):
            flat[pl.ds(start, 1), :] = tile[first : first + 1, column : column + LANES]

        @pl.when(b == 3)
        def _():
            for c in range(CHUNK // LANES):
                start = FRONT + 11760 + j * (CHUNK // LANES) + c
                rows(0, 369, base + c, c * LANES, 32)
                rows(384, SLICE - 384, start, c * LANES, 32)
                row_at(376, start + 192 * 32, c * LANES)

        @pl.when(b == 7)
        def _():
            for c in range(CHUNK // LANES):
                rows(0, 177, base + c, c * LANES, 32)

            @pl.when(j < 3)
            def _():
                for c in range(2):
                    row_at(184, FRONT + 5584 + CONV * 6 + 2 * j + c, c * LANES)

            @pl.when(j < 15)
            def _():
                start = FRONT + 5584 + lax.rem(j, 5) * (384 * 6) + lax.div(j, 5) * 2
                for c in range(2):
                    rows(192, 384, start + c, c * LANES, 6)

            @pl.when(j == 15)
            def _():
                for p in range(3):
                    for c in range(2):
                        rows(192 + 128 * p, 128, FRONT + 5584 + 1920 * 6 + 2 * p + c, c * LANES, 6)

    def combine(part, j, o, relay):
        place = part * N_CHUNK + j
        above = (part <= z) & (z < Z - 1)
        below = (part >= z) & (z > 0)

        @pl.when(above)
        def _():
            arriving(0, place, 0)

        @pl.when(below)
        def _():
            arriving(1, place, 1)

        if relay:
            x_copy(2 * part + y, j, 0).wait_recv()
            copy = pltpu.make_async_copy(far_ref.at[(2 * part + y) * N_FAR + j], z_in.at[2], sem.at[2])
            copy.start()
            copy.wait()
            tile[...] = as_float(z_in[2])
        else:
            product(2 * part + y, j)
        y_copy(part, j, 0).wait_recv()
        tile[...] += as_float(y_in[part * N_NEAR + j])

        @pl.when(above)
        def _():
            arrived(0, place, 0)

        @pl.when(below)
        def _():
            arrived(1, place, 1)

        @pl.when(part == z)
        def _():
            if relay:

                @pl.when(j == 0)
                def _():
                    pl.semaphore_wait(hello, 1)

                @pl.when(j > 0)
                def _():
                    back_copy(j - 1).wait_send()

                z_out[Z - 1] = to_low(tile[...])
                back_copy(j).start()
            else:
                keep(j)

        @pl.when(part != z)
        def _():
            @pl.when(j > 0)
            def _():
                z_copy(part, j, o, True).wait_send()

            z_out[o] = to_low(tile[...])

            @pl.when(part < z)
            def _():
                z_copy(part, j, o, True).start()

            @pl.when(part > z)
            def _():
                z_copy(part, j, o, False).start()

    def rounds(chunks, relay):
        steps = Z * chunks

        def step_body(step, carry):
            @pl.when(step < steps)
            def _():
                send_y(step, relay)

            if not relay:

                @pl.when(step < 2 * Z * N_FAR)
                def _():
                    send_x(step)

            late = step - LAG
            part, o = owner(jnp.maximum(late, 0)), lax.rem(jnp.maximum(late, 0), Z)
            j = lax.div(jnp.maximum(late, 0), Z) - hops_to(part)

            @pl.when((late >= 0) & (j >= 0) & (j < chunks))
            def _():
                combine(part, j, o, relay)

            if not relay:
                turn = lax.div(step, TURN_EVERY)
                part, o = owner(turn), lax.rem(turn, Z)
                p = lax.div(turn, Z) - hops_to(part)

                @pl.when((lax.rem(step, TURN_EVERY) == 0) & (p >= 0) & (p < 2 * N_TURN))
                def _():
                    combine_turned(part, p, o)

            return carry

        count = steps + LAG + (Z - 1) * Z
        if not relay:
            count = max(count, TURN_EVERY * Z * (2 * N_TURN + Z - 1))
        lax.fori_loop(0, count, step_body, 0)
        for slot in range(SLOTS):
            (y_relay if relay else y_copy)(0, 0, slot).wait_send()
        for o in range(Z - 1):
            z_copy(0, 0, o, True).wait_send()
            if not relay:
                z_copy(0, 0, Z + o, True).wait_send()
        if not relay:
            for i in range(N_TURN):
                turn_copy(i).wait_send()

    @pl.when(section == 1)
    def _():
        loads = [
            pltpu.make_async_copy(source, target, load.at[i])
            for i, (source, target) in enumerate(
                [(xt_hbm, xt_ref), (x2t_hbm, x2t_ref), (gp_hbm, gp_ref)]
                + [
                    (source.at[half], g_ref.at[:, pl.ds((2 * layer + half) * CONV, CONV)])
                    for layer, source in enumerate((g0_hbm, g1_hbm))
                    for half in range(2)
                ]
            )
        ]
        for copy in loads:
            copy.start()
        barrier = pltpu.get_barrier_semaphore()
        pl.semaphore_signal(barrier, inc=1, device_id={"batch": b + 1 - 2 * y}, device_id_type=MESH)

        @pl.when(z > 0)
        def _():
            pl.semaphore_signal(barrier, inc=1, device_id={"batch": b - 2}, device_id_type=MESH)

        @pl.when(z < Z - 1)
        def _():
            pl.semaphore_signal(barrier, inc=1, device_id={"batch": b + 2}, device_id_type=MESH)

        pl.semaphore_wait(barrier, 2 + jnp.where(z > 0, 1, 0) + jnp.where(z < Z - 1, 1, 0))
        pl.semaphore_signal(hello, inc=1, device_id={"section": 3}, device_id_type=MESH)
        for copy in loads:
            copy.wait()
        flat[FRONT + share - 64 : FRONT + share, :] = jnp.zeros((64, LANES), F32)
        rounds(N_FIRST, False)
        for slot in range(SLOTS):
            x_copy(0, 0, slot).wait_send()

        def back(j, carry):
            back_copy(j).wait_recv()
            tile[...] = as_float(ret[j])
            keep(N_NEAR + j)
            return carry

        lax.fori_loop(0, N_FAR, back, 0)
        copy = pltpu.make_async_copy(flat.at[pl.ds(FRONT, share)], out_ref, sem.at[0])
        copy.start()
        copy.wait()

    @pl.when(section == 3)
    def _():
        rounds(N_FAR, True)
        back_copy(N_FAR - 1).wait_send()


def reduce_all(xt, x2t, g0, g1, gp, row, share):
    chunk = (SLICE, CHUNK)
    side = (SIDE_ROWS, LANES)
    dma = pltpu.SemaphoreType.DMA
    places = Z * N_CHUNK
    return pl.pallas_call(
        functools.partial(reduce_kernel, share),
        out_shape=[
            jax.ShapeDtypeStruct((share, LANES), F32),
            jax.ShapeDtypeStruct((2, places) + chunk, BF),
            jax.ShapeDtypeStruct((2 * Z * N_FAR,) + chunk, BF),
        ],
        in_specs=[hbm()] * 6,
        out_specs=[hbm()] * 3,
        scratch_shapes=[
            pltpu.VMEM(xt.shape, BF),
            pltpu.VMEM(x2t.shape, BF),
            pltpu.VMEM((gp.shape[0], 4 * CONV), BF),
            pltpu.VMEM(gp.shape, BF),
            dma((7,)),
            pltpu.VMEM(chunk, F32),
            pltpu.VMEM((SIDE_CHUNKS * SIDE_ROWS, LANES), F32),
            pltpu.VMEM((SLOTS,) + chunk, BF),
            pltpu.VMEM((Z * N_NEAR,) + chunk, BF),
            pltpu.VMEM((2 * Z - 1,) + chunk, BF),
            pltpu.VMEM((3,) + chunk, BF),
            pltpu.VMEM((SLOTS,) + chunk, BF),
            pltpu.VMEM((N_FAR,) + chunk, BF),
            pltpu.VMEM((N_TURN,) + chunk, BF),
            pltpu.VMEM((N_TURN,) + chunk, BF),
            dma((N_TURN,)),
            dma((N_TURN,)),
            dma((SLOTS,)),
            dma((Z * N_NEAR,)),
            dma((2 * Z - 1,)),
            dma((2, places)),
            dma((SLOTS,)),
            dma((2 * Z * N_FAR,)),
            dma,
            dma((N_FAR,)),
            pltpu.SemaphoreType.REGULAR,
            dma((3,)),
            pltpu.VMEM(side, BF),
            pltpu.VMEM((SIDE_CHUNKS,) + side, BF),
            pltpu.VMEM((SIDE_CHUNKS,) + side, BF),
            pltpu.VMEM((SIDE_CHUNKS,) + side, BF),
            dma((SIDE_CHUNKS,)),
            dma((SIDE_CHUNKS,)),
            dma((SIDE_CHUNKS,)),
            dma((SIDE_CHUNKS,)),
            dma,
            dma,
            dma,
            pltpu.SemaphoreType.REGULAR,
        ],
        compiler_params=pltpu.CompilerParams(
            collective_id=1, has_side_effects=True, vmem_limit_bytes=60 << 20
        ),
    )(xt, x2t, g0, g1, gp, row)


CNN_GRADS = (CONV // LANES) * LANES + TABLE_ROWS


def cnn_sum_kernel(in_ref, out_ref, low, y_in, z_in, send, recv):
    section = lax.axis_index("section")
    b = lax.axis_index("batch")
    y, z = lax.rem(b, 2), lax.div(b, 2)
    barrier = pltpu.get_barrier_semaphore()

    def along(target, other, i):
        return pltpu.make_async_remote_copy(
            low, target, send, recv.at[i], device_id={"batch": other}, device_id_type=MESH
        )

    @pl.when(section == 0)
    def _():
        pairs = [(y == 0, b + 1), (y == 1, b - 1), ((y == 0) & (z > 0), b - 2), ((y == 0) & (z < Z - 1), b + 2)]
        for condition, other in pairs:

            @pl.when(condition)
            def _():
                pl.semaphore_signal(barrier, inc=1, device_id={"batch": other}, device_id_type=MESH)

        pl.semaphore_wait(barrier, sum(jnp.where(condition, 1, 0) for condition, _ in pairs))
        out_ref[...] = in_ref[...]

        @pl.when(y == 1)
        def _():
            low[...] = to_low(out_ref[...])
            along(y_in, b - 1, 0).start()
            along(y_in, b - 1, 0).wait_send()

        @pl.when(y == 0)
        def _():
            along(y_in, b + 1, 0).wait_recv()
            out_ref[...] += as_float(y_in[...])

            @pl.when(z < Z - 1)
            def _():
                along(z_in, b + 2, 1).wait_recv()
                out_ref[...] += as_float(z_in[...])

            @pl.when(z > 0)
            def _():
                low[...] = to_low(out_ref[...])
                along(z_in, b - 2, 1).start()
                along(z_in, b - 2, 1).wait_send()


def cnn_sum(grads):
    low = pltpu.VMEM((CNN_GRADS, LANES), BF)
    dma = pltpu.SemaphoreType.DMA
    return pl.pallas_call(
        cnn_sum_kernel,
        out_shape=jax.ShapeDtypeStruct((CNN_GRADS, LANES), F32),
        in_specs=[vmem()],
        out_specs=vmem(),
        scratch_shapes=[
            low,
            low,
            low,
            dma,
            dma((2,)),
        ],
        compiler_params=pltpu.CompilerParams(
            collective_id=3, has_side_effects=True, vmem_limit_bytes=24 << 20
        ),
    )(grads)


PIECES = 19


def assemble_kernel(cnn_ref, total_ref, out_ref, buffer, fetch, store):
    section = lax.axis_index("section")
    rows = out_ref.shape[0] // PIECES

    def part(i):
        return pl.ds(i * rows, rows)

    for i in range(PIECES):
        pltpu.make_async_copy(total_ref.at[part(i)], buffer.at[part(i)], fetch.at[i]).start()
    for i in range(PIECES):
        pltpu.make_async_copy(total_ref.at[part(i)], buffer.at[part(i)], fetch.at[i]).wait()
        pltpu.make_async_copy(buffer.at[part(i)], out_ref.at[part(i)], store.at[i]).start()
    for i in range(PIECES):
        pltpu.make_async_copy(buffer.at[part(i)], out_ref.at[part(i)], store.at[i]).wait()

    @pl.when((section == 0) & (lax.axis_index("batch") == 0))
    def _():
        head = buffer.at[pl.ds(0, CNN_ROWS)]
        for copy in (
            pltpu.make_async_copy(cnn_ref, head, fetch.at[0]),
            pltpu.make_async_copy(head, out_ref.at[pl.ds(0, CNN_ROWS)], store.at[0]),
        ):
            copy.start()
            copy.wait()


def assemble(cnn, total):
    return pl.pallas_call(
        assemble_kernel,
        out_shape=jax.ShapeDtypeStruct(total.shape, F32),
        in_specs=[hbm()] * 2,
        out_specs=hbm(),
        scratch_shapes=[
            pltpu.VMEM(total.shape, F32),
            pltpu.SemaphoreType.DMA((PIECES,)),
            pltpu.SemaphoreType.DMA((PIECES,)),
        ],
        compiler_params=pltpu.CompilerParams(vmem_limit_bytes=60 << 20),
    )(cnn, total)


def on_section(numbers, function, *operands):
    shapes = jax.eval_shape(function, *operands)
    leaves, tree = jax.tree.flatten(shapes)

    def idle(*unused):
        return jax.tree.unflatten(
            tree,
            pl.pallas_call(
                lambda *refs: None,
                out_shape=[jax.ShapeDtypeStruct(s.shape, s.dtype) for s in leaves],
                out_specs=[hbm()] * len(leaves),
            )(),
        )

    section = lax.axis_index("section")
    here = sum(jnp.where(section == n, 1, 0) for n in numbers) > 0
    return lax.cond(here, function, idle, *operands)


def shards(char_ids, word_lengths, params, cotangent):
    section = lax.axis_index("section")
    n_batch = lax.axis_size("batch")
    words_all = lax.all_gather(
        jnp.concatenate([char_ids, word_lengths[:, None]], axis=1), "section", axis=0, tiled=True
    )
    params, words_all = lax.optimization_barrier((params, words_all))
    ck, tt = cnn_params(params)
    group = words_all.shape[0]
    quarter, words, half = group // 4, group // len(CNN), group // 2
    ids_all, column_all = words_all[:, :CHAR_LEN], words_all[:, CHAR_LEN:]
    row_all = column_all.T
    ends_all = stage_bounds(column_all, len(CNN))
    place = jnp.maximum(section - 1, 0)

    def mine(array, axis=0):
        return lax.dynamic_slice_in_dim(array, place * words, words, axis)

    pooled_part = on_section(
        CNN, chars_forward, ends_all[place], mine(ids_all), mine(column_all), mine(row_all, 1), ck, tt
    )
    pooled, cot, w0, w1, wp, vec = start_highways(params, pooled_part, cotangent)
    params, pooled = lax.optimization_barrier((params, pooled))
    encoder_weights = start_encoder(params)
    pooled, encoder_weights = lax.optimization_barrier((pooled, encoder_weights))
    projected, x1, x2, *kept = on_section((1,), highway_forward, w0, w1, wp, vec, pooled)
    (encoder_in,) = hand_over(
        6, [(1, 2, 0, 0, half, 0, 0), (1, 3, 0, half, half, 0, 0)], [projected], [((half, D), BF)]
    )
    x2, encoder_in = lax.optimization_barrier((x2, encoder_in))
    xt, x2t = stack_highways(pooled, x1, x2)
    encoder_in, xt = lax.optimization_barrier((encoder_in, xt))
    layer, back, joined, mixed, att, normed, activated, inner, branch, sums = on_section(
        (2, 3), encoder, encoder_in, cot, *encoder_weights
    )
    items = [(2, 1, 0, 0, half, 0, 0), (3, 1, 0, 0, half, 0, half)]
    items += [(2 + s // 2, s, 1, s % 2 * quarter, quarter, 1, 0) for s in range(4)]
    items += [(3 if k < 4 else 2, 2 if k < 4 else 3, 2 + k, 0, half, 2 + k, 0) for k in range(8)]
    items += [(2, 3, 10, 0, 8, 10, 0), (3, 2, 10, 0, 8, 10, 0)]
    own_rows = [encoder_in, mixed, joined, att, normed, activated, inner, branch, sums]
    grad_highway, layer_out, *other_rows = hand_over(
        7,
        items,
        [back, layer, *own_rows],
        [((group, D), BF), ((quarter, D), BF)] + [(value.shape, value.dtype) for value in own_rows],
        late=(2,),
    )
    grad_pooled, grad0, grad1 = on_section(
        (1,), highway_backward, w0, w1, wp, pooled, x1, *kept, grad_highway
    )
    (grad_part,) = hand_over(8, [(1, 0, 0, 0, group, 0, 0)], [grad_pooled], [((group, CONV), BF)])
    other_rows, grad_part = lax.optimization_barrier((other_rows, grad_part))
    side = side_rows(own_rows, other_rows)
    share = params.shape[1] // n_batch // LANES
    by_kernels = n_batch == 2 * Z and share == SIDE_SHARE
    if by_kernels:
        total, *_ = reduce_all(xt, x2t, grad0, grad1, grad_highway, side, share)
        grad_part, total = lax.optimization_barrier((grad_part, total))
    cnn_part = on_section((0,), chars_backward, ends_all, ids_all, column_all, row_all, ck, tt, grad_part)
    if not by_kernels:
        return (layer_out, summed_rows(params.shape[1], cnn_part, pooled, x1, x2, grad0, grad1, grad_highway, side))
    cnn_total = cnn_sum(cnn_part)

    def first_row(grads):
        flat = cnn_gradient(grads)
        return jnp.pad(flat, (0, CNN_ROWS * LANES - flat.shape[0])).reshape(-1, LANES)

    cnn_row = on_section((0,), first_row, cnn_total)
    total = assemble(cnn_row, total)
    return (layer_out, total.reshape(1, -1))


def summed_rows(size, cnn_part, pooled, x1, x2, grad0, grad1, grad_highway, side):
    first = lax.axis_index("batch") == 0
    cnn_flat = cnn_gradient(lax.psum(jnp.where(lax.axis_index("section") == 0, cnn_part, 0.0), ("section", "batch")))

    def wide(flat):
        return jnp.pad(as_float(flat), (0, size - flat.shape[0]))

    def highways():
        ones = jnp.ones((1, pooled.shape[0]), BF)
        pieces = []
        both = [jnp.concatenate([grad[0], grad[1]], axis=1) for grad in (grad0, grad1)]
        for x, g in ((pooled, both[0]), (x1, both[1]), (x2, grad_highway)):
            pieces += [matmul_tn(x, g).reshape(-1), matmul(ones, g).reshape(-1)]
        return wide(jnp.concatenate(pieces))

    row = lax.switch(
        lax.axis_index("section"),
        [
            lambda: wide(jnp.where(first, cnn_flat, 0.0)),
            highways,
            lambda: wide(side.reshape(-1)),
            lambda: wide(side.reshape(-1)),
        ],
    )
    return lax.psum_scatter(row, "batch", scatter_dimension=0, tiled=True).reshape(1, -1)


def solution(mesh):
    return jax.shard_map(
        shards,
        mesh=mesh,
        in_specs=(
            P(("section", "batch"), None),
            P(("section", "batch")),
            P("section", None),
            P(("section", "batch"), None),
        ),
        out_specs=(P(("section", "batch"), None), P("section", "batch")),
        check_vma=False,
    )
```
